32 devices in a mesh: groups: 2 (over x), dp: 16 (over z, y, core).
Axes of the slice: x: 2, y: 2, z: 4, core: 2. Of those that a mesh axis runs over, the one named last changes fastest.
Arguments:
- logits: bfloat16 [64, 32000], P(('groups', 'dp')), parts along dimension 0, may hold values from -4 to 152
- embed: bfloat16 [32000, 4096], P('dp'), may hold values from -512 to 512
- norm_gain: bfloat16 [4096], replicated, may hold values from 0.25 to 1.75
- w_gate: bfloat16 [4096, 14336], P(None, 'dp'), may hold values from -0.09375 to 0.09375
- w_up: bfloat16 [4096, 14336], P(None, 'dp'), may hold values from -0.09375 to 0.09375
- w_down: bfloat16 [14336, 4096], P('dp'), may hold values from -0.046875 to 0.046875
- head: bfloat16 [4096], replicated, may hold values from -0.09375 to 0.09375
- counts: int32 [8], P('groups'), parts along dimension 0, may hold values from 2 to 8, as said below
Outputs:
- guidance: bfloat16 [64, 32000], P(('groups', 'dp')), parts along dimension 0
- rewards: float32 [8], P('groups'), parts along dimension 0
The draws below stay inside these ranges and needn't reach their ends.
There are 2 independent parts, one for each index of `groups`. The reference program is written for one: setup_inputs(seed, part) draws one part's arguments, and reference() takes and returns one part's arrays. A program takes and returns all parts, laid end to end along the dimension named above; an argument that names none is the same for every part. Nothing has to cross between parts.
Inputs may be any that keep to these rules, and one draw needn't show every extreme that they name: `counts`: some request is full in every draw.
All inputs are finite; a program needn't handle non-finite values.
Results may differ from the reference program's by a relative error of at most 0.0095.
Values may be sent and summed in bfloat16 or wider, within the bound.
No kernel may reach another device: no remote copies, remote signals or barrier semaphores. Data moves between devices by JAX's collectives and lax.ppermute only.
A program may use at most 128 MiB of HBM per device.

```python
import math
import jax
import jax.numpy as jnp
from jax import lax

D = 4096
FF = 14336
VOC = 32000
REQS = 4
TOKENS = 32
LEN = 8


def draw_logits(key, part):
    key = jax.random.fold_in(key, 11)
    first = jax.random.fold_in(key, 0)
    base = jax.random.normal(first, (TOKENS, VOC), jnp.float32)
    return jnp.clip(base, -4.0, 4.0).astype(jnp.bfloat16)


def draw_counts(key, part):
    key = jax.random.fold_in(key, 23)
    first, second = jax.random.split(key)
    drawn = jax.random.randint(first, (REQS,), LEN // 4, LEN + 1)
    chosen = jax.random.randint(second, (), 0, REQS)
    return jnp.where(jnp.arange(REQS) == chosen, LEN, drawn).astype(jnp.int32)


def levels(rng, extent, cuts, least, top_value):
    def one(dim, blocks):
        steps = jax.random.uniform(jax.random.fold_in(jax.random.fold_in(rng, 6), dim), (blocks,), jnp.float32, least / len(cuts), top_value / len(cuts))
        return jnp.repeat(jnp.exp(steps), extent[dim] // blocks).reshape((-1,) + (1,) * (len(extent) - dim - 1))

    gain = one(*cuts[0])
    for cut in cuts[1:]:
        gain = gain * one(*cut)
    return gain


def noise(key, dims, scale, bound, shards=(), kind=jnp.bfloat16):
    values = scale * jax.random.normal(key, dims, jnp.float32)
    if shards:
        values = values * levels(key, dims, shards, -0.22, 0.18)
    return jnp.clip(values, -bound, bound).astype(kind)


def setup_inputs(seed: int = 0, part: int = 0) -> dict:
    splits = jax.random.split(jax.random.key(seed), 9)
    part_keys = jax.random.split(jax.random.fold_in(splits[8], part), 9)
    logits = draw_logits(jax.random.fold_in(jax.random.fold_in(splits[8], part), 71), part)
    embed = noise(splits[1], (VOC, D), (VOC ** 0.5 / 2), 512.0, ((0, 16),))
    norm_gain = jnp.clip(1.0 + 0.15 * jax.random.normal(splits[2], (D,), jnp.float32), 0.25, 1.75).astype(jnp.bfloat16)
    w_gate = noise(splits[3], (D, FF), D ** -0.5, 0.09375, ((1, 16),))
    w_up = noise(splits[4], (D, FF), D ** -0.5, 0.09375, ((1, 16),))
    w_down = noise(splits[5], (FF, D), FF ** -0.5, 0.046875, ((0, 16),))
    head = noise(splits[6], (D,), D ** -0.5, 0.09375)
    counts = draw_counts(jax.random.fold_in(jax.random.fold_in(splits[8], part), 71), part)
    return {"logits": logits, "embed": embed, "norm_gain": norm_gain, "w_gate": w_gate, "w_up": w_up, "w_down": w_down, "head": head, "counts": counts}


def reference(logits, embed, norm_gain, w_gate, w_up, w_down, head, counts):
    f32 = jnp.float32
    probs32 = jax.nn.softmax(logits.astype(f32), axis=-1)
    probs = probs32.astype(jnp.bfloat16)
    x0 = jnp.dot(probs, embed, preferred_element_type=f32)
    inv = lax.rsqrt(lax.optimization_barrier(jnp.mean(x0 * x0, axis=-1, keepdims=True)) + 1e-05)
    gain32 = norm_gain.astype(f32)
    normed = (x0 * inv * gain32).astype(jnp.bfloat16)
    a_gate = jnp.dot(normed, w_gate, preferred_element_type=f32)
    b_up = jnp.dot(normed, w_up, preferred_element_type=f32)
    sigma = jax.nn.sigmoid(a_gate)
    active = a_gate * sigma
    hidden = (active * b_up).astype(jnp.bfloat16)
    head32 = head.astype(f32)
    branch = jnp.dot(hidden, w_down, preferred_element_type=f32)
    score = jnp.dot(x0 + branch, head32, precision=lax.Precision.HIGHEST)
    position = jnp.arange(TOKENS, dtype=jnp.int32)
    request = position // LEN
    member = request[:, None] == jnp.arange(REQS, dtype=jnp.int32)[None, :]
    limit = lax.optimization_barrier(jnp.sum(jnp.where(member, counts[None, :], 0), axis=-1))
    valid = (position % LEN < limit).astype(f32)
    rewards = jnp.dot(valid * score, member.astype(f32), precision=lax.Precision.HIGHEST) / counts.astype(f32)
    upstream = (valid[:, None] * head32[None, :]).astype(jnp.bfloat16)
    d_hidden = jnp.dot(upstream, w_down.T, preferred_element_type=f32)
    d_gate = (d_hidden * b_up * sigma * (1.0 + a_gate * (1.0 - sigma))).astype(jnp.bfloat16)
    d_up = (d_hidden * active).astype(jnp.bfloat16)
    d_normed = jnp.dot(d_gate, w_gate.T, preferred_element_type=f32) + jnp.dot(d_up, w_up.T, preferred_element_type=f32)
    scaled = d_normed * gain32
    d_input = inv * scaled - x0 * inv * inv * inv * lax.optimization_barrier(jnp.mean(scaled * x0, axis=-1, keepdims=True)) + valid[:, None] * head32[None, :]
    d_input = d_input.astype(jnp.bfloat16)
    d_probs = jnp.dot(d_input, embed.T, preferred_element_type=f32)
    d_logits = probs32 * (d_probs - lax.optimization_barrier(jnp.sum(probs32 * d_probs, axis=-1, keepdims=True)))
    guidance = (math.sqrt(VOC) * d_logits).astype(jnp.bfloat16)
    return (guidance, rewards)
```

```python
import math

import jax
import jax.numpy as jnp
from jax import lax
from jax.sharding import PartitionSpec as P

VOC = 32000


def exchange(blocks):
    return lax.all_to_all(blocks, "dp", split_axis=0, concat_axis=0, tiled=True)


def split3(value):
    hi = lax.reduce_precision(value, 8, 7)
    rest = value - hi
    mid = lax.reduce_precision(rest, 8, 7)
    low = rest - mid
    return jnp.stack([hi, mid, low], axis=-1).astype(jnp.bfloat16)


def all_sum(part, devices):
    tokens, width = part.shape
    own = width // devices
    blocks = part.reshape(tokens, devices, own).transpose(1, 0, 2)
    mine = jnp.sum(exchange(blocks).astype(jnp.float32), axis=0).astype(jnp.bfloat16)
    whole = exchange(jnp.broadcast_to(mine[None], (devices, tokens, own)))
    return whole.transpose(1, 0, 2).reshape(tokens, width).astype(jnp.float32)


def body(logits, embed, norm_gain, w_gate, w_up, w_down, head, counts):
    f32, bf16 = jnp.float32, jnp.bfloat16
    devices = lax.axis_size("dp")
    rows, voc = logits.shape
    part = voc // devices
    requests = counts.shape[0]
    total = rows * devices
    request_len = total // requests
    gain32 = norm_gain.astype(f32)
    head32 = head.astype(f32)
    probs32 = jax.nn.softmax(logits.astype(f32), axis=-1)
    probs = probs32.astype(bf16)
    slices = exchange(probs.reshape(rows, devices, part).transpose(1, 0, 2)).reshape(total, part)
    down_head = jnp.sum(w_down.astype(f32) * head32[None, :], axis=-1)
    position = jnp.arange(total, dtype=jnp.int32)
    member = (position // request_len)[:, None] == jnp.arange(requests, dtype=jnp.int32)[None, :]
    limit = jnp.sum(jnp.where(member, counts[None, :], 0), axis=-1)
    valid = (position % request_len < limit).astype(f32)
    partial_value = jnp.dot(slices, embed, preferred_element_type=f32)
    score_x = jnp.sum(partial_value * head32[None, :], axis=-1)
    x0 = all_sum(partial_value.astype(bf16), devices)
    inv = lax.rsqrt(jnp.mean(x0 * x0, axis=-1, keepdims=True) + 1e-05)
    normed = (x0 * inv * gain32).astype(bf16)
    a_gate = jnp.dot(normed, w_gate, preferred_element_type=f32)
    b_up = jnp.dot(normed, w_up, preferred_element_type=f32)
    sigma = jax.nn.sigmoid(a_gate)
    active = a_gate * sigma
    hidden = (active * b_up).astype(bf16).astype(f32)
    d_hidden = valid[:, None] * down_head[None, :]
    d_gate = (d_hidden * b_up * sigma * (1.0 + a_gate * (1.0 - sigma))).astype(bf16)
    d_up = (d_hidden * active).astype(bf16)
    score = score_x + jnp.sum(hidden * down_head[None, :], axis=-1)
    own_rewards = jnp.sum(jnp.where(member, (valid * score)[:, None], 0.0), axis=0)
    d_part = jnp.einsum("tf,df->td", d_gate, w_gate, preferred_element_type=f32)
    d_part = d_part + jnp.einsum("tf,df->td", d_up, w_up, preferred_element_type=f32)
    d_normed = all_sum(d_part.astype(bf16), devices)
    scaled = d_normed * gain32
    d_input = inv * scaled - x0 * inv * inv * inv * jnp.mean(scaled * x0, axis=-1, keepdims=True)
    d_input = (d_input + valid[:, None] * head32[None, :]).astype(bf16)
    d_slices = jnp.einsum("td,vd->tv", d_input, embed, preferred_element_type=f32).astype(bf16)
    extra = split3(own_rewards).reshape(1, 1, requests * 3)
    extra = jnp.broadcast_to(extra, (devices, rows, requests * 3))
    back = exchange(jnp.concatenate([d_slices.reshape(devices, rows, part), extra], axis=-1))
    sums = jnp.sum(back[:, 0, part:].astype(f32).reshape(devices, requests, 3), axis=(0, 2))
    rewards = sums / counts.astype(f32)
    d_probs = back[:, :, :part].transpose(1, 0, 2).reshape(rows, voc).astype(f32)
    d_logits = probs32 * (d_probs - jnp.sum(probs32 * d_probs, axis=-1, keepdims=True))
    guidance = (math.sqrt(VOC) * d_logits).astype(bf16)
    return (guidance, rewards)


def solution(mesh):
    placed = (
        P(("groups", "dp"), None),
        P("dp", None),
        P(),
        P(None, "dp"),
        P(None, "dp"),
        P("dp", None),
        P(),
        P("groups"),
    )
    return jax.shard_map(
        body,
        mesh=mesh,
        in_specs=placed,
        out_specs=(P(("groups", "dp"), None), P("groups")),
        check_vma=False,
    )
```

```python
import math

import jax
import jax.numpy as jnp
from jax import lax
from jax.sharding import PartitionSpec as P

VOC = 32000


def exchange(blocks):
    return lax.all_to_all(blocks, "dp", split_axis=0, concat_axis=0, tiled=True)


def split3(value):
    hi = lax.reduce_precision(value, 8, 7)
    rest = value - hi
    mid = lax.reduce_precision(rest, 8, 7)
    low = rest - mid
    return jnp.stack([hi, mid, low], axis=-1).astype(jnp.bfloat16)


def swap(value, mask, devices):
    return lax.ppermute(value, "dp", [(i, i ^ mask) for i in range(devices)])


def pick(blocks, index):
    return lax.dynamic_index_in_dim(blocks, index, 0, keepdims=False)


def gather_doubling(mine, devices):
    rank = lax.axis_index("dp")
    held = mine[None]
    mask = devices // 2
    while mask:
        got = swap(held, mask, devices)
        upper = (rank & mask) != 0
        held = jnp.where(upper, jnp.concatenate([got, held]), jnp.concatenate([held, got]))
        mask //= 2
    return held


def reverse_bits(value, devices):
    bits = devices.bit_length() - 1
    return sum(((value >> i) & 1) << (bits - 1 - i) for i in range(bits))


def all_sum(part, devices):
    tokens, width = part.shape
    own = width // devices
    blocks = part.reshape(tokens, devices, own).transpose(1, 0, 2)
    blocks = jnp.stack([blocks[reverse_bits(r, devices)] for r in range(devices)])
    mine = jnp.sum(exchange(blocks).astype(jnp.float32), axis=0).astype(jnp.bfloat16)
    whole = gather_doubling(mine, devices)
    return whole.transpose(1, 0, 2).reshape(tokens, width).astype(jnp.float32)


def all_sum_chips(part, devices):
    tokens, width = part.shape
    own = width // devices
    chips = devices // 2
    rank = lax.axis_index("dp")
    core, chip = rank % 2, rank // 2
    blocks = part.reshape(tokens, 2, chips, own).transpose(1, 2, 0, 3)
    got = swap(pick(blocks, 1 - core), 1, devices)
    half = (pick(blocks, core).astype(jnp.float32) + got.astype(jnp.float32)).astype(jnp.bfloat16)
    total = pick(half, chip).astype(jnp.float32)
    arrived = [swap(pick(half, chip ^ s), 2 * s, devices) for s in range(1, chips)]
    for block in arrived:
        total = total + block.astype(jnp.float32)
    mine = total.astype(jnp.bfloat16)
    held = jnp.stack([mine] + [swap(mine, 2 * s, devices) for s in range(1, chips)])
    held = jnp.stack([pick(held, chip ^ s) for s in range(chips)])
    got = swap(held, 1, devices)
    whole = jnp.where(core == 1, jnp.stack([got, held]), jnp.stack([held, got]))
    return whole.reshape(devices, tokens, own).transpose(1, 0, 2).reshape(tokens, width).astype(jnp.float32)


def body(logits, embed, norm_gain, w_gate, w_up, w_down, head, counts):
    f32, bf16 = jnp.float32, jnp.bfloat16
    devices = lax.axis_size("dp")
    rows, voc = logits.shape
    part = voc // devices
    requests = counts.shape[0]
    total = rows * devices
    request_len = total // requests
    gain32 = norm_gain.astype(f32)
    head32 = head.astype(f32)
    probs32 = jax.nn.softmax(logits.astype(f32), axis=-1)
    probs = probs32.astype(bf16)
    slices = exchange(probs.reshape(rows, devices, part).transpose(1, 0, 2)).reshape(total, part)
    down_head = jnp.sum(w_down.astype(f32) * head32[None, :], axis=-1)
    position = jnp.arange(total, dtype=jnp.int32)
    member = (position // request_len)[:, None] == jnp.arange(requests, dtype=jnp.int32)[None, :]
    limit = jnp.sum(jnp.where(member, counts[None, :], 0), axis=-1)
    valid = (position % request_len < limit).astype(f32)
    partial_value = jnp.dot(slices, embed, preferred_element_type=f32)
    score_x = jnp.sum(partial_value * head32[None, :], axis=-1)
    x0 = all_sum(partial_value.astype(bf16), devices)
    inv = lax.rsqrt(jnp.mean(x0 * x0, axis=-1, keepdims=True) + 1e-05)
    normed = (x0 * inv * gain32).astype(bf16)
    a_gate = jnp.dot(normed, w_gate, preferred_element_type=f32)
    b_up = jnp.dot(normed, w_up, preferred_element_type=f32)
    sigma = jax.nn.sigmoid(a_gate)
    active = a_gate * sigma
    hidden = (active * b_up).astype(bf16).astype(f32)
    d_hidden = valid[:, None] * down_head[None, :]
    d_gate = (d_hidden * b_up * sigma * (1.0 + a_gate * (1.0 - sigma))).astype(bf16)
    d_up = (d_hidden * active).astype(bf16)
    score = score_x + jnp.sum(hidden * down_head[None, :], axis=-1)
    own_rewards = jnp.sum(jnp.where(member, (valid * score)[:, None], 0.0), axis=0)
    d_part = jnp.einsum("tf,df->td", d_gate, w_gate, preferred_element_type=f32)
    d_part = d_part + jnp.einsum("tf,df->td", d_up, w_up, preferred_element_type=f32)
    d_normed = all_sum_chips(d_part.astype(bf16), devices)
    scaled = d_normed * gain32
    d_input = inv * scaled - x0 * inv * inv * inv * jnp.mean(scaled * x0, axis=-1, keepdims=True)
    d_input = (d_input + valid[:, None] * head32[None, :]).astype(bf16)
    d_slices = jnp.einsum("td,vd->tv", d_input, embed, preferred_element_type=f32).astype(bf16)
    extra = split3(own_rewards).reshape(1, 1, requests * 3)
    extra = jnp.broadcast_to(extra, (devices, rows, requests * 3))
    back = exchange(jnp.concatenate([d_slices.reshape(devices, rows, part), extra], axis=-1))
    sums = jnp.sum(back[:, 0, part:].astype(f32).reshape(devices, requests, 3), axis=(0, 2))
    rewards = sums / counts.astype(f32)
    d_probs = back[:, :, :part].transpose(1, 0, 2).reshape(rows, voc).astype(f32)
    d_logits = probs32 * (d_probs - jnp.sum(probs32 * d_probs, axis=-1, keepdims=True))
    guidance = (math.sqrt(VOC) * d_logits).astype(bf16)
    return (guidance, rewards)


def solution(mesh):
    placed = (
        P(("groups", "dp"), None),
        P("dp", None),
        P(),
        P(None, "dp"),
        P(None, "dp"),
        P("dp", None),
        P(),
        P("groups"),
    )
    return jax.shard_map(
        body,
        mesh=mesh,
        in_specs=placed,
        out_specs=(P(("groups", "dp"), None), P("groups")),
        check_vma=False,
    )
```

```python
import math

import jax
import jax.numpy as jnp
from jax import lax
from jax.sharding import PartitionSpec as P

VOC = 32000


def exchange(blocks):
    return lax.all_to_all(blocks, "dp", split_axis=0, concat_axis=0, tiled=True)


def split3(value):
    hi = lax.reduce_precision(value, 8, 7)
    rest = value - hi
    mid = lax.reduce_precision(rest, 8, 7)
    low = rest - mid
    return jnp.stack([hi, mid, low], axis=-1).astype(jnp.bfloat16)


def swap_cores(value, devices):
    return lax.ppermute(value, "dp", [(i, i ^ 1) for i in range(devices)])


def exchange_chips(blocks, devices):
    groups = [list(range(core, devices, 2)) for core in range(2)]
    return lax.all_to_all(
        blocks, "dp", split_axis=0, concat_axis=0, axis_index_groups=groups, tiled=True
    )


def pick(blocks, index):
    return lax.dynamic_index_in_dim(blocks, index, 0, keepdims=False)


def all_sum(part, devices):
    tokens, width = part.shape
    own = width // devices
    chips = devices // 2
    core = lax.axis_index("dp") % 2
    blocks = part.reshape(tokens, 2, chips, own).transpose(1, 2, 0, 3)
    got = swap_cores(pick(blocks, 1 - core), devices)
    half = (pick(blocks, core).astype(jnp.float32) + got.astype(jnp.float32)).astype(jnp.bfloat16)
    arrived = exchange_chips(half, devices)
    mine = jnp.sum(arrived.astype(jnp.float32), axis=0).astype(jnp.bfloat16)
    held = exchange_chips(jnp.broadcast_to(mine[None], (chips, tokens, own)), devices)
    got = swap_cores(held, devices)
    whole = jnp.where(core == 1, jnp.stack([got, held]), jnp.stack([held, got]))
    return whole.reshape(devices, tokens, own).transpose(1, 0, 2).reshape(tokens, width).astype(jnp.float32)


def body(logits, embed, norm_gain, w_gate, w_up, w_down, head, counts):
    f32, bf16 = jnp.float32, jnp.bfloat16
    devices = lax.axis_size("dp")
    rows, voc = logits.shape
    part = voc // devices
    requests = counts.shape[0]
    total = rows * devices
    request_len = total // requests
    gain32 = norm_gain.astype(f32)
    head32 = head.astype(f32)
    probs32 = jax.nn.softmax(logits.astype(f32), axis=-1)
    probs = probs32.astype(bf16)
    slices = exchange(probs.reshape(rows, devices, part).transpose(1, 0, 2)).reshape(total, part)
    down_head = jnp.sum(w_down.astype(f32) * head32[None, :], axis=-1)
    position = jnp.arange(total, dtype=jnp.int32)
    member = (position // request_len)[:, None] == jnp.arange(requests, dtype=jnp.int32)[None, :]
    limit = jnp.sum(jnp.where(member, counts[None, :], 0), axis=-1)
    valid = (position % request_len < limit).astype(f32)
    partial_value = jnp.dot(slices, embed, preferred_element_type=f32)
    score_x = jnp.sum(partial_value * head32[None, :], axis=-1)
    x0 = all_sum(partial_value.astype(bf16), devices)
    inv = lax.rsqrt(jnp.mean(x0 * x0, axis=-1, keepdims=True) + 1e-05)
    normed = (x0 * inv * gain32).astype(bf16)
    a_gate = jnp.dot(normed, w_gate, preferred_element_type=f32)
    b_up = jnp.dot(normed, w_up, preferred_element_type=f32)
    sigma = jax.nn.sigmoid(a_gate)
    active = a_gate * sigma
    hidden = (active * b_up).astype(bf16).astype(f32)
    d_hidden = valid[:, None] * down_head[None, :]
    d_gate = (d_hidden * b_up * sigma * (1.0 + a_gate * (1.0 - sigma))).astype(bf16)
    d_up = (d_hidden * active).astype(bf16)
    score = score_x + jnp.sum(hidden * down_head[None, :], axis=-1)
    own_rewards = jnp.sum(jnp.where(member, (valid * score)[:, None], 0.0), axis=0)
    d_part = jnp.einsum("tf,df->td", d_gate, w_gate, preferred_element_type=f32)
    d_part = d_part + jnp.einsum("tf,df->td", d_up, w_up, preferred_element_type=f32)
    d_normed = all_sum(d_part.astype(bf16), devices)
    scaled = d_normed * gain32
    d_input = inv * scaled - x0 * inv * inv * inv * jnp.mean(scaled * x0, axis=-1, keepdims=True)
    d_input = (d_input + valid[:, None] * head32[None, :]).astype(bf16)
    d_slices = jnp.einsum("td,vd->tv", d_input, embed, preferred_element_type=f32).astype(bf16)
    extra = split3(own_rewards).reshape(1, 1, requests * 3)
    extra = jnp.broadcast_to(extra, (devices, rows, requests * 3))
    back = exchange(jnp.concatenate([d_slices.reshape(devices, rows, part), extra], axis=-1))
    sums = jnp.sum(back[:, 0, part:].astype(f32).reshape(devices, requests, 3), axis=(0, 2))
    rewards = sums / counts.astype(f32)
    d_probs = back[:, :, :part].transpose(1, 0, 2).reshape(rows, voc).astype(f32)
    d_logits = probs32 * (d_probs - jnp.sum(probs32 * d_probs, axis=-1, keepdims=True))
    guidance = (math.sqrt(VOC) * d_logits).astype(bf16)
    return (guidance, rewards)


def solution(mesh):
    placed = (
        P(("groups", "dp"), None),
        P("dp", None),
        P(),
        P(None, "dp"),
        P(None, "dp"),
        P("dp", None),
        P(),
        P("groups"),
    )
    return jax.shard_map(
        body,
        mesh=mesh,
        in_specs=placed,
        out_specs=(P(("groups", "dp"), None), P("groups")),
        check_vma=False,
    )
```

```python
import functools
import math

import jax
import jax.numpy as jnp
from jax import lax
from jax.experimental import pallas as pl
from jax.experimental.pallas import tpu as pltpu
from jax.sharding import PartitionSpec as P

VOC = 32000
F32, BF16 = jnp.float32, jnp.bfloat16
VMEM_BYTES = 12 * 1024 * 1024


def swap_cores(value, devices):
    return lax.ppermute(value, "dp", [(i, i ^ 1) for i in range(devices)])


def exchange(blocks):
    return lax.all_to_all(blocks, "dp", split_axis=0, concat_axis=0, tiled=True)


def exchange_chips(blocks, devices):
    groups = [list(range(core, devices, 2)) for core in range(2)]
    return lax.all_to_all(
        blocks, "dp", split_axis=0, concat_axis=0, axis_index_groups=groups, tiled=True
    )


def split3(value):
    hi = lax.reduce_precision(value, 8, 7)
    rest = value - hi
    mid = lax.reduce_precision(rest, 8, 7)
    low = rest - mid
    return jnp.stack([hi, mid, low], axis=-1).astype(BF16)


def call(kernel, outs, *args, resident=(), flops=0, scratch=()):
    size = sum(math.prod(a.shape) * a.dtype.itemsize for a in args)
    args = [
        pltpu.with_memory_space_constraint(a, pltpu.VMEM) if i in resident else a
        for i, a in enumerate(args)
    ]
    return pl.pallas_call(
        kernel,
        out_shape=outs,
        in_specs=[pl.BlockSpec(memory_space=pltpu.VMEM)] * len(args),
        out_specs=[pl.BlockSpec(memory_space=pltpu.VMEM)] * len(outs),
        scratch_shapes=list(scratch),
        compiler_params=pltpu.CompilerParams(vmem_limit_bytes=VMEM_BYTES),
        cost_estimate=pl.CostEstimate(flops=flops, bytes_accessed=size, transcendentals=0),
    )(*args)


def resident_kernel(source_ref, after_ref, out_ref, sems):
    del after_ref
    count = sems.shape[0]
    rows = source_ref.shape[0] // count
    copies = [
        pltpu.make_async_copy(
            source_ref.at[pl.ds(i * rows, rows)], out_ref.at[pl.ds(i * rows, rows)], sems.at[i]
        )
        for i in range(count)
    ]
    for copy in copies:
        copy.start()
    for copy in copies:
        copy.wait()


def make_resident(source, after):
    count = next(c for c in (5, 1) if source.shape[0] % (16 * c) == 0 or c == 1)
    return pl.pallas_call(
        resident_kernel,
        out_shape=pltpu.VMEM(source.shape, source.dtype),
        in_specs=[pl.BlockSpec(memory_space=pltpu.HBM), pl.BlockSpec(memory_space=pl.ANY)],
        out_specs=pl.BlockSpec(memory_space=pltpu.VMEM),
        scratch_shapes=[pltpu.SemaphoreType.DMA((count,))],
        compiler_params=pltpu.CompilerParams(vmem_limit_bytes=VMEM_BYTES),
        cost_estimate=pl.CostEstimate(
            flops=0, bytes_accessed=math.prod(source.shape) * 2, transcendentals=0
        ),
    )(pltpu.with_memory_space_constraint(source, pltpu.HBM), after)


def half_kernel(other, slices_ref, embed_ref, head_ref, out_ref, score_ref):
    chips, _, own = out_ref.shape
    core = lax.axis_index("dp") % 2
    half = (1 - core) if other else core
    score_ref[...] = jnp.zeros_like(score_ref)

    def step(j, _):
        columns = pl.ds(pl.multiple_of((half * chips + j) * own, own), own)
        part = jnp.dot(slices_ref[...], embed_ref[:, columns], preferred_element_type=F32)
        score_ref[...] += jnp.sum(
            part * head_ref[:, columns].astype(F32), axis=-1, keepdims=True
        )
        out_ref[j] = part.astype(out_ref.dtype)
        return 0

    lax.fori_loop(0, chips, step, 0)


def hidden_kernel(
    mine_ref, got_ref, gain_ref, gate_ref, up_ref, down_ref, valid_ref,
    send_ref, keep_ref, score_ref, a_ref, b_ref,
):
    chips, total, own = mine_ref.shape
    width = 2 * chips * own
    core = lax.axis_index("dp") % 2

    def square(j, acc):
        x, y = mine_ref[j].astype(F32), got_ref[j].astype(F32)
        return acc + jnp.sum(x * x + y * y, axis=-1, keepdims=True)

    squares = lax.fori_loop(0, chips, square, jnp.zeros((total, 1), F32))
    inv = lax.rsqrt(squares / width + 1e-05)
    a_ref[...] = jnp.zeros_like(a_ref)
    b_ref[...] = jnp.zeros_like(b_ref)

    def forward(ref, half):
        def step(j, _):
            rows = pl.ds(pl.multiple_of((half * chips + j) * own, own), own)
            gain = gain_ref[:, rows].astype(F32)
            normed = (ref[j].astype(F32) * inv * gain).astype(BF16)
            a_ref[...] += jnp.dot(normed, gate_ref[rows, :], preferred_element_type=F32)
            b_ref[...] += jnp.dot(normed, up_ref[rows, :], preferred_element_type=F32)
            return 0

        lax.fori_loop(0, chips, step, 0)

    forward(mine_ref, core)
    forward(got_ref, 1 - core)
    a, b = a_ref[...], b_ref[...]
    sigma = jax.nn.sigmoid(a)
    active = a * sigma
    down = down_ref[...]
    hidden = (active * b).astype(BF16).astype(F32)
    score_ref[...] = jnp.sum(hidden * down, axis=-1, keepdims=True)
    d_hidden = valid_ref[...] * down
    d_gate = (d_hidden * b * sigma * (1.0 + a * (1.0 - sigma))).astype(BF16)
    d_up = (d_hidden * active).astype(BF16)
    contract = (((1,), (1,)), ((), ()))

    def backward(ref, half):
        def step(j, _):
            rows = pl.ds(pl.multiple_of((half * chips + j) * own, own), own)
            part = lax.dot_general(
                d_gate, gate_ref[rows, :], contract, preferred_element_type=F32
            ) + lax.dot_general(d_up, up_ref[rows, :], contract, preferred_element_type=F32)
            ref[j] = part.astype(ref.dtype)
            return 0

        lax.fori_loop(0, chips, step, 0)

    backward(send_ref, 1 - core)
    backward(keep_ref, core)


def input_kernel(
    mine_ref, got_ref, d_mine_ref, d_got_ref, gain_ref, head_ref, valid_ref, embed_ref,
    out_ref, dx_ref,
):
    chips, total, own = mine_ref.shape
    width = 2 * chips * own
    core = lax.axis_index("dp") % 2
    sources = ((mine_ref, d_mine_ref, core), (got_ref, d_got_ref, 1 - core))
    squares = jnp.zeros((total, 1), F32)
    dots = jnp.zeros((total, 1), F32)
    for x_ref, d_ref, half in sources:
        for j in range(chips):
            columns = pl.ds(pl.multiple_of((half * chips + j) * own, own), own)
            x = x_ref[j].astype(F32)
            g = d_ref[j].astype(F32) * gain_ref[:, columns].astype(F32)
            squares += jnp.sum(x * x, axis=-1, keepdims=True)
            dots += jnp.sum(g * x, axis=-1, keepdims=True)
    inv = lax.rsqrt(squares / width + 1e-05)
    mean = dots / width
    valid = valid_ref[...]
    for x_ref, d_ref, half in sources:
        for j in range(chips):
            columns = pl.ds(pl.multiple_of((half * chips + j) * own, own), own)
            x = x_ref[j].astype(F32)
            g = d_ref[j].astype(F32) * gain_ref[:, columns].astype(F32)
            dx = inv * g - x * inv * inv * inv * mean
            dx_ref[:, columns] = (dx + valid * head_ref[:, columns].astype(F32)).astype(BF16)
    voc = embed_ref.shape[0]
    contract = (((1,), (1,)), ((), ()))
    tile = 256

    def step(j, _):
        rows = pl.ds(pl.multiple_of(j * tile, tile), tile)
        out_ref[:, rows] = lax.dot_general(
            dx_ref[...], embed_ref[rows, :], contract, preferred_element_type=F32
        ).astype(out_ref.dtype)
        return 0

    whole = voc // tile
    if whole:
        lax.fori_loop(0, whole, step, 0)
    if voc % tile:
        out_ref[:, whole * tile :] = lax.dot_general(
            dx_ref[...], embed_ref[whole * tile :, :], contract, preferred_element_type=F32
        ).astype(out_ref.dtype)


def swap_sum(send, keep, devices):
    return (keep.astype(F32) + swap_cores(send, devices).astype(F32)).astype(BF16)


def sum_and_gather(half, devices):
    total = jnp.sum(exchange_chips(half, devices).astype(F32), axis=0).astype(BF16)
    held = exchange_chips(jnp.broadcast_to(total[None], half.shape), devices)
    return held, swap_cores(held, devices)


def pick(blocks, index):
    return lax.dynamic_index_in_dim(blocks, index, 0, keepdims=False)


def split_halves(part, devices):
    total, width = part.shape
    core = lax.axis_index("dp") % 2
    blocks = part.reshape(total, 2, devices // 2, width // devices).transpose(1, 2, 0, 3)
    return pick(blocks, 1 - core).astype(BF16), pick(blocks, core)


def join_halves(mine, got):
    core = lax.axis_index("dp") % 2
    blocks = jnp.where(core == 1, jnp.stack([got, mine]), jnp.stack([mine, got]))
    _, chips, total, own = blocks.shape
    return blocks.transpose(2, 0, 1, 3).reshape(total, 2 * chips * own).astype(F32)


def norm_scale(x0):
    return lax.rsqrt(jnp.mean(x0 * x0, axis=-1, keepdims=True) + 1e-05)


def plain_half(slices, embed, head_row, devices):
    part = jnp.dot(slices, embed, preferred_element_type=F32)
    score = jnp.sum(part * head_row.astype(F32), axis=-1, keepdims=True)
    return *split_halves(part, devices), score


def plain_hidden(mine, got, gain_row, w_gate, w_up, down, valid, devices):
    x0 = join_halves(mine, got)
    normed = (x0 * norm_scale(x0) * gain_row.astype(F32)).astype(BF16)
    a = jnp.dot(normed, w_gate, preferred_element_type=F32)
    b = jnp.dot(normed, w_up, preferred_element_type=F32)
    sigma = jax.nn.sigmoid(a)
    active = a * sigma
    hidden = (active * b).astype(BF16).astype(F32)
    d_hidden = valid * down
    d_gate = (d_hidden * b * sigma * (1.0 + a * (1.0 - sigma))).astype(BF16)
    d_up = (d_hidden * active).astype(BF16)
    part = jnp.einsum("tf,df->td", d_gate, w_gate, preferred_element_type=F32)
    part = part + jnp.einsum("tf,df->td", d_up, w_up, preferred_element_type=F32)
    return *split_halves(part, devices), jnp.sum(hidden * down, axis=-1, keepdims=True)


def plain_input(mine, got, d_mine, d_got, gain_row, head_row, valid, embed):
    x0 = join_halves(mine, got)
    inv = norm_scale(x0)
    scaled = join_halves(d_mine, d_got) * gain_row.astype(F32)
    dx = inv * scaled - x0 * inv * inv * inv * jnp.mean(scaled * x0, axis=-1, keepdims=True)
    dx = (dx + valid * head_row.astype(F32)).astype(BF16)
    return jnp.einsum("td,vd->tv", dx, embed, preferred_element_type=F32).astype(BF16)


def body(logits, embed, norm_gain, w_gate, w_up, w_down, head, counts):
    devices = lax.axis_size("dp")
    rows, voc = logits.shape
    part = voc // devices
    width = embed.shape[1]
    hidden = w_gate.shape[1]
    own, chips = width // devices, devices // 2
    requests = counts.shape[0]
    total = rows * devices
    request_len = total // requests
    head32 = head.astype(F32)
    head_row, gain_row = head.reshape(1, width), norm_gain.reshape(1, width)
    probs32 = jax.nn.softmax(logits.astype(F32), axis=-1)
    probs = probs32.astype(BF16)
    blocked = probs.reshape(rows, devices, part).transpose(1, 0, 2)
    slices = exchange(blocked).reshape(total, part)
    down_head = jnp.sum(w_down.astype(F32) * head32[None, :], axis=-1)
    position = jnp.arange(total, dtype=jnp.int32)
    member = (position // request_len)[:, None] == jnp.arange(requests, dtype=jnp.int32)[None, :]
    limit = jnp.sum(jnp.where(member, counts[None, :], 0), axis=-1)
    valid = (position % request_len < limit).astype(F32)

    def blocks(dtype):
        return jax.ShapeDtypeStruct((chips, total, own), dtype)

    column = jax.ShapeDtypeStruct((total, 1), F32)
    flops = total * part * width
    down_row, valid_column = down_head.reshape(1, hidden), valid[:, None]
    tiled = own % 128 == 0 and hidden % 128 == 0 and total % 16 == 0
    if tiled:
        table = make_resident(embed, blocked)
        send, score_a = call(
            functools.partial(half_kernel, True), [blocks(BF16), column],
            slices, table, head_row, resident=(1,), flops=flops,
        )
        keep, score_b = call(
            functools.partial(half_kernel, False), [blocks(F32), column],
            slices, table, head_row, resident=(1,), flops=flops,
        )
        score_x = score_a + score_b
    else:
        send, keep, score_x = plain_half(slices, embed, head_row, devices)
    x_mine, x_got = sum_and_gather(swap_sum(send, keep, devices), devices)
    if tiled:
        wide = pltpu.VMEM((total, hidden), F32)
        send, keep, score_u = call(
            hidden_kernel, [blocks(BF16), blocks(F32), column],
            x_mine, x_got, gain_row, w_gate, w_up, down_row, valid_column,
            resident=(3, 4), flops=8 * total * hidden * width, scratch=(wide, wide),
        )
    else:
        send, keep, score_u = plain_hidden(
            x_mine, x_got, gain_row, w_gate, w_up, down_row, valid_column, devices
        )
    d_mine, d_got = sum_and_gather(swap_sum(send, keep, devices), devices)
    score = (score_x + score_u)[:, 0]
    own_rewards = jnp.sum(jnp.where(member, (valid * score)[:, None], 0.0), axis=0)
    sources = (x_mine, x_got, d_mine, d_got, gain_row, head_row, valid_column)
    if tiled:
        (d_slices,) = call(
            input_kernel, [jax.ShapeDtypeStruct((total, part), BF16)], *sources, table,
            resident=(7,), flops=2 * flops, scratch=(pltpu.VMEM((total, width), BF16),),
        )
    else:
        d_slices = plain_input(*sources, embed)
    extra = split3(own_rewards).reshape(1, 1, requests * 3)
    extra = jnp.broadcast_to(extra, (devices, rows, requests * 3))
    back = exchange(jnp.concatenate([d_slices.reshape(devices, rows, part), extra], axis=-1))
    sums = jnp.sum(back[:, 0, part:].astype(F32).reshape(devices, requests, 3), axis=(0, 2))
    rewards = sums / counts.astype(F32)
    d_probs = back[:, :, :part].transpose(1, 0, 2).reshape(rows, voc).astype(F32)
    d_logits = probs32 * (d_probs - jnp.sum(probs32 * d_probs, axis=-1, keepdims=True))
    guidance = (math.sqrt(VOC) * d_logits).astype(BF16)
    return (guidance, rewards)


def solution(mesh):
    placed = (
        P(("groups", "dp"), None),
        P("dp", None),
        P(),
        P(None, "dp"),
        P(None, "dp"),
        P("dp", None),
        P(),
        P("groups"),
    )
    return jax.shard_map(
        body,
        mesh=mesh,
        in_specs=placed,
        out_specs=(P(("groups", "dp"), None), P("groups")),
        check_vma=False,
    )
```

```python
import functools
import math

import jax
import jax.numpy as jnp
from jax import lax
from jax.experimental import pallas as pl
from jax.experimental.pallas import tpu as pltpu
from jax.sharding import PartitionSpec as P

VOC = 32000
F32, BF16 = jnp.float32, jnp.bfloat16
VMEM_BYTES = 12 * 1024 * 1024


def swap_cores(value, devices):
    return lax.ppermute(value, "dp", [(i, i ^ 1) for i in range(devices)])


def exchange(blocks):
    return lax.all_to_all(blocks, "dp", split_axis=0, concat_axis=0, tiled=True)


def exchange_chips(blocks, devices):
    groups = [list(range(core, devices, 2)) for core in range(2)]
    return lax.all_to_all(
        blocks, "dp", split_axis=0, concat_axis=0, axis_index_groups=groups, tiled=True
    )


def split3(value):
    hi = lax.reduce_precision(value, 8, 7)
    rest = value - hi
    mid = lax.reduce_precision(rest, 8, 7)
    low = rest - mid
    return jnp.stack([hi, mid, low], axis=-1).astype(BF16)


HBM_SPEC = pl.BlockSpec(memory_space=pltpu.HBM)
VMEM_SPEC = pl.BlockSpec(memory_space=pltpu.VMEM)


def call(kernel, outs, *args, streamed=(), flops=0, scratch=(), room=0):
    size = sum(math.prod(a.shape) * a.dtype.itemsize for a in args)
    args = [
        pltpu.with_memory_space_constraint(a, pltpu.HBM) if i in streamed else a
        for i, a in enumerate(args)
    ]
    return pl.pallas_call(
        kernel,
        out_shape=outs,
        in_specs=[HBM_SPEC if i in streamed else VMEM_SPEC for i in range(len(args))],
        out_specs=[VMEM_SPEC] * len(outs),
        scratch_shapes=list(scratch),
        compiler_params=pltpu.CompilerParams(vmem_limit_bytes=VMEM_BYTES + room),
        cost_estimate=pl.CostEstimate(flops=flops, bytes_accessed=size, transcendentals=0),
    )(*args)


def struct(shape, dtype):
    return jax.ShapeDtypeStruct(shape, dtype)


def this_core():
    return lax.axis_index("dp") % 2


def span(start, size):
    return pl.ds(pl.multiple_of(start, size), size)


def softmax_kernel(logits_ref, out_ref, top_ref, scale_ref):
    devices, _, part = out_ref.shape
    x = logits_ref[...].astype(F32)
    top = jnp.max(x, axis=-1, keepdims=True)
    e = jnp.exp(x - top)
    scale = 1.0 / jnp.sum(e, axis=-1, keepdims=True)
    probs = e * scale
    for d in range(devices):
        out_ref[d] = probs[:, d * part : (d + 1) * part].astype(BF16)
    top_ref[...] = top
    scale_ref[...] = scale


def final_kernel(
    logits_ref, top_ref, scale_ref, back_ref, counts_ref, out_ref, rewards_ref, d_ref
):
    devices, _, padded = back_ref.shape
    part = out_ref.shape[1] // devices
    requests = counts_ref.shape[1]
    sums = jnp.zeros((1, requests), F32)
    for d in range(devices):
        block = back_ref[d].astype(F32)
        d_ref[:, d * part : (d + 1) * part] = block[:, :part]
        for i in range(3):
            start = part + i * requests
            sums += block[:1, start : start + requests]
    rewards_ref[...] = sums / counts_ref[...]
    probs = jnp.exp(logits_ref[...].astype(F32) - top_ref[...]) * scale_ref[...]
    d_probs = d_ref[...]
    mean = jnp.sum(probs * d_probs, axis=-1, keepdims=True)
    out_ref[...] = (math.sqrt(VOC) * (probs * (d_probs - mean))).astype(BF16)


def half_kernel(other, slices_ref, embed_ref, head_ref, out_ref, score_ref, table, sems):
    chips, _, own = out_ref.shape
    core = this_core()
    half = (1 - core) if other else core

    def columns(j):
        return span((half * chips + j) * own, own)

    def copy(j):
        return pltpu.make_async_copy(embed_ref.at[:, columns(j)], table.at[j], sems.at[j])

    for j in range(chips):
        copy(j).start()
    slices = slices_ref[...]
    score = jnp.zeros(score_ref.shape, F32)
    for j in range(chips):
        copy(j).wait()
        part = jnp.dot(slices, table[j], preferred_element_type=F32)
        score += jnp.sum(part * head_ref[:, columns(j)].astype(F32), axis=-1, keepdims=True)
        out_ref[j] = part.astype(out_ref.dtype)
    score_ref[...] = score


def hidden_kernel(
    mine_ref, got_ref, gain_ref, gate_ref, up_ref, down_ref, valid_ref,
    send_ref, keep_ref, score_ref, gate, up, a_ref, b_ref, sems,
):
    chips, total, own = mine_ref.shape
    width = 2 * chips * own
    core = this_core()
    order = [(mine_ref, core, j) for j in range(chips)] + [
        (got_ref, 1 - core, j) for j in range(chips)
    ]

    def rows(half, j):
        return span((half * chips + j) * own, own)

    def copies(i):
        _, half, j = order[i]
        r = rows(half, j)
        return (
            pltpu.make_async_copy(gate_ref.at[r], gate.at[r], sems.at[0, i]),
            pltpu.make_async_copy(up_ref.at[r], up.at[r], sems.at[1, i]),
        )

    for i in range(2 * chips):
        for copy in copies(i):
            copy.start()
    squares = jnp.zeros((total, 1), F32)
    for j in range(chips):
        x, y = mine_ref[j].astype(F32), got_ref[j].astype(F32)
        squares += jnp.sum(x * x + y * y, axis=-1, keepdims=True)
    inv = lax.rsqrt(squares / width + 1e-05)
    for i, (ref, half, j) in enumerate(order):
        r = rows(half, j)
        normed = (ref[j].astype(F32) * inv * gain_ref[:, r].astype(F32)).astype(BF16)
        for copy in copies(i):
            copy.wait()
        a = jnp.dot(normed, gate[r], preferred_element_type=F32)
        b = jnp.dot(normed, up[r], preferred_element_type=F32)
        a_ref[...] = a_ref[...] + a if i else a
        b_ref[...] = b_ref[...] + b if i else b
    a, b = a_ref[...], b_ref[...]
    sigma = jax.nn.sigmoid(a)
    active = a * sigma
    down = down_ref[...]
    hidden = (active * b).astype(BF16).astype(F32)
    score_ref[...] = jnp.sum(hidden * down, axis=-1, keepdims=True)
    d_hidden = valid_ref[...] * down
    d_gate = (d_hidden * b * sigma * (1.0 + a * (1.0 - sigma))).astype(BF16)
    d_up = (d_hidden * active).astype(BF16)
    contract = (((1,), (1,)), ((), ()))
    for ref, half in ((send_ref, 1 - core), (keep_ref, core)):
        for j in range(chips):
            r = rows(half, j)
            part = lax.dot_general(d_gate, gate[r], contract, preferred_element_type=F32)
            part += lax.dot_general(d_up, up[r], contract, preferred_element_type=F32)
            ref[j] = part.astype(ref.dtype)


def input_kernel(
    mine_ref, got_ref, d_mine_ref, d_got_ref, gain_ref, head_ref, valid_ref,
    score_a_ref, score_b_ref, score_c_ref, member_ref, embed_ref,
    out_ref, dx_ref, table, sems,
):
    chips, total, own = mine_ref.shape
    devices, per, _ = out_ref.shape
    voc = embed_ref.shape[0]
    requests = member_ref.shape[1]
    width = 2 * chips * own
    core = this_core()
    tile = 256
    starts = [(i, min(tile, voc - i)) for i in range(0, voc, tile)]

    def copy(i):
        start, size = starts[i]
        return pltpu.make_async_copy(
            embed_ref.at[pl.ds(start, size)], table.at[pl.ds(start, size)], sems.at[i]
        )

    for i in range(len(starts)):
        copy(i).start()
    sources = ((mine_ref, d_mine_ref, core), (got_ref, d_got_ref, 1 - core))
    squares = jnp.zeros((total, 1), F32)
    dots = jnp.zeros((total, 1), F32)
    for x_ref, d_ref, half in sources:
        for j in range(chips):
            x = x_ref[j].astype(F32)
            g = d_ref[j].astype(F32) * gain_ref[:, span((half * chips + j) * own, own)].astype(F32)
            squares += jnp.sum(x * x, axis=-1, keepdims=True)
            dots += jnp.sum(g * x, axis=-1, keepdims=True)
    inv = lax.rsqrt(squares / width + 1e-05)
    mean = dots / width
    valid = valid_ref[...]
    for x_ref, d_ref, half in sources:
        for j in range(chips):
            columns = span((half * chips + j) * own, own)
            x = x_ref[j].astype(F32)
            g = d_ref[j].astype(F32) * gain_ref[:, columns].astype(F32)
            dx = inv * g - x * inv * inv * inv * mean
            dx_ref[:, columns] = (dx + valid * head_ref[:, columns].astype(F32)).astype(BF16)
    score = score_a_ref[...] + score_b_ref[...] + score_c_ref[...]
    value = jnp.sum(member_ref[...] * (valid * score), axis=0, keepdims=True)
    pieces = []
    for _ in range(3):
        piece = value.astype(BF16)
        pieces.append(piece)
        value = value - piece.astype(F32)
    for i, piece in enumerate(pieces):
        start = voc + i * requests
        spread = jnp.broadcast_to(piece.astype(F32), (per, requests)).astype(BF16)
        for d in range(devices):
            out_ref[d, :, start : start + requests] = spread
    contract = (((1,), (1,)), ((), ()))
    dx = dx_ref[...]
    for i, (start, size) in enumerate(starts):
        copy(i).wait()
        part = lax.dot_general(
            dx, table[start : start + size, :], contract, preferred_element_type=F32
        )
        for d in range(devices):
            out_ref[d, :, start : start + size] = part[d * per : (d + 1) * per].astype(BF16)


def swap_sum(send, keep, devices):
    return (keep.astype(F32) + swap_cores(send, devices).astype(F32)).astype(BF16)


def sum_and_gather(half, devices):
    total = jnp.sum(exchange_chips(half, devices).astype(F32), axis=0).astype(BF16)
    held = exchange_chips(jnp.broadcast_to(total[None], half.shape), devices)
    return held, swap_cores(held, devices)


def pick(blocks, index):
    return lax.dynamic_index_in_dim(blocks, index, 0, keepdims=False)


def split_halves(part, devices):
    total, width = part.shape
    core = lax.axis_index("dp") % 2
    blocks = part.reshape(total, 2, devices // 2, width // devices).transpose(1, 2, 0, 3)
    return pick(blocks, 1 - core).astype(BF16), pick(blocks, core)


def join_halves(mine, got):
    core = lax.axis_index("dp") % 2
    blocks = jnp.where(core == 1, jnp.stack([got, mine]), jnp.stack([mine, got]))
    _, chips, total, own = blocks.shape
    return blocks.transpose(2, 0, 1, 3).reshape(total, 2 * chips * own).astype(F32)


def norm_scale(x0):
    return lax.rsqrt(jnp.mean(x0 * x0, axis=-1, keepdims=True) + 1e-05)


def plain_half(slices, embed, head_row, devices):
    part = jnp.dot(slices, embed, preferred_element_type=F32)
    score = jnp.sum(part * head_row.astype(F32), axis=-1, keepdims=True)
    return *split_halves(part, devices), score


def plain_hidden(mine, got, gain_row, w_gate, w_up, down, valid, devices):
    x0 = join_halves(mine, got)
    normed = (x0 * norm_scale(x0) * gain_row.astype(F32)).astype(BF16)
    a = jnp.dot(normed, w_gate, preferred_element_type=F32)
    b = jnp.dot(normed, w_up, preferred_element_type=F32)
    sigma = jax.nn.sigmoid(a)
    active = a * sigma
    hidden = (active * b).astype(BF16).astype(F32)
    d_hidden = valid * down
    d_gate = (d_hidden * b * sigma * (1.0 + a * (1.0 - sigma))).astype(BF16)
    d_up = (d_hidden * active).astype(BF16)
    part = jnp.einsum("tf,df->td", d_gate, w_gate, preferred_element_type=F32)
    part = part + jnp.einsum("tf,df->td", d_up, w_up, preferred_element_type=F32)
    return *split_halves(part, devices), jnp.sum(hidden * down, axis=-1, keepdims=True)


def plain_input(mine, got, d_mine, d_got, gain_row, head_row, valid, embed):
    x0 = join_halves(mine, got)
    inv = norm_scale(x0)
    scaled = join_halves(d_mine, d_got) * gain_row.astype(F32)
    dx = inv * scaled - x0 * inv * inv * inv * jnp.mean(scaled * x0, axis=-1, keepdims=True)
    dx = (dx + valid * head_row.astype(F32)).astype(BF16)
    return jnp.einsum("td,vd->tv", dx, embed, preferred_element_type=F32).astype(BF16)


def body(logits, embed, norm_gain, w_gate, w_up, w_down, head, counts):
    devices = lax.axis_size("dp")
    rows, voc = logits.shape
    part = voc // devices
    width = embed.shape[1]
    hidden = w_gate.shape[1]
    own, chips = width // devices, devices // 2
    requests = counts.shape[0]
    total = rows * devices
    request_len = total // requests
    tiled = own % 128 == 0 and hidden % 128 == 0 and total % 16 == 0 and part % 16 == 0
    head32 = head.astype(F32)
    head_row, gain_row = head.reshape(1, width), norm_gain.reshape(1, width)
    if tiled:
        column = struct((rows, 1), F32)
        blocked, top, scale = call(
            softmax_kernel, [struct((devices, rows, part), BF16), column, column], logits
        )
    else:
        probs32 = jax.nn.softmax(logits.astype(F32), axis=-1)
        blocked = probs32.astype(BF16).reshape(rows, devices, part).transpose(1, 0, 2)
    slices = exchange(blocked).reshape(total, part)
    down_head = jnp.sum(w_down.astype(F32) * head32[None, :], axis=-1)
    position = jnp.arange(total, dtype=jnp.int32)
    member = (position // request_len)[:, None] == jnp.arange(requests, dtype=jnp.int32)[None, :]
    limit = jnp.sum(jnp.where(member, counts[None, :], 0), axis=-1, keepdims=True)
    valid = (position[:, None] % request_len < limit).astype(F32)
    member = member.astype(F32)
    down_row = down_head.reshape(1, hidden)
    column = struct((total, 1), F32)
    half = (chips, total, own)
    flops = total * part * width
    if tiled:
        table = [pltpu.VMEM((chips, part, own), BF16), pltpu.SemaphoreType.DMA((chips,))]
        args = dict(streamed=(1,), flops=flops, scratch=table, room=part * width)
        send, score_a = call(
            functools.partial(half_kernel, True), [struct(half, BF16), column],
            slices, embed, head_row, **args,
        )
        keep, score_b = call(
            functools.partial(half_kernel, False), [struct(half, F32), column],
            slices, embed, head_row, **args,
        )
    else:
        send, keep, score_a = plain_half(slices, embed, head_row, devices)
        score_b = jnp.zeros_like(score_a)
    x_mine, x_got = sum_and_gather(swap_sum(send, keep, devices), devices)
    if tiled:
        wide, weight = pltpu.VMEM((total, hidden), F32), pltpu.VMEM((width, hidden), BF16)
        send, keep, score_c = call(
            hidden_kernel, [struct(half, BF16), struct(half, F32), column],
            x_mine, x_got, gain_row, w_gate, w_up, down_row, valid,
            streamed=(3, 4), flops=8 * total * hidden * width, room=4 * width * hidden,
            scratch=(weight, weight, wide, wide, pltpu.SemaphoreType.DMA((2, devices))),
        )
    else:
        send, keep, score_c = plain_hidden(
            x_mine, x_got, gain_row, w_gate, w_up, down_row, valid, devices
        )
    d_mine, d_got = sum_and_gather(swap_sum(send, keep, devices), devices)
    sources = (x_mine, x_got, d_mine, d_got, gain_row, head_row, valid)
    padded = part + 3 * requests
    if tiled:
        (d_slices,) = call(
            input_kernel, [struct((devices, rows, padded), BF16)],
            *sources, score_a, score_b, score_c, member, embed,
            streamed=(11,), flops=2 * flops, room=2 * part * width,
            scratch=(
                pltpu.VMEM((total, width), BF16), pltpu.VMEM((part, width), BF16),
                pltpu.SemaphoreType.DMA((-(-part // 256),)),
            ),
        )
    else:
        d_slices = plain_input(*sources, embed).reshape(devices, rows, part)
        score = valid * (score_a + score_b + score_c)
        extra = split3(jnp.sum(member * score, axis=0)).reshape(1, 1, requests * 3)
        extra = jnp.broadcast_to(extra, (devices, rows, requests * 3))
        d_slices = jnp.concatenate([d_slices, extra], axis=-1)
    back = exchange(d_slices)
    counts32 = counts.astype(F32)
    if tiled:
        guidance, rewards = call(
            final_kernel, [struct((rows, voc), BF16), struct((1, requests), F32)],
            logits, top, scale, back, counts32.reshape(1, requests),
            scratch=(pltpu.VMEM((rows, voc), F32),),
        )
        return (guidance, rewards.reshape(requests))
    sums = jnp.sum(back[:, 0, part:].astype(F32).reshape(devices, requests, 3), axis=(0, 2))
    rewards = sums / counts32
    d_probs = back[:, :, :part].transpose(1, 0, 2).reshape(rows, voc).astype(F32)
    d_logits = probs32 * (d_probs - jnp.sum(probs32 * d_probs, axis=-1, keepdims=True))
    guidance = (math.sqrt(VOC) * d_logits).astype(BF16)
    return (guidance, rewards)


def solution(mesh):
    placed = (
        P(("groups", "dp"), None),
        P("dp", None),
        P(),
        P(None, "dp"),
        P(None, "dp"),
        P("dp", None),
        P(),
        P("groups"),
    )
    return jax.shard_map(
        body,
        mesh=mesh,
        in_specs=placed,
        out_specs=(P(("groups", "dp"), None), P("groups")),
        check_vma=False,
    )
```

```python
import functools
import math

import jax
import jax.numpy as jnp
from jax import lax
from jax.experimental import pallas as pl
from jax.experimental.pallas import tpu as pltpu
from jax.sharding import PartitionSpec as P

VOC = 32000
F32, BF16 = jnp.float32, jnp.bfloat16
VMEM_BYTES = 12 * 1024 * 1024


def swap_cores(value, devices):
    return lax.ppermute(value, "dp", [(i, i ^ 1) for i in range(devices)])


def exchange(blocks):
    return lax.all_to_all(blocks, "dp", split_axis=0, concat_axis=0, tiled=True)


def exchange_chips(blocks, devices):
    groups = [list(range(core, devices, 2)) for core in range(2)]
    return lax.all_to_all(
        blocks, "dp", split_axis=0, concat_axis=0, axis_index_groups=groups, tiled=True
    )


def split3(value):
    hi = lax.reduce_precision(value, 8, 7)
    rest = value - hi
    mid = lax.reduce_precision(rest, 8, 7)
    low = rest - mid
    return jnp.stack([hi, mid, low], axis=-1).astype(BF16)


HBM_SPEC = pl.BlockSpec(memory_space=pltpu.HBM)
VMEM_SPEC = pl.BlockSpec(memory_space=pltpu.VMEM)
SMEM_SPEC = pl.BlockSpec(memory_space=pltpu.SMEM)


WINDOW = 6


def call(kernel, outs, *args, streamed=(), kept=(), scalars=(), flops=0, scratch=(), room=0):
    size = sum(math.prod(a.shape) * a.dtype.itemsize for a in args)
    places = {i: pltpu.HBM for i in streamed} | {i: pltpu.VMEM for i in kept}
    specs = [
        HBM_SPEC if i in streamed else SMEM_SPEC if i in scalars else VMEM_SPEC
        for i in range(len(args))
    ]
    return pl.pallas_call(
        kernel,
        out_shape=outs,
        in_specs=specs,
        out_specs=[VMEM_SPEC] * len(outs),
        scratch_shapes=list(scratch),
        compiler_params=pltpu.CompilerParams(vmem_limit_bytes=VMEM_BYTES + room),
        cost_estimate=pl.CostEstimate(flops=flops, bytes_accessed=size, transcendentals=0),
    )(*[
        pltpu.with_memory_space_constraint(a, places[i]) if i in places else a
        for i, a in enumerate(args)
    ])


class Stream:
    def __init__(self, copies):
        self.copies = copies
        self.done = 0
        for copy in copies[:WINDOW]:
            copy.start()

    def wait(self, count):
        while self.done < count:
            self.copies[self.done].wait()
            self.done += 1
            if self.done + WINDOW <= len(self.copies):
                self.copies[self.done + WINDOW - 1].start()


def struct(shape, dtype):
    return jax.ShapeDtypeStruct(shape, dtype)


def this_core():
    return lax.axis_index("dp") % 2


def span(start, size):
    return pl.ds(pl.multiple_of(start, size), size)


def softmax_kernel(logits_ref, out_ref, top_ref, scale_ref):
    devices, _, part = out_ref.shape
    x = logits_ref[...].astype(F32)
    top = jnp.max(x, axis=-1, keepdims=True)
    e = jnp.exp(x - top)
    scale = 1.0 / jnp.sum(e, axis=-1, keepdims=True)
    probs = e * scale
    for d in range(devices):
        out_ref[d] = probs[:, d * part : (d + 1) * part].astype(BF16)
    top_ref[...] = top
    scale_ref[...] = scale


def final_kernel(
    logits_ref, top_ref, scale_ref, back_ref, counts_ref, out_ref, rewards_ref, d_ref
):
    devices, _, padded = back_ref.shape
    part = out_ref.shape[1] // devices
    requests = counts_ref.shape[1]
    sums = jnp.zeros((1, requests), F32)
    for d in range(devices):
        block = back_ref[d].astype(F32)
        d_ref[:, d * part : (d + 1) * part] = block[:, :part]
        for i in range(3):
            start = part + i * requests
            sums += block[:1, start : start + requests]
    rewards_ref[...] = sums / counts_ref[...]
    probs = jnp.exp(logits_ref[...].astype(F32) - top_ref[...]) * scale_ref[...]
    d_probs = d_ref[...]
    mean = jnp.sum(probs * d_probs, axis=-1, keepdims=True)
    out_ref[...] = (math.sqrt(VOC) * (probs * (d_probs - mean))).astype(BF16)


def valid_column(counts_ref, total):
    requests = counts_ref.shape[0]
    length = total // requests
    position = lax.broadcasted_iota(jnp.int32, (total, 1), 0)
    valid = jnp.zeros((total, 1), F32)
    for r in range(requests):
        inside = (position >= r * length) & (position < r * length + counts_ref[r])
        valid = jnp.where(inside, 1.0, valid)
    return valid, position // length


def half_kernel(other, slices_ref, embed_ref, head_ref, out_ref, score_ref, table, sems):
    chips, _, own = out_ref.shape
    part = embed_ref.shape[0]
    cuts = sems.shape[0] // chips
    core = this_core()
    half = (1 - core) if other else core
    rows = part // cuts

    def columns(j):
        return span((half * chips + j) * own, own)

    stream = Stream([
        pltpu.make_async_copy(
            embed_ref.at[pl.ds(i * rows, rows), columns(j)],
            table.at[j, pl.ds(i * rows, rows)],
            sems.at[j * cuts + i],
        )
        for j in range(chips)
        for i in range(cuts)
    ])
    slices = slices_ref[...]
    score = jnp.zeros(score_ref.shape, F32)
    for j in range(chips):
        stream.wait((j + 1) * cuts)
        part = jnp.dot(slices, table[j], preferred_element_type=F32)
        score += jnp.sum(part * head_ref[:, columns(j)].astype(F32), axis=-1, keepdims=True)
        out_ref[j] = part.astype(out_ref.dtype)
    score_ref[...] = score


def down_kernel(head_ref, down_ref, out_ref, table, sems):
    steps = sems.shape[0]
    rows = down_ref.shape[0] // steps
    stream = Stream([
        pltpu.make_async_copy(
            down_ref.at[pl.ds(i * rows, rows)], table.at[pl.ds(i * rows, rows)], sems.at[i]
        )
        for i in range(steps)
    ])
    head = jnp.broadcast_to(head_ref[...].astype(F32), (16, head_ref.shape[1])).astype(BF16)
    contract = (((1,), (1,)), ((), ()))
    for i in range(steps):
        stream.wait(i + 1)
        part = lax.dot_general(
            head, table[i * rows : (i + 1) * rows], contract, preferred_element_type=F32
        )
        out_ref[:, i * rows : (i + 1) * rows] = part[:1]


def forward_half(x_ref, gain_ref, gate_ref, up_ref, gate, up, sems, half, sums):
    chips, _, own = x_ref.shape

    def rows(j):
        return span((half * chips + j) * own, own)

    stream = Stream([
        pltpu.make_async_copy(source.at[rows(j)], target.at[pl.ds(j * own, own)], sems.at[k, j])
        for j in range(chips)
        for k, (source, target) in enumerate(((gate_ref, gate), (up_ref, up)))
    ])
    a, b, squares = sums
    scaled = []
    for j in range(chips):
        x = x_ref[j].astype(F32)
        squares = squares + jnp.sum(x * x, axis=-1, keepdims=True)
        scaled.append((x * gain_ref[:, rows(j)].astype(F32)).astype(BF16))
    for j in range(chips):
        r = slice(j * own, (j + 1) * own)
        stream.wait(2 * (j + 1))
        a = a + jnp.dot(scaled[j], gate[r], preferred_element_type=F32)
        b = b + jnp.dot(scaled[j], up[r], preferred_element_type=F32)
    return a, b, squares


def backward_half(d_gate, d_up, gate, up, out_ref):
    chips, _, own = out_ref.shape
    contract = (((1,), (1,)), ((), ()))
    for j in range(chips):
        r = slice(j * own, (j + 1) * own)
        part = lax.dot_general(d_gate, gate[r], contract, preferred_element_type=F32)
        part += lax.dot_general(d_up, up[r], contract, preferred_element_type=F32)
        out_ref[j] = part.astype(out_ref.dtype)


def first_kernel(
    x_ref, gain_ref, gate_ref, up_ref, a_ref, b_ref, squares_ref, gate, up, sems
):
    zeros = jnp.zeros(a_ref.shape, F32)
    sums = (zeros, zeros, jnp.zeros(squares_ref.shape, F32))
    sums = forward_half(x_ref, gain_ref, gate_ref, up_ref, gate, up, sems, this_core(), sums)
    a_ref[...], b_ref[...], squares_ref[...] = sums


def second_kernel(
    x_ref, gain_ref, gate_ref, up_ref, a_ref, b_ref, squares_ref, down_ref, counts_ref,
    send_ref, score_ref, d_gate_ref, d_up_ref, gate, up, sems,
):
    total = x_ref.shape[1]
    width = gate_ref.shape[0]
    sums = (a_ref[...], b_ref[...], squares_ref[...])
    a, b, squares = forward_half(
        x_ref, gain_ref, gate_ref, up_ref, gate, up, sems, 1 - this_core(), sums
    )
    inv = lax.rsqrt(squares / width + 1e-05)
    a, b = a * inv, b * inv
    sigma = jax.nn.sigmoid(a)
    active = a * sigma
    down = down_ref[...]
    hidden = (active * b).astype(BF16).astype(F32)
    score_ref[...] = jnp.sum(hidden * down, axis=-1, keepdims=True)
    valid, _ = valid_column(counts_ref, total)
    d_hidden = valid * down
    d_gate = (d_hidden * b * sigma * (1.0 + a * (1.0 - sigma))).astype(BF16)
    d_up = (d_hidden * active).astype(BF16)
    d_gate_ref[...], d_up_ref[...] = d_gate, d_up
    backward_half(d_gate, d_up, gate, up, send_ref)


def third_kernel(d_gate_ref, d_up_ref, gate_ref, up_ref, keep_ref):
    backward_half(d_gate_ref[...], d_up_ref[...], gate_ref, up_ref, keep_ref)


def input_kernel(
    mine_ref, got_ref, d_mine_ref, d_got_ref, gain_ref, head_ref,
    score_a_ref, score_b_ref, score_c_ref, counts_ref, embed_ref,
    out_ref, dx_ref, table, sems,
):
    chips, total, own = mine_ref.shape
    devices, per, _ = out_ref.shape
    voc = embed_ref.shape[0]
    requests = counts_ref.shape[0]
    width = 2 * chips * own
    core = this_core()
    tile = 256
    fine = 64
    stream = Stream([
        pltpu.make_async_copy(
            embed_ref.at[pl.ds(i, min(fine, voc - i))],
            table.at[pl.ds(i, min(fine, voc - i))],
            sems.at[i // fine],
        )
        for i in range(0, voc, fine)
    ])
    sources = ((mine_ref, d_mine_ref, core), (got_ref, d_got_ref, 1 - core))
    squares = jnp.zeros((total, 1), F32)
    dots = jnp.zeros((total, 1), F32)
    for x_ref, d_ref, half in sources:
        for j in range(chips):
            x = x_ref[j].astype(F32)
            g = d_ref[j].astype(F32) * gain_ref[:, span((half * chips + j) * own, own)].astype(F32)
            squares += jnp.sum(x * x, axis=-1, keepdims=True)
            dots += jnp.sum(g * x, axis=-1, keepdims=True)
    inv = lax.rsqrt(squares / width + 1e-05)
    mean = dots / width
    valid, request = valid_column(counts_ref, total)
    for x_ref, d_ref, half in sources:
        for j in range(chips):
            columns = span((half * chips + j) * own, own)
            x = x_ref[j].astype(F32)
            g = d_ref[j].astype(F32) * gain_ref[:, columns].astype(F32)
            dx = inv * g - x * inv * inv * inv * mean
            dx_ref[:, columns] = (dx + valid * head_ref[:, columns].astype(F32)).astype(BF16)
    score = valid * (score_a_ref[...] + score_b_ref[...] + score_c_ref[...])
    member = request == lax.broadcasted_iota(jnp.int32, (total, requests), 1)
    value = jnp.sum(jnp.where(member, score, 0.0), axis=0, keepdims=True)
    pieces = []
    for _ in range(3):
        piece = value.astype(BF16).astype(F32)
        pieces.append(piece)
        value = value - piece
    for i, piece in enumerate(pieces):
        start = voc + i * requests
        spread = jnp.broadcast_to(piece, (per, requests)).astype(BF16)
        for d in range(devices):
            out_ref[d, :, start : start + requests] = spread
    contract = (((1,), (1,)), ((), ()))
    dx = dx_ref[...]
    for start in range(0, voc, tile):
        end = min(start + tile, voc)
        stream.wait(-(-end // fine))
        part = lax.dot_general(dx, table[start:end, :], contract, preferred_element_type=F32)
        for d in range(devices):
            out_ref[d, :, start:end] = part[d * per : (d + 1) * per].astype(BF16)


def swap_sum(send, keep, devices):
    return (keep.astype(F32) + swap_cores(send, devices).astype(F32)).astype(BF16)


def sum_and_gather(half, devices):
    total = jnp.sum(exchange_chips(half, devices).astype(F32), axis=0).astype(BF16)
    return exchange_chips(jnp.broadcast_to(total[None], half.shape), devices)


def pick(blocks, index):
    return lax.dynamic_index_in_dim(blocks, index, 0, keepdims=False)


def split_halves(part, devices):
    total, width = part.shape
    core = lax.axis_index("dp") % 2
    blocks = part.reshape(total, 2, devices // 2, width // devices).transpose(1, 2, 0, 3)
    return pick(blocks, 1 - core).astype(BF16), pick(blocks, core)


def join_halves(mine, got):
    core = lax.axis_index("dp") % 2
    blocks = jnp.where(core == 1, jnp.stack([got, mine]), jnp.stack([mine, got]))
    _, chips, total, own = blocks.shape
    return blocks.transpose(2, 0, 1, 3).reshape(total, 2 * chips * own).astype(F32)


def norm_scale(x0):
    return lax.rsqrt(jnp.mean(x0 * x0, axis=-1, keepdims=True) + 1e-05)


def plain_half(slices, embed, head_row, devices):
    part = jnp.dot(slices, embed, preferred_element_type=F32)
    score = jnp.sum(part * head_row.astype(F32), axis=-1, keepdims=True)
    return *split_halves(part, devices), score


def plain_hidden(mine, got, gain_row, w_gate, w_up, down, valid, devices):
    x0 = join_halves(mine, got)
    normed = (x0 * norm_scale(x0) * gain_row.astype(F32)).astype(BF16)
    a = jnp.dot(normed, w_gate, preferred_element_type=F32)
    b = jnp.dot(normed, w_up, preferred_element_type=F32)
    sigma = jax.nn.sigmoid(a)
    active = a * sigma
    hidden = (active * b).astype(BF16).astype(F32)
    d_hidden = valid * down
    d_gate = (d_hidden * b * sigma * (1.0 + a * (1.0 - sigma))).astype(BF16)
    d_up = (d_hidden * active).astype(BF16)
    part = jnp.einsum("tf,df->td", d_gate, w_gate, preferred_element_type=F32)
    part = part + jnp.einsum("tf,df->td", d_up, w_up, preferred_element_type=F32)
    return *split_halves(part, devices), jnp.sum(hidden * down, axis=-1, keepdims=True)


def plain_input(mine, got, d_mine, d_got, gain_row, head_row, valid, embed):
    x0 = join_halves(mine, got)
    inv = norm_scale(x0)
    scaled = join_halves(d_mine, d_got) * gain_row.astype(F32)
    dx = inv * scaled - x0 * inv * inv * inv * jnp.mean(scaled * x0, axis=-1, keepdims=True)
    dx = (dx + valid * head_row.astype(F32)).astype(BF16)
    return jnp.einsum("td,vd->tv", dx, embed, preferred_element_type=F32).astype(BF16)


def body(logits, embed, norm_gain, w_gate, w_up, w_down, head, counts):
    devices = lax.axis_size("dp")
    rows, voc = logits.shape
    part = voc // devices
    width = embed.shape[1]
    hidden = w_gate.shape[1]
    own, chips = width // devices, devices // 2
    requests = counts.shape[0]
    total = rows * devices
    request_len = total // requests
    tiled = own % 128 == 0 and hidden % 128 == 0 and total % 16 == 0 and part % 16 == 0
    head_row, gain_row = head.reshape(1, width), norm_gain.reshape(1, width)
    if tiled:
        column = struct((rows, 1), F32)
        blocked, top, scale = call(
            softmax_kernel, [struct((devices, rows, part), BF16), column, column], logits
        )
    else:
        probs32 = jax.nn.softmax(logits.astype(F32), axis=-1)
        blocked = probs32.astype(BF16).reshape(rows, devices, part).transpose(1, 0, 2)
    slices = exchange(blocked).reshape(total, part)
    column = struct((total, 1), F32)
    half = (chips, total, own)
    flops = total * part * width
    if tiled:
        cuts = 2 if part % 32 == 0 else 1
        table = [pltpu.VMEM((chips, part, own), BF16), pltpu.SemaphoreType.DMA((cuts * chips,))]
        args = dict(streamed=(1,), flops=flops, scratch=table, room=part * width)
        send, score_a = call(
            functools.partial(half_kernel, True), [struct(half, BF16), column],
            slices, embed, head_row, **args,
        )
        keep, score_b = call(
            functools.partial(half_kernel, False), [struct(half, F32), column],
            slices, embed, head_row, **args,
        )
    else:
        send, keep, score_a = plain_half(slices, embed, head_row, devices)
    x_mine = sum_and_gather(swap_sum(send, keep, devices), devices)
    x_got = swap_cores(x_mine, devices)
    if tiled:
        steps = hidden // 128
        (down_row,) = call(
            down_kernel, [struct((1, hidden), F32)], head_row, w_down,
            streamed=(1,), flops=2 * hidden * width, room=2 * hidden * width,
            scratch=(pltpu.VMEM((hidden, width), BF16), pltpu.SemaphoreType.DMA((steps,))),
        )
        wide = struct((total, hidden), F32)
        weight = (width // 2, hidden)
        sems = pltpu.SemaphoreType.DMA((2, chips))
        args = dict(streamed=(2, 3), flops=2 * total * hidden * width, room=2 * width * hidden)
        a, b, squares, gate, up = call(
            first_kernel,
            [wide, wide, column, pltpu.VMEM(weight, BF16), pltpu.VMEM(weight, BF16)],
            x_mine, gain_row, w_gate, w_up, scratch=(sems,), **args,
        )
        narrow = struct((total, hidden), BF16)
        send, score_c, d_gate, d_up = call(
            second_kernel, [struct(half, BF16), column, narrow, narrow],
            x_got, gain_row, w_gate, w_up, a, b, squares, down_row, counts,
            scratch=(pltpu.VMEM(weight, BF16), pltpu.VMEM(weight, BF16), sems),
            scalars=(8,), **args,
        )
        (keep,) = call(
            third_kernel, [struct(half, F32)], d_gate, d_up, gate, up,
            kept=(2, 3), flops=2 * total * hidden * width,
        )
    else:
        down_row = jnp.sum(w_down.astype(F32) * head.astype(F32)[None, :], axis=-1)[None]
        position = jnp.arange(total, dtype=jnp.int32)[:, None]
        member = position // request_len == jnp.arange(requests, dtype=jnp.int32)[None, :]
        limit = jnp.sum(jnp.where(member, counts[None, :], 0), axis=-1, keepdims=True)
        valid = (position % request_len < limit).astype(F32)
        send, keep, score_c = plain_hidden(
            x_mine, x_got, gain_row, w_gate, w_up, down_row, valid, devices
        )
    d_mine = sum_and_gather(swap_sum(send, keep, devices), devices)
    d_got = swap_cores(d_mine, devices)
    sources = (x_mine, x_got, d_mine, d_got, gain_row, head_row)
    padded = part + 3 * requests
    if tiled:
        (d_slices,) = call(
            input_kernel, [struct((devices, rows, padded), BF16)],
            *sources, score_a, score_b, score_c, counts, embed,
            scalars=(9,), streamed=(10,), flops=2 * flops, room=2 * part * width,
            scratch=(
                pltpu.VMEM((total, width), BF16), pltpu.VMEM((part, width), BF16),
                pltpu.SemaphoreType.DMA((-(-part // 64),)),
            ),
        )
    else:
        d_slices = plain_input(*sources, valid, embed).reshape(devices, rows, part)
        score = jnp.where(member, valid * (score_a + score_c), 0.0)
        extra = split3(jnp.sum(score, axis=0)).reshape(1, 1, requests * 3)
        extra = jnp.broadcast_to(extra, (devices, rows, requests * 3))
        d_slices = jnp.concatenate([d_slices, extra], axis=-1)
    back = exchange(d_slices)
    counts32 = counts.astype(F32)
    if tiled:
        guidance, rewards = call(
            final_kernel, [struct((rows, voc), BF16), struct((1, requests), F32)],
            logits, top, scale, back, counts32.reshape(1, requests),
            scratch=(pltpu.VMEM((rows, voc), F32),),
        )
        return (guidance, rewards.reshape(requests))
    sums = jnp.sum(back[:, 0, part:].astype(F32).reshape(devices, requests, 3), axis=(0, 2))
    rewards = sums / counts32
    d_probs = back[:, :, :part].transpose(1, 0, 2).reshape(rows, voc).astype(F32)
    d_logits = probs32 * (d_probs - jnp.sum(probs32 * d_probs, axis=-1, keepdims=True))
    guidance = (math.sqrt(VOC) * d_logits).astype(BF16)
    return (guidance, rewards)


def solution(mesh):
    placed = (
        P(("groups", "dp"), None),
        P("dp", None),
        P(),
        P(None, "dp"),
        P(None, "dp"),
        P("dp", None),
        P(),
        P("groups"),
    )
    return jax.shard_map(
        body,
        mesh=mesh,
        in_specs=placed,
        out_specs=(P(("groups", "dp"), None), P("groups")),
        check_vma=False,
    )
```

```python
import functools
import math

import jax
import jax.numpy as jnp
from jax import lax
from jax.experimental import pallas as pl
from jax.experimental.pallas import tpu as pltpu
from jax.sharding import PartitionSpec as P

VOC = 32000
F32, BF16 = jnp.float32, jnp.bfloat16
VMEM_BYTES = 12 * 1024 * 1024


def swap_cores(value, devices):
    return lax.ppermute(value, "dp", [(i, i ^ 1) for i in range(devices)])


def exchange(blocks):
    return lax.all_to_all(blocks, "dp", split_axis=0, concat_axis=0, tiled=True)


def exchange_chips(blocks, devices):
    groups = [list(range(core, devices, 2)) for core in range(2)]
    return lax.all_to_all(
        blocks, "dp", split_axis=0, concat_axis=0, axis_index_groups=groups, tiled=True
    )


def split3(value):
    hi = lax.reduce_precision(value, 8, 7)
    rest = value - hi
    mid = lax.reduce_precision(rest, 8, 7)
    low = rest - mid
    return jnp.stack([hi, mid, low], axis=-1).astype(BF16)


HBM_SPEC = pl.BlockSpec(memory_space=pltpu.HBM)
VMEM_SPEC = pl.BlockSpec(memory_space=pltpu.VMEM)
SMEM_SPEC = pl.BlockSpec(memory_space=pltpu.SMEM)


WINDOW = 128


def call(kernel, outs, *args, streamed=(), kept=(), scalars=(), flops=0, scratch=(), room=0):
    size = sum(math.prod(a.shape) * a.dtype.itemsize for a in args)
    places = {i: pltpu.HBM for i in streamed} | {i: pltpu.VMEM for i in kept}
    specs = [
        HBM_SPEC if i in streamed else SMEM_SPEC if i in scalars else VMEM_SPEC
        for i in range(len(args))
    ]
    return pl.pallas_call(
        kernel,
        out_shape=outs,
        in_specs=specs,
        out_specs=[VMEM_SPEC] * len(outs),
        scratch_shapes=list(scratch),
        compiler_params=pltpu.CompilerParams(vmem_limit_bytes=VMEM_BYTES + room),
        cost_estimate=pl.CostEstimate(flops=flops, bytes_accessed=size, transcendentals=0),
    )(*[
        pltpu.with_memory_space_constraint(a, places[i]) if i in places else a
        for i, a in enumerate(args)
    ])


class Stream:
    def __init__(self, copies):
        self.copies = copies
        self.done = 0
        for copy in copies[:WINDOW]:
            copy.start()

    def wait(self, count):
        while self.done < count:
            self.copies[self.done].wait()
            self.done += 1
            if self.done + WINDOW <= len(self.copies):
                self.copies[self.done + WINDOW - 1].start()


def struct(shape, dtype):
    return jax.ShapeDtypeStruct(shape, dtype)


def this_core():
    return lax.axis_index("dp") % 2


def span(start, size):
    return pl.ds(pl.multiple_of(start, size), size)


def softmax_kernel(logits_ref, out_ref, top_ref, scale_ref):
    devices, _, part = out_ref.shape
    x = logits_ref[...].astype(F32)
    top = jnp.max(x, axis=-1, keepdims=True)
    e = jnp.exp(x - top)
    scale = 1.0 / jnp.sum(e, axis=-1, keepdims=True)
    probs = e * scale
    for d in range(devices):
        out_ref[d] = probs[:, d * part : (d + 1) * part].astype(BF16)
    top_ref[...] = top
    scale_ref[...] = scale


def final_kernel(
    logits_ref, top_ref, scale_ref, back_ref, counts_ref, out_ref, rewards_ref, d_ref
):
    devices, _, padded = back_ref.shape
    part = out_ref.shape[1] // devices
    requests = counts_ref.shape[1]
    sums = jnp.zeros((1, requests), F32)
    for d in range(devices):
        block = back_ref[d].astype(F32)
        d_ref[:, d * part : (d + 1) * part] = block[:, :part]
        for i in range(3):
            start = part + i * requests
            sums += block[:1, start : start + requests]
    rewards_ref[...] = sums / counts_ref[...]
    probs = jnp.exp(logits_ref[...].astype(F32) - top_ref[...]) * scale_ref[...]
    d_probs = d_ref[...]
    mean = jnp.sum(probs * d_probs, axis=-1, keepdims=True)
    out_ref[...] = (math.sqrt(VOC) * (probs * (d_probs - mean))).astype(BF16)


def valid_column(counts_ref, total):
    requests = counts_ref.shape[0]
    length = total // requests
    position = lax.broadcasted_iota(jnp.int32, (total, 1), 0)
    valid = jnp.zeros((total, 1), F32)
    for r in range(requests):
        inside = (position >= r * length) & (position < r * length + counts_ref[r])
        valid = jnp.where(inside, 1.0, valid)
    return valid, position // length


def half_kernel(
    other, slices_ref, embed_ref, head_ref, after_ref, out_ref, score_ref, table, sems
):
    chips, _, own = out_ref.shape
    part = embed_ref.shape[0]
    cuts = sems.shape[0] // chips
    del after_ref
    core = this_core()
    half = (1 - core) if other else core
    rows = part // cuts

    def columns(j):
        return span((half * chips + j) * own, own)

    stream = Stream([
        pltpu.make_async_copy(
            embed_ref.at[pl.ds(i * rows, rows), columns(j)],
            table.at[j, pl.ds(i * rows, rows)],
            sems.at[j * cuts + i],
        )
        for j in range(chips)
        for i in range(cuts)
    ])
    slices = slices_ref[...]
    score = jnp.zeros(score_ref.shape, F32)
    for j in range(chips):
        stream.wait((j + 1) * cuts)
        part = jnp.dot(slices, table[j], preferred_element_type=F32)
        score += jnp.sum(part * head_ref[:, columns(j)].astype(F32), axis=-1, keepdims=True)
        out_ref[j] = part.astype(out_ref.dtype)
    score_ref[...] = score


def down_kernel(head_ref, down_ref, after_ref, out_ref, table, sems):
    del after_ref
    steps = sems.shape[0]
    rows = down_ref.shape[0] // steps
    stream = Stream([
        pltpu.make_async_copy(
            down_ref.at[pl.ds(i * rows, rows)], table.at[pl.ds(i * rows, rows)], sems.at[i]
        )
        for i in range(steps)
    ])
    head = jnp.broadcast_to(head_ref[...].astype(F32), (16, head_ref.shape[1])).astype(BF16)
    contract = (((1,), (1,)), ((), ()))
    for i in range(steps):
        stream.wait(i + 1)
        part = lax.dot_general(
            head, table[i * rows : (i + 1) * rows], contract, preferred_element_type=F32
        )
        out_ref[:, i * rows : (i + 1) * rows] = part[:1]


def forward_half(x_ref, gain_ref, gate_ref, up_ref, gate, up, sems, half, sums):
    chips, _, own = x_ref.shape

    def rows(j):
        return span((half * chips + j) * own, own)

    stream = Stream([
        pltpu.make_async_copy(source.at[rows(j)], target.at[pl.ds(j * own, own)], sems.at[k, j])
        for j in range(chips)
        for k, (source, target) in enumerate(((gate_ref, gate), (up_ref, up)))
    ])
    a, b, squares = sums
    scaled = []
    for j in range(chips):
        x = x_ref[j].astype(F32)
        squares = squares + jnp.sum(x * x, axis=-1, keepdims=True)
        scaled.append((x * gain_ref[:, rows(j)].astype(F32)).astype(BF16))
    for j in range(chips):
        r = slice(j * own, (j + 1) * own)
        stream.wait(2 * (j + 1))
        a = a + jnp.dot(scaled[j], gate[r], preferred_element_type=F32)
        b = b + jnp.dot(scaled[j], up[r], preferred_element_type=F32)
    return a, b, squares


def backward_half(d_gate, d_up, gate, up, out_ref):
    chips, _, own = out_ref.shape
    contract = (((1,), (1,)), ((), ()))
    for j in range(chips):
        r = slice(j * own, (j + 1) * own)
        part = lax.dot_general(d_gate, gate[r], contract, preferred_element_type=F32)
        part += lax.dot_general(d_up, up[r], contract, preferred_element_type=F32)
        out_ref[j] = part.astype(out_ref.dtype)


def first_kernel(
    x_ref, gain_ref, gate_ref, up_ref, a_ref, b_ref, squares_ref, gate, up, sems
):
    zeros = jnp.zeros(a_ref.shape, F32)
    sums = (zeros, zeros, jnp.zeros(squares_ref.shape, F32))
    sums = forward_half(x_ref, gain_ref, gate_ref, up_ref, gate, up, sems, this_core(), sums)
    a_ref[...], b_ref[...], squares_ref[...] = sums


def second_kernel(
    x_ref, gain_ref, gate_ref, up_ref, a_ref, b_ref, squares_ref, down_ref, counts_ref,
    send_ref, score_ref, d_gate_ref, d_up_ref, gate, up, sems,
):
    total = x_ref.shape[1]
    width = gate_ref.shape[0]
    sums = (a_ref[...], b_ref[...], squares_ref[...])
    a, b, squares = forward_half(
        x_ref, gain_ref, gate_ref, up_ref, gate, up, sems, 1 - this_core(), sums
    )
    inv = lax.rsqrt(squares / width + 1e-05)
    a, b = a * inv, b * inv
    sigma = jax.nn.sigmoid(a)
    active = a * sigma
    down = down_ref[...]
    hidden = (active * b).astype(BF16).astype(F32)
    score_ref[...] = jnp.sum(hidden * down, axis=-1, keepdims=True)
    valid, _ = valid_column(counts_ref, total)
    d_hidden = valid * down
    d_gate = (d_hidden * b * sigma * (1.0 + a * (1.0 - sigma))).astype(BF16)
    d_up = (d_hidden * active).astype(BF16)
    d_gate_ref[...], d_up_ref[...] = d_gate, d_up
    backward_half(d_gate, d_up, gate, up, send_ref)


def third_kernel(d_gate_ref, d_up_ref, gate_ref, up_ref, keep_ref):
    backward_half(d_gate_ref[...], d_up_ref[...], gate_ref, up_ref, keep_ref)


def input_kernel(
    mine_ref, got_ref, d_mine_ref, d_got_ref, gain_ref, head_ref,
    score_a_ref, score_b_ref, score_c_ref, counts_ref, embed_ref,
    out_ref, dx_ref, table, sems,
):
    chips, total, own = mine_ref.shape
    devices, per, _ = out_ref.shape
    voc = embed_ref.shape[0]
    requests = counts_ref.shape[0]
    width = 2 * chips * own
    core = this_core()
    tile = 256
    fine = 32
    stream = Stream([
        pltpu.make_async_copy(
            embed_ref.at[pl.ds(i, min(fine, voc - i))],
            table.at[pl.ds(i, min(fine, voc - i))],
            sems.at[i // fine],
        )
        for i in range(0, voc, fine)
    ])
    sources = ((mine_ref, d_mine_ref, core), (got_ref, d_got_ref, 1 - core))
    squares = jnp.zeros((total, 1), F32)
    dots = jnp.zeros((total, 1), F32)
    for x_ref, d_ref, half in sources:
        for j in range(chips):
            x = x_ref[j].astype(F32)
            g = d_ref[j].astype(F32) * gain_ref[:, span((half * chips + j) * own, own)].astype(F32)
            squares += jnp.sum(x * x, axis=-1, keepdims=True)
            dots += jnp.sum(g * x, axis=-1, keepdims=True)
    inv = lax.rsqrt(squares / width + 1e-05)
    mean = dots / width
    valid, request = valid_column(counts_ref, total)
    for x_ref, d_ref, half in sources:
        for j in range(chips):
            columns = span((half * chips + j) * own, own)
            x = x_ref[j].astype(F32)
            g = d_ref[j].astype(F32) * gain_ref[:, columns].astype(F32)
            dx = inv * g - x * inv * inv * inv * mean
            dx_ref[:, columns] = (dx + valid * head_ref[:, columns].astype(F32)).astype(BF16)
    score = valid * (score_a_ref[...] + score_b_ref[...] + score_c_ref[...])
    member = request == lax.broadcasted_iota(jnp.int32, (total, requests), 1)
    value = jnp.sum(jnp.where(member, score, 0.0), axis=0, keepdims=True)
    pieces = []
    for _ in range(3):
        piece = value.astype(BF16).astype(F32)
        pieces.append(piece)
        value = value - piece
    for i, piece in enumerate(pieces):
        start = voc + i * requests
        spread = jnp.broadcast_to(piece, (per, requests)).astype(BF16)
        for d in range(devices):
            out_ref[d, :, start : start + requests] = spread
    contract = (((1,), (1,)), ((), ()))
    dx = dx_ref[...]
    for start in range(0, voc, tile):
        end = min(start + tile, voc)
        stream.wait(-(-end // fine))
        part = lax.dot_general(dx, table[start:end, :], contract, preferred_element_type=F32)
        for d in range(devices):
            out_ref[d, :, start:end] = part[d * per : (d + 1) * per].astype(BF16)


def swap_sum(send, keep, devices):
    return (keep.astype(F32) + swap_cores(send, devices).astype(F32)).astype(BF16)


def sum_and_gather(half, devices):
    total = jnp.sum(exchange_chips(half, devices).astype(F32), axis=0).astype(BF16)
    return exchange_chips(jnp.broadcast_to(total[None], half.shape), devices)


def pick(blocks, index):
    return lax.dynamic_index_in_dim(blocks, index, 0, keepdims=False)


def split_halves(part, devices):
    total, width = part.shape
    core = lax.axis_index("dp") % 2
    blocks = part.reshape(total, 2, devices // 2, width // devices).transpose(1, 2, 0, 3)
    return pick(blocks, 1 - core).astype(BF16), pick(blocks, core)


def join_halves(mine, got):
    core = lax.axis_index("dp") % 2
    blocks = jnp.where(core == 1, jnp.stack([got, mine]), jnp.stack([mine, got]))
    _, chips, total, own = blocks.shape
    return blocks.transpose(2, 0, 1, 3).reshape(total, 2 * chips * own).astype(F32)


def norm_scale(x0):
    return lax.rsqrt(jnp.mean(x0 * x0, axis=-1, keepdims=True) + 1e-05)


def plain_half(slices, embed, head_row, devices):
    part = jnp.dot(slices, embed, preferred_element_type=F32)
    score = jnp.sum(part * head_row.astype(F32), axis=-1, keepdims=True)
    return *split_halves(part, devices), score


def plain_hidden(mine, got, gain_row, w_gate, w_up, down, valid, devices):
    x0 = join_halves(mine, got)
    normed = (x0 * norm_scale(x0) * gain_row.astype(F32)).astype(BF16)
    a = jnp.dot(normed, w_gate, preferred_element_type=F32)
    b = jnp.dot(normed, w_up, preferred_element_type=F32)
    sigma = jax.nn.sigmoid(a)
    active = a * sigma
    hidden = (active * b).astype(BF16).astype(F32)
    d_hidden = valid * down
    d_gate = (d_hidden * b * sigma * (1.0 + a * (1.0 - sigma))).astype(BF16)
    d_up = (d_hidden * active).astype(BF16)
    part = jnp.einsum("tf,df->td", d_gate, w_gate, preferred_element_type=F32)
    part = part + jnp.einsum("tf,df->td", d_up, w_up, preferred_element_type=F32)
    return *split_halves(part, devices), jnp.sum(hidden * down, axis=-1, keepdims=True)


def plain_input(mine, got, d_mine, d_got, gain_row, head_row, valid, embed):
    x0 = join_halves(mine, got)
    inv = norm_scale(x0)
    scaled = join_halves(d_mine, d_got) * gain_row.astype(F32)
    dx = inv * scaled - x0 * inv * inv * inv * jnp.mean(scaled * x0, axis=-1, keepdims=True)
    dx = (dx + valid * head_row.astype(F32)).astype(BF16)
    return jnp.einsum("td,vd->tv", dx, embed, preferred_element_type=F32).astype(BF16)


def body(logits, embed, norm_gain, w_gate, w_up, w_down, head, counts):
    devices = lax.axis_size("dp")
    rows, voc = logits.shape
    part = voc // devices
    width = embed.shape[1]
    hidden = w_gate.shape[1]
    own, chips = width // devices, devices // 2
    requests = counts.shape[0]
    total = rows * devices
    request_len = total // requests
    tiled = own % 128 == 0 and hidden % 128 == 0 and total % 16 == 0 and part % 16 == 0
    head_row, gain_row = head.reshape(1, width), norm_gain.reshape(1, width)
    if tiled:
        column = struct((rows, 1), F32)
        blocked, top, scale = call(
            softmax_kernel, [struct((devices, rows, part), BF16), column, column], logits
        )
    else:
        probs32 = jax.nn.softmax(logits.astype(F32), axis=-1)
        blocked = probs32.astype(BF16).reshape(rows, devices, part).transpose(1, 0, 2)
    slices = exchange(blocked).reshape(total, part)
    column = struct((total, 1), F32)
    half = (chips, total, own)
    flops = total * part * width
    if tiled:
        steps = hidden // 128
        (down_row,) = call(
            down_kernel, [struct((1, hidden), F32)], head_row, w_down, blocked,
            streamed=(1,), flops=2 * hidden * width, room=2 * hidden * width,
            scratch=(pltpu.VMEM((hidden, width), BF16), pltpu.SemaphoreType.DMA((steps,))),
        )
        cuts = 5 if part % 80 == 0 else 1
        table = [pltpu.VMEM((chips, part, own), BF16), pltpu.SemaphoreType.DMA((cuts * chips,))]
        args = dict(streamed=(1,), flops=flops, scratch=table, room=part * width)
        send, score_a = call(
            functools.partial(half_kernel, True), [struct(half, BF16), column],
            slices, embed, head_row, down_row, **args,
        )
        keep, score_b = call(
            functools.partial(half_kernel, False), [struct(half, F32), column],
            slices, embed, head_row, down_row, **args,
        )
    else:
        send, keep, score_a = plain_half(slices, embed, head_row, devices)
    x_mine = sum_and_gather(swap_sum(send, keep, devices), devices)
    x_got = swap_cores(x_mine, devices)
    if tiled:
        wide = struct((total, hidden), F32)
        weight = (width // 2, hidden)
        sems = pltpu.SemaphoreType.DMA((2, chips))
        args = dict(streamed=(2, 3), flops=2 * total * hidden * width, room=2 * width * hidden)
        a, b, squares, gate, up = call(
            first_kernel,
            [wide, wide, column, pltpu.VMEM(weight, BF16), pltpu.VMEM(weight, BF16)],
            x_mine, gain_row, w_gate, w_up, scratch=(sems,), **args,
        )
        narrow = struct((total, hidden), BF16)
        send, score_c, d_gate, d_up = call(
            second_kernel, [struct(half, BF16), column, narrow, narrow],
            x_got, gain_row, w_gate, w_up, a, b, squares, down_row, counts,
            scratch=(pltpu.VMEM(weight, BF16), pltpu.VMEM(weight, BF16), sems),
            scalars=(8,), **args,
        )
        (keep,) = call(
            third_kernel, [struct(half, F32)], d_gate, d_up, gate, up,
            kept=(2, 3), flops=2 * total * hidden * width,
        )
    else:
        down_row = jnp.sum(w_down.astype(F32) * head.astype(F32)[None, :], axis=-1)[None]
        position = jnp.arange(total, dtype=jnp.int32)[:, None]
        member = position // request_len == jnp.arange(requests, dtype=jnp.int32)[None, :]
        limit = jnp.sum(jnp.where(member, counts[None, :], 0), axis=-1, keepdims=True)
        valid = (position % request_len < limit).astype(F32)
        send, keep, score_c = plain_hidden(
            x_mine, x_got, gain_row, w_gate, w_up, down_row, valid, devices
        )
    d_mine = sum_and_gather(swap_sum(send, keep, devices), devices)
    d_got = swap_cores(d_mine, devices)
    sources = (x_mine, x_got, d_mine, d_got, gain_row, head_row)
    padded = part + 3 * requests
    if tiled:
        (d_slices,) = call(
            input_kernel, [struct((devices, rows, padded), BF16)],
            *sources, score_a, score_b, score_c, counts, embed,
            scalars=(9,), streamed=(10,), flops=2 * flops, room=2 * part * width,
            scratch=(
                pltpu.VMEM((total, width), BF16), pltpu.VMEM((part, width), BF16),
                pltpu.SemaphoreType.DMA((-(-part // 32),)),
            ),
        )
    else:
        d_slices = plain_input(*sources, valid, embed).reshape(devices, rows, part)
        score = jnp.where(member, valid * (score_a + score_c), 0.0)
        extra = split3(jnp.sum(score, axis=0)).reshape(1, 1, requests * 3)
        extra = jnp.broadcast_to(extra, (devices, rows, requests * 3))
        d_slices = jnp.concatenate([d_slices, extra], axis=-1)
    back = exchange(d_slices)
    counts32 = counts.astype(F32)
    if tiled:
        guidance, rewards = call(
            final_kernel, [struct((rows, voc), BF16), struct((1, requests), F32)],
            logits, top, scale, back, counts32.reshape(1, requests),
            scratch=(pltpu.VMEM((rows, voc), F32),),
        )
        return (guidance, rewards.reshape(requests))
    sums = jnp.sum(back[:, 0, part:].astype(F32).reshape(devices, requests, 3), axis=(0, 2))
    rewards = sums / counts32
    d_probs = back[:, :, :part].transpose(1, 0, 2).reshape(rows, voc).astype(F32)
    d_logits = probs32 * (d_probs - jnp.sum(probs32 * d_probs, axis=-1, keepdims=True))
    guidance = (math.sqrt(VOC) * d_logits).astype(BF16)
    return (guidance, rewards)


def solution(mesh):
    placed = (
        P(("groups", "dp"), None),
        P("dp", None),
        P(),
        P(None, "dp"),
        P(None, "dp"),
        P("dp", None),
        P(),
        P("groups"),
    )
    return jax.shard_map(
        body,
        mesh=mesh,
        in_specs=placed,
        out_specs=(P(("groups", "dp"), None), P("groups")),
        check_vma=False,
    )
```

```python
import functools
import math

import jax
import jax.numpy as jnp
from jax import lax
from jax.experimental import pallas as pl
from jax.experimental.pallas import tpu as pltpu
from jax.sharding import PartitionSpec as P

VOC = 32000
F32, BF16 = jnp.float32, jnp.bfloat16
VMEM_BYTES = 12 * 1024 * 1024


def swap_cores(value, devices):
    return lax.ppermute(value, "dp", [(i, i ^ 1) for i in range(devices)])


def exchange(blocks):
    return lax.all_to_all(blocks, "dp", split_axis=0, concat_axis=0, tiled=True)


def exchange_chips(blocks, devices):
    groups = [list(range(core, devices, 2)) for core in range(2)]
    return lax.all_to_all(
        blocks, "dp", split_axis=0, concat_axis=0, axis_index_groups=groups, tiled=True
    )


def split3(value):
    hi = lax.reduce_precision(value, 8, 7)
    rest = value - hi
    mid = lax.reduce_precision(rest, 8, 7)
    low = rest - mid
    return jnp.stack([hi, mid, low], axis=-1).astype(BF16)


HBM_SPEC = pl.BlockSpec(memory_space=pltpu.HBM)
VMEM_SPEC = pl.BlockSpec(memory_space=pltpu.VMEM)
SMEM_SPEC = pl.BlockSpec(memory_space=pltpu.SMEM)


WINDOW = 128


def call(kernel, outs, *args, streamed=(), kept=(), scalars=(), flops=0, scratch=(), room=0):
    size = sum(math.prod(a.shape) * a.dtype.itemsize for a in args)
    places = {i: pltpu.HBM for i in streamed} | {i: pltpu.VMEM for i in kept}
    specs = [
        HBM_SPEC if i in streamed else SMEM_SPEC if i in scalars else VMEM_SPEC
        for i in range(len(args))
    ]
    return pl.pallas_call(
        kernel,
        out_shape=outs,
        in_specs=specs,
        out_specs=[VMEM_SPEC] * len(outs),
        scratch_shapes=list(scratch),
        compiler_params=pltpu.CompilerParams(vmem_limit_bytes=VMEM_BYTES + room),
        cost_estimate=pl.CostEstimate(flops=flops, bytes_accessed=size, transcendentals=0),
    )(*[
        pltpu.with_memory_space_constraint(a, places[i]) if i in places else a
        for i, a in enumerate(args)
    ])


class Stream:
    def __init__(self, copies):
        self.copies = copies
        self.done = 0
        for copy in copies[:WINDOW]:
            copy.start()

    def wait(self, count):
        while self.done < count:
            self.copies[self.done].wait()
            self.done += 1
            if self.done + WINDOW <= len(self.copies):
                self.copies[self.done + WINDOW - 1].start()


def struct(shape, dtype):
    return jax.ShapeDtypeStruct(shape, dtype)


def this_core():
    return lax.axis_index("dp") % 2


def span(start, size):
    return pl.ds(pl.multiple_of(start, size), size)


def softmax_kernel(logits_ref, out_ref, top_ref, scale_ref):
    devices, _, part = out_ref.shape
    x = logits_ref[...].astype(F32)
    top = jnp.max(x, axis=-1, keepdims=True)
    e = jnp.exp(x - top)
    scale = 1.0 / jnp.sum(e, axis=-1, keepdims=True)
    probs = e * scale
    for d in range(devices):
        out_ref[d] = probs[:, d * part : (d + 1) * part].astype(BF16)
    top_ref[...] = top
    scale_ref[...] = scale


def final_kernel(
    logits_ref, top_ref, scale_ref, back_ref, counts_ref, out_ref, rewards_ref, d_ref
):
    devices, _, padded = back_ref.shape
    part = out_ref.shape[1] // devices
    requests = counts_ref.shape[1]
    sums = jnp.zeros((1, requests), F32)
    for d in range(devices):
        block = back_ref[d].astype(F32)
        d_ref[:, d * part : (d + 1) * part] = block[:, :part]
        for i in range(3):
            start = part + i * requests
            sums += block[:1, start : start + requests]
    rewards_ref[...] = sums / counts_ref[...]
    probs = jnp.exp(logits_ref[...].astype(F32) - top_ref[...]) * scale_ref[...]
    d_probs = d_ref[...]
    mean = jnp.sum(probs * d_probs, axis=-1, keepdims=True)
    out_ref[...] = (math.sqrt(VOC) * (probs * (d_probs - mean))).astype(BF16)


def valid_column(counts_ref, total):
    requests = counts_ref.shape[0]
    length = total // requests
    position = lax.broadcasted_iota(jnp.int32, (total, 1), 0)
    valid = jnp.zeros((total, 1), F32)
    for r in range(requests):
        inside = (position >= r * length) & (position < r * length + counts_ref[r])
        valid = jnp.where(inside, 1.0, valid)
    return valid, position // length


def half_kernel(
    other, slices_ref, embed_ref, head_ref, after_ref, out_ref, score_ref, table, acc, sems
):
    chips, total, own = out_ref.shape
    part = embed_ref.shape[0]
    del after_ref
    core = this_core()
    half = (1 - core) if other else core
    columns = span(half * chips * own, chips * own)
    tile, fine = 256, 128
    stream = Stream([
        pltpu.make_async_copy(
            embed_ref.at[pl.ds(i, min(fine, part - i)), columns],
            table.at[pl.ds(i, min(fine, part - i))],
            sems.at[i // fine],
        )
        for i in range(0, part, fine)
    ])
    for start in range(0, part, tile):
        end = min(start + tile, part)
        stream.wait(-(-end // fine))
        product = jnp.dot(
            slices_ref[:, start:end], table[start:end], preferred_element_type=F32
        )
        acc[...] = acc[...] + product if start else product
    score_ref[...] = jnp.sum(
        acc[...] * head_ref[:, columns].astype(F32), axis=-1, keepdims=True
    )
    for j in range(chips):
        out_ref[j] = acc[:, j * own : (j + 1) * own].astype(out_ref.dtype)


def down_kernel(head_ref, down_ref, after_ref, out_ref, table, sems):
    del after_ref
    steps = sems.shape[0]
    rows = down_ref.shape[0] // steps
    stream = Stream([
        pltpu.make_async_copy(
            down_ref.at[pl.ds(i * rows, rows)], table.at[pl.ds(i * rows, rows)], sems.at[i]
        )
        for i in range(steps)
    ])
    head = jnp.broadcast_to(head_ref[...].astype(F32), (16, head_ref.shape[1])).astype(BF16)
    contract = (((1,), (1,)), ((), ()))
    for i in range(steps):
        stream.wait(i + 1)
        part = lax.dot_general(
            head, table[i * rows : (i + 1) * rows], contract, preferred_element_type=F32
        )
        out_ref[:, i * rows : (i + 1) * rows] = part[:1]


def forward_half(x_ref, gain_ref, gate_ref, up_ref, gate, up, sems, half, sums):
    chips, _, own = x_ref.shape

    def rows(j):
        return span((half * chips + j) * own, own)

    stream = Stream([
        pltpu.make_async_copy(source.at[rows(j)], target.at[pl.ds(j * own, own)], sems.at[k, j])
        for j in range(chips)
        for k, (source, target) in enumerate(((gate_ref, gate), (up_ref, up)))
    ])
    a, b, squares = sums
    scaled = []
    for j in range(chips):
        x = x_ref[j].astype(F32)
        squares = squares + jnp.sum(x * x, axis=-1, keepdims=True)
        scaled.append((x * gain_ref[:, rows(j)].astype(F32)).astype(BF16))
    for j in range(chips):
        r = slice(j * own, (j + 1) * own)
        stream.wait(2 * (j + 1))
        a = a + jnp.dot(scaled[j], gate[r], preferred_element_type=F32)
        b = b + jnp.dot(scaled[j], up[r], preferred_element_type=F32)
    return a, b, squares


def backward_half(d_gate, d_up, gate, up, out_ref):
    chips, _, own = out_ref.shape
    contract = (((1,), (1,)), ((), ()))
    for j in range(chips):
        r = slice(j * own, (j + 1) * own)
        part = lax.dot_general(d_gate, gate[r], contract, preferred_element_type=F32)
        part += lax.dot_general(d_up, up[r], contract, preferred_element_type=F32)
        out_ref[j] = part.astype(out_ref.dtype)


def first_kernel(
    x_ref, gain_ref, gate_ref, up_ref, a_ref, b_ref, squares_ref, gate, up, sems
):
    zeros = jnp.zeros(a_ref.shape, F32)
    sums = (zeros, zeros, jnp.zeros(squares_ref.shape, F32))
    sums = forward_half(x_ref, gain_ref, gate_ref, up_ref, gate, up, sems, this_core(), sums)
    a_ref[...], b_ref[...], squares_ref[...] = sums


def second_kernel(
    x_ref, gain_ref, gate_ref, up_ref, a_ref, b_ref, squares_ref, down_ref, counts_ref,
    send_ref, score_ref, d_gate_ref, d_up_ref, gate, up, sems,
):
    total = x_ref.shape[1]
    width = gate_ref.shape[0]
    sums = (a_ref[...], b_ref[...], squares_ref[...])
    a, b, squares = forward_half(
        x_ref, gain_ref, gate_ref, up_ref, gate, up, sems, 1 - this_core(), sums
    )
    inv = lax.rsqrt(squares / width + 1e-05)
    a, b = a * inv, b * inv
    sigma = jax.nn.sigmoid(a)
    active = a * sigma
    down = down_ref[...]
    hidden = (active * b).astype(BF16).astype(F32)
    score_ref[...] = jnp.sum(hidden * down, axis=-1, keepdims=True)
    valid, _ = valid_column(counts_ref, total)
    d_hidden = valid * down
    d_gate = (d_hidden * b * sigma * (1.0 + a * (1.0 - sigma))).astype(BF16)
    d_up = (d_hidden * active).astype(BF16)
    d_gate_ref[...], d_up_ref[...] = d_gate, d_up
    backward_half(d_gate, d_up, gate, up, send_ref)


def third_kernel(d_gate_ref, d_up_ref, gate_ref, up_ref, keep_ref):
    backward_half(d_gate_ref[...], d_up_ref[...], gate_ref, up_ref, keep_ref)


def input_kernel(
    mine_ref, got_ref, d_mine_ref, d_got_ref, gain_ref, head_ref,
    score_a_ref, score_b_ref, score_c_ref, counts_ref, embed_ref,
    out_ref, dx_ref, table, sems,
):
    chips, total, own = mine_ref.shape
    voc = embed_ref.shape[0]
    requests = counts_ref.shape[0]
    width = 2 * chips * own
    core = this_core()
    tile = 256
    fine = 64
    stream = Stream([
        pltpu.make_async_copy(
            embed_ref.at[pl.ds(i, min(fine, voc - i))],
            table.at[pl.ds(i, min(fine, voc - i))],
            sems.at[i // fine],
        )
        for i in range(0, voc, fine)
    ])
    sources = ((mine_ref, d_mine_ref, core), (got_ref, d_got_ref, 1 - core))
    squares = jnp.zeros((total, 1), F32)
    dots = jnp.zeros((total, 1), F32)
    for x_ref, d_ref, half in sources:
        for j in range(chips):
            x = x_ref[j].astype(F32)
            g = d_ref[j].astype(F32) * gain_ref[:, span((half * chips + j) * own, own)].astype(F32)
            squares += jnp.sum(x * x, axis=-1, keepdims=True)
            dots += jnp.sum(g * x, axis=-1, keepdims=True)
    inv = lax.rsqrt(squares / width + 1e-05)
    mean = dots / width
    valid, request = valid_column(counts_ref, total)
    for x_ref, d_ref, half in sources:
        for j in range(chips):
            columns = span((half * chips + j) * own, own)
            x = x_ref[j].astype(F32)
            g = d_ref[j].astype(F32) * gain_ref[:, columns].astype(F32)
            dx = inv * g - x * inv * inv * inv * mean
            dx_ref[:, columns] = (dx + valid * head_ref[:, columns].astype(F32)).astype(BF16)
    score = valid * (score_a_ref[...] + score_b_ref[...] + score_c_ref[...])
    member = request == lax.broadcasted_iota(jnp.int32, (total, requests), 1)
    value = jnp.sum(jnp.where(member, score, 0.0), axis=0, keepdims=True)
    pieces = []
    for _ in range(3):
        piece = value.astype(BF16).astype(F32)
        pieces.append(piece)
        value = value - piece
    for i, piece in enumerate(pieces):
        start = voc + i * requests
        spread = jnp.broadcast_to(piece, (total, requests)).astype(BF16)
        out_ref[:, start : start + requests] = spread
    contract = (((1,), (1,)), ((), ()))
    dx = dx_ref[...]
    for start in range(0, voc, tile):
        end = min(start + tile, voc)
        stream.wait(-(-end // fine))
        part = lax.dot_general(dx, table[start:end, :], contract, preferred_element_type=F32)
        out_ref[:, start:end] = part.astype(BF16)


def swap_sum(send, keep, devices):
    return (keep.astype(F32) + swap_cores(send, devices).astype(F32)).astype(BF16)


def sum_and_gather(half, devices):
    total = jnp.sum(exchange_chips(half, devices).astype(F32), axis=0).astype(BF16)
    return exchange_chips(jnp.broadcast_to(total[None], half.shape), devices)


def pick(blocks, index):
    return lax.dynamic_index_in_dim(blocks, index, 0, keepdims=False)


def split_halves(part, devices):
    total, width = part.shape
    core = lax.axis_index("dp") % 2
    blocks = part.reshape(total, 2, devices // 2, width // devices).transpose(1, 2, 0, 3)
    return pick(blocks, 1 - core).astype(BF16), pick(blocks, core)


def join_halves(mine, got):
    core = lax.axis_index("dp") % 2
    blocks = jnp.where(core == 1, jnp.stack([got, mine]), jnp.stack([mine, got]))
    _, chips, total, own = blocks.shape
    return blocks.transpose(2, 0, 1, 3).reshape(total, 2 * chips * own).astype(F32)


def norm_scale(x0):
    return lax.rsqrt(jnp.mean(x0 * x0, axis=-1, keepdims=True) + 1e-05)


def plain_half(slices, embed, head_row, devices):
    part = jnp.dot(slices, embed, preferred_element_type=F32)
    score = jnp.sum(part * head_row.astype(F32), axis=-1, keepdims=True)
    return *split_halves(part, devices), score


def plain_hidden(mine, got, gain_row, w_gate, w_up, down, valid, devices):
    x0 = join_halves(mine, got)
    normed = (x0 * norm_scale(x0) * gain_row.astype(F32)).astype(BF16)
    a = jnp.dot(normed, w_gate, preferred_element_type=F32)
    b = jnp.dot(normed, w_up, preferred_element_type=F32)
    sigma = jax.nn.sigmoid(a)
    active = a * sigma
    hidden = (active * b).astype(BF16).astype(F32)
    d_hidden = valid * down
    d_gate = (d_hidden * b * sigma * (1.0 + a * (1.0 - sigma))).astype(BF16)
    d_up = (d_hidden * active).astype(BF16)
    part = jnp.einsum("tf,df->td", d_gate, w_gate, preferred_element_type=F32)
    part = part + jnp.einsum("tf,df->td", d_up, w_up, preferred_element_type=F32)
    return *split_halves(part, devices), jnp.sum(hidden * down, axis=-1, keepdims=True)


def plain_input(mine, got, d_mine, d_got, gain_row, head_row, valid, embed):
    x0 = join_halves(mine, got)
    inv = norm_scale(x0)
    scaled = join_halves(d_mine, d_got) * gain_row.astype(F32)
    dx = inv * scaled - x0 * inv * inv * inv * jnp.mean(scaled * x0, axis=-1, keepdims=True)
    dx = (dx + valid * head_row.astype(F32)).astype(BF16)
    return jnp.einsum("td,vd->tv", dx, embed, preferred_element_type=F32).astype(BF16)


def body(logits, embed, norm_gain, w_gate, w_up, w_down, head, counts):
    devices = lax.axis_size("dp")
    rows, voc = logits.shape
    part = voc // devices
    width = embed.shape[1]
    hidden = w_gate.shape[1]
    own, chips = width // devices, devices // 2
    requests = counts.shape[0]
    total = rows * devices
    request_len = total // requests
    tiled = own % 128 == 0 and hidden % 128 == 0 and total % 16 == 0 and part % 16 == 0
    head_row, gain_row = head.reshape(1, width), norm_gain.reshape(1, width)
    if tiled:
        column = struct((rows, 1), F32)
        blocked, top, scale = call(
            softmax_kernel, [struct((devices, rows, part), BF16), column, column], logits
        )
    else:
        probs32 = jax.nn.softmax(logits.astype(F32), axis=-1)
        blocked = probs32.astype(BF16).reshape(rows, devices, part).transpose(1, 0, 2)
    slices = exchange(blocked).reshape(total, part)
    column = struct((total, 1), F32)
    half = (chips, total, own)
    flops = total * part * width
    if tiled:
        steps = hidden // 128
        (down_row,) = call(
            down_kernel, [struct((1, hidden), F32)], head_row, w_down, blocked,
            streamed=(1,), flops=2 * hidden * width, room=2 * hidden * width,
            scratch=(pltpu.VMEM((hidden, width), BF16), pltpu.SemaphoreType.DMA((steps,))),
        )
        table = [
            pltpu.VMEM((part, width // 2), BF16), pltpu.VMEM((total, width // 2), F32),
            pltpu.SemaphoreType.DMA((-(-part // 128),)),
        ]
        args = dict(streamed=(1,), flops=flops, scratch=table, room=part * width)
        send, score_a = call(
            functools.partial(half_kernel, True), [struct(half, BF16), column],
            slices, embed, head_row, down_row, **args,
        )
        keep, score_b = call(
            functools.partial(half_kernel, False), [struct(half, F32), column],
            slices, embed, head_row, down_row, **args,
        )
    else:
        send, keep, score_a = plain_half(slices, embed, head_row, devices)
    x_mine = sum_and_gather(swap_sum(send, keep, devices), devices)
    x_got = swap_cores(x_mine, devices)
    if tiled:
        wide = struct((total, hidden), F32)
        weight = (width // 2, hidden)
        sems = pltpu.SemaphoreType.DMA((2, chips))
        args = dict(streamed=(2, 3), flops=2 * total * hidden * width, room=2 * width * hidden)
        a, b, squares, gate, up = call(
            first_kernel,
            [wide, wide, column, pltpu.VMEM(weight, BF16), pltpu.VMEM(weight, BF16)],
            x_mine, gain_row, w_gate, w_up, scratch=(sems,), **args,
        )
        narrow = struct((total, hidden), BF16)
        send, score_c, d_gate, d_up = call(
            second_kernel, [struct(half, BF16), column, narrow, narrow],
            x_got, gain_row, w_gate, w_up, a, b, squares, down_row, counts,
            scratch=(pltpu.VMEM(weight, BF16), pltpu.VMEM(weight, BF16), sems),
            scalars=(8,), **args,
        )
        (keep,) = call(
            third_kernel, [struct(half, F32)], d_gate, d_up, gate, up,
            kept=(2, 3), flops=2 * total * hidden * width,
        )
    else:
        down_row = jnp.sum(w_down.astype(F32) * head.astype(F32)[None, :], axis=-1)[None]
        position = jnp.arange(total, dtype=jnp.int32)[:, None]
        member = position // request_len == jnp.arange(requests, dtype=jnp.int32)[None, :]
        limit = jnp.sum(jnp.where(member, counts[None, :], 0), axis=-1, keepdims=True)
        valid = (position % request_len < limit).astype(F32)
        send, keep, score_c = plain_hidden(
            x_mine, x_got, gain_row, w_gate, w_up, down_row, valid, devices
        )
    d_mine = sum_and_gather(swap_sum(send, keep, devices), devices)
    d_got = swap_cores(d_mine, devices)
    sources = (x_mine, x_got, d_mine, d_got, gain_row, head_row)
    padded = part + 3 * requests
    if tiled:
        (d_slices,) = call(
            input_kernel, [struct((total, padded), BF16)],
            *sources, score_a, score_b, score_c, counts, embed,
            scalars=(9,), streamed=(10,), flops=2 * flops, room=2 * part * width,
            scratch=(
                pltpu.VMEM((total, width), BF16), pltpu.VMEM((part, width), BF16),
                pltpu.SemaphoreType.DMA((-(-part // 64),)),
            ),
        )
    else:
        d_slices = plain_input(*sources, valid, embed)
        score = jnp.where(member, valid * (score_a + score_c), 0.0)
        extra = split3(jnp.sum(score, axis=0)).reshape(1, requests * 3)
        extra = jnp.broadcast_to(extra, (total, requests * 3))
        d_slices = jnp.concatenate([d_slices, extra], axis=-1)
    back = exchange(d_slices.reshape(devices, rows, padded))
    counts32 = counts.astype(F32)
    if tiled:
        guidance, rewards = call(
            final_kernel, [struct((rows, voc), BF16), struct((1, requests), F32)],
            logits, top, scale, back, counts32.reshape(1, requests),
            scratch=(pltpu.VMEM((rows, voc), F32),),
        )
        return (guidance, rewards.reshape(requests))
    sums = jnp.sum(back[:, 0, part:].astype(F32).reshape(devices, requests, 3), axis=(0, 2))
    rewards = sums / counts32
    d_probs = back[:, :, :part].transpose(1, 0, 2).reshape(rows, voc).astype(F32)
    d_logits = probs32 * (d_probs - jnp.sum(probs32 * d_probs, axis=-1, keepdims=True))
    guidance = (math.sqrt(VOC) * d_logits).astype(BF16)
    return (guidance, rewards)


def solution(mesh):
    placed = (
        P(("groups", "dp"), None),
        P("dp", None),
        P(),
        P(None, "dp"),
        P(None, "dp"),
        P("dp", None),
        P(),
        P("groups"),
    )
    return jax.shard_map(
        body,
        mesh=mesh,
        in_specs=placed,
        out_specs=(P(("groups", "dp"), None), P("groups")),
        check_vma=False,
    )
```

```python
import functools
import math

import jax
import jax.numpy as jnp
from jax import lax
from jax.experimental import pallas as pl
from jax.experimental.pallas import tpu as pltpu
from jax.sharding import PartitionSpec as P

VOC = 32000
F32, BF16 = jnp.float32, jnp.bfloat16
VMEM_BYTES = 12 * 1024 * 1024


def swap_cores(value, devices):
    return lax.ppermute(value, "dp", [(i, i ^ 1) for i in range(devices)])


def exchange(blocks):
    return lax.all_to_all(blocks, "dp", split_axis=0, concat_axis=0, tiled=True)


def exchange_chips(blocks, devices):
    groups = [list(range(core, devices, 2)) for core in range(2)]
    return lax.all_to_all(
        blocks, "dp", split_axis=0, concat_axis=0, axis_index_groups=groups, tiled=True
    )


def split3(value):
    hi = lax.reduce_precision(value, 8, 7)
    rest = value - hi
    mid = lax.reduce_precision(rest, 8, 7)
    low = rest - mid
    return jnp.stack([hi, mid, low], axis=-1).astype(BF16)


HBM_SPEC = pl.BlockSpec(memory_space=pltpu.HBM)
VMEM_SPEC = pl.BlockSpec(memory_space=pltpu.VMEM)
SMEM_SPEC = pl.BlockSpec(memory_space=pltpu.SMEM)


WINDOW = 128


def call(kernel, outs, *args, streamed=(), kept=(), scalars=(), flops=0, scratch=(), room=0):
    size = sum(math.prod(a.shape) * a.dtype.itemsize for a in args)
    places = {i: pltpu.HBM for i in streamed} | {i: pltpu.VMEM for i in kept}
    specs = [
        HBM_SPEC if i in streamed else SMEM_SPEC if i in scalars else VMEM_SPEC
        for i in range(len(args))
    ]
    return pl.pallas_call(
        kernel,
        out_shape=outs,
        in_specs=specs,
        out_specs=[VMEM_SPEC] * len(outs),
        scratch_shapes=list(scratch),
        compiler_params=pltpu.CompilerParams(vmem_limit_bytes=VMEM_BYTES + room),
        cost_estimate=pl.CostEstimate(flops=flops, bytes_accessed=size, transcendentals=0),
    )(*[
        pltpu.with_memory_space_constraint(a, places[i]) if i in places else a
        for i, a in enumerate(args)
    ])


class Stream:
    def __init__(self, copies):
        self.copies = copies
        self.done = 0
        for copy in copies[:WINDOW]:
            copy.start()

    def wait(self, count):
        while self.done < count:
            self.copies[self.done].wait()
            self.done += 1
            if self.done + WINDOW <= len(self.copies):
                self.copies[self.done + WINDOW - 1].start()


def struct(shape, dtype):
    return jax.ShapeDtypeStruct(shape, dtype)


def this_core():
    return lax.axis_index("dp") % 2


def span(start, size):
    return pl.ds(pl.multiple_of(start, size), size)


def softmax_kernel(logits_ref, out_ref, top_ref, scale_ref):
    devices, _, part = out_ref.shape
    x = logits_ref[...].astype(F32)
    top = jnp.max(x, axis=-1, keepdims=True)
    e = jnp.exp(x - top)
    scale = 1.0 / jnp.sum(e, axis=-1, keepdims=True)
    probs = e * scale
    for d in range(devices):
        out_ref[d] = probs[:, d * part : (d + 1) * part].astype(BF16)
    top_ref[...] = top
    scale_ref[...] = scale


def final_kernel(
    logits_ref, top_ref, scale_ref, back_ref, counts_ref, out_ref, rewards_ref, d_ref
):
    devices, _, padded = back_ref.shape
    part = out_ref.shape[1] // devices
    requests = counts_ref.shape[1]
    sums = jnp.zeros((1, requests), F32)
    for d in range(devices):
        block = back_ref[d].astype(F32)
        d_ref[:, d * part : (d + 1) * part] = block[:, :part]
        for i in range(3):
            start = part + i * requests
            sums += block[:1, start : start + requests]
    rewards_ref[...] = sums / counts_ref[...]
    probs = jnp.exp(logits_ref[...].astype(F32) - top_ref[...]) * scale_ref[...]
    d_probs = d_ref[...]
    mean = jnp.sum(probs * d_probs, axis=-1, keepdims=True)
    out_ref[...] = (math.sqrt(VOC) * (probs * (d_probs - mean))).astype(BF16)


def valid_column(counts_ref, total):
    requests = counts_ref.shape[0]
    length = total // requests
    position = lax.broadcasted_iota(jnp.int32, (total, 1), 0)
    valid = jnp.zeros((total, 1), F32)
    for r in range(requests):
        inside = (position >= r * length) & (position < r * length + counts_ref[r])
        valid = jnp.where(inside, 1.0, valid)
    return valid, position // length


def ready_kernel(starts, *refs):
    count = len(starts)
    sources, outs, sems = refs[:count], refs[count + 1 : -1], refs[-1]
    fine = 128
    copies = [
        pltpu.make_async_copy(
            source.at[span(start() + i, fine)], out.at[pl.ds(i, fine)], sems.at[k, i // fine]
        )
        for k, (source, out, start) in enumerate(zip(sources, outs, starts))
        for i in range(0, out.shape[0], fine)
    ]
    for copy in copies:
        copy.start()
    for copy in copies:
        copy.wait()


def first_rows(rows, sources, starts, after):
    count = len(sources)
    return call(
        functools.partial(ready_kernel, starts),
        [pltpu.VMEM((rows, a.shape[1]), a.dtype) for a in sources],
        *sources, after, streamed=range(count),
        scratch=(pltpu.SemaphoreType.DMA((count, rows // 128)),),
    )


def half_kernel(
    other, slices_ref, ready_ref, embed_ref, head_ref, out_ref, score_ref, table, acc, sems
):
    chips, total, own = out_ref.shape
    part, ready = embed_ref.shape[0], ready_ref.shape[0]
    core = this_core()
    half = (1 - core) if other else core
    columns = span(half * chips * own, chips * own)
    tile, fine = 256, 128
    stream = Stream([
        pltpu.make_async_copy(
            embed_ref.at[pl.ds(i, min(fine, part - i)), columns],
            table.at[pl.ds(i - ready, min(fine, part - i))],
            sems.at[i // fine],
        )
        for i in range(ready, part, fine)
    ])
    acc[...] = jnp.dot(
        slices_ref[:, :ready], ready_ref[:, columns], preferred_element_type=F32
    )
    for start in range(ready, part, tile):
        end = min(start + tile, part)
        stream.wait(-(-(end - ready) // fine))
        acc[...] += jnp.dot(
            slices_ref[:, start:end], table[start - ready : end - ready],
            preferred_element_type=F32,
        )
    score_ref[...] = jnp.sum(
        acc[...] * head_ref[:, columns].astype(F32), axis=-1, keepdims=True
    )
    for j in range(chips):
        out_ref[j] = acc[:, j * own : (j + 1) * own].astype(out_ref.dtype)


def down_kernel(head_ref, down_ref, after_ref, out_ref, table, sems):
    del after_ref
    steps = sems.shape[0]
    rows = down_ref.shape[0] // steps
    stream = Stream([
        pltpu.make_async_copy(
            down_ref.at[pl.ds(i * rows, rows)], table.at[pl.ds(i * rows, rows)], sems.at[i]
        )
        for i in range(steps)
    ])
    head = jnp.broadcast_to(head_ref[...].astype(F32), (16, head_ref.shape[1])).astype(BF16)
    contract = (((1,), (1,)), ((), ()))
    for i in range(steps):
        stream.wait(i + 1)
        part = lax.dot_general(
            head, table[i * rows : (i + 1) * rows], contract, preferred_element_type=F32
        )
        out_ref[:, i * rows : (i + 1) * rows] = part[:1]


def weight_rows(j, own, ready, gate, up):
    skip = ready[0].shape[0] // own if ready else 0
    if j < skip:
        return ready, slice(j * own, (j + 1) * own)
    return (gate, up), slice((j - skip) * own, (j - skip + 1) * own)


def forward_half(x_ref, gain_ref, gate_ref, up_ref, gate, up, sems, half, sums, ready=()):
    chips, _, own = x_ref.shape
    skip = ready[0].shape[0] // own if ready else 0

    def rows(j):
        return span((half * chips + j) * own, own)

    stream = Stream([
        pltpu.make_async_copy(
            source.at[rows(j)], target.at[pl.ds((j - skip) * own, own)], sems.at[k, j]
        )
        for j in range(skip, chips)
        for k, (source, target) in enumerate(((gate_ref, gate), (up_ref, up)))
    ])
    a, b, squares = sums
    scaled = []
    for j in range(chips):
        x = x_ref[j].astype(F32)
        squares = squares + jnp.sum(x * x, axis=-1, keepdims=True)
        scaled.append((x * gain_ref[:, rows(j)].astype(F32)).astype(BF16))
    for j in range(chips):
        (g, u), r = weight_rows(j, own, ready, gate, up)
        if j >= skip:
            stream.wait(2 * (j - skip + 1))
        a = a + jnp.dot(scaled[j], g[r], preferred_element_type=F32)
        b = b + jnp.dot(scaled[j], u[r], preferred_element_type=F32)
    return a, b, squares


def backward_half(d_gate, d_up, gate, up, out_ref, ready=()):
    chips, _, own = out_ref.shape
    contract = (((1,), (1,)), ((), ()))
    for j in range(chips):
        (g, u), r = weight_rows(j, own, ready, gate, up)
        part = lax.dot_general(d_gate, g[r], contract, preferred_element_type=F32)
        part += lax.dot_general(d_up, u[r], contract, preferred_element_type=F32)
        out_ref[j] = part.astype(out_ref.dtype)


def first_kernel(
    x_ref, gain_ref, gate_ref, up_ref, gate_0, up_0,
    a_ref, b_ref, squares_ref, gate, up, sems,
):
    zeros = jnp.zeros(a_ref.shape, F32)
    sums = (zeros, zeros, jnp.zeros(squares_ref.shape, F32))
    sums = forward_half(
        x_ref, gain_ref, gate_ref, up_ref, gate, up, sems, this_core(), sums, (gate_0, up_0)
    )
    a_ref[...], b_ref[...], squares_ref[...] = sums


def second_kernel(
    x_ref, gain_ref, gate_ref, up_ref, a_ref, b_ref, squares_ref, down_ref, counts_ref,
    send_ref, score_ref, d_gate_ref, d_up_ref, gate, up, sems,
):
    total = x_ref.shape[1]
    width = gate_ref.shape[0]
    sums = (a_ref[...], b_ref[...], squares_ref[...])
    a, b, squares = forward_half(
        x_ref, gain_ref, gate_ref, up_ref, gate, up, sems, 1 - this_core(), sums
    )
    inv = lax.rsqrt(squares / width + 1e-05)
    a, b = a * inv, b * inv
    sigma = jax.nn.sigmoid(a)
    active = a * sigma
    down = down_ref[...]
    hidden = (active * b).astype(BF16).astype(F32)
    score_ref[...] = jnp.sum(hidden * down, axis=-1, keepdims=True)
    valid, _ = valid_column(counts_ref, total)
    d_hidden = valid * down
    d_gate = (d_hidden * b * sigma * (1.0 + a * (1.0 - sigma))).astype(BF16)
    d_up = (d_hidden * active).astype(BF16)
    d_gate_ref[...], d_up_ref[...] = d_gate, d_up
    backward_half(d_gate, d_up, gate, up, send_ref)


def third_kernel(d_gate_ref, d_up_ref, gate_0, up_0, gate_ref, up_ref, keep_ref):
    d_gate, d_up = d_gate_ref[...], d_up_ref[...]
    backward_half(d_gate, d_up, gate_ref, up_ref, keep_ref, (gate_0, up_0))


def input_kernel(
    mine_ref, got_ref, d_mine_ref, d_got_ref, gain_ref, head_ref,
    score_a_ref, score_b_ref, score_c_ref, counts_ref, ready_ref, embed_ref,
    out_ref, dx_ref, table, sems,
):
    chips, total, own = mine_ref.shape
    voc = embed_ref.shape[0]
    requests = counts_ref.shape[0]
    width = 2 * chips * own
    core = this_core()
    ready = ready_ref.shape[0]
    tile, fine = 256, 64

    def copy(start, size):
        return pltpu.make_async_copy(
            embed_ref.at[pl.ds(start, size)],
            table.at[pl.ds(start - ready, size)],
            sems.at[start // fine],
        )

    pieces_of = range(ready, voc, fine)
    for start in pieces_of:
        copy(start, min(fine, voc - start)).start()
    sources = ((mine_ref, d_mine_ref, core), (got_ref, d_got_ref, 1 - core))
    squares = jnp.zeros((total, 1), F32)
    dots = jnp.zeros((total, 1), F32)
    for x_ref, d_ref, half in sources:
        for j in range(chips):
            x = x_ref[j].astype(F32)
            g = d_ref[j].astype(F32) * gain_ref[:, span((half * chips + j) * own, own)].astype(F32)
            squares += jnp.sum(x * x, axis=-1, keepdims=True)
            dots += jnp.sum(g * x, axis=-1, keepdims=True)
    inv = lax.rsqrt(squares / width + 1e-05)
    mean = dots / width
    valid, request = valid_column(counts_ref, total)
    for x_ref, d_ref, half in sources:
        for j in range(chips):
            columns = span((half * chips + j) * own, own)
            x = x_ref[j].astype(F32)
            g = d_ref[j].astype(F32) * gain_ref[:, columns].astype(F32)
            dx = inv * g - x * inv * inv * inv * mean
            dx_ref[:, columns] = (dx + valid * head_ref[:, columns].astype(F32)).astype(BF16)
    score = valid * (score_a_ref[...] + score_b_ref[...] + score_c_ref[...])
    member = request == lax.broadcasted_iota(jnp.int32, (total, requests), 1)
    value = jnp.sum(jnp.where(member, score, 0.0), axis=0, keepdims=True)
    pieces = []
    for _ in range(3):
        piece = value.astype(BF16).astype(F32)
        pieces.append(piece)
        value = value - piece
    for i, piece in enumerate(pieces):
        start = voc + i * requests
        spread = jnp.broadcast_to(piece, (total, requests)).astype(BF16)
        out_ref[:, start : start + requests] = spread
    contract = (((1,), (1,)), ((), ()))

    def product(weights):
        return lax.dot_general(
            dx_ref[...], weights, contract, preferred_element_type=F32
        ).astype(BF16)

    out_ref[:, :ready] = product(ready_ref[...])

    def step(j, _):
        start = pl.multiple_of(j * tile, tile)
        for i in range(0, tile, fine):
            copy(pl.multiple_of(start + i, fine), fine).wait()
        rows = pl.ds(pl.multiple_of(start - ready, tile), tile)
        out_ref[:, pl.ds(start, tile)] = product(table[rows, :])
        return 0

    whole = voc // tile
    lax.fori_loop(ready // tile, whole, step, 0)
    if voc % tile:
        last = whole * tile
        for start in range(last, voc, fine):
            copy(start, min(fine, voc - start)).wait()
        out_ref[:, last:voc] = product(table[last - ready :, :])


def swap_sum(send, keep, devices):
    return (keep.astype(F32) + swap_cores(send, devices).astype(F32)).astype(BF16)


def chip_sum(half, devices):
    return jnp.sum(exchange_chips(half, devices).astype(F32), axis=0).astype(BF16)


def chip_gather(total, devices):
    return exchange_chips(jnp.broadcast_to(total[None], (devices // 2,) + total.shape), devices)


def pick(blocks, index):
    return lax.dynamic_index_in_dim(blocks, index, 0, keepdims=False)


def split_halves(part, devices):
    total, width = part.shape
    core = lax.axis_index("dp") % 2
    blocks = part.reshape(total, 2, devices // 2, width // devices).transpose(1, 2, 0, 3)
    return pick(blocks, 1 - core).astype(BF16), pick(blocks, core)


def join_halves(mine, got):
    core = lax.axis_index("dp") % 2
    blocks = jnp.where(core == 1, jnp.stack([got, mine]), jnp.stack([mine, got]))
    _, chips, total, own = blocks.shape
    return blocks.transpose(2, 0, 1, 3).reshape(total, 2 * chips * own).astype(F32)


def norm_scale(x0):
    return lax.rsqrt(jnp.mean(x0 * x0, axis=-1, keepdims=True) + 1e-05)


def plain_half(slices, embed, head_row, devices):
    part = jnp.dot(slices, embed, preferred_element_type=F32)
    score = jnp.sum(part * head_row.astype(F32), axis=-1, keepdims=True)
    return *split_halves(part, devices), score


def plain_hidden(mine, got, gain_row, w_gate, w_up, down, valid, devices):
    x0 = join_halves(mine, got)
    normed = (x0 * norm_scale(x0) * gain_row.astype(F32)).astype(BF16)
    a = jnp.dot(normed, w_gate, preferred_element_type=F32)
    b = jnp.dot(normed, w_up, preferred_element_type=F32)
    sigma = jax.nn.sigmoid(a)
    active = a * sigma
    hidden = (active * b).astype(BF16).astype(F32)
    d_hidden = valid * down
    d_gate = (d_hidden * b * sigma * (1.0 + a * (1.0 - sigma))).astype(BF16)
    d_up = (d_hidden * active).astype(BF16)
    part = jnp.einsum("tf,df->td", d_gate, w_gate, preferred_element_type=F32)
    part = part + jnp.einsum("tf,df->td", d_up, w_up, preferred_element_type=F32)
    return *split_halves(part, devices), jnp.sum(hidden * down, axis=-1, keepdims=True)


def plain_input(mine, got, d_mine, d_got, gain_row, head_row, valid, embed):
    x0 = join_halves(mine, got)
    inv = norm_scale(x0)
    scaled = join_halves(d_mine, d_got) * gain_row.astype(F32)
    dx = inv * scaled - x0 * inv * inv * inv * jnp.mean(scaled * x0, axis=-1, keepdims=True)
    dx = (dx + valid * head_row.astype(F32)).astype(BF16)
    return jnp.einsum("td,vd->tv", dx, embed, preferred_element_type=F32).astype(BF16)


def body(logits, embed, norm_gain, w_gate, w_up, w_down, head, counts):
    devices = lax.axis_size("dp")
    rows, voc = logits.shape
    part = voc // devices
    width = embed.shape[1]
    hidden = w_gate.shape[1]
    own, chips = width // devices, devices // 2
    requests = counts.shape[0]
    total = rows * devices
    request_len = total // requests
    tiled = own % 128 == 0 and hidden % 128 == 0 and total % 16 == 0 and part % 16 == 0 and part > 512
    head_row, gain_row = head.reshape(1, width), norm_gain.reshape(1, width)
    if tiled:
        column = struct((rows, 1), F32)
        blocked, top, scale = call(
            softmax_kernel, [struct((devices, rows, part), BF16), column, column], logits
        )
    else:
        probs32 = jax.nn.softmax(logits.astype(F32), axis=-1)
        blocked = probs32.astype(BF16).reshape(rows, devices, part).transpose(1, 0, 2)
    slices = exchange(blocked).reshape(total, part)
    column = struct((total, 1), F32)
    half = (chips, total, own)
    flops = total * part * width
    if tiled:
        (first,) = first_rows(256, [embed], [lambda: 0], blocked)
        table = [
            pltpu.VMEM((part - 256, width // 2), BF16), pltpu.VMEM((total, width // 2), F32),
            pltpu.SemaphoreType.DMA((-(-part // 128),)),
        ]
        args = dict(
            streamed=(2,), kept=(1,), flops=flops, scratch=table, room=part * width
        )
        send, score_a = call(
            functools.partial(half_kernel, True), [struct(half, BF16), column],
            slices, first, embed, head_row, **args,
        )
        keep, score_b = call(
            functools.partial(half_kernel, False), [struct(half, F32), column],
            slices, first, embed, head_row, **args,
        )
    else:
        send, keep, score_a = plain_half(slices, embed, head_row, devices)
    summed = swap_sum(send, keep, devices)
    if tiled:
        steps = hidden // 128
        (down_row,) = call(
            down_kernel, [struct((1, hidden), F32)], head_row, w_down, summed,
            streamed=(1,), flops=2 * hidden * width, room=2 * hidden * width,
            scratch=(pltpu.VMEM((hidden, width), BF16), pltpu.SemaphoreType.DMA((steps,))),
        )
    else:
        down_row = jnp.sum(w_down.astype(F32) * head.astype(F32)[None, :], axis=-1)[None]
    total_x = chip_sum(summed, devices)
    if tiled:
        total_x, down_row = lax.optimization_barrier((total_x, down_row))
    x_mine = chip_gather(total_x, devices)
    x_got = swap_cores(x_mine, devices)
    if tiled:
        weights = [w_gate, w_up]
        starts = [lambda: this_core() * (width // 2)] * 2
        gate_0, up_0 = first_rows(2 * own, weights, starts, total_x)
        wide = struct((total, hidden), F32)
        weight, rest = (width // 2, hidden), (width // 2 - 2 * own, hidden)
        sems = pltpu.SemaphoreType.DMA((2, chips))
        args = dict(streamed=(2, 3), flops=2 * total * hidden * width, room=2 * width * hidden)
        a, b, squares, gate, up = call(
            first_kernel,
            [wide, wide, column, pltpu.VMEM(rest, BF16), pltpu.VMEM(rest, BF16)],
            x_mine, gain_row, w_gate, w_up, gate_0, up_0, scratch=(sems,), kept=(4, 5), **args,
        )
        narrow = struct((total, hidden), BF16)
        send, score_c, d_gate, d_up = call(
            second_kernel, [struct(half, BF16), column, narrow, narrow],
            x_got, gain_row, w_gate, w_up, a, b, squares, down_row, counts,
            scratch=(pltpu.VMEM(weight, BF16), pltpu.VMEM(weight, BF16), sems),
            scalars=(8,), **args,
        )
        (keep,) = call(
            third_kernel, [struct(half, F32)], d_gate, d_up, gate_0, up_0, gate, up,
            kept=(2, 3, 4, 5), flops=2 * total * hidden * width,
        )
    else:
        position = jnp.arange(total, dtype=jnp.int32)[:, None]
        member = position // request_len == jnp.arange(requests, dtype=jnp.int32)[None, :]
        limit = jnp.sum(jnp.where(member, counts[None, :], 0), axis=-1, keepdims=True)
        valid = (position % request_len < limit).astype(F32)
        send, keep, score_c = plain_hidden(
            x_mine, x_got, gain_row, w_gate, w_up, down_row, valid, devices
        )
    total_d = chip_sum(swap_sum(send, keep, devices), devices)
    d_mine = chip_gather(total_d, devices)
    d_got = swap_cores(d_mine, devices)
    sources = (x_mine, x_got, d_mine, d_got, gain_row, head_row)
    padded = part + 3 * requests
    if tiled:
        (first,) = first_rows(256, [embed], [lambda: 0], total_d)
        (d_slices,) = call(
            input_kernel, [struct((total, padded), BF16)],
            *sources, score_a, score_b, score_c, counts, first, embed,
            scalars=(9,), kept=(10,), streamed=(11,), flops=2 * flops, room=2 * part * width,
            scratch=(
                pltpu.VMEM((total, width), BF16), pltpu.VMEM((part - 256, width), BF16),
                pltpu.SemaphoreType.DMA((-(-part // 64),)),
            ),
        )
    else:
        d_slices = plain_input(*sources, valid, embed)
        score = jnp.where(member, valid * (score_a + score_c), 0.0)
        extra = split3(jnp.sum(score, axis=0)).reshape(1, requests * 3)
        extra = jnp.broadcast_to(extra, (total, requests * 3))
        d_slices = jnp.concatenate([d_slices, extra], axis=-1)
    back = exchange(d_slices.reshape(devices, rows, padded))
    counts32 = counts.astype(F32)
    if tiled:
        guidance, rewards = call(
            final_kernel, [struct((rows, voc), BF16), struct((1, requests), F32)],
            logits, top, scale, back, counts32.reshape(1, requests),
            scratch=(pltpu.VMEM((rows, voc), F32),),
        )
        return (guidance, rewards.reshape(requests))
    sums = jnp.sum(back[:, 0, part:].astype(F32).reshape(devices, requests, 3), axis=(0, 2))
    rewards = sums / counts32
    d_probs = back[:, :, :part].transpose(1, 0, 2).reshape(rows, voc).astype(F32)
    d_logits = probs32 * (d_probs - jnp.sum(probs32 * d_probs, axis=-1, keepdims=True))
    guidance = (math.sqrt(VOC) * d_logits).astype(BF16)
    return (guidance, rewards)


def solution(mesh):
    placed = (
        P(("groups", "dp"), None),
        P("dp", None),
        P(),
        P(None, "dp"),
        P(None, "dp"),
        P("dp", None),
        P(),
        P("groups"),
    )
    return jax.shard_map(
        body,
        mesh=mesh,
        in_specs=placed,
        out_specs=(P(("groups", "dp"), None), P("groups")),
        check_vma=False,
    )
```

```python
import functools
import math

import jax
import jax.numpy as jnp
from jax import lax
from jax.experimental import pallas as pl
from jax.experimental.pallas import tpu as pltpu
from jax.sharding import PartitionSpec as P

VOC = 32000
F32, BF16 = jnp.float32, jnp.bfloat16
VMEM_BYTES = 12 * 1024 * 1024


def swap_cores(value, devices):
    return lax.ppermute(value, "dp", [(i, i ^ 1) for i in range(devices)])


def exchange(blocks):
    return lax.all_to_all(blocks, "dp", split_axis=0, concat_axis=0, tiled=True)


def exchange_chips(blocks, devices):
    groups = [list(range(core, devices, 2)) for core in range(2)]
    return lax.all_to_all(
        blocks, "dp", split_axis=0, concat_axis=0, axis_index_groups=groups, tiled=True
    )


def split3(value):
    hi = lax.reduce_precision(value, 8, 7)
    rest = value - hi
    mid = lax.reduce_precision(rest, 8, 7)
    low = rest - mid
    return jnp.stack([hi, mid, low], axis=-1).astype(BF16)


HBM_SPEC = pl.BlockSpec(memory_space=pltpu.HBM)
VMEM_SPEC = pl.BlockSpec(memory_space=pltpu.VMEM)
SMEM_SPEC = pl.BlockSpec(memory_space=pltpu.SMEM)


WINDOW = 128


def call(kernel, outs, *args, streamed=(), kept=(), scalars=(), flops=0, scratch=(), room=0):
    size = sum(math.prod(a.shape) * a.dtype.itemsize for a in args)
    places = {i: pltpu.HBM for i in streamed} | {i: pltpu.VMEM for i in kept}
    specs = [
        HBM_SPEC if i in streamed else SMEM_SPEC if i in scalars else VMEM_SPEC
        for i in range(len(args))
    ]
    return pl.pallas_call(
        kernel,
        out_shape=outs,
        in_specs=specs,
        out_specs=[VMEM_SPEC] * len(outs),
        scratch_shapes=list(scratch),
        compiler_params=pltpu.CompilerParams(vmem_limit_bytes=VMEM_BYTES + room),
        cost_estimate=pl.CostEstimate(flops=flops, bytes_accessed=size, transcendentals=0),
    )(*[
        pltpu.with_memory_space_constraint(a, places[i]) if i in places else a
        for i, a in enumerate(args)
    ])


class Stream:
    def __init__(self, copies):
        self.copies = copies
        self.done = 0
        for copy in copies[:WINDOW]:
            copy.start()

    def wait(self, count):
        while self.done < count:
            self.copies[self.done].wait()
            self.done += 1
            if self.done + WINDOW <= len(self.copies):
                self.copies[self.done + WINDOW - 1].start()


def struct(shape, dtype):
    return jax.ShapeDtypeStruct(shape, dtype)


def this_core():
    return lax.axis_index("dp") % 2


def span(start, size):
    return pl.ds(pl.multiple_of(start, size), size)


def softmax_kernel(logits_ref, out_ref, top_ref, scale_ref):
    devices, _, part = out_ref.shape
    x = logits_ref[...].astype(F32)
    top = jnp.max(x, axis=-1, keepdims=True)
    e = jnp.exp(x - top)
    scale = 1.0 / jnp.sum(e, axis=-1, keepdims=True)
    probs = e * scale
    for d in range(devices):
        out_ref[d] = probs[:, d * part : (d + 1) * part].astype(BF16)
    top_ref[...] = top
    scale_ref[...] = scale


def final_kernel(
    logits_ref, top_ref, scale_ref, back_ref, counts_ref, out_ref, rewards_ref, d_ref
):
    devices, _, padded = back_ref.shape
    part = out_ref.shape[1] // devices
    requests = counts_ref.shape[1]
    sums = jnp.zeros((1, requests), F32)
    for d in range(devices):
        block = back_ref[d].astype(F32)
        d_ref[:, d * part : (d + 1) * part] = block[:, :part]
        for i in range(3):
            start = part + i * requests
            sums += block[:1, start : start + requests]
    rewards_ref[...] = sums / counts_ref[...]
    probs = jnp.exp(logits_ref[...].astype(F32) - top_ref[...]) * scale_ref[...]
    d_probs = d_ref[...]
    mean = jnp.sum(probs * d_probs, axis=-1, keepdims=True)
    out_ref[...] = (math.sqrt(VOC) * (probs * (d_probs - mean))).astype(BF16)


def valid_column(counts_ref, total):
    requests = counts_ref.shape[0]
    length = total // requests
    position = lax.broadcasted_iota(jnp.int32, (total, 1), 0)
    valid = jnp.zeros((total, 1), F32)
    for r in range(requests):
        inside = (position >= r * length) & (position < r * length + counts_ref[r])
        valid = jnp.where(inside, 1.0, valid)
    return valid, position // length


def ready_kernel(starts, *refs):
    count = len(starts)
    sources, outs, sems = refs[:count], refs[count + 1 : -1], refs[-1]
    fine = 128
    copies = [
        pltpu.make_async_copy(
            source.at[span(start() + i, fine)], out.at[pl.ds(i, fine)], sems.at[k, i // fine]
        )
        for k, (source, out, start) in enumerate(zip(sources, outs, starts))
        for i in range(0, out.shape[0], fine)
    ]
    for copy in copies:
        copy.start()
    for copy in copies:
        copy.wait()


def first_rows(rows, sources, starts, after):
    count = len(sources)
    return call(
        functools.partial(ready_kernel, starts),
        [pltpu.VMEM((rows, a.shape[1]), a.dtype) for a in sources],
        *sources, after, streamed=range(count),
        scratch=(pltpu.SemaphoreType.DMA((count, rows // 128)),),
    )


def half_kernel(
    other, slices_ref, ready_ref, embed_ref, head_ref, out_ref, score_ref, table, acc, sems
):
    chips, total, own = out_ref.shape
    part, ready = embed_ref.shape[0], ready_ref.shape[0]
    core = this_core()
    half = (1 - core) if other else core
    columns = span(half * chips * own, chips * own)
    tile, fine = 256, 128
    stream = Stream([
        pltpu.make_async_copy(
            embed_ref.at[pl.ds(i, min(fine, part - i)), columns],
            table.at[pl.ds(i - ready, min(fine, part - i))],
            sems.at[i // fine],
        )
        for i in range(ready, part, fine)
    ])
    acc[...] = jnp.dot(
        slices_ref[:, :ready], ready_ref[:, columns], preferred_element_type=F32
    )
    for start in range(ready, part, tile):
        end = min(start + tile, part)
        stream.wait(-(-(end - ready) // fine))
        acc[...] += jnp.dot(
            slices_ref[:, start:end], table[start - ready : end - ready],
            preferred_element_type=F32,
        )
    score_ref[...] = jnp.sum(
        acc[...] * head_ref[:, columns].astype(F32), axis=-1, keepdims=True
    )
    for j in range(chips):
        out_ref[j] = acc[:, j * own : (j + 1) * own].astype(out_ref.dtype)


def down_kernel(head_ref, down_ref, after_ref, out_ref, table, sems):
    del after_ref
    steps = sems.shape[0]
    rows = down_ref.shape[0] // steps
    stream = Stream([
        pltpu.make_async_copy(
            down_ref.at[pl.ds(i * rows, rows)], table.at[pl.ds(i * rows, rows)], sems.at[i]
        )
        for i in range(steps)
    ])
    head = jnp.broadcast_to(head_ref[...].astype(F32), (16, head_ref.shape[1])).astype(BF16)
    contract = (((1,), (1,)), ((), ()))
    for i in range(steps):
        stream.wait(i + 1)
        part = lax.dot_general(
            head, table[i * rows : (i + 1) * rows], contract, preferred_element_type=F32
        )
        out_ref[:, i * rows : (i + 1) * rows] = part[:1]


def forward_half(x_ref, gain_ref, gate_ref, up_ref, gate, up, sems, half, sums):
    chips, _, own = x_ref.shape

    def rows(j):
        return span((half * chips + j) * own, own)

    stream = Stream([
        pltpu.make_async_copy(
            source.at[rows(j)], target.at[pl.ds(j * own, own)], sems.at[k, j]
        )
        for j in range(chips)
        for k, (source, target) in enumerate(((gate_ref, gate), (up_ref, up)))
    ])
    a, b, squares = sums
    scaled = []
    for j in range(chips):
        x = x_ref[j].astype(F32)
        squares = squares + jnp.sum(x * x, axis=-1, keepdims=True)
        scaled.append((x * gain_ref[:, rows(j)].astype(F32)).astype(BF16))
    for j in range(chips):
        r = slice(j * own, (j + 1) * own)
        stream.wait(2 * (j + 1))
        a = a + jnp.dot(scaled[j], gate[r], preferred_element_type=F32)
        b = b + jnp.dot(scaled[j], up[r], preferred_element_type=F32)
    return a, b, squares


def backward_half(d_gate, d_up, gate, up, out_ref):
    chips, _, own = out_ref.shape
    contract = (((1,), (1,)), ((), ()))
    for j in range(chips):
        r = slice(j * own, (j + 1) * own)
        part = lax.dot_general(d_gate, gate[r], contract, preferred_element_type=F32)
        part += lax.dot_general(d_up, up[r], contract, preferred_element_type=F32)
        out_ref[j] = part.astype(out_ref.dtype)


def first_kernel(
    x_ref, gain_ref, gate_ref, up_ref, a_ref, b_ref, squares_ref, gate, up, sems
):
    zeros = jnp.zeros(a_ref.shape, F32)
    sums = (zeros, zeros, jnp.zeros(squares_ref.shape, F32))
    sums = forward_half(x_ref, gain_ref, gate_ref, up_ref, gate, up, sems, this_core(), sums)
    a_ref[...], b_ref[...], squares_ref[...] = sums


def second_kernel(
    x_ref, gain_ref, gate_ref, up_ref, a_ref, b_ref, squares_ref, down_ref, counts_ref,
    send_ref, score_ref, inv_ref, d_gate_ref, d_up_ref, gate, up, sems,
):
    total = x_ref.shape[1]
    width = gate_ref.shape[0]
    sums = (a_ref[...], b_ref[...], squares_ref[...])
    a, b, squares = forward_half(
        x_ref, gain_ref, gate_ref, up_ref, gate, up, sems, 1 - this_core(), sums
    )
    inv = lax.rsqrt(squares / width + 1e-05)
    inv_ref[...] = inv
    a, b = a * inv, b * inv
    sigma = jax.nn.sigmoid(a)
    active = a * sigma
    down = down_ref[...]
    hidden = (active * b).astype(BF16).astype(F32)
    score_ref[...] = jnp.sum(hidden * down, axis=-1, keepdims=True)
    valid, _ = valid_column(counts_ref, total)
    d_hidden = valid * down
    d_gate = (d_hidden * b * sigma * (1.0 + a * (1.0 - sigma))).astype(BF16)
    d_up = (d_hidden * active).astype(BF16)
    d_gate_ref[...], d_up_ref[...] = d_gate, d_up
    backward_half(d_gate, d_up, gate, up, send_ref)


def third_kernel(d_gate_ref, d_up_ref, gate_ref, up_ref, keep_ref):
    backward_half(d_gate_ref[...], d_up_ref[...], gate_ref, up_ref, keep_ref)


def table_steps(lhs_ref, embed_ref, ready, table, sems, columns, first_rows, emit):
    voc, skip = embed_ref.shape[0], ready.shape[0]
    tile, fine = 256, 128
    contract = (((1,), (1,)), ((), ()))

    def copy(start, size):
        source = embed_ref.at[pl.ds(start, size), columns]
        return pltpu.make_async_copy(
            source, table.at[pl.ds(start - skip, size)], sems.at[start // fine]
        )

    def product(weights):
        return lax.dot_general(lhs_ref[...], weights, contract, preferred_element_type=F32)

    for start in range(skip, voc, fine):
        copy(start, min(fine, voc - start)).start()
    emit(pl.ds(0, skip), product(first_rows()))

    def step(j, _):
        start = pl.multiple_of(j * tile, tile)
        for i in range(0, tile, fine):
            copy(pl.multiple_of(start + i, fine), fine).wait()
        rows = pl.ds(pl.multiple_of(start - skip, tile), tile)
        emit(pl.ds(start, tile), product(table[rows, :]))
        return 0

    whole = voc // tile
    lax.fori_loop(skip // tile, whole, step, 0)
    if voc % tile:
        last = whole * tile
        for start in range(last, voc, fine):
            copy(start, min(fine, voc - start)).wait()
        emit(pl.ds(last, voc - last), product(table[last - skip :, :]))


def early_kernel(
    mine_ref, got_ref, head_ref, after_ref, embed_ref,
    x_out, head_out, ready, lhs_ref, table, sems, ready_sem,
):
    chips, total, own = mine_ref.shape
    del after_ref
    core = this_core()
    bring = pltpu.make_async_copy(embed_ref.at[pl.ds(0, ready.shape[0])], ready, ready_sem)
    bring.start()
    for ref, half in ((mine_ref, core), (got_ref, 1 - core)):
        for j in range(chips):
            lhs_ref[:total, span((half * chips + j) * own, own)] = ref[j]
    extra = (lhs_ref.shape[0] - total, head_ref.shape[1])
    lhs_ref[total:, :] = jnp.broadcast_to(head_ref[...].astype(F32), extra).astype(BF16)

    def rows():
        bring.wait()
        return ready[...]

    def emit(rows, part):
        x_out[:, rows] = part[:total]
        head_out[:, rows] = part[total : total + 1]

    table_steps(
        lhs_ref, embed_ref, ready, table, sems, pl.ds(0, embed_ref.shape[1]), rows, emit
    )


def scale_half(d_ref, gain_ref, half, lhs_ref):
    chips, _, own = d_ref.shape
    for j in range(chips):
        gain = gain_ref[:, span((half * chips + j) * own, own)].astype(F32)
        lhs_ref[:, j * own : (j + 1) * own] = (d_ref[j].astype(F32) * gain).astype(BF16)


def own_kernel(d_ref, gain_ref, ready_ref, embed_ref, out_ref, lhs_ref, table, sems):
    chips, _, own = d_ref.shape
    half = this_core()
    columns = span(half * chips * own, chips * own)
    scale_half(d_ref, gain_ref, half, lhs_ref)

    def emit(rows, part):
        out_ref[:, rows] = part

    table_steps(
        lhs_ref, embed_ref, ready_ref, table, sems, columns,
        lambda: ready_ref[:, columns], emit,
    )


def input_kernel(
    mine_ref, got_ref, d_mine_ref, d_got_ref, gain_ref, own_ref, x_ref, head_ref, inv_ref,
    score_a_ref, score_b_ref, score_c_ref, counts_ref, ready_ref, embed_ref,
    out_ref, lhs_ref, table, sems,
):
    chips, total, own = mine_ref.shape
    voc = embed_ref.shape[0]
    requests = counts_ref.shape[0]
    core = this_core()
    half = 1 - core
    columns = span(half * chips * own, chips * own)
    scale_half(d_got_ref, gain_ref, half, lhs_ref)
    dots = jnp.zeros((total, 1), F32)
    for x, d, h in ((mine_ref, d_mine_ref, core), (got_ref, d_got_ref, half)):
        for j in range(chips):
            gain = gain_ref[:, span((h * chips + j) * own, own)].astype(F32)
            g = d[j].astype(F32) * gain
            dots += jnp.sum(g * x[j].astype(F32), axis=-1, keepdims=True)
    inv = inv_ref[...]
    weight = inv * inv * inv * (dots / (2 * chips * own))
    valid, request = valid_column(counts_ref, total)
    score = valid * (score_a_ref[...] + score_b_ref[...] + score_c_ref[...])
    member = request == lax.broadcasted_iota(jnp.int32, (total, requests), 1)
    value = jnp.sum(jnp.where(member, score, 0.0), axis=0, keepdims=True)
    for i in range(3):
        piece = value.astype(BF16).astype(F32)
        start = voc + i * requests
        spread = jnp.broadcast_to(piece, (total, requests)).astype(BF16)
        out_ref[:, start : start + requests] = spread
        value = value - piece

    def emit(rows, part):
        d_probs = inv * (own_ref[:, rows] + part) - weight * x_ref[:, rows]
        out_ref[:, rows] = (d_probs + valid * head_ref[:, rows]).astype(BF16)

    table_steps(
        lhs_ref, embed_ref, ready_ref, table, sems, columns,
        lambda: ready_ref[:, columns], emit,
    )


def swap_sum(send, keep, devices):
    return (keep.astype(F32) + swap_cores(send, devices).astype(F32)).astype(BF16)


def chip_sum(half, devices):
    return jnp.sum(exchange_chips(half, devices).astype(F32), axis=0).astype(BF16)


def chip_gather(total, devices):
    return exchange_chips(jnp.broadcast_to(total[None], (devices // 2,) + total.shape), devices)


def pick(blocks, index):
    return lax.dynamic_index_in_dim(blocks, index, 0, keepdims=False)


def split_halves(part, devices):
    total, width = part.shape
    core = lax.axis_index("dp") % 2
    blocks = part.reshape(total, 2, devices // 2, width // devices).transpose(1, 2, 0, 3)
    return pick(blocks, 1 - core).astype(BF16), pick(blocks, core)


def join_halves(mine, got):
    core = lax.axis_index("dp") % 2
    blocks = jnp.where(core == 1, jnp.stack([got, mine]), jnp.stack([mine, got]))
    _, chips, total, own = blocks.shape
    return blocks.transpose(2, 0, 1, 3).reshape(total, 2 * chips * own).astype(F32)


def norm_scale(x0):
    return lax.rsqrt(jnp.mean(x0 * x0, axis=-1, keepdims=True) + 1e-05)


def plain_half(slices, embed, head_row, devices):
    part = jnp.dot(slices, embed, preferred_element_type=F32)
    score = jnp.sum(part * head_row.astype(F32), axis=-1, keepdims=True)
    return *split_halves(part, devices), score


def plain_hidden(mine, got, gain_row, w_gate, w_up, down, valid, devices):
    x0 = join_halves(mine, got)
    normed = (x0 * norm_scale(x0) * gain_row.astype(F32)).astype(BF16)
    a = jnp.dot(normed, w_gate, preferred_element_type=F32)
    b = jnp.dot(normed, w_up, preferred_element_type=F32)
    sigma = jax.nn.sigmoid(a)
    active = a * sigma
    hidden = (active * b).astype(BF16).astype(F32)
    d_hidden = valid * down
    d_gate = (d_hidden * b * sigma * (1.0 + a * (1.0 - sigma))).astype(BF16)
    d_up = (d_hidden * active).astype(BF16)
    part = jnp.einsum("tf,df->td", d_gate, w_gate, preferred_element_type=F32)
    part = part + jnp.einsum("tf,df->td", d_up, w_up, preferred_element_type=F32)
    return *split_halves(part, devices), jnp.sum(hidden * down, axis=-1, keepdims=True)


def plain_input(mine, got, d_mine, d_got, gain_row, head_row, valid, embed):
    x0 = join_halves(mine, got)
    inv = norm_scale(x0)
    scaled = join_halves(d_mine, d_got) * gain_row.astype(F32)
    dx = inv * scaled - x0 * inv * inv * inv * jnp.mean(scaled * x0, axis=-1, keepdims=True)
    dx = (dx + valid * head_row.astype(F32)).astype(BF16)
    return jnp.einsum("td,vd->tv", dx, embed, preferred_element_type=F32).astype(BF16)


def body(logits, embed, norm_gain, w_gate, w_up, w_down, head, counts):
    devices = lax.axis_size("dp")
    rows, voc = logits.shape
    part = voc // devices
    width = embed.shape[1]
    hidden = w_gate.shape[1]
    own, chips = width // devices, devices // 2
    requests = counts.shape[0]
    total = rows * devices
    request_len = total // requests
    tiled = own % 128 == 0 and hidden % 128 == 0 and total % 16 == 0 and part % 16 == 0 and part > 512
    head_row, gain_row = head.reshape(1, width), norm_gain.reshape(1, width)
    if tiled:
        column = struct((rows, 1), F32)
        blocked, top, scale = call(
            softmax_kernel, [struct((devices, rows, part), BF16), column, column], logits
        )
    else:
        probs32 = jax.nn.softmax(logits.astype(F32), axis=-1)
        blocked = probs32.astype(BF16).reshape(rows, devices, part).transpose(1, 0, 2)
    slices = exchange(blocked).reshape(total, part)
    column = struct((total, 1), F32)
    half = (chips, total, own)
    flops = total * part * width
    if tiled:
        (first,) = first_rows(256, [embed], [lambda: 0], blocked)
        table = [
            pltpu.VMEM((part - 256, width // 2), BF16), pltpu.VMEM((total, width // 2), F32),
            pltpu.SemaphoreType.DMA((-(-part // 128),)),
        ]
        args = dict(
            streamed=(2,), kept=(1,), flops=flops, scratch=table, room=part * width
        )
        send, score_a = call(
            functools.partial(half_kernel, True), [struct(half, BF16), column],
            slices, first, embed, head_row, **args,
        )
        keep, score_b = call(
            functools.partial(half_kernel, False), [struct(half, F32), column],
            slices, first, embed, head_row, **args,
        )
    else:
        send, keep, score_a = plain_half(slices, embed, head_row, devices)
    summed = swap_sum(send, keep, devices)
    if tiled:
        steps = hidden // 128
        (down_row,) = call(
            down_kernel, [struct((1, hidden), F32)], head_row, w_down, summed,
            streamed=(1,), flops=2 * hidden * width, room=2 * hidden * width,
            scratch=(pltpu.VMEM((hidden, width), BF16), pltpu.SemaphoreType.DMA((steps,))),
        )
    else:
        down_row = jnp.sum(w_down.astype(F32) * head.astype(F32)[None, :], axis=-1)[None]
    total_x = chip_sum(summed, devices)
    if tiled:
        total_x, down_row = lax.optimization_barrier((total_x, down_row))
    x_mine = chip_gather(total_x, devices)
    x_got = swap_cores(x_mine, devices)
    if tiled:
        wide = struct((total, hidden), F32)
        weight = (width // 2, hidden)
        sems = pltpu.SemaphoreType.DMA((2, chips))
        args = dict(streamed=(2, 3), flops=2 * total * hidden * width, room=2 * width * hidden)
        a, b, squares, gate, up = call(
            first_kernel,
            [wide, wide, column, pltpu.VMEM(weight, BF16), pltpu.VMEM(weight, BF16)],
            x_mine, gain_row, w_gate, w_up, scratch=(sems,), **args,
        )
        narrow = struct((total, hidden), BF16)
        send, score_c, inv, d_gate, d_up = call(
            second_kernel, [struct(half, BF16), column, column, narrow, narrow],
            x_got, gain_row, w_gate, w_up, a, b, squares, down_row, counts,
            scratch=(pltpu.VMEM(weight, BF16), pltpu.VMEM(weight, BF16), sems),
            scalars=(8,), **args,
        )
        (keep,) = call(
            third_kernel, [struct(half, F32)], d_gate, d_up, gate, up,
            kept=(2, 3), flops=2 * total * hidden * width,
        )
    else:
        position = jnp.arange(total, dtype=jnp.int32)[:, None]
        member = position // request_len == jnp.arange(requests, dtype=jnp.int32)[None, :]
        limit = jnp.sum(jnp.where(member, counts[None, :], 0), axis=-1, keepdims=True)
        valid = (position % request_len < limit).astype(F32)
        send, keep, score_c = plain_hidden(
            x_mine, x_got, gain_row, w_gate, w_up, down_row, valid, devices
        )
    summed_d = swap_sum(send, keep, devices)
    total_d = chip_sum(summed_d, devices)
    padded = part + 3 * requests
    if tiled:
        ready = 256
        products = struct((total, part), F32)
        sems = pltpu.SemaphoreType.DMA((-(-part // 128),))
        x_product, head_product, first = call(
            early_kernel,
            [products, struct((1, part), F32), pltpu.VMEM((ready, width), BF16)],
            x_mine, x_got, head_row, summed_d, embed,
            streamed=(4,), flops=2 * flops, room=2 * part * width,
            scratch=(
                pltpu.VMEM((total + 16, width), BF16), pltpu.VMEM((part - ready, width), BF16),
                sems, pltpu.SemaphoreType.DMA,
            ),
        )
        total_d, x_product, head_product, first = lax.optimization_barrier(
            (total_d, x_product, head_product, first)
        )
    d_mine = chip_gather(total_d, devices)
    d_got = swap_cores(d_mine, devices)
    if tiled:
        args = dict(
            flops=flops, room=part * width,
            scratch=(
                pltpu.VMEM((total, width // 2), BF16),
                pltpu.VMEM((part - ready, width // 2), BF16), sems,
            ),
        )
        (own_product,) = call(
            own_kernel, [products], d_mine, gain_row, first, embed,
            kept=(2,), streamed=(3,), **args,
        )
        (d_slices,) = call(
            input_kernel, [struct((total, padded), BF16)],
            x_mine, x_got, d_mine, d_got, gain_row, own_product, x_product, head_product, inv,
            score_a, score_b, score_c, counts, first, embed,
            scalars=(12,), kept=(13,), streamed=(14,), **args,
        )
    else:
        d_slices = plain_input(
            x_mine, x_got, d_mine, d_got, gain_row, head_row, valid, embed
        )
        score = jnp.where(member, valid * (score_a + score_c), 0.0)
        extra = split3(jnp.sum(score, axis=0)).reshape(1, requests * 3)
        extra = jnp.broadcast_to(extra, (total, requests * 3))
        d_slices = jnp.concatenate([d_slices, extra], axis=-1)
    back = exchange(d_slices.reshape(devices, rows, padded))
    counts32 = counts.astype(F32)
    if tiled:
        guidance, rewards = call(
            final_kernel, [struct((rows, voc), BF16), struct((1, requests), F32)],
            logits, top, scale, back, counts32.reshape(1, requests),
            scratch=(pltpu.VMEM((rows, voc), F32),),
        )
        return (guidance, rewards.reshape(requests))
    sums = jnp.sum(back[:, 0, part:].astype(F32).reshape(devices, requests, 3), axis=(0, 2))
    rewards = sums / counts32
    d_probs = back[:, :, :part].transpose(1, 0, 2).reshape(rows, voc).astype(F32)
    d_logits = probs32 * (d_probs - jnp.sum(probs32 * d_probs, axis=-1, keepdims=True))
    guidance = (math.sqrt(VOC) * d_logits).astype(BF16)
    return (guidance, rewards)


def solution(mesh):
    placed = (
        P(("groups", "dp"), None),
        P("dp", None),
        P(),
        P(None, "dp"),
        P(None, "dp"),
        P("dp", None),
        P(),
        P("groups"),
    )
    return jax.shard_map(
        body,
        mesh=mesh,
        in_specs=placed,
        out_specs=(P(("groups", "dp"), None), P("groups")),
        check_vma=False,
    )
```

```python
import functools
import math

import jax
import jax.numpy as jnp
from jax import lax
from jax.experimental import pallas as pl
from jax.experimental.pallas import tpu as pltpu
from jax.sharding import PartitionSpec as P

VOC = 32000
F32, BF16 = jnp.float32, jnp.bfloat16
VMEM_BYTES = 12 * 1024 * 1024


def swap_cores(value, devices):
    return lax.ppermute(value, "dp", [(i, i ^ 1) for i in range(devices)])


def exchange(blocks):
    return lax.all_to_all(blocks, "dp", split_axis=0, concat_axis=0, tiled=True)


def exchange_chips(blocks, devices):
    groups = [list(range(core, devices, 2)) for core in range(2)]
    return lax.all_to_all(
        blocks, "dp", split_axis=0, concat_axis=0, axis_index_groups=groups, tiled=True
    )


def split3(value):
    hi = lax.reduce_precision(value, 8, 7)
    rest = value - hi
    mid = lax.reduce_precision(rest, 8, 7)
    low = rest - mid
    return jnp.stack([hi, mid, low], axis=-1).astype(BF16)


HBM_SPEC = pl.BlockSpec(memory_space=pltpu.HBM)
VMEM_SPEC = pl.BlockSpec(memory_space=pltpu.VMEM)
SMEM_SPEC = pl.BlockSpec(memory_space=pltpu.SMEM)


WINDOW = 128


def call(kernel, outs, *args, streamed=(), kept=(), scalars=(), flops=0, scratch=(), room=0):
    size = sum(math.prod(a.shape) * a.dtype.itemsize for a in args)
    places = {i: pltpu.HBM for i in streamed} | {i: pltpu.VMEM for i in kept}
    specs = [
        HBM_SPEC if i in streamed else SMEM_SPEC if i in scalars else VMEM_SPEC
        for i in range(len(args))
    ]
    return pl.pallas_call(
        kernel,
        out_shape=outs,
        in_specs=specs,
        out_specs=[VMEM_SPEC] * len(outs),
        scratch_shapes=list(scratch),
        compiler_params=pltpu.CompilerParams(vmem_limit_bytes=VMEM_BYTES + room),
        cost_estimate=pl.CostEstimate(flops=flops, bytes_accessed=size, transcendentals=0),
    )(*[
        pltpu.with_memory_space_constraint(a, places[i]) if i in places else a
        for i, a in enumerate(args)
    ])


class Stream:
    def __init__(self, copies):
        self.copies = copies
        self.done = 0
        for copy in copies[:WINDOW]:
            copy.start()

    def wait(self, count):
        while self.done < count:
            self.copies[self.done].wait()
            self.done += 1
            if self.done + WINDOW <= len(self.copies):
                self.copies[self.done + WINDOW - 1].start()


def struct(shape, dtype):
    return jax.ShapeDtypeStruct(shape, dtype)


def this_core():
    return lax.axis_index("dp") % 2


def span(start, size):
    return pl.ds(pl.multiple_of(start, size), size)


def softmax_kernel(logits_ref, out_ref, top_ref, scale_ref):
    devices, _, part = out_ref.shape
    x = logits_ref[...].astype(F32)
    top = jnp.max(x, axis=-1, keepdims=True)
    e = jnp.exp(x - top)
    scale = 1.0 / jnp.sum(e, axis=-1, keepdims=True)
    probs = e * scale
    for d in range(devices):
        out_ref[d] = probs[:, d * part : (d + 1) * part].astype(BF16)
    top_ref[...] = top
    scale_ref[...] = scale


def final_kernel(
    logits_ref, top_ref, scale_ref, back_ref, counts_ref, out_ref, rewards_ref, d_ref
):
    devices, _, padded = back_ref.shape
    part = out_ref.shape[1] // devices
    requests = counts_ref.shape[1]
    sums = jnp.zeros((1, requests), F32)
    for d in range(devices):
        block = back_ref[d].astype(F32)
        d_ref[:, d * part : (d + 1) * part] = block[:, :part]
        for i in range(3):
            start = part + i * requests
            sums += block[:1, start : start + requests]
    rewards_ref[...] = sums / counts_ref[...]
    probs = jnp.exp(logits_ref[...].astype(F32) - top_ref[...]) * scale_ref[...]
    d_probs = d_ref[...]
    mean = jnp.sum(probs * d_probs, axis=-1, keepdims=True)
    out_ref[...] = (math.sqrt(VOC) * (probs * (d_probs - mean))).astype(BF16)


def valid_column(counts_ref, total):
    requests = counts_ref.shape[0]
    length = total // requests
    position = lax.broadcasted_iota(jnp.int32, (total, 1), 0)
    valid = jnp.zeros((total, 1), F32)
    for r in range(requests):
        inside = (position >= r * length) & (position < r * length + counts_ref[r])
        valid = jnp.where(inside, 1.0, valid)
    return valid, position // length


def ready_kernel(starts, *refs):
    count = len(starts)
    sources, outs, sems = refs[:count], refs[count + 1 : -1], refs[-1]
    fine = 128
    copies = [
        pltpu.make_async_copy(
            source.at[span(start() + i, fine)], out.at[pl.ds(i, fine)], sems.at[k, i // fine]
        )
        for k, (source, out, start) in enumerate(zip(sources, outs, starts))
        for i in range(0, out.shape[0], fine)
    ]
    for copy in copies:
        copy.start()
    for copy in copies:
        copy.wait()


def first_rows(rows, sources, starts, after):
    count = len(sources)
    return call(
        functools.partial(ready_kernel, starts),
        [pltpu.VMEM((rows, a.shape[1]), a.dtype) for a in sources],
        *sources, after, streamed=range(count),
        scratch=(pltpu.SemaphoreType.DMA((count, rows // 128)),),
    )


def half_kernel(
    other, slices_ref, ready_ref, embed_ref, head_ref, out_ref, score_ref, table, acc, sems
):
    chips, total, own = out_ref.shape
    part, ready = embed_ref.shape[0], ready_ref.shape[0]
    core = this_core()
    half = (1 - core) if other else core
    columns = span(half * chips * own, chips * own)
    tile, fine = 256, 128
    stream = Stream([
        pltpu.make_async_copy(
            embed_ref.at[pl.ds(i, min(fine, part - i)), columns],
            table.at[pl.ds(i - ready, min(fine, part - i))],
            sems.at[i // fine],
        )
        for i in range(ready, part, fine)
    ])
    acc[...] = jnp.dot(
        slices_ref[:, :ready], ready_ref[:, columns], preferred_element_type=F32
    )
    for start in range(ready, part, tile):
        end = min(start + tile, part)
        stream.wait(-(-(end - ready) // fine))
        acc[...] += jnp.dot(
            slices_ref[:, start:end], table[start - ready : end - ready],
            preferred_element_type=F32,
        )
    score_ref[...] = jnp.sum(
        acc[...] * head_ref[:, columns].astype(F32), axis=-1, keepdims=True
    )
    for j in range(chips):
        out_ref[j] = acc[:, j * own : (j + 1) * own].astype(out_ref.dtype)


def down_kernel(head_ref, down_ref, after_ref, out_ref, table, sems):
    del after_ref
    width = down_ref.shape[1]
    lanes = 128

    def copy(j):
        rows = span(j * lanes, lanes)
        return pltpu.make_async_copy(down_ref.at[rows], table.at[rows], sems.at[j])

    steps = sems.shape[0]
    for j in range(steps):
        copy(j).start()

    def step(j, _):
        copy(j).wait()
        rows = span(j * lanes, lanes)
        total = jnp.zeros((lanes, lanes), F32)
        for k in range(0, width, lanes):
            head = head_ref[:, k : k + lanes].astype(F32)
            total += table[rows, k : k + lanes].astype(F32) * head
        out_ref[:, rows] = jnp.sum(total.T, axis=0, keepdims=True)
        return 0

    lax.fori_loop(0, steps, step, 0)


def forward_half(x_ref, gain_ref, gate_ref, up_ref, gate, up, sems, half, sums):
    chips, _, own = x_ref.shape

    def rows(j):
        return span((half * chips + j) * own, own)

    stream = Stream([
        pltpu.make_async_copy(
            source.at[rows(j)], target.at[pl.ds(j * own, own)], sems.at[k, j]
        )
        for j in range(chips)
        for k, (source, target) in enumerate(((gate_ref, gate), (up_ref, up)))
    ])
    a, b, squares = sums
    scaled = []
    for j in range(chips):
        x = x_ref[j].astype(F32)
        squares = squares + jnp.sum(x * x, axis=-1, keepdims=True)
        scaled.append((x * gain_ref[:, rows(j)].astype(F32)).astype(BF16))
    for j in range(chips):
        r = slice(j * own, (j + 1) * own)
        stream.wait(2 * (j + 1))
        a = a + jnp.dot(scaled[j], gate[r], preferred_element_type=F32)
        b = b + jnp.dot(scaled[j], up[r], preferred_element_type=F32)
    return a, b, squares


def backward_half(d_gate, d_up, gate, up, out_ref):
    chips, _, own = out_ref.shape
    contract = (((1,), (1,)), ((), ()))
    for j in range(chips):
        r = slice(j * own, (j + 1) * own)
        part = lax.dot_general(d_gate, gate[r], contract, preferred_element_type=F32)
        part += lax.dot_general(d_up, up[r], contract, preferred_element_type=F32)
        out_ref[j] = part.astype(out_ref.dtype)


def first_kernel(
    x_ref, gain_ref, gate_ref, up_ref, a_ref, b_ref, squares_ref, gate, up, sems
):
    zeros = jnp.zeros(a_ref.shape, F32)
    sums = (zeros, zeros, jnp.zeros(squares_ref.shape, F32))
    sums = forward_half(x_ref, gain_ref, gate_ref, up_ref, gate, up, sems, this_core(), sums)
    a_ref[...], b_ref[...], squares_ref[...] = sums


def second_kernel(
    x_ref, gain_ref, gate_ref, up_ref, a_ref, b_ref, squares_ref, down_ref, counts_ref,
    send_ref, score_ref, d_gate_ref, d_up_ref, gate, up, sems,
):
    total = x_ref.shape[1]
    width = gate_ref.shape[0]
    sums = (a_ref[...], b_ref[...], squares_ref[...])
    a, b, squares = forward_half(
        x_ref, gain_ref, gate_ref, up_ref, gate, up, sems, 1 - this_core(), sums
    )
    inv = lax.rsqrt(squares / width + 1e-05)
    a, b = a * inv, b * inv
    sigma = jax.nn.sigmoid(a)
    active = a * sigma
    down = down_ref[...]
    hidden = (active * b).astype(BF16).astype(F32)
    score_ref[...] = jnp.sum(hidden * down, axis=-1, keepdims=True)
    valid, _ = valid_column(counts_ref, total)
    d_hidden = valid * down
    d_gate = (d_hidden * b * sigma * (1.0 + a * (1.0 - sigma))).astype(BF16)
    d_up = (d_hidden * active).astype(BF16)
    d_gate_ref[...], d_up_ref[...] = d_gate, d_up
    backward_half(d_gate, d_up, gate, up, send_ref)


def third_kernel(d_gate_ref, d_up_ref, gate_ref, up_ref, keep_ref):
    backward_half(d_gate_ref[...], d_up_ref[...], gate_ref, up_ref, keep_ref)


def input_kernel(
    mine_ref, got_ref, d_mine_ref, d_got_ref, gain_ref, head_ref,
    score_a_ref, score_b_ref, score_c_ref, counts_ref, ready_ref, embed_ref,
    out_ref, dx_ref, table, sems,
):
    chips, total, own = mine_ref.shape
    voc = embed_ref.shape[0]
    requests = counts_ref.shape[0]
    width = 2 * chips * own
    core = this_core()
    ready = ready_ref.shape[0]
    tile, fine = 256, 64

    def copy(start, size):
        return pltpu.make_async_copy(
            embed_ref.at[pl.ds(start, size)],
            table.at[pl.ds(start - ready, size)],
            sems.at[start // fine],
        )

    pieces_of = range(ready, voc, fine)
    for start in pieces_of:
        copy(start, min(fine, voc - start)).start()
    sources = ((mine_ref, d_mine_ref, core), (got_ref, d_got_ref, 1 - core))
    squares = jnp.zeros((total, 1), F32)
    dots = jnp.zeros((total, 1), F32)
    for x_ref, d_ref, half in sources:
        for j in range(chips):
            x = x_ref[j].astype(F32)
            g = d_ref[j].astype(F32) * gain_ref[:, span((half * chips + j) * own, own)].astype(F32)
            squares += jnp.sum(x * x, axis=-1, keepdims=True)
            dots += jnp.sum(g * x, axis=-1, keepdims=True)
    inv = lax.rsqrt(squares / width + 1e-05)
    mean = dots / width
    valid, request = valid_column(counts_ref, total)
    for x_ref, d_ref, half in sources:
        for j in range(chips):
            columns = span((half * chips + j) * own, own)
            x = x_ref[j].astype(F32)
            g = d_ref[j].astype(F32) * gain_ref[:, columns].astype(F32)
            dx = inv * g - x * inv * inv * inv * mean
            dx = dx + valid * head_ref[:, columns].astype(F32)
            dx_ref[columns, :] = dx.T.astype(BF16)
    score = valid * (score_a_ref[...] + score_b_ref[...] + score_c_ref[...])
    member = request == lax.broadcasted_iota(jnp.int32, (total, requests), 1)
    value = jnp.sum(jnp.where(member, score, 0.0), axis=0, keepdims=True)
    pieces = []
    for _ in range(3):
        piece = value.astype(BF16).astype(F32)
        pieces.append(piece)
        value = value - piece
    for i, piece in enumerate(pieces):
        start = voc + i * requests
        spread = jnp.broadcast_to(piece, (total, requests)).astype(BF16)
        out_ref[:, start : start + requests] = spread
    def product(weights, rows):
        part = jnp.dot(weights[rows, :], dx_ref[...], preferred_element_type=F32)
        return part.T.astype(BF16)

    out_ref[:, :ready] = product(ready_ref, pl.ds(0, ready))

    def step(j, _):
        start = pl.multiple_of(j * tile, tile)
        for i in range(0, tile, fine):
            copy(pl.multiple_of(start + i, fine), fine).wait()
        rows = pl.ds(pl.multiple_of(start - ready, tile), tile)
        out_ref[:, pl.ds(start, tile)] = product(table, rows)
        return 0

    whole = voc // tile
    lax.fori_loop(ready // tile, whole, step, 0)
    if voc % tile:
        last = whole * tile
        for start in range(last, voc, fine):
            copy(start, min(fine, voc - start)).wait()
        out_ref[:, last:voc] = product(table, pl.ds(last - ready, voc - last))


def swap_sum(send, keep, devices):
    return (keep.astype(F32) + swap_cores(send, devices).astype(F32)).astype(BF16)


def chip_sum(half, devices):
    return jnp.sum(exchange_chips(half, devices).astype(F32), axis=0).astype(BF16)


def chip_gather(total, devices):
    return exchange_chips(jnp.broadcast_to(total[None], (devices // 2,) + total.shape), devices)


def pick(blocks, index):
    return lax.dynamic_index_in_dim(blocks, index, 0, keepdims=False)


def split_halves(part, devices):
    total, width = part.shape
    core = lax.axis_index("dp") % 2
    blocks = part.reshape(total, 2, devices // 2, width // devices).transpose(1, 2, 0, 3)
    return pick(blocks, 1 - core).astype(BF16), pick(blocks, core)


def join_halves(mine, got):
    core = lax.axis_index("dp") % 2
    blocks = jnp.where(core == 1, jnp.stack([got, mine]), jnp.stack([mine, got]))
    _, chips, total, own = blocks.shape
    return blocks.transpose(2, 0, 1, 3).reshape(total, 2 * chips * own).astype(F32)


def norm_scale(x0):
    return lax.rsqrt(jnp.mean(x0 * x0, axis=-1, keepdims=True) + 1e-05)


def plain_half(slices, embed, head_row, devices):
    part = jnp.dot(slices, embed, preferred_element_type=F32)
    score = jnp.sum(part * head_row.astype(F32), axis=-1, keepdims=True)
    return *split_halves(part, devices), score


def plain_hidden(mine, got, gain_row, w_gate, w_up, down, valid, devices):
    x0 = join_halves(mine, got)
    normed = (x0 * norm_scale(x0) * gain_row.astype(F32)).astype(BF16)
    a = jnp.dot(normed, w_gate, preferred_element_type=F32)
    b = jnp.dot(normed, w_up, preferred_element_type=F32)
    sigma = jax.nn.sigmoid(a)
    active = a * sigma
    hidden = (active * b).astype(BF16).astype(F32)
    d_hidden = valid * down
    d_gate = (d_hidden * b * sigma * (1.0 + a * (1.0 - sigma))).astype(BF16)
    d_up = (d_hidden * active).astype(BF16)
    part = jnp.einsum("tf,df->td", d_gate, w_gate, preferred_element_type=F32)
    part = part + jnp.einsum("tf,df->td", d_up, w_up, preferred_element_type=F32)
    return *split_halves(part, devices), jnp.sum(hidden * down, axis=-1, keepdims=True)


def plain_input(mine, got, d_mine, d_got, gain_row, head_row, valid, embed):
    x0 = join_halves(mine, got)
    inv = norm_scale(x0)
    scaled = join_halves(d_mine, d_got) * gain_row.astype(F32)
    dx = inv * scaled - x0 * inv * inv * inv * jnp.mean(scaled * x0, axis=-1, keepdims=True)
    dx = (dx + valid * head_row.astype(F32)).astype(BF16)
    return jnp.einsum("td,vd->tv", dx, embed, preferred_element_type=F32).astype(BF16)


def body(logits, embed, norm_gain, w_gate, w_up, w_down, head, counts):
    devices = lax.axis_size("dp")
    rows, voc = logits.shape
    part = voc // devices
    width = embed.shape[1]
    hidden = w_gate.shape[1]
    own, chips = width // devices, devices // 2
    requests = counts.shape[0]
    total = rows * devices
    request_len = total // requests
    tiled = own % 128 == 0 and hidden % 128 == 0 and total % 16 == 0 and part % 16 == 0 and part > 512
    head_row, gain_row = head.reshape(1, width), norm_gain.reshape(1, width)
    if tiled:
        column = struct((rows, 1), F32)
        blocked, top, scale = call(
            softmax_kernel, [struct((devices, rows, part), BF16), column, column], logits
        )
    else:
        probs32 = jax.nn.softmax(logits.astype(F32), axis=-1)
        blocked = probs32.astype(BF16).reshape(rows, devices, part).transpose(1, 0, 2)
    slices = exchange(blocked).reshape(total, part)
    column = struct((total, 1), F32)
    half = (chips, total, own)
    flops = total * part * width
    if tiled:
        (down_row,) = call(
            down_kernel, [struct((1, hidden), F32)], head_row, w_down, blocked,
            streamed=(1,), flops=2 * hidden * width, room=2 * hidden * width,
            scratch=(
                pltpu.VMEM((hidden, width), BF16), pltpu.SemaphoreType.DMA((hidden // 128,)),
            ),
        )
        (first,) = first_rows(256, [embed], [lambda: 0], down_row)
        table = [
            pltpu.VMEM((part - 256, width // 2), BF16), pltpu.VMEM((total, width // 2), F32),
            pltpu.SemaphoreType.DMA((-(-part // 128),)),
        ]
        args = dict(
            streamed=(2,), kept=(1,), flops=flops, scratch=table, room=part * width
        )
        send, score_a = call(
            functools.partial(half_kernel, True), [struct(half, BF16), column],
            slices, first, embed, head_row, **args,
        )
        keep, score_b = call(
            functools.partial(half_kernel, False), [struct(half, F32), column],
            slices, first, embed, head_row, **args,
        )
    else:
        send, keep, score_a = plain_half(slices, embed, head_row, devices)
    summed = swap_sum(send, keep, devices)
    x_mine = chip_gather(chip_sum(summed, devices), devices)
    x_got = swap_cores(x_mine, devices)
    if tiled:
        wide = struct((total, hidden), F32)
        weight = (width // 2, hidden)
        sems = pltpu.SemaphoreType.DMA((2, chips))
        args = dict(streamed=(2, 3), flops=2 * total * hidden * width, room=2 * width * hidden)
        a, b, squares, gate, up = call(
            first_kernel,
            [wide, wide, column, pltpu.VMEM(weight, BF16), pltpu.VMEM(weight, BF16)],
            x_mine, gain_row, w_gate, w_up, scratch=(sems,), **args,
        )
        narrow = struct((total, hidden), BF16)
        send, score_c, d_gate, d_up = call(
            second_kernel, [struct(half, BF16), column, narrow, narrow],
            x_got, gain_row, w_gate, w_up, a, b, squares, down_row, counts,
            scratch=(pltpu.VMEM(weight, BF16), pltpu.VMEM(weight, BF16), sems),
            scalars=(8,), **args,
        )
        (keep,) = call(
            third_kernel, [struct(half, F32)], d_gate, d_up, gate, up,
            kept=(2, 3), flops=2 * total * hidden * width,
        )
    else:
        down_row = jnp.sum(w_down.astype(F32) * head.astype(F32)[None, :], axis=-1)[None]
        position = jnp.arange(total, dtype=jnp.int32)[:, None]
        member = position // request_len == jnp.arange(requests, dtype=jnp.int32)[None, :]
        limit = jnp.sum(jnp.where(member, counts[None, :], 0), axis=-1, keepdims=True)
        valid = (position % request_len < limit).astype(F32)
        send, keep, score_c = plain_hidden(
            x_mine, x_got, gain_row, w_gate, w_up, down_row, valid, devices
        )
    total_d = chip_sum(swap_sum(send, keep, devices), devices)
    d_mine = chip_gather(total_d, devices)
    d_got = swap_cores(d_mine, devices)
    sources = (x_mine, x_got, d_mine, d_got, gain_row, head_row)
    padded = part + 3 * requests
    if tiled:
        (first,) = first_rows(256, [embed], [lambda: 0], total_d)
        (d_slices,) = call(
            input_kernel, [struct((total, padded), BF16)],
            *sources, score_a, score_b, score_c, counts, first, embed,
            scalars=(9,), kept=(10,), streamed=(11,), flops=2 * flops, room=2 * part * width,
            scratch=(
                pltpu.VMEM((width, total), BF16), pltpu.VMEM((part - 256, width), BF16),
                pltpu.SemaphoreType.DMA((-(-part // 64),)),
            ),
        )
    else:
        d_slices = plain_input(*sources, valid, embed)
        score = jnp.where(member, valid * (score_a + score_c), 0.0)
        extra = split3(jnp.sum(score, axis=0)).reshape(1, requests * 3)
        extra = jnp.broadcast_to(extra, (total, requests * 3))
        d_slices = jnp.concatenate([d_slices, extra], axis=-1)
    back = exchange(d_slices.reshape(devices, rows, padded))
    counts32 = counts.astype(F32)
    if tiled:
        guidance, rewards = call(
            final_kernel, [struct((rows, voc), BF16), struct((1, requests), F32)],
            logits, top, scale, back, counts32.reshape(1, requests),
            scratch=(pltpu.VMEM((rows, voc), F32),),
        )
        return (guidance, rewards.reshape(requests))
    sums = jnp.sum(back[:, 0, part:].astype(F32).reshape(devices, requests, 3), axis=(0, 2))
    rewards = sums / counts32
    d_probs = back[:, :, :part].transpose(1, 0, 2).reshape(rows, voc).astype(F32)
    d_logits = probs32 * (d_probs - jnp.sum(probs32 * d_probs, axis=-1, keepdims=True))
    guidance = (math.sqrt(VOC) * d_logits).astype(BF16)
    return (guidance, rewards)


def solution(mesh):
    placed = (
        P(("groups", "dp"), None),
        P("dp", None),
        P(),
        P(None, "dp"),
        P(None, "dp"),
        P("dp", None),
        P(),
        P("groups"),
    )
    return jax.shard_map(
        body,
        mesh=mesh,
        in_specs=placed,
        out_specs=(P(("groups", "dp"), None), P("groups")),
        check_vma=False,
    )
```

```python
import functools
import math

import jax
import jax.numpy as jnp
from jax import lax
from jax.experimental import pallas as pl
from jax.experimental.pallas import tpu as pltpu
from jax.sharding import PartitionSpec as P

VOC = 32000
F32, BF16 = jnp.float32, jnp.bfloat16
VMEM_BYTES = 12 * 1024 * 1024


def swap_cores(value, devices):
    return lax.ppermute(value, "dp", [(i, i ^ 1) for i in range(devices)])


def exchange(blocks):
    return lax.all_to_all(blocks, "dp", split_axis=0, concat_axis=0, tiled=True)


def exchange_chips(blocks, devices):
    groups = [list(range(core, devices, 2)) for core in range(2)]
    return lax.all_to_all(
        blocks, "dp", split_axis=0, concat_axis=0, axis_index_groups=groups, tiled=True
    )


def split3(value):
    hi = lax.reduce_precision(value, 8, 7)
    rest = value - hi
    mid = lax.reduce_precision(rest, 8, 7)
    low = rest - mid
    return jnp.stack([hi, mid, low], axis=-1).astype(BF16)


HBM_SPEC = pl.BlockSpec(memory_space=pltpu.HBM)
VMEM_SPEC = pl.BlockSpec(memory_space=pltpu.VMEM)
SMEM_SPEC = pl.BlockSpec(memory_space=pltpu.SMEM)


WINDOW = 128


def call(kernel, outs, *args, streamed=(), kept=(), scalars=(), flops=0, scratch=(), room=0):
    size = sum(math.prod(a.shape) * a.dtype.itemsize for a in args)
    places = {i: pltpu.HBM for i in streamed} | {i: pltpu.VMEM for i in kept}
    specs = [
        HBM_SPEC if i in streamed else SMEM_SPEC if i in scalars else VMEM_SPEC
        for i in range(len(args))
    ]
    return pl.pallas_call(
        kernel,
        out_shape=outs,
        in_specs=specs,
        out_specs=[VMEM_SPEC] * len(outs),
        scratch_shapes=list(scratch),
        compiler_params=pltpu.CompilerParams(vmem_limit_bytes=VMEM_BYTES + room),
        cost_estimate=pl.CostEstimate(flops=flops, bytes_accessed=size, transcendentals=0),
    )(*[
        pltpu.with_memory_space_constraint(a, places[i]) if i in places else a
        for i, a in enumerate(args)
    ])


class Stream:
    def __init__(self, copies):
        self.copies = copies
        self.done = 0
        for copy in copies[:WINDOW]:
            copy.start()

    def wait(self, count):
        while self.done < count:
            self.copies[self.done].wait()
            self.done += 1
            if self.done + WINDOW <= len(self.copies):
                self.copies[self.done + WINDOW - 1].start()


def struct(shape, dtype):
    return jax.ShapeDtypeStruct(shape, dtype)


def this_core():
    return lax.axis_index("dp") % 2


def span(start, size):
    return pl.ds(pl.multiple_of(start, size), size)


def softmax_kernel(logits_ref, out_ref, top_ref, scale_ref):
    devices, _, part = out_ref.shape
    x = logits_ref[...].astype(F32)
    top = jnp.max(x, axis=-1, keepdims=True)
    e = jnp.exp(x - top)
    scale = 1.0 / jnp.sum(e, axis=-1, keepdims=True)
    probs = e * scale
    for d in range(devices):
        out_ref[d] = probs[:, d * part : (d + 1) * part].astype(BF16)
    top_ref[...] = top
    scale_ref[...] = scale


def final_kernel(
    logits_ref, top_ref, scale_ref, back_ref, counts_ref, out_ref, rewards_ref, d_ref
):
    devices, _, padded = back_ref.shape
    part = out_ref.shape[1] // devices
    requests = counts_ref.shape[1]
    sums = jnp.zeros((1, requests), F32)
    for d in range(devices):
        block = back_ref[d].astype(F32)
        d_ref[:, d * part : (d + 1) * part] = block[:, :part]
        for i in range(3):
            start = part + i * requests
            sums += block[:1, start : start + requests]
    rewards_ref[...] = sums / counts_ref[...]
    probs = jnp.exp(logits_ref[...].astype(F32) - top_ref[...]) * scale_ref[...]
    d_probs = d_ref[...]
    mean = jnp.sum(probs * d_probs, axis=-1, keepdims=True)
    out_ref[...] = (math.sqrt(VOC) * (probs * (d_probs - mean))).astype(BF16)


def valid_column(counts_ref, total):
    requests = counts_ref.shape[0]
    length = total // requests
    position = lax.broadcasted_iota(jnp.int32, (total, 1), 0)
    valid = jnp.zeros((total, 1), F32)
    for r in range(requests):
        inside = (position >= r * length) & (position < r * length + counts_ref[r])
        valid = jnp.where(inside, 1.0, valid)
    return valid, position // length


def bring(source_ref, out_ref, sems, columns):
    fine = 128
    return [
        pltpu.make_async_copy(
            source_ref.at[pl.ds(i, fine), columns], out_ref.at[pl.ds(i, fine)], sems.at[i // fine]
        )
        for i in range(0, out_ref.shape[0], fine)
    ]


def ready_kernel(split, source_ref, after_ref, out_ref, sems):
    del after_ref
    width = out_ref.shape[1]
    columns = span((1 - this_core()) * width, width) if split else pl.ds(0, width)
    copies = bring(source_ref, out_ref, sems, columns)
    for copy in copies:
        copy.start()
    for copy in copies:
        copy.wait()


def first_rows(rows, source, after, split):
    width = source.shape[1] // 2 if split else source.shape[1]
    return call(
        functools.partial(ready_kernel, split), [pltpu.VMEM((rows, width), source.dtype)],
        source, after, streamed=(0,), scratch=(pltpu.SemaphoreType.DMA((rows // 128,)),),
    )[0]


def half_kernel(other, slices_ref, ready_ref, embed_ref, head_ref, out_ref, score_ref, *rest):
    next_ref, table, acc, sems, next_sems = rest if other else (None, *rest, None)
    chips, total, own = out_ref.shape
    part, ready = embed_ref.shape[0], ready_ref.shape[0]
    core = this_core()
    half = (1 - core) if other else core
    columns = span(half * chips * own, chips * own)
    tile, fine = 256, 128
    stream = Stream([
        pltpu.make_async_copy(
            embed_ref.at[pl.ds(i, min(fine, part - i)), columns],
            table.at[pl.ds(i - ready, min(fine, part - i))],
            sems.at[i // fine],
        )
        for i in range(ready, part, fine)
    ])
    following = []
    if other:
        following = bring(embed_ref, next_ref, next_sems, span(core * chips * own, chips * own))
        for copy in following:
            copy.start()
    acc[...] = jnp.dot(slices_ref[:, :ready], ready_ref[...], preferred_element_type=F32)
    for start in range(ready, part, tile):
        end = min(start + tile, part)
        stream.wait(-(-(end - ready) // fine))
        acc[...] += jnp.dot(
            slices_ref[:, start:end], table[start - ready : end - ready],
            preferred_element_type=F32,
        )
    score_ref[...] = jnp.sum(
        acc[...] * head_ref[:, columns].astype(F32), axis=-1, keepdims=True
    )
    for j in range(chips):
        out_ref[j] = acc[:, j * own : (j + 1) * own].astype(out_ref.dtype)
    for copy in following:
        copy.wait()


def down_kernel(head_ref, down_ref, after_ref, out_ref, table, sems):
    del after_ref
    width = down_ref.shape[1]
    lanes = 128

    def copy(j):
        rows = span(j * lanes, lanes)
        return pltpu.make_async_copy(down_ref.at[rows], table.at[rows], sems.at[j])

    steps = sems.shape[0]
    for j in range(steps):
        copy(j).start()

    def step(j, _):
        copy(j).wait()
        rows = span(j * lanes, lanes)
        total = jnp.zeros((lanes, lanes), F32)
        for k in range(0, width, lanes):
            head = head_ref[:, k : k + lanes].astype(F32)
            total += table[rows, k : k + lanes].astype(F32) * head
        out_ref[:, rows] = jnp.sum(total.T, axis=0, keepdims=True)
        return 0

    lax.fori_loop(0, steps, step, 0)


def bring_blocks(refs, half, blocks, own, chips, sems):
    return [
        pltpu.make_async_copy(
            source.at[span((half * chips + j) * own, own)],
            target.at[pl.ds((j - blocks[0]) * own, own)],
            sems.at[k, j - blocks[0]],
        )
        for j in blocks
        for k, (source, target) in enumerate(refs)
    ]


def forward_half(x_ref, gain_ref, half, sums, weights, wait):
    chips, _, own = x_ref.shape
    a, b, squares = sums
    scaled = []
    for j in range(chips):
        x = x_ref[j].astype(F32)
        squares = squares + jnp.sum(x * x, axis=-1, keepdims=True)
        gain = gain_ref[:, span((half * chips + j) * own, own)].astype(F32)
        scaled.append((x * gain).astype(BF16))
    for j in range(chips):
        wait(j)
        gate, up = weights(j)
        a = a + jnp.dot(scaled[j], gate, preferred_element_type=F32)
        b = b + jnp.dot(scaled[j], up, preferred_element_type=F32)
    return a, b, squares


def backward_half(d_gate, d_up, weights, out_ref):
    contract = (((1,), (1,)), ((), ()))
    for j in range(out_ref.shape[0]):
        gate, up = weights(j)
        part = lax.dot_general(d_gate, gate, contract, preferred_element_type=F32)
        part += lax.dot_general(d_up, up, contract, preferred_element_type=F32)
        out_ref[j] = part.astype(out_ref.dtype)


def first_kernel(
    x_ref, gain_ref, gate_ref, up_ref,
    a_ref, b_ref, squares_ref, gate, up, next_gate, next_up, sems, next_sems,
):
    chips, _, own = x_ref.shape
    core = this_core()
    refs = ((gate_ref, gate), (up_ref, up))
    stream = Stream(bring_blocks(refs, core, range(chips), own, chips, sems))
    refs = ((gate_ref, next_gate), (up_ref, next_up))
    ahead = range(next_gate.shape[0] // own)
    following = bring_blocks(refs, 1 - core, ahead, own, chips, next_sems)
    for copy in following:
        copy.start()
    zeros = jnp.zeros(a_ref.shape, F32)
    sums = (zeros, zeros, jnp.zeros(squares_ref.shape, F32))

    def weights(j):
        r = slice(j * own, (j + 1) * own)
        return gate[r], up[r]

    a_ref[...], b_ref[...], squares_ref[...] = forward_half(
        x_ref, gain_ref, core, sums, weights, lambda j: stream.wait(2 * (j + 1))
    )
    for copy in following:
        copy.wait()


def second_kernel(
    x_ref, gain_ref, gate_ref, up_ref, first_gate, first_up,
    a_ref, b_ref, squares_ref, down_ref, counts_ref,
    send_ref, score_ref, d_gate_ref, d_up_ref, gate, up, sems,
):
    chips, total, own = x_ref.shape
    width = gate_ref.shape[0]
    half = 1 - this_core()
    skip = first_gate.shape[0] // own
    refs = ((gate_ref, gate), (up_ref, up))
    stream = Stream(bring_blocks(refs, half, range(skip, chips), own, chips, sems))

    def weights(j):
        if j < skip:
            r = slice(j * own, (j + 1) * own)
            return first_gate[r], first_up[r]
        r = slice((j - skip) * own, (j - skip + 1) * own)
        return gate[r], up[r]

    sums = (a_ref[...], b_ref[...], squares_ref[...])
    a, b, squares = forward_half(
        x_ref, gain_ref, half, sums, weights, lambda j: stream.wait(2 * (j - skip + 1))
    )
    inv = lax.rsqrt(squares / width + 1e-05)
    a, b = a * inv, b * inv
    sigma = jax.nn.sigmoid(a)
    active = a * sigma
    down = down_ref[...]
    hidden = (active * b).astype(BF16).astype(F32)
    score_ref[...] = jnp.sum(hidden * down, axis=-1, keepdims=True)
    valid, _ = valid_column(counts_ref, total)
    d_hidden = valid * down
    d_gate = (d_hidden * b * sigma * (1.0 + a * (1.0 - sigma))).astype(BF16)
    d_up = (d_hidden * active).astype(BF16)
    d_gate_ref[...], d_up_ref[...] = d_gate, d_up
    backward_half(d_gate, d_up, weights, send_ref)


def third_kernel(d_gate_ref, d_up_ref, gate_ref, up_ref, keep_ref):
    own = keep_ref.shape[2]

    def weights(j):
        r = slice(j * own, (j + 1) * own)
        return gate_ref[r], up_ref[r]

    backward_half(d_gate_ref[...], d_up_ref[...], weights, keep_ref)


def input_kernel(
    mine_ref, got_ref, d_mine_ref, d_got_ref, gain_ref, head_ref,
    score_a_ref, score_b_ref, score_c_ref, counts_ref, ready_ref, embed_ref,
    out_ref, dx_ref, table, sems,
):
    chips, total, own = mine_ref.shape
    voc = embed_ref.shape[0]
    requests = counts_ref.shape[0]
    width = 2 * chips * own
    core = this_core()
    ready = ready_ref.shape[0]
    tile, fine = 512, 256

    def copy(start, size):
        return pltpu.make_async_copy(
            embed_ref.at[pl.ds(start, size)],
            table.at[pl.ds(start - ready, size)],
            sems.at[start // fine],
        )

    pieces_of = range(ready, voc, fine)
    for start in pieces_of:
        copy(start, min(fine, voc - start)).start()
    sources = ((mine_ref, d_mine_ref, core), (got_ref, d_got_ref, 1 - core))
    squares = jnp.zeros((total, 1), F32)
    dots = jnp.zeros((total, 1), F32)
    for x_ref, d_ref, half in sources:
        for j in range(chips):
            x = x_ref[j].astype(F32)
            g = d_ref[j].astype(F32) * gain_ref[:, span((half * chips + j) * own, own)].astype(F32)
            squares += jnp.sum(x * x, axis=-1, keepdims=True)
            dots += jnp.sum(g * x, axis=-1, keepdims=True)
    inv = lax.rsqrt(squares / width + 1e-05)
    mean = dots / width
    valid, request = valid_column(counts_ref, total)
    for x_ref, d_ref, half in sources:
        for j in range(chips):
            columns = span((half * chips + j) * own, own)
            x = x_ref[j].astype(F32)
            g = d_ref[j].astype(F32) * gain_ref[:, columns].astype(F32)
            dx = inv * g - x * inv * inv * inv * mean
            dx_ref[:, columns] = (dx + valid * head_ref[:, columns].astype(F32)).astype(BF16)
    score = valid * (score_a_ref[...] + score_b_ref[...] + score_c_ref[...])
    member = request == lax.broadcasted_iota(jnp.int32, (total, requests), 1)
    value = jnp.sum(jnp.where(member, score, 0.0), axis=0, keepdims=True)
    pieces = []
    for _ in range(3):
        piece = value.astype(BF16).astype(F32)
        pieces.append(piece)
        value = value - piece
    for i, piece in enumerate(pieces):
        start = voc + i * requests
        spread = jnp.broadcast_to(piece, (total, requests)).astype(BF16)
        out_ref[:, start : start + requests] = spread
    contract = (((1,), (1,)), ((), ()))

    def product(weights):
        return lax.dot_general(
            dx_ref[...], weights, contract, preferred_element_type=F32
        ).astype(BF16)

    out_ref[:, :ready] = product(ready_ref[...])

    def step(j, _):
        start = pl.multiple_of(ready + j * tile, fine)
        for i in range(0, tile, fine):
            copy(pl.multiple_of(start + i, fine), fine).wait()
        rows = pl.ds(pl.multiple_of(j * tile, tile), tile)
        out_ref[:, pl.ds(start, tile)] = product(table[rows, :])
        return 0

    whole = (voc - ready) // tile
    lax.fori_loop(0, whole, step, 0)
    last = ready + whole * tile
    if last < voc:
        for start in range(last, voc, fine):
            copy(start, min(fine, voc - start)).wait()
        out_ref[:, last:voc] = product(table[last - ready :, :])


def swap_sum(send, keep, devices):
    return (keep.astype(F32) + swap_cores(send, devices).astype(F32)).astype(BF16)


def chip_sum(half, devices):
    return jnp.sum(exchange_chips(half, devices).astype(F32), axis=0).astype(BF16)


def chip_gather(total, devices):
    return exchange_chips(jnp.broadcast_to(total[None], (devices // 2,) + total.shape), devices)


def pick(blocks, index):
    return lax.dynamic_index_in_dim(blocks, index, 0, keepdims=False)


def split_halves(part, devices):
    total, width = part.shape
    core = lax.axis_index("dp") % 2
    blocks = part.reshape(total, 2, devices // 2, width // devices).transpose(1, 2, 0, 3)
    return pick(blocks, 1 - core).astype(BF16), pick(blocks, core)


def join_halves(mine, got):
    core = lax.axis_index("dp") % 2
    blocks = jnp.where(core == 1, jnp.stack([got, mine]), jnp.stack([mine, got]))
    _, chips, total, own = blocks.shape
    return blocks.transpose(2, 0, 1, 3).reshape(total, 2 * chips * own).astype(F32)


def norm_scale(x0):
    return lax.rsqrt(jnp.mean(x0 * x0, axis=-1, keepdims=True) + 1e-05)


def plain_half(slices, embed, head_row, devices):
    part = jnp.dot(slices, embed, preferred_element_type=F32)
    score = jnp.sum(part * head_row.astype(F32), axis=-1, keepdims=True)
    return *split_halves(part, devices), score


def plain_hidden(mine, got, gain_row, w_gate, w_up, down, valid, devices):
    x0 = join_halves(mine, got)
    normed = (x0 * norm_scale(x0) * gain_row.astype(F32)).astype(BF16)
    a = jnp.dot(normed, w_gate, preferred_element_type=F32)
    b = jnp.dot(normed, w_up, preferred_element_type=F32)
    sigma = jax.nn.sigmoid(a)
    active = a * sigma
    hidden = (active * b).astype(BF16).astype(F32)
    d_hidden = valid * down
    d_gate = (d_hidden * b * sigma * (1.0 + a * (1.0 - sigma))).astype(BF16)
    d_up = (d_hidden * active).astype(BF16)
    part = jnp.einsum("tf,df->td", d_gate, w_gate, preferred_element_type=F32)
    part = part + jnp.einsum("tf,df->td", d_up, w_up, preferred_element_type=F32)
    return *split_halves(part, devices), jnp.sum(hidden * down, axis=-1, keepdims=True)


def plain_input(mine, got, d_mine, d_got, gain_row, head_row, valid, embed):
    x0 = join_halves(mine, got)
    inv = norm_scale(x0)
    scaled = join_halves(d_mine, d_got) * gain_row.astype(F32)
    dx = inv * scaled - x0 * inv * inv * inv * jnp.mean(scaled * x0, axis=-1, keepdims=True)
    dx = (dx + valid * head_row.astype(F32)).astype(BF16)
    return jnp.einsum("td,vd->tv", dx, embed, preferred_element_type=F32).astype(BF16)


def body(logits, embed, norm_gain, w_gate, w_up, w_down, head, counts):
    devices = lax.axis_size("dp")
    rows, voc = logits.shape
    part = voc // devices
    width = embed.shape[1]
    hidden = w_gate.shape[1]
    own, chips = width // devices, devices // 2
    requests = counts.shape[0]
    total = rows * devices
    request_len = total // requests
    tiled = own % 128 == 0 and hidden % 128 == 0 and total % 16 == 0 and part % 16 == 0 and part > 512
    head_row, gain_row = head.reshape(1, width), norm_gain.reshape(1, width)
    if tiled:
        column = struct((rows, 1), F32)
        blocked, top, scale = call(
            softmax_kernel, [struct((devices, rows, part), BF16), column, column], logits
        )
    else:
        probs32 = jax.nn.softmax(logits.astype(F32), axis=-1)
        blocked = probs32.astype(BF16).reshape(rows, devices, part).transpose(1, 0, 2)
    slices = exchange(blocked).reshape(total, part)
    column = struct((total, 1), F32)
    half = (chips, total, own)
    flops = total * part * width
    if tiled:
        (down_row,) = call(
            down_kernel, [struct((1, hidden), F32)], head_row, w_down, blocked,
            streamed=(1,), flops=2 * hidden * width, room=2 * hidden * width,
            scratch=(
                pltpu.VMEM((hidden, width), BF16), pltpu.SemaphoreType.DMA((hidden // 128,)),
            ),
        )
        ready = 512
        first = first_rows(ready, embed, down_row, True)
        table = (
            pltpu.VMEM((part - ready, width // 2), BF16), pltpu.VMEM((total, width // 2), F32),
            pltpu.SemaphoreType.DMA((-(-part // 128),)),
        )
        args = dict(streamed=(2,), kept=(1,), flops=flops, room=part * width)
        send, score_a, first = call(
            functools.partial(half_kernel, True),
            [struct(half, BF16), column, pltpu.VMEM(first.shape, BF16)],
            slices, first, embed, head_row,
            scratch=(*table, pltpu.SemaphoreType.DMA((ready // 128,))), **args,
        )
        keep, score_b = call(
            functools.partial(half_kernel, False), [struct(half, F32), column],
            slices, first, embed, head_row, scratch=table, **args,
        )
    else:
        send, keep, score_a = plain_half(slices, embed, head_row, devices)
    summed = swap_sum(send, keep, devices)
    x_mine = chip_gather(chip_sum(summed, devices), devices)
    x_got = swap_cores(x_mine, devices)
    if tiled:
        wide = struct((total, hidden), F32)
        weight = pltpu.VMEM((width // 2, hidden), BF16)
        ahead = pltpu.VMEM((2 * own, hidden), BF16)
        rest = pltpu.VMEM((width // 2 - 2 * own, hidden), BF16)
        sems, next_sems = pltpu.SemaphoreType.DMA((2, chips)), pltpu.SemaphoreType.DMA((2, 2))
        args = dict(streamed=(2, 3), flops=2 * total * hidden * width, room=2 * width * hidden)
        a, b, squares, gate, up, next_gate, next_up = call(
            first_kernel, [wide, wide, column, weight, weight, ahead, ahead],
            x_mine, gain_row, w_gate, w_up, scratch=(sems, next_sems), **args,
        )
        narrow = struct((total, hidden), BF16)
        send, score_c, d_gate, d_up = call(
            second_kernel, [struct(half, BF16), column, narrow, narrow],
            x_got, gain_row, w_gate, w_up, next_gate, next_up,
            a, b, squares, down_row, counts,
            scratch=(rest, rest, sems), kept=(4, 5), scalars=(10,), **args,
        )
        (keep,) = call(
            third_kernel, [struct(half, F32)], d_gate, d_up, gate, up,
            kept=(2, 3), flops=2 * total * hidden * width,
        )
    else:
        down_row = jnp.sum(w_down.astype(F32) * head.astype(F32)[None, :], axis=-1)[None]
        position = jnp.arange(total, dtype=jnp.int32)[:, None]
        member = position // request_len == jnp.arange(requests, dtype=jnp.int32)[None, :]
        limit = jnp.sum(jnp.where(member, counts[None, :], 0), axis=-1, keepdims=True)
        valid = (position % request_len < limit).astype(F32)
        send, keep, score_c = plain_hidden(
            x_mine, x_got, gain_row, w_gate, w_up, down_row, valid, devices
        )
    total_d = chip_sum(swap_sum(send, keep, devices), devices)
    d_mine = chip_gather(total_d, devices)
    d_got = swap_cores(d_mine, devices)
    sources = (x_mine, x_got, d_mine, d_got, gain_row, head_row)
    padded = part + 3 * requests
    if tiled:
        first = first_rows(256, embed, total_d, False)
        (d_slices,) = call(
            input_kernel, [struct((total, padded), BF16)],
            *sources, score_a, score_b, score_c, counts, first, embed,
            scalars=(9,), kept=(10,), streamed=(11,), flops=2 * flops, room=2 * part * width,
            scratch=(
                pltpu.VMEM((total, width), BF16), pltpu.VMEM((part - 256, width), BF16),
                pltpu.SemaphoreType.DMA((-(-part // 256),)),
            ),
        )
    else:
        d_slices = plain_input(*sources, valid, embed)
        score = jnp.where(member, valid * (score_a + score_c), 0.0)
        extra = split3(jnp.sum(score, axis=0)).reshape(1, requests * 3)
        extra = jnp.broadcast_to(extra, (total, requests * 3))
        d_slices = jnp.concatenate([d_slices, extra], axis=-1)
    back = exchange(d_slices.reshape(devices, rows, padded))
    counts32 = counts.astype(F32)
    if tiled:
        guidance, rewards = call(
            final_kernel, [struct((rows, voc), BF16), struct((1, requests), F32)],
            logits, top, scale, back, counts32.reshape(1, requests),
            scratch=(pltpu.VMEM((rows, voc), F32),),
        )
        return (guidance, rewards.reshape(requests))
    sums = jnp.sum(back[:, 0, part:].astype(F32).reshape(devices, requests, 3), axis=(0, 2))
    rewards = sums / counts32
    d_probs = back[:, :, :part].transpose(1, 0, 2).reshape(rows, voc).astype(F32)
    d_logits = probs32 * (d_probs - jnp.sum(probs32 * d_probs, axis=-1, keepdims=True))
    guidance = (math.sqrt(VOC) * d_logits).astype(BF16)
    return (guidance, rewards)


def solution(mesh):
    placed = (
        P(("groups", "dp"), None),
        P("dp", None),
        P(),
        P(None, "dp"),
        P(None, "dp"),
        P("dp", None),
        P(),
        P("groups"),
    )
    return jax.shard_map(
        body,
        mesh=mesh,
        in_specs=placed,
        out_specs=(P(("groups", "dp"), None), P("groups")),
        check_vma=False,
    )
```

```python
import functools
import math

import jax
import jax.numpy as jnp
from jax import lax
from jax.experimental import pallas as pl
from jax.experimental.pallas import tpu as pltpu
from jax.sharding import PartitionSpec as P

VOC = 32000
F32, BF16 = jnp.float32, jnp.bfloat16
VMEM_BYTES = 12 * 1024 * 1024


def swap_cores(value, devices):
    return lax.ppermute(value, "dp", [(i, i ^ 1) for i in range(devices)])


def exchange(blocks):
    return lax.all_to_all(blocks, "dp", split_axis=0, concat_axis=0, tiled=True)


def exchange_chips(blocks, devices):
    groups = [list(range(core, devices, 2)) for core in range(2)]
    return lax.all_to_all(
        blocks, "dp", split_axis=0, concat_axis=0, axis_index_groups=groups, tiled=True
    )


def split3(value):
    hi = lax.reduce_precision(value, 8, 7)
    rest = value - hi
    mid = lax.reduce_precision(rest, 8, 7)
    low = rest - mid
    return jnp.stack([hi, mid, low], axis=-1).astype(BF16)


HBM_SPEC = pl.BlockSpec(memory_space=pltpu.HBM)
VMEM_SPEC = pl.BlockSpec(memory_space=pltpu.VMEM)
SMEM_SPEC = pl.BlockSpec(memory_space=pltpu.SMEM)


WINDOW = 128


def call(kernel, outs, *args, streamed=(), kept=(), scalars=(), flops=0, scratch=(), room=0):
    size = sum(math.prod(a.shape) * a.dtype.itemsize for a in args)
    places = {i: pltpu.HBM for i in streamed} | {i: pltpu.VMEM for i in kept}
    specs = [
        HBM_SPEC if i in streamed else SMEM_SPEC if i in scalars else VMEM_SPEC
        for i in range(len(args))
    ]
    return pl.pallas_call(
        kernel,
        out_shape=outs,
        in_specs=specs,
        out_specs=[VMEM_SPEC] * len(outs),
        scratch_shapes=list(scratch),
        compiler_params=pltpu.CompilerParams(vmem_limit_bytes=VMEM_BYTES + room),
        cost_estimate=pl.CostEstimate(flops=flops, bytes_accessed=size, transcendentals=0),
    )(*[
        pltpu.with_memory_space_constraint(a, places[i]) if i in places else a
        for i, a in enumerate(args)
    ])


class Stream:
    def __init__(self, copies):
        self.copies = copies
        self.done = 0
        for copy in copies[:WINDOW]:
            copy.start()

    def wait(self, count):
        while self.done < count:
            self.copies[self.done].wait()
            self.done += 1
            if self.done + WINDOW <= len(self.copies):
                self.copies[self.done + WINDOW - 1].start()


def struct(shape, dtype):
    return jax.ShapeDtypeStruct(shape, dtype)


def this_core():
    return lax.axis_index("dp") % 2


def span(start, size):
    return pl.ds(pl.multiple_of(start, size), size)


def softmax_kernel(logits_ref, out_ref, top_ref, scale_ref):
    devices, _, part = out_ref.shape
    x = logits_ref[...].astype(F32)
    top = jnp.max(x, axis=-1, keepdims=True)
    e = jnp.exp(x - top)
    scale = 1.0 / jnp.sum(e, axis=-1, keepdims=True)
    probs = e * scale
    for d in range(devices):
        out_ref[d] = probs[:, d * part : (d + 1) * part].astype(BF16)
    top_ref[...] = top
    scale_ref[...] = scale


def final_kernel(
    logits_ref, top_ref, scale_ref, back_ref, counts_ref, out_ref, rewards_ref, d_ref
):
    devices, _, padded = back_ref.shape
    part = out_ref.shape[1] // devices
    requests = counts_ref.shape[1]
    sums = jnp.zeros((1, requests), F32)
    for d in range(devices):
        block = back_ref[d].astype(F32)
        d_ref[:, d * part : (d + 1) * part] = block[:, :part]
        for i in range(3):
            start = part + i * requests
            sums += block[:1, start : start + requests]
    rewards_ref[...] = sums / counts_ref[...]
    probs = jnp.exp(logits_ref[...].astype(F32) - top_ref[...]) * scale_ref[...]
    d_probs = d_ref[...]
    mean = jnp.sum(probs * d_probs, axis=-1, keepdims=True)
    out_ref[...] = (math.sqrt(VOC) * (probs * (d_probs - mean))).astype(BF16)


def valid_column(counts_ref, total):
    requests = counts_ref.shape[0]
    length = total // requests
    position = lax.broadcasted_iota(jnp.int32, (total, 1), 0)
    valid = jnp.zeros((total, 1), F32)
    for r in range(requests):
        inside = (position >= r * length) & (position < r * length + counts_ref[r])
        valid = jnp.where(inside, 1.0, valid)
    return valid, position // length


def bring(source_ref, out_ref, sems, columns):
    fine = 128
    return [
        pltpu.make_async_copy(
            source_ref.at[pl.ds(i, fine), columns], out_ref.at[pl.ds(i, fine)], sems.at[i // fine]
        )
        for i in range(0, out_ref.shape[0], fine)
    ]


def ready_kernel(split, source_ref, after_ref, out_ref, sems):
    del after_ref
    width = out_ref.shape[1]
    columns = span((1 - this_core()) * width, width) if split else pl.ds(0, width)
    copies = bring(source_ref, out_ref, sems, columns)
    for copy in copies:
        copy.start()
    for copy in copies:
        copy.wait()


def first_rows(rows, source, after, split):
    width = source.shape[1] // 2 if split else source.shape[1]
    return call(
        functools.partial(ready_kernel, split), [pltpu.VMEM((rows, width), source.dtype)],
        source, after, streamed=(0,), scratch=(pltpu.SemaphoreType.DMA((rows // 128,)),),
    )[0]


def half_kernel(other, slices_ref, ready_ref, embed_ref, head_ref, out_ref, score_ref, *rest):
    next_ref, table, acc, sems, next_sems = rest if other else (None, *rest, None)
    chips, total, own = out_ref.shape
    part, ready = embed_ref.shape[0], ready_ref.shape[0]
    core = this_core()
    half = (1 - core) if other else core
    columns = span(half * chips * own, chips * own)
    tile, fine = 256, 128
    stream = Stream([
        pltpu.make_async_copy(
            embed_ref.at[pl.ds(i, min(fine, part - i)), columns],
            table.at[pl.ds(i - ready, min(fine, part - i))],
            sems.at[i // fine],
        )
        for i in range(ready, part, fine)
    ])
    following = []
    if other:
        following = bring(embed_ref, next_ref, next_sems, span(core * chips * own, chips * own))
        for copy in following:
            copy.start()
    acc[...] = jnp.dot(slices_ref[:, :ready], ready_ref[...], preferred_element_type=F32)
    for start in range(ready, part, tile):
        end = min(start + tile, part)
        stream.wait(-(-(end - ready) // fine))
        acc[...] += jnp.dot(
            slices_ref[:, start:end], table[start - ready : end - ready],
            preferred_element_type=F32,
        )
    score_ref[...] = jnp.sum(
        acc[...] * head_ref[:, columns].astype(F32), axis=-1, keepdims=True
    )
    for j in range(chips):
        out_ref[j] = acc[:, j * own : (j + 1) * own].astype(out_ref.dtype)
    for copy in following:
        copy.wait()


def early_kernel(
    head_ref, down_ref, embed_ref, gate_ref, up_ref, after_ref,
    out_ref, first, both, table, sems, first_sems, both_sems,
):
    del after_ref
    width, lanes = down_ref.shape[1], 128
    core = this_core()

    def copy(j):
        rows = span(j * lanes, lanes)
        return pltpu.make_async_copy(down_ref.at[rows], table.at[rows], sems.at[j])

    steps = sems.shape[0]
    for j in range(steps):
        copy(j).start()
    half = width // 2
    own = both.shape[0] // 2
    chips = half // own
    others = bring(embed_ref, first, first_sems, span((1 - core) * half, half))
    others += bring_blocks(gate_ref, up_ref, both, core, range(2), own, chips, both_sems)
    for other in others:
        other.start()

    def step(j, _):
        copy(j).wait()
        rows = span(j * lanes, lanes)
        total = jnp.zeros((lanes, lanes), F32)
        for k in range(0, width, lanes):
            head = head_ref[:, k : k + lanes].astype(F32)
            total += table[rows, k : k + lanes].astype(F32) * head
        out_ref[:, rows] = jnp.sum(total.T, axis=0, keepdims=True)
        return 0

    lax.fori_loop(0, steps, step, 0)
    for other in others:
        other.wait()


def bring_blocks(gate_ref, up_ref, both, half, blocks, own, chips, sems):
    hidden = gate_ref.shape[1]
    return [
        pltpu.make_async_copy(
            source.at[span((half * chips + j) * own, own)],
            both.at[pl.ds((j - blocks[0]) * own, own), pl.ds(k * hidden, hidden)],
            sems.at[k, j - blocks[0]],
        )
        for j in blocks
        for k, source in enumerate((gate_ref, up_ref))
    ]


def weight_rows(ready, both, own):
    skip = ready.shape[0] // own

    def weights(j):
        if j < skip:
            return ready[j * own : (j + 1) * own]
        return both[(j - skip) * own : (j - skip + 1) * own]

    return skip, weights


def forward_half(x_ref, gain_ref, half, sums, weights, wait):
    chips, _, own = x_ref.shape
    products, squares = sums
    scaled = []
    for j in range(chips):
        x = x_ref[j].astype(F32)
        squares = squares + jnp.sum(x * x, axis=-1, keepdims=True)
        gain = gain_ref[:, span((half * chips + j) * own, own)].astype(F32)
        scaled.append((x * gain).astype(BF16))
    for j in range(chips):
        wait(j)
        products = products + jnp.dot(scaled[j], weights(j), preferred_element_type=F32)
    return products, squares


def backward_half(d_both, weights, out_ref):
    contract = (((1,), (1,)), ((), ()))
    for j in range(out_ref.shape[0]):
        part = lax.dot_general(d_both, weights(j), contract, preferred_element_type=F32)
        out_ref[j] = part.astype(out_ref.dtype)


def first_kernel(
    x_ref, gain_ref, gate_ref, up_ref, ready_ref,
    products_ref, squares_ref, both, ahead, sems, ahead_sems,
):
    chips, _, own = x_ref.shape
    core = this_core()
    skip, weights = weight_rows(ready_ref, both, own)
    blocks = range(skip, chips)
    stream = Stream(bring_blocks(gate_ref, up_ref, both, core, blocks, own, chips, sems))
    blocks = range(ahead.shape[0] // own)
    following = bring_blocks(gate_ref, up_ref, ahead, 1 - core, blocks, own, chips, ahead_sems)
    for copy in following:
        copy.start()
    sums = (jnp.zeros(products_ref.shape, F32), jnp.zeros(squares_ref.shape, F32))
    products_ref[...], squares_ref[...] = forward_half(
        x_ref, gain_ref, core, sums, weights, lambda j: stream.wait(2 * (j - skip + 1))
    )
    for copy in following:
        copy.wait()


def second_kernel(
    x_ref, gain_ref, gate_ref, up_ref, ready_ref, products_ref, squares_ref, down_ref, counts_ref,
    send_ref, score_ref, d_both_ref, both, sems,
):
    chips, total, own = x_ref.shape
    width, hidden = gate_ref.shape
    half = 1 - this_core()
    skip, weights = weight_rows(ready_ref, both, own)
    blocks = range(skip, chips)
    stream = Stream(bring_blocks(gate_ref, up_ref, both, half, blocks, own, chips, sems))
    sums = (products_ref[...], squares_ref[...])
    products, squares = forward_half(
        x_ref, gain_ref, half, sums, weights, lambda j: stream.wait(2 * (j - skip + 1))
    )
    inv = lax.rsqrt(squares / width + 1e-05)
    a, b = products[:, :hidden] * inv, products[:, hidden:] * inv
    sigma = jax.nn.sigmoid(a)
    active = a * sigma
    down = down_ref[...]
    rounded = (active * b).astype(BF16).astype(F32)
    score_ref[...] = jnp.sum(rounded * down, axis=-1, keepdims=True)
    valid, _ = valid_column(counts_ref, total)
    d_hidden = valid * down
    d_both_ref[:, :hidden] = (d_hidden * b * sigma * (1.0 + a * (1.0 - sigma))).astype(BF16)
    d_both_ref[:, hidden:] = (d_hidden * active).astype(BF16)
    backward_half(d_both_ref[...], weights, send_ref)


def third_kernel(d_both_ref, ready_ref, both_ref, keep_ref):
    _, weights = weight_rows(ready_ref, both_ref, keep_ref.shape[2])
    backward_half(d_both_ref[...], weights, keep_ref)


def input_kernel(
    mine_ref, got_ref, d_mine_ref, d_got_ref, gain_ref, head_ref,
    score_a_ref, score_b_ref, score_c_ref, counts_ref, ready_ref, embed_ref,
    out_ref, dx_ref, table, sems,
):
    chips, total, own = mine_ref.shape
    voc = embed_ref.shape[0]
    requests = counts_ref.shape[0]
    width = 2 * chips * own
    core = this_core()
    ready = ready_ref.shape[0]
    tile, fine, depth = 256, 128, 3
    steps = (voc - ready) // tile
    last = ready + steps * tile

    def copy(start, size):
        return pltpu.make_async_copy(
            embed_ref.at[pl.ds(start, size)],
            table.at[pl.ds(start - ready, size)],
            sems.at[start // fine],
        )

    def pieces(start, end):
        return [copy(start + i, min(fine, end - start - i)) for i in range(0, end - start, fine)]

    def step_pieces(j):
        start = pl.multiple_of(ready + j * tile, fine)
        return [copy(pl.multiple_of(start + i, fine), fine) for i in range(0, tile, fine)]

    for j in range(min(depth, steps)):
        for piece in step_pieces(j):
            piece.start()
    sources = ((mine_ref, d_mine_ref, core), (got_ref, d_got_ref, 1 - core))
    squares = jnp.zeros((total, 1), F32)
    dots = jnp.zeros((total, 1), F32)
    for x_ref, d_ref, half in sources:
        for j in range(chips):
            x = x_ref[j].astype(F32)
            g = d_ref[j].astype(F32) * gain_ref[:, span((half * chips + j) * own, own)].astype(F32)
            squares += jnp.sum(x * x, axis=-1, keepdims=True)
            dots += jnp.sum(g * x, axis=-1, keepdims=True)
    inv = lax.rsqrt(squares / width + 1e-05)
    mean = dots / width
    valid, request = valid_column(counts_ref, total)
    for x_ref, d_ref, half in sources:
        for j in range(chips):
            columns = span((half * chips + j) * own, own)
            x = x_ref[j].astype(F32)
            g = d_ref[j].astype(F32) * gain_ref[:, columns].astype(F32)
            dx = inv * g - x * inv * inv * inv * mean
            dx_ref[:, columns] = (dx + valid * head_ref[:, columns].astype(F32)).astype(BF16)
    score = valid * (score_a_ref[...] + score_b_ref[...] + score_c_ref[...])
    member = request == lax.broadcasted_iota(jnp.int32, (total, requests), 1)
    value = jnp.sum(jnp.where(member, score, 0.0), axis=0, keepdims=True)
    parts = []
    for _ in range(3):
        piece = value.astype(BF16).astype(F32)
        parts.append(piece)
        value = value - piece
    for i, piece in enumerate(parts):
        start = voc + i * requests
        spread = jnp.broadcast_to(piece, (total, requests)).astype(BF16)
        out_ref[:, start : start + requests] = spread
    contract = (((1,), (1,)), ((), ()))

    def product(weights):
        return lax.dot_general(
            dx_ref[...], weights, contract, preferred_element_type=F32
        ).astype(BF16)

    out_ref[:, :ready] = product(ready_ref[...])

    def step(j, _):
        for piece in step_pieces(j):
            piece.wait()

        @pl.when(j + depth < steps)
        def _():
            for piece in step_pieces(j + depth):
                piece.start()

        @pl.when(j + depth == steps)
        def _():
            for piece in pieces(last, voc):
                piece.start()

        rows = pl.ds(pl.multiple_of(j * tile, tile), tile)
        out_ref[:, pl.ds(pl.multiple_of(ready + j * tile, tile), tile)] = product(table[rows, :])
        return 0

    lax.fori_loop(0, steps, step, 0)
    if last < voc:
        for piece in pieces(last, voc):
            piece.wait()
        out_ref[:, last:voc] = product(table[last - ready :, :])


def swap_sum(send, keep, devices):
    return (keep.astype(F32) + swap_cores(send, devices).astype(F32)).astype(BF16)


def chip_sum(half, devices):
    return jnp.sum(exchange_chips(half, devices).astype(F32), axis=0).astype(BF16)


def chip_gather(total, devices):
    return exchange_chips(jnp.broadcast_to(total[None], (devices // 2,) + total.shape), devices)


def pick(blocks, index):
    return lax.dynamic_index_in_dim(blocks, index, 0, keepdims=False)


def split_halves(part, devices):
    total, width = part.shape
    core = lax.axis_index("dp") % 2
    blocks = part.reshape(total, 2, devices // 2, width // devices).transpose(1, 2, 0, 3)
    return pick(blocks, 1 - core).astype(BF16), pick(blocks, core)


def join_halves(mine, got):
    core = lax.axis_index("dp") % 2
    blocks = jnp.where(core == 1, jnp.stack([got, mine]), jnp.stack([mine, got]))
    _, chips, total, own = blocks.shape
    return blocks.transpose(2, 0, 1, 3).reshape(total, 2 * chips * own).astype(F32)


def norm_scale(x0):
    return lax.rsqrt(jnp.mean(x0 * x0, axis=-1, keepdims=True) + 1e-05)


def plain_half(slices, embed, head_row, devices):
    part = jnp.dot(slices, embed, preferred_element_type=F32)
    score = jnp.sum(part * head_row.astype(F32), axis=-1, keepdims=True)
    return *split_halves(part, devices), score


def plain_hidden(mine, got, gain_row, w_gate, w_up, down, valid, devices):
    x0 = join_halves(mine, got)
    normed = (x0 * norm_scale(x0) * gain_row.astype(F32)).astype(BF16)
    a = jnp.dot(normed, w_gate, preferred_element_type=F32)
    b = jnp.dot(normed, w_up, preferred_element_type=F32)
    sigma = jax.nn.sigmoid(a)
    active = a * sigma
    hidden = (active * b).astype(BF16).astype(F32)
    d_hidden = valid * down
    d_gate = (d_hidden * b * sigma * (1.0 + a * (1.0 - sigma))).astype(BF16)
    d_up = (d_hidden * active).astype(BF16)
    part = jnp.einsum("tf,df->td", d_gate, w_gate, preferred_element_type=F32)
    part = part + jnp.einsum("tf,df->td", d_up, w_up, preferred_element_type=F32)
    return *split_halves(part, devices), jnp.sum(hidden * down, axis=-1, keepdims=True)


def plain_input(mine, got, d_mine, d_got, gain_row, head_row, valid, embed):
    x0 = join_halves(mine, got)
    inv = norm_scale(x0)
    scaled = join_halves(d_mine, d_got) * gain_row.astype(F32)
    dx = inv * scaled - x0 * inv * inv * inv * jnp.mean(scaled * x0, axis=-1, keepdims=True)
    dx = (dx + valid * head_row.astype(F32)).astype(BF16)
    return jnp.einsum("td,vd->tv", dx, embed, preferred_element_type=F32).astype(BF16)


def body(logits, embed, norm_gain, w_gate, w_up, w_down, head, counts):
    devices = lax.axis_size("dp")
    rows, voc = logits.shape
    part = voc // devices
    width = embed.shape[1]
    hidden = w_gate.shape[1]
    own, chips = width // devices, devices // 2
    requests = counts.shape[0]
    total = rows * devices
    request_len = total // requests
    tiled = own % 128 == 0 and hidden % 128 == 0 and total % 16 == 0 and part % 16 == 0 and part > 512
    head_row, gain_row = head.reshape(1, width), norm_gain.reshape(1, width)
    if tiled:
        column = struct((rows, 1), F32)
        blocked, top, scale = call(
            softmax_kernel, [struct((devices, rows, part), BF16), column, column], logits
        )
    else:
        probs32 = jax.nn.softmax(logits.astype(F32), axis=-1)
        blocked = probs32.astype(BF16).reshape(rows, devices, part).transpose(1, 0, 2)
    slices = exchange(blocked).reshape(total, part)
    column = struct((total, 1), F32)
    half = (chips, total, own)
    flops = total * part * width
    if tiled:
        ready = 256
        down_row, first, both_first = call(
            early_kernel,
            [
                struct((1, hidden), F32), pltpu.VMEM((ready, width // 2), BF16),
                pltpu.VMEM((2 * own, 2 * hidden), BF16),
            ],
            head_row, w_down, embed, w_gate, w_up, blocked,
            streamed=(1, 2, 3, 4), flops=2 * hidden * width, room=2 * hidden * width,
            scratch=(
                pltpu.VMEM((hidden, width), BF16), pltpu.SemaphoreType.DMA((hidden // 128,)),
                pltpu.SemaphoreType.DMA((ready // 128,)), pltpu.SemaphoreType.DMA((2, 2)),
            ),
        )

        def table(ready):
            return (
                pltpu.VMEM((part - ready, width // 2), BF16),
                pltpu.VMEM((total, width // 2), F32),
                pltpu.SemaphoreType.DMA((-(-part // 128),)),
            )

        args = dict(streamed=(2,), kept=(1,), flops=flops, room=part * width)
        send, score_a, first = call(
            functools.partial(half_kernel, True),
            [struct(half, BF16), column, pltpu.VMEM((2 * ready, width // 2), BF16)],
            slices, first, embed, head_row,
            scratch=(*table(ready), pltpu.SemaphoreType.DMA((ready // 64,))), **args,
        )
        keep, score_b = call(
            functools.partial(half_kernel, False), [struct(half, F32), column],
            slices, first, embed, head_row, scratch=table(2 * ready), **args,
        )
    else:
        send, keep, score_a = plain_half(slices, embed, head_row, devices)
    summed = swap_sum(send, keep, devices)
    x_mine = chip_gather(chip_sum(summed, devices), devices)
    x_got = swap_cores(x_mine, devices)
    if tiled:
        weight = (width // 2 - 2 * own, 2 * hidden)
        sems, ahead_sems = pltpu.SemaphoreType.DMA((2, chips)), pltpu.SemaphoreType.DMA((2, 2))
        args = dict(
            streamed=(2, 3), kept=(4,), flops=2 * total * hidden * width, room=2 * width * hidden
        )
        products, squares, both, ahead = call(
            first_kernel,
            [
                struct((total, 2 * hidden), F32), column, pltpu.VMEM(weight, BF16),
                pltpu.VMEM(both_first.shape, BF16),
            ],
            x_mine, gain_row, w_gate, w_up, both_first, scratch=(sems, ahead_sems), **args,
        )
        send, score_c, d_both = call(
            second_kernel,
            [struct(half, BF16), column, struct((total, 2 * hidden), BF16)],
            x_got, gain_row, w_gate, w_up, ahead, products, squares, down_row, counts,
            scratch=(pltpu.VMEM(weight, BF16), sems), scalars=(8,), **args,
        )
        (keep,) = call(
            third_kernel, [struct(half, F32)], d_both, both_first, both,
            kept=(1, 2), flops=2 * total * hidden * width,
        )
    else:
        down_row = jnp.sum(w_down.astype(F32) * head.astype(F32)[None, :], axis=-1)[None]
        position = jnp.arange(total, dtype=jnp.int32)[:, None]
        member = position // request_len == jnp.arange(requests, dtype=jnp.int32)[None, :]
        limit = jnp.sum(jnp.where(member, counts[None, :], 0), axis=-1, keepdims=True)
        valid = (position % request_len < limit).astype(F32)
        send, keep, score_c = plain_hidden(
            x_mine, x_got, gain_row, w_gate, w_up, down_row, valid, devices
        )
    total_d = chip_sum(swap_sum(send, keep, devices), devices)
    d_mine = chip_gather(total_d, devices)
    d_got = swap_cores(d_mine, devices)
    sources = (x_mine, x_got, d_mine, d_got, gain_row, head_row)
    padded = part + 3 * requests
    if tiled:
        first = first_rows(256, embed, total_d, False)
        (d_slices,) = call(
            input_kernel, [struct((total, padded), BF16)],
            *sources, score_a, score_b, score_c, counts, first, embed,
            scalars=(9,), kept=(10,), streamed=(11,), flops=2 * flops, room=2 * part * width,
            scratch=(
                pltpu.VMEM((total, width), BF16), pltpu.VMEM((part - 256, width), BF16),
                pltpu.SemaphoreType.DMA((-(-part // 128),)),
            ),
        )
    else:
        d_slices = plain_input(*sources, valid, embed)
        score = jnp.where(member, valid * (score_a + score_c), 0.0)
        extra = split3(jnp.sum(score, axis=0)).reshape(1, requests * 3)
        extra = jnp.broadcast_to(extra, (total, requests * 3))
        d_slices = jnp.concatenate([d_slices, extra], axis=-1)
    back = exchange(d_slices.reshape(devices, rows, padded))
    counts32 = counts.astype(F32)
    if tiled:
        guidance, rewards = call(
            final_kernel, [struct((rows, voc), BF16), struct((1, requests), F32)],
            logits, top, scale, back, counts32.reshape(1, requests),
            scratch=(pltpu.VMEM((rows, voc), F32),),
        )
        return (guidance, rewards.reshape(requests))
    sums = jnp.sum(back[:, 0, part:].astype(F32).reshape(devices, requests, 3), axis=(0, 2))
    rewards = sums / counts32
    d_probs = back[:, :, :part].transpose(1, 0, 2).reshape(rows, voc).astype(F32)
    d_logits = probs32 * (d_probs - jnp.sum(probs32 * d_probs, axis=-1, keepdims=True))
    guidance = (math.sqrt(VOC) * d_logits).astype(BF16)
    return (guidance, rewards)


def solution(mesh):
    placed = (
        P(("groups", "dp"), None),
        P("dp", None),
        P(),
        P(None, "dp"),
        P(None, "dp"),
        P("dp", None),
        P(),
        P("groups"),
    )
    return jax.shard_map(
        body,
        mesh=mesh,
        in_specs=placed,
        out_specs=(P(("groups", "dp"), None), P("groups")),
        check_vma=False,
    )
```

```python
import functools
import math

import jax
import jax.numpy as jnp
from jax import lax
from jax.experimental import pallas as pl
from jax.experimental.pallas import tpu as pltpu
from jax.sharding import PartitionSpec as P

VOC = 32000
F32, BF16 = jnp.float32, jnp.bfloat16
VMEM_BYTES = 12 * 1024 * 1024


def swap_cores(value, devices):
    return lax.ppermute(value, "dp", [(i, i ^ 1) for i in range(devices)])


def exchange(blocks):
    return lax.all_to_all(blocks, "dp", split_axis=0, concat_axis=0, tiled=True)


def exchange_chips(blocks, devices):
    groups = [list(range(core, devices, 2)) for core in range(2)]
    return lax.all_to_all(
        blocks, "dp", split_axis=0, concat_axis=0, axis_index_groups=groups, tiled=True
    )


def split3(value):
    hi = lax.reduce_precision(value, 8, 7)
    rest = value - hi
    mid = lax.reduce_precision(rest, 8, 7)
    low = rest - mid
    return jnp.stack([hi, mid, low], axis=-1).astype(BF16)


HBM_SPEC = pl.BlockSpec(memory_space=pltpu.HBM)
VMEM_SPEC = pl.BlockSpec(memory_space=pltpu.VMEM)
SMEM_SPEC = pl.BlockSpec(memory_space=pltpu.SMEM)


WINDOW = 128


def call(kernel, outs, *args, streamed=(), kept=(), scalars=(), flops=0, scratch=(), room=0):
    size = sum(math.prod(a.shape) * a.dtype.itemsize for a in args)
    places = {i: pltpu.HBM for i in streamed} | {i: pltpu.VMEM for i in kept}
    specs = [
        HBM_SPEC if i in streamed else SMEM_SPEC if i in scalars else VMEM_SPEC
        for i in range(len(args))
    ]
    return pl.pallas_call(
        kernel,
        out_shape=outs,
        in_specs=specs,
        out_specs=[VMEM_SPEC] * len(outs),
        scratch_shapes=list(scratch),
        compiler_params=pltpu.CompilerParams(vmem_limit_bytes=VMEM_BYTES + room),
        cost_estimate=pl.CostEstimate(flops=flops, bytes_accessed=size, transcendentals=0),
    )(*[
        pltpu.with_memory_space_constraint(a, places[i]) if i in places else a
        for i, a in enumerate(args)
    ])


class Stream:
    def __init__(self, copies):
        self.copies = copies
        self.done = 0
        for copy in copies[:WINDOW]:
            copy.start()

    def wait(self, count):
        while self.done < count:
            self.copies[self.done].wait()
            self.done += 1
            if self.done + WINDOW <= len(self.copies):
                self.copies[self.done + WINDOW - 1].start()


def struct(shape, dtype):
    return jax.ShapeDtypeStruct(shape, dtype)


def this_core():
    return lax.axis_index("dp") % 2


def span(start, size):
    return pl.ds(pl.multiple_of(start, size), size)


def softmax_kernel(logits_ref, out_ref, probs_ref):
    devices, _, part = out_ref.shape
    x = logits_ref[...].astype(F32)
    e = jnp.exp(x - jnp.max(x, axis=-1, keepdims=True))
    probs = e * (1.0 / jnp.sum(e, axis=-1, keepdims=True))
    probs_ref[...] = probs
    for d in range(devices):
        out_ref[d] = probs[:, d * part : (d + 1) * part].astype(BF16)


def final_kernel(probs_ref, back_ref, counts_ref, out_ref, rewards_ref, d_ref):
    devices, _, padded = back_ref.shape
    part = out_ref.shape[1] // devices
    requests = counts_ref.shape[0]
    sums = jnp.zeros((1, requests), F32)
    for d in range(devices):
        block = back_ref[d].astype(F32)
        d_ref[:, d * part : (d + 1) * part] = block[:, :part]
        for i in range(3):
            start = part + i * requests
            sums += block[:1, start : start + requests]
    lane = lax.broadcasted_iota(jnp.int32, (1, requests), 1)
    counts = jnp.ones((1, requests), F32)
    for r in range(requests):
        counts = jnp.where(lane == r, counts_ref[r].astype(F32), counts)
    rewards_ref[...] = sums / counts
    probs, d_probs = probs_ref[...], d_ref[...]
    mean = jnp.sum(probs * d_probs, axis=-1, keepdims=True)
    out_ref[...] = (math.sqrt(VOC) * (probs * (d_probs - mean))).astype(BF16)


def valid_column(counts_ref, total):
    requests = counts_ref.shape[0]
    length = total // requests
    position = lax.broadcasted_iota(jnp.int32, (total, 1), 0)
    valid = jnp.zeros((total, 1), F32)
    for r in range(requests):
        inside = (position >= r * length) & (position < r * length + counts_ref[r])
        valid = jnp.where(inside, 1.0, valid)
    return valid, position // length


def bring(source_ref, out_ref, sems, columns):
    fine = 128
    return [
        pltpu.make_async_copy(
            source_ref.at[pl.ds(i, fine), columns], out_ref.at[pl.ds(i, fine)], sems.at[i // fine]
        )
        for i in range(0, out_ref.shape[0], fine)
    ]


def ready_kernel(split, source_ref, after_ref, out_ref, sems):
    del after_ref
    width = out_ref.shape[1]
    columns = span((1 - this_core()) * width, width) if split else pl.ds(0, width)
    copies = bring(source_ref, out_ref, sems, columns)
    for copy in copies:
        copy.start()
    for copy in copies:
        copy.wait()


def first_rows(rows, source, after, split):
    width = source.shape[1] // 2 if split else source.shape[1]
    return call(
        functools.partial(ready_kernel, split), [pltpu.VMEM((rows, width), source.dtype)],
        source, after, streamed=(0,), scratch=(pltpu.SemaphoreType.DMA((rows // 128,)),),
    )[0]


def half_kernel(other, slices_ref, ready_ref, embed_ref, head_ref, out_ref, score_ref, *rest):
    next_ref, table, acc, sems, next_sems = rest if other else (None, *rest, None)
    chips, total, own = out_ref.shape
    part, ready = embed_ref.shape[0], ready_ref.shape[0]
    core = this_core()
    half = (1 - core) if other else core
    columns = span(half * chips * own, chips * own)
    tile, fine = 256, 128
    stream = Stream([
        pltpu.make_async_copy(
            embed_ref.at[pl.ds(i, min(fine, part - i)), columns],
            table.at[pl.ds(i - ready, min(fine, part - i))],
            sems.at[i // fine],
        )
        for i in range(ready, part, fine)
    ])
    following = []
    if other:
        following = bring(embed_ref, next_ref, next_sems, span(core * chips * own, chips * own))
        for copy in following:
            copy.start()
    acc[...] = jnp.dot(slices_ref[:, :ready], ready_ref[...], preferred_element_type=F32)
    for start in range(ready, part, tile):
        end = min(start + tile, part)
        stream.wait(-(-(end - ready) // fine))
        acc[...] += jnp.dot(
            slices_ref[:, start:end], table[start - ready : end - ready],
            preferred_element_type=F32,
        )
    score_ref[...] = jnp.sum(
        acc[...] * head_ref[:, columns].astype(F32), axis=-1, keepdims=True
    )
    for j in range(chips):
        out_ref[j] = acc[:, j * own : (j + 1) * own].astype(out_ref.dtype)
    for copy in following:
        copy.wait()


def early_kernel(
    head_ref, down_ref, embed_ref, gate_ref, up_ref, after_ref, greeting_ref,
    out_ref, first, both, table, sems, first_sems, both_sems,
):
    del after_ref, greeting_ref
    width, lanes = down_ref.shape[1], 128
    core = this_core()

    def copy(j):
        rows = span(j * lanes, lanes)
        return pltpu.make_async_copy(down_ref.at[rows], table.at[rows], sems.at[j])

    steps = sems.shape[0]
    for j in range(steps):
        copy(j).start()
    half = width // 2
    own = both.shape[0] // 2
    chips = half // own
    others = bring(embed_ref, first, first_sems, span((1 - core) * half, half))
    others += bring_blocks(gate_ref, up_ref, both, core, range(2), own, chips, both_sems)
    for other in others:
        other.start()

    def step(j, _):
        copy(j).wait()
        rows = span(j * lanes, lanes)
        total = jnp.zeros((lanes, lanes), F32)
        for k in range(0, width, lanes):
            head = head_ref[:, k : k + lanes].astype(F32)
            total += table[rows, k : k + lanes].astype(F32) * head
        out_ref[:, rows] = jnp.sum(total.T, axis=0, keepdims=True)
        return 0

    lax.fori_loop(0, steps, step, 0)
    for other in others:
        other.wait()


def bring_blocks(gate_ref, up_ref, both, half, blocks, own, chips, sems):
    hidden = gate_ref.shape[1]
    return [
        pltpu.make_async_copy(
            source.at[span((half * chips + j) * own, own)],
            both.at[pl.ds((j - blocks[0]) * own, own), pl.ds(k * hidden, hidden)],
            sems.at[k, j - blocks[0]],
        )
        for j in blocks
        for k, source in enumerate((gate_ref, up_ref))
    ]


def weight_rows(ready, both, own):
    skip = ready.shape[0] // own

    def weights(j):
        if j < skip:
            return ready[j * own : (j + 1) * own]
        return both[(j - skip) * own : (j - skip + 1) * own]

    return skip, weights


def forward_half(x_ref, gain_ref, half, sums, weights, wait):
    chips, _, own = x_ref.shape
    products, squares = sums
    scaled = []
    wide = jnp.zeros(x_ref.shape[1:], F32)
    for j in range(chips):
        x = x_ref[j].astype(F32)
        wide = wide + x * x
        gain = gain_ref[:, span((half * chips + j) * own, own)].astype(F32)
        scaled.append((x * gain).astype(BF16))
    squares = squares + jnp.sum(wide, axis=-1, keepdims=True)
    for j in range(chips):
        wait(j)
        products = products + jnp.dot(scaled[j], weights(j), preferred_element_type=F32)
    return products, squares


def backward_half(d_both, weights, out_ref):
    contract = (((1,), (1,)), ((), ()))
    for j in range(out_ref.shape[0]):
        part = lax.dot_general(d_both, weights(j), contract, preferred_element_type=F32)
        out_ref[j] = part.astype(out_ref.dtype)


def first_kernel(
    x_ref, gain_ref, gate_ref, up_ref, ready_ref,
    products_ref, squares_ref, both, ahead, sems, ahead_sems,
):
    chips, _, own = x_ref.shape
    core = this_core()
    skip, weights = weight_rows(ready_ref, both, own)
    blocks = range(skip, chips)
    stream = Stream(bring_blocks(gate_ref, up_ref, both, core, blocks, own, chips, sems))
    blocks = range(ahead.shape[0] // own)
    following = bring_blocks(gate_ref, up_ref, ahead, 1 - core, blocks, own, chips, ahead_sems)
    for copy in following:
        copy.start()
    sums = (jnp.zeros(products_ref.shape, F32), jnp.zeros(squares_ref.shape, F32))
    products_ref[...], squares_ref[...] = forward_half(
        x_ref, gain_ref, core, sums, weights, lambda j: stream.wait(2 * (j - skip + 1))
    )
    for copy in following:
        copy.wait()


def second_kernel(
    x_ref, gain_ref, gate_ref, up_ref, ready_ref, products_ref, squares_ref, down_ref, counts_ref,
    send_ref, score_ref, inv_ref, d_both_ref, both, sems,
):
    chips, total, own = x_ref.shape
    width, hidden = gate_ref.shape
    half = 1 - this_core()
    skip, weights = weight_rows(ready_ref, both, own)
    blocks = range(skip, chips)
    stream = Stream(bring_blocks(gate_ref, up_ref, both, half, blocks, own, chips, sems))
    sums = (products_ref[...], squares_ref[...])
    products, squares = forward_half(
        x_ref, gain_ref, half, sums, weights, lambda j: stream.wait(2 * (j - skip + 1))
    )
    inv = lax.rsqrt(squares / width + 1e-05)
    inv_ref[...] = inv
    a, b = products[:, :hidden] * inv, products[:, hidden:] * inv
    sigma = jax.nn.sigmoid(a)
    active = a * sigma
    down = down_ref[...]
    rounded = (active * b).astype(BF16).astype(F32)
    score_ref[...] = jnp.sum(rounded * down, axis=-1, keepdims=True)
    valid, _ = valid_column(counts_ref, total)
    d_hidden = valid * down
    d_both_ref[:, :hidden] = (d_hidden * b * sigma * (1.0 + a * (1.0 - sigma))).astype(BF16)
    d_both_ref[:, hidden:] = (d_hidden * active).astype(BF16)
    backward_half(d_both_ref[...], weights, send_ref)


def third_kernel(d_both_ref, ready_ref, both_ref, keep_ref):
    _, weights = weight_rows(ready_ref, both_ref, keep_ref.shape[2])
    backward_half(d_both_ref[...], weights, keep_ref)


def input_kernel(
    mine_ref, got_ref, d_mine_ref, d_got_ref, gain_ref, head_ref, inv_ref,
    score_a_ref, score_b_ref, score_c_ref, counts_ref, ready_ref, embed_ref,
    out_ref, dx_ref, table, sems,
):
    chips, total, own = mine_ref.shape
    voc = embed_ref.shape[0]
    requests = counts_ref.shape[0]
    width = 2 * chips * own
    core = this_core()
    ready = ready_ref.shape[0]
    tile, fine = 256, 64
    steps = (voc - ready) // tile
    last = ready + steps * tile

    def copy(start, size):
        return pltpu.make_async_copy(
            embed_ref.at[pl.ds(start, size)],
            table.at[pl.ds(start - ready, size)],
            sems.at[start // fine],
        )

    def pieces(start, end):
        return [copy(start + i, min(fine, end - start - i)) for i in range(0, end - start, fine)]

    def step_pieces(j):
        start = pl.multiple_of(ready + j * tile, fine)
        return [copy(pl.multiple_of(start + i, fine), fine) for i in range(0, tile, fine)]

    for piece in pieces(ready, voc):
        piece.start()
    sources = ((mine_ref, d_mine_ref, core), (got_ref, d_got_ref, 1 - core))
    wide = jnp.zeros((total, own), F32)
    for x_ref, d_ref, half in sources:
        for j in range(chips):
            gain = gain_ref[:, span((half * chips + j) * own, own)].astype(F32)
            wide += d_ref[j].astype(F32) * gain * x_ref[j].astype(F32)
    inv = inv_ref[...]
    weight = inv * inv * inv * (jnp.sum(wide, axis=-1, keepdims=True) / width)
    valid, request = valid_column(counts_ref, total)
    for x_ref, d_ref, half in sources:
        for j in range(chips):
            columns = span((half * chips + j) * own, own)
            x = x_ref[j].astype(F32)
            g = d_ref[j].astype(F32) * gain_ref[:, columns].astype(F32)
            dx = inv * g - x * weight
            dx_ref[:, columns] = (dx + valid * head_ref[:, columns].astype(F32)).astype(BF16)
    score = valid * (score_a_ref[...] + score_b_ref[...] + score_c_ref[...])
    member = request == lax.broadcasted_iota(jnp.int32, (total, requests), 1)
    value = jnp.sum(jnp.where(member, score, 0.0), axis=0, keepdims=True)
    parts = []
    for _ in range(3):
        piece = value.astype(BF16).astype(F32)
        parts.append(piece)
        value = value - piece
    for i, piece in enumerate(parts):
        start = voc + i * requests
        spread = jnp.broadcast_to(piece, (total, requests)).astype(BF16)
        out_ref[:, start : start + requests] = spread
    contract = (((1,), (1,)), ((), ()))

    def product(weights):
        return lax.dot_general(
            dx_ref[...], weights, contract, preferred_element_type=F32
        ).astype(BF16)

    out_ref[:, :ready] = product(ready_ref[...])

    def step(j, _):
        for piece in step_pieces(j):
            piece.wait()

        rows = pl.ds(pl.multiple_of(j * tile, tile), tile)
        out_ref[:, pl.ds(pl.multiple_of(ready + j * tile, tile), tile)] = product(table[rows, :])
        return 0

    lax.fori_loop(0, steps, step, 0)
    if last < voc:
        for piece in pieces(last, voc):
            piece.wait()
        out_ref[:, last:voc] = product(table[last - ready :, :])


def swap_sum(send, keep, devices):
    return (keep.astype(F32) + swap_cores(send, devices).astype(F32)).astype(BF16)


def chip_sum(half, devices):
    return jnp.sum(exchange_chips(half, devices).astype(F32), axis=0).astype(BF16)


def chip_gather(total, devices):
    return exchange_chips(jnp.broadcast_to(total[None], (devices // 2,) + total.shape), devices)


def pick(blocks, index):
    return lax.dynamic_index_in_dim(blocks, index, 0, keepdims=False)


def split_halves(part, devices):
    total, width = part.shape
    core = lax.axis_index("dp") % 2
    blocks = part.reshape(total, 2, devices // 2, width // devices).transpose(1, 2, 0, 3)
    return pick(blocks, 1 - core).astype(BF16), pick(blocks, core)


def join_halves(mine, got):
    core = lax.axis_index("dp") % 2
    blocks = jnp.where(core == 1, jnp.stack([got, mine]), jnp.stack([mine, got]))
    _, chips, total, own = blocks.shape
    return blocks.transpose(2, 0, 1, 3).reshape(total, 2 * chips * own).astype(F32)


def norm_scale(x0):
    return lax.rsqrt(jnp.mean(x0 * x0, axis=-1, keepdims=True) + 1e-05)


def plain_half(slices, embed, head_row, devices):
    part = jnp.dot(slices, embed, preferred_element_type=F32)
    score = jnp.sum(part * head_row.astype(F32), axis=-1, keepdims=True)
    return *split_halves(part, devices), score


def plain_hidden(mine, got, gain_row, w_gate, w_up, down, valid, devices):
    x0 = join_halves(mine, got)
    normed = (x0 * norm_scale(x0) * gain_row.astype(F32)).astype(BF16)
    a = jnp.dot(normed, w_gate, preferred_element_type=F32)
    b = jnp.dot(normed, w_up, preferred_element_type=F32)
    sigma = jax.nn.sigmoid(a)
    active = a * sigma
    hidden = (active * b).astype(BF16).astype(F32)
    d_hidden = valid * down
    d_gate = (d_hidden * b * sigma * (1.0 + a * (1.0 - sigma))).astype(BF16)
    d_up = (d_hidden * active).astype(BF16)
    part = jnp.einsum("tf,df->td", d_gate, w_gate, preferred_element_type=F32)
    part = part + jnp.einsum("tf,df->td", d_up, w_up, preferred_element_type=F32)
    return *split_halves(part, devices), jnp.sum(hidden * down, axis=-1, keepdims=True)


def plain_input(mine, got, d_mine, d_got, gain_row, head_row, valid, embed):
    x0 = join_halves(mine, got)
    inv = norm_scale(x0)
    scaled = join_halves(d_mine, d_got) * gain_row.astype(F32)
    dx = inv * scaled - x0 * inv * inv * inv * jnp.mean(scaled * x0, axis=-1, keepdims=True)
    dx = (dx + valid * head_row.astype(F32)).astype(BF16)
    return jnp.einsum("td,vd->tv", dx, embed, preferred_element_type=F32).astype(BF16)


def body(logits, embed, norm_gain, w_gate, w_up, w_down, head, counts):
    devices = lax.axis_size("dp")
    rows, voc = logits.shape
    part = voc // devices
    width = embed.shape[1]
    hidden = w_gate.shape[1]
    own, chips = width // devices, devices // 2
    requests = counts.shape[0]
    total = rows * devices
    request_len = total // requests
    tiled = own % 128 == 0 and hidden % 128 == 0 and total % 16 == 0 and part % 16 == 0 and part > 512
    head_row, gain_row = head.reshape(1, width), norm_gain.reshape(1, width)
    if tiled:
        around = [(i, (i + devices // 4) % devices) for i in range(devices)]
        greeting = lax.ppermute(gain_row[:, :128], "dp", around)
        blocked, probs = call(
            softmax_kernel,
            [struct((devices, rows, part), BF16), pltpu.VMEM((rows, voc), F32)], logits,
        )
    else:
        probs32 = jax.nn.softmax(logits.astype(F32), axis=-1)
        blocked = probs32.astype(BF16).reshape(rows, devices, part).transpose(1, 0, 2)
    slices = exchange(blocked).reshape(total, part)
    column = struct((total, 1), F32)
    half = (chips, total, own)
    flops = total * part * width
    if tiled:
        ready = 256
        down_row, first, both_first = call(
            early_kernel,
            [
                struct((1, hidden), F32), pltpu.VMEM((ready, width // 2), BF16),
                pltpu.VMEM((2 * own, 2 * hidden), BF16),
            ],
            head_row, w_down, embed, w_gate, w_up, blocked, greeting,
            streamed=(1, 2, 3, 4), flops=2 * hidden * width, room=2 * hidden * width,
            scratch=(
                pltpu.VMEM((hidden, width), BF16), pltpu.SemaphoreType.DMA((hidden // 128,)),
                pltpu.SemaphoreType.DMA((ready // 128,)), pltpu.SemaphoreType.DMA((2, 2)),
            ),
        )

        def table(ready):
            return (
                pltpu.VMEM((part - ready, width // 2), BF16),
                pltpu.VMEM((total, width // 2), F32),
                pltpu.SemaphoreType.DMA((-(-part // 128),)),
            )

        args = dict(streamed=(2,), kept=(1,), flops=flops, room=part * width)
        send, score_a, first = call(
            functools.partial(half_kernel, True),
            [struct(half, BF16), column, pltpu.VMEM((2 * ready, width // 2), BF16)],
            slices, first, embed, head_row,
            scratch=(*table(ready), pltpu.SemaphoreType.DMA((ready // 64,))), **args,
        )
        keep, score_b = call(
            functools.partial(half_kernel, False), [struct(half, F32), column],
            slices, first, embed, head_row, scratch=table(2 * ready), **args,
        )
    else:
        send, keep, score_a = plain_half(slices, embed, head_row, devices)
    summed = swap_sum(send, keep, devices)
    x_mine = chip_gather(chip_sum(summed, devices), devices)
    x_got = swap_cores(x_mine, devices)
    if tiled:
        weight = (width // 2 - 2 * own, 2 * hidden)
        sems, ahead_sems = pltpu.SemaphoreType.DMA((2, chips)), pltpu.SemaphoreType.DMA((2, 2))
        args = dict(
            streamed=(2, 3), kept=(4,), flops=2 * total * hidden * width, room=2 * width * hidden
        )
        products, squares, both, ahead = call(
            first_kernel,
            [
                struct((total, 2 * hidden), F32), column, pltpu.VMEM(weight, BF16),
                pltpu.VMEM(both_first.shape, BF16),
            ],
            x_mine, gain_row, w_gate, w_up, both_first, scratch=(sems, ahead_sems), **args,
        )
        send, score_c, inv, d_both = call(
            second_kernel,
            [struct(half, BF16), column, column, struct((total, 2 * hidden), BF16)],
            x_got, gain_row, w_gate, w_up, ahead, products, squares, down_row, counts,
            scratch=(pltpu.VMEM(weight, BF16), sems), scalars=(8,), **args,
        )
        (keep,) = call(
            third_kernel, [struct(half, F32)], d_both, both_first, both,
            kept=(1, 2), flops=2 * total * hidden * width,
        )
    else:
        down_row = jnp.sum(w_down.astype(F32) * head.astype(F32)[None, :], axis=-1)[None]
        position = jnp.arange(total, dtype=jnp.int32)[:, None]
        member = position // request_len == jnp.arange(requests, dtype=jnp.int32)[None, :]
        limit = jnp.sum(jnp.where(member, counts[None, :], 0), axis=-1, keepdims=True)
        valid = (position % request_len < limit).astype(F32)
        send, keep, score_c = plain_hidden(
            x_mine, x_got, gain_row, w_gate, w_up, down_row, valid, devices
        )
    total_d = chip_sum(swap_sum(send, keep, devices), devices)
    d_mine = chip_gather(total_d, devices)
    d_got = swap_cores(d_mine, devices)
    padded = part + 3 * requests
    if tiled:
        first = first_rows(256, embed, total_d, False)
        (d_slices,) = call(
            input_kernel, [struct((total, padded), BF16)],
            x_mine, x_got, d_mine, d_got, gain_row, head_row, inv,
            score_a, score_b, score_c, counts, first, embed,
            scalars=(10,), kept=(11,), streamed=(12,), flops=2 * flops, room=2 * part * width,
            scratch=(
                pltpu.VMEM((total, width), BF16), pltpu.VMEM((part - 256, width), BF16),
                pltpu.SemaphoreType.DMA((-(-part // 64),)),
            ),
        )
    else:
        d_slices = plain_input(x_mine, x_got, d_mine, d_got, gain_row, head_row, valid, embed)
        score = jnp.where(member, valid * (score_a + score_c), 0.0)
        extra = split3(jnp.sum(score, axis=0)).reshape(1, requests * 3)
        extra = jnp.broadcast_to(extra, (total, requests * 3))
        d_slices = jnp.concatenate([d_slices, extra], axis=-1)
    back = exchange(d_slices.reshape(devices, rows, padded))
    if tiled:
        guidance, rewards = call(
            final_kernel, [struct((rows, voc), BF16), struct((1, requests), F32)],
            probs, back, counts, kept=(0,), scalars=(2,),
            scratch=(pltpu.VMEM((rows, voc), F32),),
        )
        return (guidance, rewards.reshape(requests))
    sums = jnp.sum(back[:, 0, part:].astype(F32).reshape(devices, requests, 3), axis=(0, 2))
    rewards = sums / counts.astype(F32)
    d_probs = back[:, :, :part].transpose(1, 0, 2).reshape(rows, voc).astype(F32)
    d_logits = probs32 * (d_probs - jnp.sum(probs32 * d_probs, axis=-1, keepdims=True))
    guidance = (math.sqrt(VOC) * d_logits).astype(BF16)
    return (guidance, rewards)


def solution(mesh):
    placed = (
        P(("groups", "dp"), None),
        P("dp", None),
        P(),
        P(None, "dp"),
        P(None, "dp"),
        P("dp", None),
        P(),
        P("groups"),
    )
    return jax.shard_map(
        body,
        mesh=mesh,
        in_specs=placed,
        out_specs=(P(("groups", "dp"), None), P("groups")),
        check_vma=False,
    )
```

```python
import functools
import math

import jax
import jax.numpy as jnp
from jax import lax
from jax.experimental import pallas as pl
from jax.experimental.pallas import tpu as pltpu
from jax.sharding import PartitionSpec as P

VOC = 32000
F32, BF16 = jnp.float32, jnp.bfloat16
VMEM_BYTES = 12 * 1024 * 1024


def swap_cores(value, devices):
    return lax.ppermute(value, "dp", [(i, i ^ 1) for i in range(devices)])


def exchange(blocks):
    return lax.all_to_all(blocks, "dp", split_axis=0, concat_axis=0, tiled=True)


def exchange_chips(blocks, devices):
    groups = [list(range(core, devices, 2)) for core in range(2)]
    return lax.all_to_all(
        blocks, "dp", split_axis=0, concat_axis=0, axis_index_groups=groups, tiled=True
    )


def split3(value):
    hi = lax.reduce_precision(value, 8, 7)
    rest = value - hi
    mid = lax.reduce_precision(rest, 8, 7)
    low = rest - mid
    return jnp.stack([hi, mid, low], axis=-1).astype(BF16)


HBM_SPEC = pl.BlockSpec(memory_space=pltpu.HBM)
VMEM_SPEC = pl.BlockSpec(memory_space=pltpu.VMEM)
SMEM_SPEC = pl.BlockSpec(memory_space=pltpu.SMEM)


WINDOW = 128


def call(kernel, outs, *args, streamed=(), kept=(), scalars=(), flops=0, scratch=(), room=0):
    size = sum(math.prod(a.shape) * a.dtype.itemsize for a in args)
    places = {i: pltpu.HBM for i in streamed} | {i: pltpu.VMEM for i in kept}
    specs = [
        HBM_SPEC if i in streamed else SMEM_SPEC if i in scalars else VMEM_SPEC
        for i in range(len(args))
    ]
    return pl.pallas_call(
        kernel,
        out_shape=outs,
        in_specs=specs,
        out_specs=[VMEM_SPEC] * len(outs),
        scratch_shapes=list(scratch),
        compiler_params=pltpu.CompilerParams(vmem_limit_bytes=VMEM_BYTES + room),
        cost_estimate=pl.CostEstimate(flops=flops, bytes_accessed=size, transcendentals=0),
    )(*[
        pltpu.with_memory_space_constraint(a, places[i]) if i in places else a
        for i, a in enumerate(args)
    ])


class Stream:
    def __init__(self, copies):
        self.copies = copies
        self.done = 0
        for copy in copies[:WINDOW]:
            copy.start()

    def wait(self, count):
        while self.done < count:
            self.copies[self.done].wait()
            self.done += 1
            if self.done + WINDOW <= len(self.copies):
                self.copies[self.done + WINDOW - 1].start()


def struct(shape, dtype):
    return jax.ShapeDtypeStruct(shape, dtype)


def this_core():
    return lax.axis_index("dp") % 2


def span(start, size):
    return pl.ds(pl.multiple_of(start, size), size)


def softmax_kernel(logits_ref, out_ref, probs_ref):
    devices, _, part = out_ref.shape
    x = logits_ref[...].astype(F32)
    e = jnp.exp(x - jnp.max(x, axis=-1, keepdims=True))
    probs = e * (1.0 / jnp.sum(e, axis=-1, keepdims=True))
    probs_ref[...] = probs
    for d in range(devices):
        out_ref[d] = probs[:, d * part : (d + 1) * part].astype(BF16)


def final_kernel(probs_ref, back_ref, counts_ref, out_ref, rewards_ref, d_ref):
    devices, _, padded = back_ref.shape
    part = out_ref.shape[1] // devices
    requests = counts_ref.shape[1]
    sums = jnp.zeros((1, requests), F32)
    for d in range(devices):
        block = back_ref[d].astype(F32)
        d_ref[:, d * part : (d + 1) * part] = block[:, :part]
        for i in range(3):
            start = part + i * requests
            sums += block[:1, start : start + requests]
    rewards_ref[...] = sums / counts_ref[...]
    probs, d_probs = probs_ref[...], d_ref[...]
    mean = jnp.sum(probs * d_probs, axis=-1, keepdims=True)
    out_ref[...] = (math.sqrt(VOC) * (probs * (d_probs - mean))).astype(BF16)


def valid_column(counts_ref, total):
    requests = counts_ref.shape[0]
    length = total // requests
    position = lax.broadcasted_iota(jnp.int32, (total, 1), 0)
    valid = jnp.zeros((total, 1), F32)
    for r in range(requests):
        inside = (position >= r * length) & (position < r * length + counts_ref[r])
        valid = jnp.where(inside, 1.0, valid)
    return valid


def bring(source_ref, out_ref, sems, columns):
    fine = 128
    return [
        pltpu.make_async_copy(
            source_ref.at[pl.ds(i, fine), columns], out_ref.at[pl.ds(i, fine)], sems.at[i // fine]
        )
        for i in range(0, out_ref.shape[0], fine)
    ]


def ready_kernel(split, source_ref, after_ref, out_ref, sems):
    del after_ref
    width = out_ref.shape[1]
    columns = span((1 - this_core()) * width, width) if split else pl.ds(0, width)
    copies = bring(source_ref, out_ref, sems, columns)
    for copy in copies:
        copy.start()
    for copy in copies:
        copy.wait()


def first_rows(rows, source, after, split):
    width = source.shape[1] // 2 if split else source.shape[1]
    return call(
        functools.partial(ready_kernel, split), [pltpu.VMEM((rows, width), source.dtype)],
        source, after, streamed=(0,), scratch=(pltpu.SemaphoreType.DMA((rows // 128,)),),
    )[0]


def half_kernel(other, slices_ref, ready_ref, embed_ref, head_ref, out_ref, score_ref, *rest):
    next_ref, table, acc, sems, next_sems = rest if other else (None, *rest, None)
    chips, total, own = out_ref.shape
    part, ready = embed_ref.shape[0], ready_ref.shape[0]
    core = this_core()
    half = (1 - core) if other else core
    columns = span(half * chips * own, chips * own)
    tile, fine = 256, 128
    stream = Stream([
        pltpu.make_async_copy(
            embed_ref.at[pl.ds(i, min(fine, part - i)), columns],
            table.at[pl.ds(i - ready, min(fine, part - i))],
            sems.at[i // fine],
        )
        for i in range(ready, part, fine)
    ])
    following = []
    if other:
        following = bring(embed_ref, next_ref, next_sems, span(core * chips * own, chips * own))
        for copy in following:
            copy.start()
    acc[...] = jnp.dot(slices_ref[:, :ready], ready_ref[...], preferred_element_type=F32)
    for start in range(ready, part, tile):
        end = min(start + tile, part)
        stream.wait(-(-(end - ready) // fine))
        acc[...] += jnp.dot(
            slices_ref[:, start:end], table[start - ready : end - ready],
            preferred_element_type=F32,
        )
    score_ref[...] = jnp.sum(
        acc[...] * head_ref[:, columns].astype(F32), axis=-1, keepdims=True
    )
    for j in range(chips):
        out_ref[j] = acc[:, j * own : (j + 1) * own].astype(out_ref.dtype)
    for copy in following:
        copy.wait()


def early_kernel(
    head_ref, down_ref, embed_ref, gate_ref, up_ref, counts_ref, after_ref, greeting_ref,
    out_ref, valid_ref, counts_row, first, both, table, sems, first_sems, both_sems,
):
    del after_ref, greeting_ref
    width, lanes = down_ref.shape[1], 128
    core = this_core()

    def copy(j):
        rows = span(j * lanes, lanes)
        return pltpu.make_async_copy(down_ref.at[rows], table.at[rows], sems.at[j])

    steps = sems.shape[0]
    for j in range(steps):
        copy(j).start()
    half = width // 2
    own = both.shape[0] // 2
    chips = half // own
    others = bring(embed_ref, first, first_sems, span((1 - core) * half, half))
    others += bring_blocks(gate_ref, up_ref, both, core, range(2), own, chips, both_sems)
    for other in others:
        other.start()
    valid_ref[...] = valid_column(counts_ref, valid_ref.shape[0])
    lane = lax.broadcasted_iota(jnp.int32, counts_row.shape, 1)
    counts = jnp.ones(counts_row.shape, F32)
    for r in range(counts_row.shape[1]):
        counts = jnp.where(lane == r, counts_ref[r].astype(F32), counts)
    counts_row[...] = counts

    def step(j, _):
        copy(j).wait()
        rows = span(j * lanes, lanes)
        total = jnp.zeros((lanes, lanes), F32)
        for k in range(0, width, lanes):
            head = head_ref[:, k : k + lanes].astype(F32)
            total += table[rows, k : k + lanes].astype(F32) * head
        out_ref[:, rows] = jnp.sum(total.T, axis=0, keepdims=True)
        return 0

    lax.fori_loop(0, steps, step, 0)
    for other in others:
        other.wait()


def bring_blocks(gate_ref, up_ref, both, half, blocks, own, chips, sems):
    hidden = gate_ref.shape[1]
    return [
        pltpu.make_async_copy(
            source.at[span((half * chips + j) * own, own)],
            both.at[pl.ds((j - blocks[0]) * own, own), pl.ds(k * hidden, hidden)],
            sems.at[k, j - blocks[0]],
        )
        for j in blocks
        for k, source in enumerate((gate_ref, up_ref))
    ]


def weight_rows(ready, both, own):
    skip = ready.shape[0] // own

    def weights(j):
        if j < skip:
            return ready[j * own : (j + 1) * own]
        return both[(j - skip) * own : (j - skip + 1) * own]

    return skip, weights


def forward_half(x_ref, gain_ref, half, sums, weights, wait):
    chips, _, own = x_ref.shape
    products, squares = sums
    scaled = []
    wide = jnp.zeros(x_ref.shape[1:], F32)
    for j in range(chips):
        x = x_ref[j].astype(F32)
        wide = wide + x * x
        gain = gain_ref[:, span((half * chips + j) * own, own)].astype(F32)
        scaled.append((x * gain).astype(BF16))
    squares = squares + jnp.sum(wide, axis=-1, keepdims=True)
    for j in range(chips):
        wait(j)
        products = products + jnp.dot(scaled[j], weights(j), preferred_element_type=F32)
    return products, squares


def backward_half(d_both, weights, out_ref):
    contract = (((1,), (1,)), ((), ()))
    for j in range(out_ref.shape[0]):
        part = lax.dot_general(d_both, weights(j), contract, preferred_element_type=F32)
        out_ref[j] = part.astype(out_ref.dtype)


def first_kernel(
    x_ref, gain_ref, gate_ref, up_ref, ready_ref,
    products_ref, squares_ref, both, ahead, sems, ahead_sems,
):
    chips, _, own = x_ref.shape
    core = this_core()
    skip, weights = weight_rows(ready_ref, both, own)
    blocks = range(skip, chips)
    stream = Stream(bring_blocks(gate_ref, up_ref, both, core, blocks, own, chips, sems))
    blocks = range(ahead.shape[0] // own)
    following = bring_blocks(gate_ref, up_ref, ahead, 1 - core, blocks, own, chips, ahead_sems)
    for copy in following:
        copy.start()
    sums = (jnp.zeros(products_ref.shape, F32), jnp.zeros(squares_ref.shape, F32))
    products_ref[...], squares_ref[...] = forward_half(
        x_ref, gain_ref, core, sums, weights, lambda j: stream.wait(2 * (j - skip + 1))
    )
    for copy in following:
        copy.wait()


def second_kernel(
    x_ref, gain_ref, gate_ref, up_ref, ready_ref, products_ref, squares_ref, down_ref, valid_ref,
    send_ref, score_ref, inv_ref, d_both_ref, both, sems,
):
    chips, total, own = x_ref.shape
    width, hidden = gate_ref.shape
    half = 1 - this_core()
    skip, weights = weight_rows(ready_ref, both, own)
    blocks = range(skip, chips)
    stream = Stream(bring_blocks(gate_ref, up_ref, both, half, blocks, own, chips, sems))
    sums = (products_ref[...], squares_ref[...])
    products, squares = forward_half(
        x_ref, gain_ref, half, sums, weights, lambda j: stream.wait(2 * (j - skip + 1))
    )
    inv = lax.rsqrt(squares / width + 1e-05)
    inv_ref[...] = inv
    a, b = products[:, :hidden] * inv, products[:, hidden:] * inv
    sigma = jax.nn.sigmoid(a)
    active = a * sigma
    down = down_ref[...]
    rounded = (active * b).astype(BF16).astype(F32)
    score_ref[...] = jnp.sum(rounded * down, axis=-1, keepdims=True)
    d_hidden = valid_ref[...] * down
    d_both_ref[:, :hidden] = (d_hidden * b * sigma * (1.0 + a * (1.0 - sigma))).astype(BF16)
    d_both_ref[:, hidden:] = (d_hidden * active).astype(BF16)
    backward_half(d_both_ref[...], weights, send_ref)


def third_kernel(d_both_ref, ready_ref, both_ref, keep_ref):
    _, weights = weight_rows(ready_ref, both_ref, keep_ref.shape[2])
    backward_half(d_both_ref[...], weights, keep_ref)


def input_kernel(
    mine_ref, got_ref, d_mine_ref, d_got_ref, gain_ref, head_ref, inv_ref,
    score_a_ref, score_b_ref, score_c_ref, valid_ref, counts_ref, ready_ref, embed_ref,
    out_ref, dx_ref, table, sems,
):
    chips, total, own = mine_ref.shape
    voc = embed_ref.shape[0]
    requests = counts_ref.shape[1]
    width = 2 * chips * own
    core = this_core()
    ready = ready_ref.shape[0]
    tile, fine = 256, 64
    steps = (voc - ready) // tile
    last = ready + steps * tile

    def copy(start, size):
        return pltpu.make_async_copy(
            embed_ref.at[pl.ds(start, size)],
            table.at[pl.ds(start - ready, size)],
            sems.at[start // fine],
        )

    def pieces(start, end):
        return [copy(start + i, min(fine, end - start - i)) for i in range(0, end - start, fine)]

    def step_pieces(j):
        start = pl.multiple_of(ready + j * tile, fine)
        return [copy(pl.multiple_of(start + i, fine), fine) for i in range(0, tile, fine)]

    for piece in pieces(ready, voc):
        piece.start()
    sources = ((mine_ref, d_mine_ref, core), (got_ref, d_got_ref, 1 - core))
    wide = jnp.zeros((total, own), F32)
    for x_ref, d_ref, half in sources:
        for j in range(chips):
            gain = gain_ref[:, span((half * chips + j) * own, own)].astype(F32)
            wide += d_ref[j].astype(F32) * gain * x_ref[j].astype(F32)
    inv = inv_ref[...]
    weight = inv * inv * inv * (jnp.sum(wide, axis=-1, keepdims=True) / width)
    valid = valid_ref[...]
    request = lax.broadcasted_iota(jnp.int32, (total, requests), 0) // (total // requests)
    for x_ref, d_ref, half in sources:
        for j in range(chips):
            columns = span((half * chips + j) * own, own)
            x = x_ref[j].astype(F32)
            g = d_ref[j].astype(F32) * gain_ref[:, columns].astype(F32)
            dx = inv * g - x * weight
            dx_ref[:, columns] = (dx + valid * head_ref[:, columns].astype(F32)).astype(BF16)
    score = valid * (score_a_ref[...] + score_b_ref[...] + score_c_ref[...])
    member = request == lax.broadcasted_iota(jnp.int32, (total, requests), 1)
    value = jnp.sum(jnp.where(member, score, 0.0), axis=0, keepdims=True)
    parts = []
    for _ in range(3):
        piece = value.astype(BF16).astype(F32)
        parts.append(piece)
        value = value - piece
    for i, piece in enumerate(parts):
        start = voc + i * requests
        spread = jnp.broadcast_to(piece, (total, requests)).astype(BF16)
        out_ref[:, start : start + requests] = spread
    contract = (((1,), (1,)), ((), ()))

    def product(weights):
        return lax.dot_general(
            dx_ref[...], weights, contract, preferred_element_type=F32
        ).astype(BF16)

    out_ref[:, :ready] = product(ready_ref[...])

    def step(j, _):
        for piece in step_pieces(j):
            piece.wait()

        rows = pl.ds(pl.multiple_of(j * tile, tile), tile)
        out_ref[:, pl.ds(pl.multiple_of(ready + j * tile, tile), tile)] = product(table[rows, :])
        return 0

    lax.fori_loop(0, steps, step, 0)
    if last < voc:
        for piece in pieces(last, voc):
            piece.wait()
        out_ref[:, last:voc] = product(table[last - ready :, :])


def swap_sum(send, keep, devices):
    return (keep.astype(F32) + swap_cores(send, devices).astype(F32)).astype(BF16)


def chip_sum(half, devices):
    return jnp.sum(exchange_chips(half, devices).astype(F32), axis=0).astype(BF16)


def chip_gather(total, devices):
    return exchange_chips(jnp.broadcast_to(total[None], (devices // 2,) + total.shape), devices)


def pick(blocks, index):
    return lax.dynamic_index_in_dim(blocks, index, 0, keepdims=False)


def split_halves(part, devices):
    total, width = part.shape
    core = lax.axis_index("dp") % 2
    blocks = part.reshape(total, 2, devices // 2, width // devices).transpose(1, 2, 0, 3)
    return pick(blocks, 1 - core).astype(BF16), pick(blocks, core)


def join_halves(mine, got):
    core = lax.axis_index("dp") % 2
    blocks = jnp.where(core == 1, jnp.stack([got, mine]), jnp.stack([mine, got]))
    _, chips, total, own = blocks.shape
    return blocks.transpose(2, 0, 1, 3).reshape(total, 2 * chips * own).astype(F32)


def norm_scale(x0):
    return lax.rsqrt(jnp.mean(x0 * x0, axis=-1, keepdims=True) + 1e-05)


def plain_half(slices, embed, head_row, devices):
    part = jnp.dot(slices, embed, preferred_element_type=F32)
    score = jnp.sum(part * head_row.astype(F32), axis=-1, keepdims=True)
    return *split_halves(part, devices), score


def plain_hidden(mine, got, gain_row, w_gate, w_up, down, valid, devices):
    x0 = join_halves(mine, got)
    normed = (x0 * norm_scale(x0) * gain_row.astype(F32)).astype(BF16)
    a = jnp.dot(normed, w_gate, preferred_element_type=F32)
    b = jnp.dot(normed, w_up, preferred_element_type=F32)
    sigma = jax.nn.sigmoid(a)
    active = a * sigma
    hidden = (active * b).astype(BF16).astype(F32)
    d_hidden = valid * down
    d_gate = (d_hidden * b * sigma * (1.0 + a * (1.0 - sigma))).astype(BF16)
    d_up = (d_hidden * active).astype(BF16)
    part = jnp.einsum("tf,df->td", d_gate, w_gate, preferred_element_type=F32)
    part = part + jnp.einsum("tf,df->td", d_up, w_up, preferred_element_type=F32)
    return *split_halves(part, devices), jnp.sum(hidden * down, axis=-1, keepdims=True)


def plain_input(mine, got, d_mine, d_got, gain_row, head_row, valid, embed):
    x0 = join_halves(mine, got)
    inv = norm_scale(x0)
    scaled = join_halves(d_mine, d_got) * gain_row.astype(F32)
    dx = inv * scaled - x0 * inv * inv * inv * jnp.mean(scaled * x0, axis=-1, keepdims=True)
    dx = (dx + valid * head_row.astype(F32)).astype(BF16)
    return jnp.einsum("td,vd->tv", dx, embed, preferred_element_type=F32).astype(BF16)


def body(logits, embed, norm_gain, w_gate, w_up, w_down, head, counts):
    devices = lax.axis_size("dp")
    rows, voc = logits.shape
    part = voc // devices
    width = embed.shape[1]
    hidden = w_gate.shape[1]
    own, chips = width // devices, devices // 2
    requests = counts.shape[0]
    total = rows * devices
    request_len = total // requests
    tiled = own % 128 == 0 and hidden % 128 == 0 and total % 16 == 0 and part % 16 == 0 and part > 512
    head_row, gain_row = head.reshape(1, width), norm_gain.reshape(1, width)
    if tiled:
        around = [(i, (i + devices // 4) % devices) for i in range(devices)]
        greeting = lax.ppermute(counts, "dp", around)
        blocked, probs = call(
            softmax_kernel,
            [struct((devices, rows, part), BF16), pltpu.VMEM((rows, voc), F32)], logits,
        )
    else:
        probs32 = jax.nn.softmax(logits.astype(F32), axis=-1)
        blocked = probs32.astype(BF16).reshape(rows, devices, part).transpose(1, 0, 2)
    if tiled:
        blocked, greeting = lax.optimization_barrier((blocked, greeting))
    slices = exchange(blocked).reshape(total, part)
    column = struct((total, 1), F32)
    half = (chips, total, own)
    flops = total * part * width
    if tiled:
        ready = 256
        down_row, valid, counts_row, first, both_first = call(
            early_kernel,
            [
                struct((1, hidden), F32), column, struct((1, requests), F32), pltpu.VMEM((ready, width // 2), BF16),
                pltpu.VMEM((2 * own, 2 * hidden), BF16),
            ],
            head_row, w_down, embed, w_gate, w_up, counts, blocked, greeting,
            streamed=(1, 2, 3, 4), scalars=(5,), flops=2 * hidden * width, room=2 * hidden * width,
            scratch=(
                pltpu.VMEM((hidden, width), BF16), pltpu.SemaphoreType.DMA((hidden // 128,)),
                pltpu.SemaphoreType.DMA((ready // 128,)), pltpu.SemaphoreType.DMA((2, 2)),
            ),
        )
        table = (
            pltpu.VMEM((part - ready, width // 2), BF16), pltpu.VMEM((total, width // 2), F32),
            pltpu.SemaphoreType.DMA((-(-part // 128),)),
        )
        args = dict(streamed=(2,), kept=(1,), flops=flops, room=part * width)
        send, score_a, first = call(
            functools.partial(half_kernel, True),
            [struct(half, BF16), column, pltpu.VMEM((ready, width // 2), BF16)],
            slices, first, embed, head_row,
            scratch=(*table, pltpu.SemaphoreType.DMA((ready // 128,))), **args,
        )
        keep, score_b = call(
            functools.partial(half_kernel, False), [struct(half, F32), column],
            slices, first, embed, head_row, scratch=table, **args,
        )
    else:
        send, keep, score_a = plain_half(slices, embed, head_row, devices)
    summed = swap_sum(send, keep, devices)
    x_mine = chip_gather(chip_sum(summed, devices), devices)
    x_got = swap_cores(x_mine, devices)
    if tiled:
        weight = (width // 2 - 2 * own, 2 * hidden)
        sems, ahead_sems = pltpu.SemaphoreType.DMA((2, chips)), pltpu.SemaphoreType.DMA((2, 2))
        args = dict(
            streamed=(2, 3), kept=(4,), flops=2 * total * hidden * width, room=2 * width * hidden
        )
        products, squares, both, ahead = call(
            first_kernel,
            [
                struct((total, 2 * hidden), F32), column, pltpu.VMEM(weight, BF16),
                pltpu.VMEM(both_first.shape, BF16),
            ],
            x_mine, gain_row, w_gate, w_up, both_first, scratch=(sems, ahead_sems), **args,
        )
        send, score_c, inv, d_both = call(
            second_kernel,
            [struct(half, BF16), column, column, struct((total, 2 * hidden), BF16)],
            x_got, gain_row, w_gate, w_up, ahead, products, squares, down_row, valid,
            scratch=(pltpu.VMEM(weight, BF16), sems), **args,
        )
        (keep,) = call(
            third_kernel, [struct(half, F32)], d_both, both_first, both,
            kept=(1, 2), flops=2 * total * hidden * width,
        )
    else:
        down_row = jnp.sum(w_down.astype(F32) * head.astype(F32)[None, :], axis=-1)[None]
        position = jnp.arange(total, dtype=jnp.int32)[:, None]
        member = position // request_len == jnp.arange(requests, dtype=jnp.int32)[None, :]
        limit = jnp.sum(jnp.where(member, counts[None, :], 0), axis=-1, keepdims=True)
        valid = (position % request_len < limit).astype(F32)
        send, keep, score_c = plain_hidden(
            x_mine, x_got, gain_row, w_gate, w_up, down_row, valid, devices
        )
    total_d = chip_sum(swap_sum(send, keep, devices), devices)
    d_mine = chip_gather(total_d, devices)
    d_got = swap_cores(d_mine, devices)
    padded = part + 3 * requests
    if tiled:
        first = first_rows(256, embed, total_d, False)
        (d_slices,) = call(
            input_kernel, [struct((total, padded), BF16)],
            x_mine, x_got, d_mine, d_got, gain_row, head_row, inv,
            score_a, score_b, score_c, valid, counts_row, first, embed,
            kept=(12,), streamed=(13,), flops=2 * flops, room=2 * part * width,
            scratch=(
                pltpu.VMEM((total, width), BF16), pltpu.VMEM((part - 256, width), BF16),
                pltpu.SemaphoreType.DMA((-(-part // 64),)),
            ),
        )
    else:
        d_slices = plain_input(x_mine, x_got, d_mine, d_got, gain_row, head_row, valid, embed)
        score = jnp.where(member, valid * (score_a + score_c), 0.0)
        extra = split3(jnp.sum(score, axis=0)).reshape(1, requests * 3)
        extra = jnp.broadcast_to(extra, (total, requests * 3))
        d_slices = jnp.concatenate([d_slices, extra], axis=-1)
    back = exchange(d_slices.reshape(devices, rows, padded))
    if tiled:
        guidance, rewards = call(
            final_kernel, [struct((rows, voc), BF16), struct((1, requests), F32)],
            probs, back, counts_row, kept=(0,),
            scratch=(pltpu.VMEM((rows, voc), F32),),
        )
        return (guidance, rewards.reshape(requests))
    sums = jnp.sum(back[:, 0, part:].astype(F32).reshape(devices, requests, 3), axis=(0, 2))
    rewards = sums / counts.astype(F32)
    d_probs = back[:, :, :part].transpose(1, 0, 2).reshape(rows, voc).astype(F32)
    d_logits = probs32 * (d_probs - jnp.sum(probs32 * d_probs, axis=-1, keepdims=True))
    guidance = (math.sqrt(VOC) * d_logits).astype(BF16)
    return (guidance, rewards)


def solution(mesh):
    placed = (
        P(("groups", "dp"), None),
        P("dp", None),
        P(),
        P(None, "dp"),
        P(None, "dp"),
        P("dp", None),
        P(),
        P("groups"),
    )
    return jax.shard_map(
        body,
        mesh=mesh,
        in_specs=placed,
        out_specs=(P(("groups", "dp"), None), P("groups")),
        check_vma=False,
    )
```

```python
import functools
import math

import jax
import jax.numpy as jnp
from jax import lax
from jax.experimental import pallas as pl
from jax.experimental.pallas import tpu as pltpu
from jax.sharding import PartitionSpec as P

VOC = 32000
F32, BF16 = jnp.float32, jnp.bfloat16
VMEM_BYTES = 12 * 1024 * 1024


def swap_cores(value, devices):
    return lax.ppermute(value, "dp", [(i, i ^ 1) for i in range(devices)])


def exchange(blocks):
    return lax.all_to_all(blocks, "dp", split_axis=0, concat_axis=0, tiled=True)


def exchange_chips(blocks, devices):
    groups = [list(range(core, devices, 2)) for core in range(2)]
    return lax.all_to_all(
        blocks, "dp", split_axis=0, concat_axis=0, axis_index_groups=groups, tiled=True
    )


def split3(value):
    hi = lax.reduce_precision(value, 8, 7)
    rest = value - hi
    mid = lax.reduce_precision(rest, 8, 7)
    low = rest - mid
    return jnp.stack([hi, mid, low], axis=-1).astype(BF16)


HBM_SPEC = pl.BlockSpec(memory_space=pltpu.HBM)
VMEM_SPEC = pl.BlockSpec(memory_space=pltpu.VMEM)
SMEM_SPEC = pl.BlockSpec(memory_space=pltpu.SMEM)


WINDOW = 128


def call(kernel, outs, *args, streamed=(), kept=(), scalars=(), flops=0, scratch=(), room=0):
    size = sum(math.prod(a.shape) * a.dtype.itemsize for a in args)
    places = {i: pltpu.HBM for i in streamed} | {i: pltpu.VMEM for i in kept}
    specs = [
        HBM_SPEC if i in streamed else SMEM_SPEC if i in scalars else VMEM_SPEC
        for i in range(len(args))
    ]
    return pl.pallas_call(
        kernel,
        out_shape=outs,
        in_specs=specs,
        out_specs=[VMEM_SPEC] * len(outs),
        scratch_shapes=list(scratch),
        compiler_params=pltpu.CompilerParams(vmem_limit_bytes=VMEM_BYTES + room),
        cost_estimate=pl.CostEstimate(flops=flops, bytes_accessed=size, transcendentals=0),
    )(*[
        pltpu.with_memory_space_constraint(a, places[i]) if i in places else a
        for i, a in enumerate(args)
    ])


class Stream:
    def __init__(self, copies):
        self.copies = copies
        self.done = 0
        for copy in copies[:WINDOW]:
            copy.start()

    def wait(self, count):
        while self.done < count:
            self.copies[self.done].wait()
            self.done += 1
            if self.done + WINDOW <= len(self.copies):
                self.copies[self.done + WINDOW - 1].start()


def struct(shape, dtype):
    return jax.ShapeDtypeStruct(shape, dtype)


def this_core():
    return lax.axis_index("dp") % 2


def span(start, size):
    return pl.ds(pl.multiple_of(start, size), size)


def softmax_kernel(logits_ref, out_ref, probs_ref):
    devices, _, part = out_ref.shape
    x = logits_ref[...].astype(F32)
    e = jnp.exp(x - jnp.max(x, axis=-1, keepdims=True))
    probs = e * (1.0 / jnp.sum(e, axis=-1, keepdims=True))
    probs_ref[...] = probs
    for d in range(devices):
        out_ref[d] = probs[:, d * part : (d + 1) * part].astype(BF16)


def final_kernel(probs_ref, back_ref, counts_ref, out_ref, rewards_ref, d_ref):
    devices, _, padded = back_ref.shape
    part = out_ref.shape[1] // devices
    requests = counts_ref.shape[1]
    sums = jnp.zeros((1, requests), F32)
    for d in range(devices):
        block = back_ref[d].astype(F32)
        d_ref[:, d * part : (d + 1) * part] = block[:, :part]
        for i in range(3):
            start = part + i * requests
            sums += block[:1, start : start + requests]
    rewards_ref[...] = sums / counts_ref[...]
    probs, d_probs = probs_ref[...], d_ref[...]
    mean = jnp.sum(probs * d_probs, axis=-1, keepdims=True)
    out_ref[...] = (math.sqrt(VOC) * (probs * (d_probs - mean))).astype(BF16)


def valid_column(counts, total):
    requests = counts.shape[1]
    length = total // requests
    position = lax.broadcasted_iota(jnp.int32, (total, requests), 0)
    start = length * lax.broadcasted_iota(jnp.int32, (total, requests), 1)
    inside = (position >= start) & (position < start + counts)
    return jnp.sum(jnp.where(inside, 1.0, 0.0), axis=-1, keepdims=True)


def bring(source_ref, out_ref, sems, columns):
    fine = 128
    return [
        pltpu.make_async_copy(
            source_ref.at[pl.ds(i, fine), columns], out_ref.at[pl.ds(i, fine)], sems.at[i // fine]
        )
        for i in range(0, out_ref.shape[0], fine)
    ]


def ready_kernel(split, source_ref, after_ref, out_ref, sems):
    del after_ref
    width = out_ref.shape[1]
    columns = span((1 - this_core()) * width, width) if split else pl.ds(0, width)
    copies = bring(source_ref, out_ref, sems, columns)
    for copy in copies:
        copy.start()
    for copy in copies:
        copy.wait()


def first_rows(rows, source, after, split):
    width = source.shape[1] // 2 if split else source.shape[1]
    return call(
        functools.partial(ready_kernel, split), [pltpu.VMEM((rows, width), source.dtype)],
        source, after, streamed=(0,), scratch=(pltpu.SemaphoreType.DMA((rows // 128,)),),
    )[0]


def half_kernel(other, slices_ref, ready_ref, embed_ref, head_ref, out_ref, score_ref, *rest):
    next_ref, table, acc, sems, next_sems = rest if other else (None, *rest, None)
    chips, total, own = out_ref.shape
    part, ready = embed_ref.shape[0], ready_ref.shape[0]
    core = this_core()
    half = (1 - core) if other else core
    columns = span(half * chips * own, chips * own)
    tile, fine = 256, 128
    stream = Stream([
        pltpu.make_async_copy(
            embed_ref.at[pl.ds(i, min(fine, part - i)), columns],
            table.at[pl.ds(i - ready, min(fine, part - i))],
            sems.at[i // fine],
        )
        for i in range(ready, part, fine)
    ])
    following = []
    if other:
        following = bring(embed_ref, next_ref, next_sems, span(core * chips * own, chips * own))
        for copy in following:
            copy.start()
    acc[...] = jnp.dot(slices_ref[:, :ready], ready_ref[...], preferred_element_type=F32)
    for start in range(ready, part, tile):
        end = min(start + tile, part)
        stream.wait(-(-(end - ready) // fine))
        acc[...] += jnp.dot(
            slices_ref[:, start:end], table[start - ready : end - ready],
            preferred_element_type=F32,
        )
    score_ref[...] = jnp.sum(
        acc[...] * head_ref[:, columns].astype(F32), axis=-1, keepdims=True
    )
    for j in range(chips):
        out_ref[j] = acc[:, j * own : (j + 1) * own].astype(out_ref.dtype)
    for copy in following:
        copy.wait()


def early_kernel(
    head_ref, down_ref, embed_ref, gate_ref, up_ref, after_ref,
    out_ref, first, both, table, sems, first_sems, both_sems,
):
    del after_ref
    width, lanes = down_ref.shape[1], 128
    core = this_core()

    def copy(j):
        rows = span(j * lanes, lanes)
        return pltpu.make_async_copy(down_ref.at[rows], table.at[rows], sems.at[j])

    steps = sems.shape[0]
    for j in range(steps):
        copy(j).start()
    half = width // 2
    own = both.shape[0] // 2
    chips = half // own
    others = bring(embed_ref, first, first_sems, span((1 - core) * half, half))
    others += bring_blocks(gate_ref, up_ref, both, core, range(2), own, chips, both_sems)
    for other in others:
        other.start()
    head = head_ref[...].astype(F32).reshape(1, width)

    def step(j, _):
        copy(j).wait()
        rows = span(j * lanes, lanes)
        total = jnp.zeros((lanes, lanes), F32)
        for k in range(0, width, lanes):
            total += table[rows, k : k + lanes].astype(F32) * head[:, k : k + lanes]
        out_ref[:, rows] = jnp.sum(total.T, axis=0, keepdims=True)
        return 0

    lax.fori_loop(0, steps, step, 0)
    for other in others:
        other.wait()


def bring_blocks(gate_ref, up_ref, both, half, blocks, own, chips, sems):
    hidden = gate_ref.shape[1]
    return [
        pltpu.make_async_copy(
            source.at[span((half * chips + j) * own, own)],
            both.at[pl.ds((j - blocks[0]) * own, own), pl.ds(k * hidden, hidden)],
            sems.at[k, j - blocks[0]],
        )
        for j in blocks
        for k, source in enumerate((gate_ref, up_ref))
    ]


def weight_rows(ready, both, own):
    skip = ready.shape[0] // own

    def weights(j):
        if j < skip:
            return ready[j * own : (j + 1) * own]
        return both[(j - skip) * own : (j - skip + 1) * own]

    return skip, weights


def forward_half(x_ref, gain_ref, half, sums, weights, wait):
    chips, _, own = x_ref.shape
    products, squares = sums
    scaled = []
    wide = jnp.zeros(x_ref.shape[1:], F32)
    for j in range(chips):
        x = x_ref[j].astype(F32)
        wide = wide + x * x
        gain = gain_ref[:, span((half * chips + j) * own, own)].astype(F32)
        scaled.append((x * gain).astype(BF16))
    squares = squares + jnp.sum(wide, axis=-1, keepdims=True)
    for j in range(chips):
        wait(j)
        products = products + jnp.dot(scaled[j], weights(j), preferred_element_type=F32)
    return products, squares


def backward_half(d_both, weights, out_ref):
    contract = (((1,), (1,)), ((), ()))
    for j in range(out_ref.shape[0]):
        part = lax.dot_general(d_both, weights(j), contract, preferred_element_type=F32)
        out_ref[j] = part.astype(out_ref.dtype)


def first_kernel(
    x_ref, gain_ref, gate_ref, up_ref, ready_ref, counts_ref,
    products_ref, squares_ref, valid_ref, counts_row, both, ahead, sems, ahead_sems,
):
    chips, _, own = x_ref.shape
    core = this_core()
    skip, weights = weight_rows(ready_ref, both, own)
    blocks = range(skip, chips)
    stream = Stream(bring_blocks(gate_ref, up_ref, both, core, blocks, own, chips, sems))
    blocks = range(ahead.shape[0] // own)
    following = bring_blocks(gate_ref, up_ref, ahead, 1 - core, blocks, own, chips, ahead_sems)
    for copy in following:
        copy.start()
    counts = counts_ref[...]
    valid_ref[...] = valid_column(counts, valid_ref.shape[0])
    counts_row[...] = counts.astype(F32)
    sums = (jnp.zeros(products_ref.shape, F32), jnp.zeros(squares_ref.shape, F32))
    products_ref[...], squares_ref[...] = forward_half(
        x_ref, gain_ref, core, sums, weights, lambda j: stream.wait(2 * (j - skip + 1))
    )
    for copy in following:
        copy.wait()


def second_kernel(
    x_ref, gain_ref, gate_ref, up_ref, ready_ref, products_ref, squares_ref, down_ref, valid_ref,
    send_ref, score_ref, inv_ref, d_both_ref, both, sems,
):
    chips, total, own = x_ref.shape
    width, hidden = gate_ref.shape
    half = 1 - this_core()
    skip, weights = weight_rows(ready_ref, both, own)
    blocks = range(skip, chips)
    stream = Stream(bring_blocks(gate_ref, up_ref, both, half, blocks, own, chips, sems))
    sums = (products_ref[...], squares_ref[...])
    products, squares = forward_half(
        x_ref, gain_ref, half, sums, weights, lambda j: stream.wait(2 * (j - skip + 1))
    )
    inv = lax.rsqrt(squares / width + 1e-05)
    inv_ref[...] = inv
    a, b = products[:, :hidden] * inv, products[:, hidden:] * inv
    sigma = jax.nn.sigmoid(a)
    active = a * sigma
    down = down_ref[...]
    rounded = (active * b).astype(BF16).astype(F32)
    score_ref[...] = jnp.sum(rounded * down, axis=-1, keepdims=True)
    d_hidden = valid_ref[...] * down
    d_both_ref[:, :hidden] = (d_hidden * b * sigma * (1.0 + a * (1.0 - sigma))).astype(BF16)
    d_both_ref[:, hidden:] = (d_hidden * active).astype(BF16)
    backward_half(d_both_ref[...], weights, send_ref)


def third_kernel(d_both_ref, ready_ref, both_ref, keep_ref):
    _, weights = weight_rows(ready_ref, both_ref, keep_ref.shape[2])
    backward_half(d_both_ref[...], weights, keep_ref)


def input_kernel(
    mine_ref, got_ref, d_mine_ref, d_got_ref, gain_ref, head_ref, inv_ref,
    score_a_ref, score_b_ref, score_c_ref, valid_ref, counts_ref, ready_ref, embed_ref,
    out_ref, dx_ref, table, sems,
):
    chips, total, own = mine_ref.shape
    voc = embed_ref.shape[0]
    requests = counts_ref.shape[1]
    width = 2 * chips * own
    core = this_core()
    ready = ready_ref.shape[0]
    tile, fine = 256, 64
    steps = (voc - ready) // tile
    last = ready + steps * tile

    def copy(start, size):
        return pltpu.make_async_copy(
            embed_ref.at[pl.ds(start, size)],
            table.at[pl.ds(start - ready, size)],
            sems.at[start // fine],
        )

    def pieces(start, end):
        return [copy(start + i, min(fine, end - start - i)) for i in range(0, end - start, fine)]

    def step_pieces(j):
        start = pl.multiple_of(ready + j * tile, fine)
        return [copy(pl.multiple_of(start + i, fine), fine) for i in range(0, tile, fine)]

    for piece in pieces(ready, voc):
        piece.start()
    sources = ((mine_ref, d_mine_ref, core), (got_ref, d_got_ref, 1 - core))
    wide = jnp.zeros((total, own), F32)
    for x_ref, d_ref, half in sources:
        for j in range(chips):
            gain = gain_ref[:, span((half * chips + j) * own, own)].astype(F32)
            wide += d_ref[j].astype(F32) * gain * x_ref[j].astype(F32)
    inv = inv_ref[...]
    weight = inv * inv * inv * (jnp.sum(wide, axis=-1, keepdims=True) / width)
    valid = valid_ref[...]
    request = lax.broadcasted_iota(jnp.int32, (total, requests), 0) // (total // requests)
    for x_ref, d_ref, half in sources:
        for j in range(chips):
            columns = span((half * chips + j) * own, own)
            x = x_ref[j].astype(F32)
            g = d_ref[j].astype(F32) * gain_ref[:, columns].astype(F32)
            dx = inv * g - x * weight
            dx_ref[:, columns] = (dx + valid * head_ref[:, columns].astype(F32)).astype(BF16)
    score = valid * (score_a_ref[...] + score_b_ref[...] + score_c_ref[...])
    member = request == lax.broadcasted_iota(jnp.int32, (total, requests), 1)
    value = jnp.sum(jnp.where(member, score, 0.0), axis=0, keepdims=True)
    parts = []
    for _ in range(3):
        piece = value.astype(BF16).astype(F32)
        parts.append(piece)
        value = value - piece
    for i, piece in enumerate(parts):
        start = voc + i * requests
        spread = jnp.broadcast_to(piece, (total, requests)).astype(BF16)
        out_ref[:, start : start + requests] = spread
    contract = (((1,), (1,)), ((), ()))

    def product(weights):
        return lax.dot_general(
            dx_ref[...], weights, contract, preferred_element_type=F32
        ).astype(BF16)

    out_ref[:, :ready] = product(ready_ref[...])

    def step(j, _):
        for piece in step_pieces(j):
            piece.wait()

        rows = pl.ds(pl.multiple_of(j * tile, tile), tile)
        out_ref[:, pl.ds(pl.multiple_of(ready + j * tile, tile), tile)] = product(table[rows, :])
        return 0

    lax.fori_loop(0, steps, step, 0)
    if last < voc:
        for piece in pieces(last, voc):
            piece.wait()
        out_ref[:, last:voc] = product(table[last - ready :, :])


def swap_sum(send, keep, devices):
    return (keep.astype(F32) + swap_cores(send, devices).astype(F32)).astype(BF16)


def chip_sum(half, devices):
    return jnp.sum(exchange_chips(half, devices).astype(F32), axis=0).astype(BF16)


def chip_gather(total, devices):
    return exchange_chips(jnp.broadcast_to(total[None], (devices // 2,) + total.shape), devices)


def pick(blocks, index):
    return lax.dynamic_index_in_dim(blocks, index, 0, keepdims=False)


def split_halves(part, devices):
    total, width = part.shape
    core = lax.axis_index("dp") % 2
    blocks = part.reshape(total, 2, devices // 2, width // devices).transpose(1, 2, 0, 3)
    return pick(blocks, 1 - core).astype(BF16), pick(blocks, core)


def join_halves(mine, got):
    core = lax.axis_index("dp") % 2
    blocks = jnp.where(core == 1, jnp.stack([got, mine]), jnp.stack([mine, got]))
    _, chips, total, own = blocks.shape
    return blocks.transpose(2, 0, 1, 3).reshape(total, 2 * chips * own).astype(F32)


def norm_scale(x0):
    return lax.rsqrt(jnp.mean(x0 * x0, axis=-1, keepdims=True) + 1e-05)


def plain_half(slices, embed, head_row, devices):
    part = jnp.dot(slices, embed, preferred_element_type=F32)
    score = jnp.sum(part * head_row.astype(F32), axis=-1, keepdims=True)
    return *split_halves(part, devices), score


def plain_hidden(mine, got, gain_row, w_gate, w_up, down, valid, devices):
    x0 = join_halves(mine, got)
    normed = (x0 * norm_scale(x0) * gain_row.astype(F32)).astype(BF16)
    a = jnp.dot(normed, w_gate, preferred_element_type=F32)
    b = jnp.dot(normed, w_up, preferred_element_type=F32)
    sigma = jax.nn.sigmoid(a)
    active = a * sigma
    hidden = (active * b).astype(BF16).astype(F32)
    d_hidden = valid * down
    d_gate = (d_hidden * b * sigma * (1.0 + a * (1.0 - sigma))).astype(BF16)
    d_up = (d_hidden * active).astype(BF16)
    part = jnp.einsum("tf,df->td", d_gate, w_gate, preferred_element_type=F32)
    part = part + jnp.einsum("tf,df->td", d_up, w_up, preferred_element_type=F32)
    return *split_halves(part, devices), jnp.sum(hidden * down, axis=-1, keepdims=True)


def plain_input(mine, got, d_mine, d_got, gain_row, head_row, valid, embed):
    x0 = join_halves(mine, got)
    inv = norm_scale(x0)
    scaled = join_halves(d_mine, d_got) * gain_row.astype(F32)
    dx = inv * scaled - x0 * inv * inv * inv * jnp.mean(scaled * x0, axis=-1, keepdims=True)
    dx = (dx + valid * head_row.astype(F32)).astype(BF16)
    return jnp.einsum("td,vd->tv", dx, embed, preferred_element_type=F32).astype(BF16)


def body(logits, embed, norm_gain, w_gate, w_up, w_down, head, counts):
    devices = lax.axis_size("dp")
    rows, voc = logits.shape
    part = voc // devices
    width = embed.shape[1]
    hidden = w_gate.shape[1]
    own, chips = width // devices, devices // 2
    requests = counts.shape[0]
    total = rows * devices
    request_len = total // requests
    tiled = own % 128 == 0 and hidden % 128 == 0 and total % 16 == 0 and part % 16 == 0 and part > 512
    head_row, gain_row = head.reshape(1, width), norm_gain.reshape(1, width)
    if tiled:
        blocked, probs = call(
            softmax_kernel,
            [struct((devices, rows, part), BF16), pltpu.VMEM((rows, voc), F32)], logits,
        )
    else:
        probs32 = jax.nn.softmax(logits.astype(F32), axis=-1)
        blocked = probs32.astype(BF16).reshape(rows, devices, part).transpose(1, 0, 2)
    slices = exchange(blocked).reshape(total, part)
    column = struct((total, 1), F32)
    half = (chips, total, own)
    flops = total * part * width
    if tiled:
        ready = 256
        down_row, first, both_first = call(
            early_kernel,
            [
                struct((1, hidden), F32), pltpu.VMEM((ready, width // 2), BF16),
                pltpu.VMEM((2 * own, 2 * hidden), BF16),
            ],
            head, w_down, embed, w_gate, w_up, blocked,
            streamed=(1, 2, 3, 4), flops=2 * hidden * width, room=2 * hidden * width,
            scratch=(
                pltpu.VMEM((hidden, width), BF16), pltpu.SemaphoreType.DMA((hidden // 128,)),
                pltpu.SemaphoreType.DMA((ready // 128,)), pltpu.SemaphoreType.DMA((2, 2)),
            ),
        )
        table = (
            pltpu.VMEM((part - ready, width // 2), BF16), pltpu.VMEM((total, width // 2), F32),
            pltpu.SemaphoreType.DMA((-(-part // 128),)),
        )
        args = dict(streamed=(2,), kept=(1,), flops=flops, room=part * width)
        send, score_a, first = call(
            functools.partial(half_kernel, True),
            [struct(half, BF16), column, pltpu.VMEM((ready, width // 2), BF16)],
            slices, first, embed, head_row,
            scratch=(*table, pltpu.SemaphoreType.DMA((ready // 128,))), **args,
        )
        keep, score_b = call(
            functools.partial(half_kernel, False), [struct(half, F32), column],
            slices, first, embed, head_row, scratch=table, **args,
        )
    else:
        send, keep, score_a = plain_half(slices, embed, head_row, devices)
    summed = swap_sum(send, keep, devices)
    x_mine = chip_gather(chip_sum(summed, devices), devices)
    x_got = swap_cores(x_mine, devices)
    if tiled:
        weight = (width // 2 - 2 * own, 2 * hidden)
        sems, ahead_sems = pltpu.SemaphoreType.DMA((2, chips)), pltpu.SemaphoreType.DMA((2, 2))
        args = dict(
            streamed=(2, 3), kept=(4,), flops=2 * total * hidden * width, room=2 * width * hidden
        )
        products, squares, valid, counts_row, both, ahead = call(
            first_kernel,
            [
                struct((total, 2 * hidden), F32), column, column, struct((1, requests), F32),
                pltpu.VMEM(weight, BF16), pltpu.VMEM(both_first.shape, BF16),
            ],
            x_mine, gain_row, w_gate, w_up, both_first, counts.reshape(1, requests),
            scratch=(sems, ahead_sems), **args,
        )
        send, score_c, inv, d_both = call(
            second_kernel,
            [struct(half, BF16), column, column, struct((total, 2 * hidden), BF16)],
            x_got, gain_row, w_gate, w_up, ahead, products, squares, down_row, valid,
            scratch=(pltpu.VMEM(weight, BF16), sems), **args,
        )
        (keep,) = call(
            third_kernel, [struct(half, F32)], d_both, both_first, both,
            kept=(1, 2), flops=2 * total * hidden * width,
        )
    else:
        down_row = jnp.sum(w_down.astype(F32) * head.astype(F32)[None, :], axis=-1)[None]
        position = jnp.arange(total, dtype=jnp.int32)[:, None]
        member = position // request_len == jnp.arange(requests, dtype=jnp.int32)[None, :]
        limit = jnp.sum(jnp.where(member, counts[None, :], 0), axis=-1, keepdims=True)
        valid = (position % request_len < limit).astype(F32)
        send, keep, score_c = plain_hidden(
            x_mine, x_got, gain_row, w_gate, w_up, down_row, valid, devices
        )
    total_d = chip_sum(swap_sum(send, keep, devices), devices)
    d_mine = chip_gather(total_d, devices)
    d_got = swap_cores(d_mine, devices)
    padded = part + 3 * requests
    if tiled:
        first = first_rows(256, embed, total_d, False)
        (d_slices,) = call(
            input_kernel, [struct((total, padded), BF16)],
            x_mine, x_got, d_mine, d_got, gain_row, head_row, inv,
            score_a, score_b, score_c, valid, counts_row, first, embed,
            kept=(12,), streamed=(13,), flops=2 * flops, room=2 * part * width,
            scratch=(
                pltpu.VMEM((total, width), BF16), pltpu.VMEM((part - 256, width), BF16),
                pltpu.SemaphoreType.DMA((-(-part // 64),)),
            ),
        )
    else:
        d_slices = plain_input(x_mine, x_got, d_mine, d_got, gain_row, head_row, valid, embed)
        score = jnp.where(member, valid * (score_a + score_c), 0.0)
        extra = split3(jnp.sum(score, axis=0)).reshape(1, requests * 3)
        extra = jnp.broadcast_to(extra, (total, requests * 3))
        d_slices = jnp.concatenate([d_slices, extra], axis=-1)
    back = exchange(d_slices.reshape(devices, rows, padded))
    if tiled:
        guidance, rewards = call(
            final_kernel, [struct((rows, voc), BF16), struct((1, requests), F32)],
            probs, back, counts_row, kept=(0,),
            scratch=(pltpu.VMEM((rows, voc), F32),),
        )
        return (guidance, rewards.reshape(requests))
    sums = jnp.sum(back[:, 0, part:].astype(F32).reshape(devices, requests, 3), axis=(0, 2))
    rewards = sums / counts.astype(F32)
    d_probs = back[:, :, :part].transpose(1, 0, 2).reshape(rows, voc).astype(F32)
    d_logits = probs32 * (d_probs - jnp.sum(probs32 * d_probs, axis=-1, keepdims=True))
    guidance = (math.sqrt(VOC) * d_logits).astype(BF16)
    return (guidance, rewards)


def solution(mesh):
    placed = (
        P(("groups", "dp"), None),
        P("dp", None),
        P(),
        P(None, "dp"),
        P(None, "dp"),
        P("dp", None),
        P(),
        P("groups"),
    )
    return jax.shard_map(
        body,
        mesh=mesh,
        in_specs=placed,
        out_specs=(P(("groups", "dp"), None), P("groups")),
        check_vma=False,
    )
```

```python
import functools
import math

import jax
import jax.numpy as jnp
from jax import lax
from jax.experimental import pallas as pl
from jax.experimental.pallas import tpu as pltpu
from jax.sharding import PartitionSpec as P

VOC = 32000
F32, BF16 = jnp.float32, jnp.bfloat16
VMEM_BYTES = 12 * 1024 * 1024


def swap_cores(value, devices):
    return lax.ppermute(value, "dp", [(i, i ^ 1) for i in range(devices)])


def exchange(blocks):
    return lax.all_to_all(blocks, "dp", split_axis=0, concat_axis=0, tiled=True)


def exchange_chips(blocks, devices):
    groups = [list(range(core, devices, 2)) for core in range(2)]
    return lax.all_to_all(
        blocks, "dp", split_axis=0, concat_axis=0, axis_index_groups=groups, tiled=True
    )


def split3(value):
    hi = lax.reduce_precision(value, 8, 7)
    rest = value - hi
    mid = lax.reduce_precision(rest, 8, 7)
    low = rest - mid
    return jnp.stack([hi, mid, low], axis=-1).astype(BF16)


HBM_SPEC = pl.BlockSpec(memory_space=pltpu.HBM)
VMEM_SPEC = pl.BlockSpec(memory_space=pltpu.VMEM)
SMEM_SPEC = pl.BlockSpec(memory_space=pltpu.SMEM)


WINDOW = 128


def call(kernel, outs, *args, streamed=(), kept=(), scalars=(), flops=0, scratch=(), room=0):
    size = sum(math.prod(a.shape) * a.dtype.itemsize for a in args)
    places = {i: pltpu.HBM for i in streamed} | {i: pltpu.VMEM for i in kept}
    specs = [
        HBM_SPEC if i in streamed else SMEM_SPEC if i in scalars else VMEM_SPEC
        for i in range(len(args))
    ]
    return pl.pallas_call(
        kernel,
        out_shape=outs,
        in_specs=specs,
        out_specs=[VMEM_SPEC] * len(outs),
        scratch_shapes=list(scratch),
        compiler_params=pltpu.CompilerParams(vmem_limit_bytes=VMEM_BYTES + room),
        cost_estimate=pl.CostEstimate(flops=flops, bytes_accessed=size, transcendentals=0),
    )(*[
        pltpu.with_memory_space_constraint(a, places[i]) if i in places else a
        for i, a in enumerate(args)
    ])


class Stream:
    def __init__(self, copies):
        self.copies = copies
        self.done = 0
        for copy in copies[:WINDOW]:
            copy.start()

    def wait(self, count):
        while self.done < count:
            self.copies[self.done].wait()
            self.done += 1
            if self.done + WINDOW <= len(self.copies):
                self.copies[self.done + WINDOW - 1].start()


def struct(shape, dtype):
    return jax.ShapeDtypeStruct(shape, dtype)


def this_core():
    return lax.axis_index("dp") % 2


def span(start, size):
    return pl.ds(pl.multiple_of(start, size), size)


def softmax_kernel(logits_ref, beside_ref, out_ref, probs_ref):
    del beside_ref
    devices, _, part = out_ref.shape
    x = logits_ref[...].astype(F32)
    e = jnp.exp(x - jnp.max(x, axis=-1, keepdims=True))
    probs = e * (1.0 / jnp.sum(e, axis=-1, keepdims=True))
    probs_ref[...] = probs
    for d in range(devices):
        out_ref[d] = probs[:, d * part : (d + 1) * part].astype(BF16)


def final_kernel(probs_ref, back_ref, counts_ref, out_ref, rewards_ref, d_ref):
    devices, _, padded = back_ref.shape
    part = out_ref.shape[1] // devices
    requests = counts_ref.shape[1]
    sums = jnp.zeros((1, requests), F32)
    for d in range(devices):
        block = back_ref[d].astype(F32)
        d_ref[:, d * part : (d + 1) * part] = block[:, :part]
        for i in range(3):
            start = part + i * requests
            sums += block[:1, start : start + requests]
    rewards_ref[...] = sums / counts_ref[...]
    probs, d_probs = probs_ref[...], d_ref[...]
    mean = jnp.sum(probs * d_probs, axis=-1, keepdims=True)
    out_ref[...] = (math.sqrt(VOC) * (probs * (d_probs - mean))).astype(BF16)


def valid_column(counts, total):
    requests = counts.shape[1]
    length = total // requests
    position = lax.broadcasted_iota(jnp.int32, (total, requests), 0)
    start = length * lax.broadcasted_iota(jnp.int32, (total, requests), 1)
    inside = (position >= start) & (position < start + counts)
    return jnp.sum(jnp.where(inside, 1.0, 0.0), axis=-1, keepdims=True)


def bring(source_ref, out_ref, sems, columns):
    fine = 128
    return [
        pltpu.make_async_copy(
            source_ref.at[pl.ds(i, fine), columns], out_ref.at[pl.ds(i, fine)], sems.at[i // fine]
        )
        for i in range(0, out_ref.shape[0], fine)
    ]


def half_kernel(other, slices_ref, ready_ref, embed_ref, head_ref, out_ref, score_ref, *rest):
    next_ref, table, acc, sems, next_sems = rest if other else (None, *rest, None)
    chips, total, own = out_ref.shape
    part, ready = embed_ref.shape[0], ready_ref.shape[0]
    core = this_core()
    half = (1 - core) if other else core
    columns = span(half * chips * own, chips * own)
    tile, fine = 256, 128
    stream = Stream([
        pltpu.make_async_copy(
            embed_ref.at[pl.ds(i, min(fine, part - i)), columns],
            table.at[pl.ds(i - ready, min(fine, part - i))],
            sems.at[i // fine],
        )
        for i in range(ready, part, fine)
    ])
    following = []
    if other:
        following = bring(embed_ref, next_ref, next_sems, span(core * chips * own, chips * own))
        for copy in following:
            copy.start()
    acc[...] = jnp.dot(slices_ref[:, :ready], ready_ref[...], preferred_element_type=F32)
    for start in range(ready, part, tile):
        end = min(start + tile, part)
        stream.wait(-(-(end - ready) // fine))
        acc[...] += jnp.dot(
            slices_ref[:, start:end], table[start - ready : end - ready],
            preferred_element_type=F32,
        )
    head = head_ref[...].astype(F32).reshape(1, 2 * chips * own)
    head = jnp.where(half == 0, head[:, : chips * own], head[:, chips * own :])
    score_ref[...] = jnp.sum(acc[...] * head, axis=-1, keepdims=True)
    for j in range(chips):
        out_ref[j] = acc[:, j * own : (j + 1) * own].astype(out_ref.dtype)
    for copy in following:
        copy.wait()


def early_kernel(
    head_ref, down_ref, embed_ref, gate_ref, up_ref, after_ref,
    out_ref, first, both, table, sems, first_sems, both_sems,
):
    del after_ref
    width, lanes = down_ref.shape[1], 128
    core = this_core()

    def copy(j):
        rows = span(j * lanes, lanes)
        return pltpu.make_async_copy(down_ref.at[rows], table.at[rows], sems.at[j])

    steps = sems.shape[0]
    for j in range(steps):
        copy(j).start()
    half = width // 2
    own = both.shape[0] // 2
    chips = half // own
    others = bring(embed_ref, first, first_sems, span((1 - core) * half, half))
    others += bring_blocks(gate_ref, up_ref, both, core, range(2), own, chips, both_sems)
    for other in others:
        other.start()
    head = head_ref[...].astype(F32).reshape(1, width)

    def step(j, _):
        copy(j).wait()
        rows = span(j * lanes, lanes)
        total = jnp.zeros((lanes, lanes), F32)
        for k in range(0, width, lanes):
            total += table[rows, k : k + lanes].astype(F32) * head[:, k : k + lanes]
        out_ref[:, rows] = jnp.sum(total.T, axis=0, keepdims=True)
        return 0

    lax.fori_loop(0, steps, step, 0)
    for other in others:
        other.wait()


def bring_blocks(gate_ref, up_ref, both, half, blocks, own, chips, sems):
    hidden = gate_ref.shape[1]
    return [
        pltpu.make_async_copy(
            source.at[span((half * chips + j) * own, own)],
            both.at[pl.ds((j - blocks[0]) * own, own), pl.ds(k * hidden, hidden)],
            sems.at[k, j - blocks[0]],
        )
        for j in blocks
        for k, source in enumerate((gate_ref, up_ref))
    ]


def weight_rows(ready, both, own):
    skip = ready.shape[0] // own

    def weights(j):
        if j < skip:
            return ready[j * own : (j + 1) * own]
        return both[(j - skip) * own : (j - skip + 1) * own]

    return skip, weights


def forward_half(x_ref, gain_ref, half, sums, weights, wait):
    chips, _, own = x_ref.shape
    products, squares = sums
    scaled = []
    wide = jnp.zeros(x_ref.shape[1:], F32)
    for j in range(chips):
        x = x_ref[j].astype(F32)
        wide = wide + x * x
        gain = gain_ref[:, span((half * chips + j) * own, own)].astype(F32)
        scaled.append((x * gain).astype(BF16))
    squares = squares + jnp.sum(wide, axis=-1, keepdims=True)
    for j in range(chips):
        wait(j)
        products = products + jnp.dot(scaled[j], weights(j), preferred_element_type=F32)
    return products, squares


def backward_half(d_both, weights, out_ref):
    contract = (((1,), (1,)), ((), ()))
    for j in range(out_ref.shape[0]):
        part = lax.dot_general(d_both, weights(j), contract, preferred_element_type=F32)
        out_ref[j] = part.astype(out_ref.dtype)


def first_kernel(
    x_ref, gain_ref, gate_ref, up_ref, ready_ref, counts_ref,
    products_ref, squares_ref, valid_ref, counts_row, both, ahead, sems, ahead_sems,
):
    chips, _, own = x_ref.shape
    core = this_core()
    skip, weights = weight_rows(ready_ref, both, own)
    blocks = range(skip, chips)
    stream = Stream(bring_blocks(gate_ref, up_ref, both, core, blocks, own, chips, sems))
    blocks = range(ahead.shape[0] // own)
    following = bring_blocks(gate_ref, up_ref, ahead, 1 - core, blocks, own, chips, ahead_sems)
    for copy in following:
        copy.start()
    counts = counts_ref[...]
    valid_ref[...] = valid_column(counts, valid_ref.shape[0])
    counts_row[...] = counts.astype(F32)
    sums = (jnp.zeros(products_ref.shape, F32), jnp.zeros(squares_ref.shape, F32))
    products_ref[...], squares_ref[...] = forward_half(
        x_ref, gain_ref, core, sums, weights, lambda j: stream.wait(2 * (j - skip + 1))
    )
    for copy in following:
        copy.wait()


def second_kernel(
    x_ref, gain_ref, gate_ref, up_ref, ready_ref, products_ref, squares_ref, down_ref, valid_ref,
    send_ref, score_ref, inv_ref, d_both_ref, both, sems,
):
    chips, total, own = x_ref.shape
    width, hidden = gate_ref.shape
    half = 1 - this_core()
    skip, weights = weight_rows(ready_ref, both, own)
    blocks = range(skip, chips)
    stream = Stream(bring_blocks(gate_ref, up_ref, both, half, blocks, own, chips, sems))
    sums = (products_ref[...], squares_ref[...])
    products, squares = forward_half(
        x_ref, gain_ref, half, sums, weights, lambda j: stream.wait(2 * (j - skip + 1))
    )
    inv = lax.rsqrt(squares / width + 1e-05)
    inv_ref[...] = inv
    a, b = products[:, :hidden] * inv, products[:, hidden:] * inv
    sigma = jax.nn.sigmoid(a)
    active = a * sigma
    down = down_ref[...]
    rounded = (active * b).astype(BF16).astype(F32)
    score_ref[...] = jnp.sum(rounded * down, axis=-1, keepdims=True)
    d_hidden = valid_ref[...] * down
    d_both_ref[:, :hidden] = (d_hidden * b * sigma * (1.0 + a * (1.0 - sigma))).astype(BF16)
    d_both_ref[:, hidden:] = (d_hidden * active).astype(BF16)
    backward_half(d_both_ref[...], weights, send_ref)


def third_kernel(d_both_ref, ready_ref, both_ref, embed_ref, keep_ref, first, sems):
    following = bring(embed_ref, first, sems, pl.ds(0, embed_ref.shape[1]))
    for copy in following:
        copy.start()
    _, weights = weight_rows(ready_ref, both_ref, keep_ref.shape[2])
    backward_half(d_both_ref[...], weights, keep_ref)
    for copy in following:
        copy.wait()


def input_kernel(
    mine_ref, got_ref, d_mine_ref, d_got_ref, gain_ref, head_ref, inv_ref,
    score_a_ref, score_b_ref, score_c_ref, valid_ref, counts_ref, ready_ref, embed_ref,
    out_ref, dx_ref, head_row, table, sems,
):
    chips, total, own = mine_ref.shape
    voc = embed_ref.shape[0]
    requests = counts_ref.shape[1]
    width = 2 * chips * own
    core = this_core()
    ready = ready_ref.shape[0]
    tile, fine = 256, 64
    steps = (voc - ready) // tile
    last = ready + steps * tile

    def copy(start, size):
        return pltpu.make_async_copy(
            embed_ref.at[pl.ds(start, size)],
            table.at[pl.ds(start - ready, size)],
            sems.at[start // fine],
        )

    def pieces(start, end):
        return [copy(start + i, min(fine, end - start - i)) for i in range(0, end - start, fine)]

    def step_pieces(j):
        start = pl.multiple_of(ready + j * tile, fine)
        return [copy(pl.multiple_of(start + i, fine), fine) for i in range(0, tile, fine)]

    for piece in pieces(ready, voc):
        piece.start()
    head_row[...] = head_ref[...].astype(F32).reshape(1, width)
    sources = ((mine_ref, d_mine_ref, core), (got_ref, d_got_ref, 1 - core))
    wide = jnp.zeros((total, own), F32)
    for x_ref, d_ref, half in sources:
        for j in range(chips):
            gain = gain_ref[:, span((half * chips + j) * own, own)].astype(F32)
            wide += d_ref[j].astype(F32) * gain * x_ref[j].astype(F32)
    inv = inv_ref[...]
    weight = inv * inv * inv * (jnp.sum(wide, axis=-1, keepdims=True) / width)
    valid = valid_ref[...]
    request = lax.broadcasted_iota(jnp.int32, (total, requests), 0) // (total // requests)
    for x_ref, d_ref, half in sources:
        for j in range(chips):
            columns = span((half * chips + j) * own, own)
            x = x_ref[j].astype(F32)
            g = d_ref[j].astype(F32) * gain_ref[:, columns].astype(F32)
            dx = inv * g - x * weight
            dx_ref[:, columns] = (dx + valid * head_row[:, columns]).astype(BF16)
    score = valid * (score_a_ref[...] + score_b_ref[...] + score_c_ref[...])
    member = request == lax.broadcasted_iota(jnp.int32, (total, requests), 1)
    value = jnp.sum(jnp.where(member, score, 0.0), axis=0, keepdims=True)
    parts = []
    for _ in range(3):
        piece = value.astype(BF16).astype(F32)
        parts.append(piece)
        value = value - piece
    for i, piece in enumerate(parts):
        start = voc + i * requests
        spread = jnp.broadcast_to(piece, (total, requests)).astype(BF16)
        out_ref[:, start : start + requests] = spread
    contract = (((1,), (1,)), ((), ()))

    def product(weights):
        return lax.dot_general(
            dx_ref[...], weights, contract, preferred_element_type=F32
        ).astype(BF16)

    out_ref[:, :ready] = product(ready_ref[...])

    def step(j, _):
        for piece in step_pieces(j):
            piece.wait()

        rows = pl.ds(pl.multiple_of(j * tile, tile), tile)
        out_ref[:, pl.ds(pl.multiple_of(ready + j * tile, tile), tile)] = product(table[rows, :])
        return 0

    lax.fori_loop(0, steps, step, 0)
    if last < voc:
        for piece in pieces(last, voc):
            piece.wait()
        out_ref[:, last:voc] = product(table[last - ready :, :])


def swap_sum(send, keep, devices):
    return (keep.astype(F32) + swap_cores(send, devices).astype(F32)).astype(BF16)


def chip_sum(half, devices):
    return jnp.sum(exchange_chips(half, devices).astype(F32), axis=0).astype(BF16)


def chip_gather(total, devices):
    return exchange_chips(jnp.broadcast_to(total[None], (devices // 2,) + total.shape), devices)


def pick(blocks, index):
    return lax.dynamic_index_in_dim(blocks, index, 0, keepdims=False)


def split_halves(part, devices):
    total, width = part.shape
    core = lax.axis_index("dp") % 2
    blocks = part.reshape(total, 2, devices // 2, width // devices).transpose(1, 2, 0, 3)
    return pick(blocks, 1 - core).astype(BF16), pick(blocks, core)


def join_halves(mine, got):
    core = lax.axis_index("dp") % 2
    blocks = jnp.where(core == 1, jnp.stack([got, mine]), jnp.stack([mine, got]))
    _, chips, total, own = blocks.shape
    return blocks.transpose(2, 0, 1, 3).reshape(total, 2 * chips * own).astype(F32)


def norm_scale(x0):
    return lax.rsqrt(jnp.mean(x0 * x0, axis=-1, keepdims=True) + 1e-05)


def plain_half(slices, embed, head_row, devices):
    part = jnp.dot(slices, embed, preferred_element_type=F32)
    score = jnp.sum(part * head_row.astype(F32), axis=-1, keepdims=True)
    return *split_halves(part, devices), score


def plain_hidden(mine, got, gain_row, w_gate, w_up, down, valid, devices):
    x0 = join_halves(mine, got)
    normed = (x0 * norm_scale(x0) * gain_row.astype(F32)).astype(BF16)
    a = jnp.dot(normed, w_gate, preferred_element_type=F32)
    b = jnp.dot(normed, w_up, preferred_element_type=F32)
    sigma = jax.nn.sigmoid(a)
    active = a * sigma
    hidden = (active * b).astype(BF16).astype(F32)
    d_hidden = valid * down
    d_gate = (d_hidden * b * sigma * (1.0 + a * (1.0 - sigma))).astype(BF16)
    d_up = (d_hidden * active).astype(BF16)
    part = jnp.einsum("tf,df->td", d_gate, w_gate, preferred_element_type=F32)
    part = part + jnp.einsum("tf,df->td", d_up, w_up, preferred_element_type=F32)
    return *split_halves(part, devices), jnp.sum(hidden * down, axis=-1, keepdims=True)


def plain_input(mine, got, d_mine, d_got, gain_row, head_row, valid, embed):
    x0 = join_halves(mine, got)
    inv = norm_scale(x0)
    scaled = join_halves(d_mine, d_got) * gain_row.astype(F32)
    dx = inv * scaled - x0 * inv * inv * inv * jnp.mean(scaled * x0, axis=-1, keepdims=True)
    dx = (dx + valid * head_row.astype(F32)).astype(BF16)
    return jnp.einsum("td,vd->tv", dx, embed, preferred_element_type=F32).astype(BF16)


def body(logits, embed, norm_gain, w_gate, w_up, w_down, head, counts):
    devices = lax.axis_size("dp")
    rows, voc = logits.shape
    part = voc // devices
    width = embed.shape[1]
    hidden = w_gate.shape[1]
    own, chips = width // devices, devices // 2
    requests = counts.shape[0]
    total = rows * devices
    request_len = total // requests
    tiled = own % 128 == 0 and hidden % 128 == 0 and total % 16 == 0 and part % 16 == 0 and part > 512
    head_row, gain_row = head.reshape(1, width), norm_gain.reshape(1, width)
    if tiled:
        blocked, probs = call(
            softmax_kernel,
            [struct((devices, rows, part), BF16), pltpu.VMEM((rows, voc), F32)], logits, head,
        )
    else:
        probs32 = jax.nn.softmax(logits.astype(F32), axis=-1)
        blocked = probs32.astype(BF16).reshape(rows, devices, part).transpose(1, 0, 2)
    slices = exchange(blocked).reshape(total, part)
    column = struct((total, 1), F32)
    half = (chips, total, own)
    flops = total * part * width
    if tiled:
        ready = 256
        down_row, first, both_first = call(
            early_kernel,
            [
                struct((1, hidden), F32), pltpu.VMEM((ready, width // 2), BF16),
                pltpu.VMEM((2 * own, 2 * hidden), BF16),
            ],
            head, w_down, embed, w_gate, w_up, blocked,
            streamed=(1, 2, 3, 4), flops=2 * hidden * width, room=2 * hidden * width,
            scratch=(
                pltpu.VMEM((hidden, width), BF16), pltpu.SemaphoreType.DMA((hidden // 128,)),
                pltpu.SemaphoreType.DMA((ready // 128,)), pltpu.SemaphoreType.DMA((2, 2)),
            ),
        )
        table = (
            pltpu.VMEM((part - ready, width // 2), BF16), pltpu.VMEM((total, width // 2), F32),
            pltpu.SemaphoreType.DMA((-(-part // 128),)),
        )
        args = dict(streamed=(2,), kept=(1,), flops=flops, room=part * width)
        send, score_a, first = call(
            functools.partial(half_kernel, True),
            [struct(half, BF16), column, pltpu.VMEM((ready, width // 2), BF16)],
            slices, first, embed, head,
            scratch=(*table, pltpu.SemaphoreType.DMA((ready // 128,))), **args,
        )
        keep, score_b = call(
            functools.partial(half_kernel, False), [struct(half, F32), column],
            slices, first, embed, head, scratch=table, **args,
        )
    else:
        send, keep, score_a = plain_half(slices, embed, head_row, devices)
    summed = swap_sum(send, keep, devices)
    x_mine = chip_gather(chip_sum(summed, devices), devices)
    x_got = swap_cores(x_mine, devices)
    if tiled:
        weight = (width // 2 - 2 * own, 2 * hidden)
        sems, ahead_sems = pltpu.SemaphoreType.DMA((2, chips)), pltpu.SemaphoreType.DMA((2, 2))
        args = dict(
            streamed=(2, 3), kept=(4,), flops=2 * total * hidden * width, room=2 * width * hidden
        )
        products, squares, valid, counts_row, both, ahead = call(
            first_kernel,
            [
                struct((total, 2 * hidden), F32), column, column, struct((1, requests), F32),
                pltpu.VMEM(weight, BF16), pltpu.VMEM(both_first.shape, BF16),
            ],
            x_mine, gain_row, w_gate, w_up, both_first, counts.reshape(1, requests),
            scratch=(sems, ahead_sems), **args,
        )
        send, score_c, inv, d_both = call(
            second_kernel,
            [struct(half, BF16), column, column, struct((total, 2 * hidden), BF16)],
            x_got, gain_row, w_gate, w_up, ahead, products, squares, down_row, valid,
            scratch=(pltpu.VMEM(weight, BF16), sems), **args,
        )
        keep, first = call(
            third_kernel, [struct(half, F32), pltpu.VMEM((ready, width), BF16)],
            d_both, both_first, both, embed,
            kept=(1, 2), streamed=(3,), flops=2 * total * hidden * width,
            scratch=(pltpu.SemaphoreType.DMA((ready // 128,)),),
        )
    else:
        down_row = jnp.sum(w_down.astype(F32) * head.astype(F32)[None, :], axis=-1)[None]
        position = jnp.arange(total, dtype=jnp.int32)[:, None]
        member = position // request_len == jnp.arange(requests, dtype=jnp.int32)[None, :]
        limit = jnp.sum(jnp.where(member, counts[None, :], 0), axis=-1, keepdims=True)
        valid = (position % request_len < limit).astype(F32)
        send, keep, score_c = plain_hidden(
            x_mine, x_got, gain_row, w_gate, w_up, down_row, valid, devices
        )
    total_d = chip_sum(swap_sum(send, keep, devices), devices)
    d_mine = chip_gather(total_d, devices)
    d_got = swap_cores(d_mine, devices)
    padded = part + 3 * requests
    if tiled:
        (d_slices,) = call(
            input_kernel, [struct((total, padded), BF16)],
            x_mine, x_got, d_mine, d_got, gain_row, head, inv,
            score_a, score_b, score_c, valid, counts_row, first, embed,
            kept=(12,), streamed=(13,), flops=2 * flops, room=2 * part * width,
            scratch=(
                pltpu.VMEM((total, width), BF16), pltpu.VMEM((1, width), F32),
                pltpu.VMEM((part - ready, width), BF16),
                pltpu.SemaphoreType.DMA((-(-part // 64),)),
            ),
        )
    else:
        d_slices = plain_input(x_mine, x_got, d_mine, d_got, gain_row, head_row, valid, embed)
        score = jnp.where(member, valid * (score_a + score_c), 0.0)
        extra = split3(jnp.sum(score, axis=0)).reshape(1, requests * 3)
        extra = jnp.broadcast_to(extra, (total, requests * 3))
        d_slices = jnp.concatenate([d_slices, extra], axis=-1)
    back = exchange(d_slices.reshape(devices, rows, padded))
    if tiled:
        guidance, rewards = call(
            final_kernel, [struct((rows, voc), BF16), struct((1, requests), F32)],
            probs, back, counts_row, kept=(0,),
            scratch=(pltpu.VMEM((rows, voc), F32),),
        )
        return (guidance, rewards.reshape(requests))
    sums = jnp.sum(back[:, 0, part:].astype(F32).reshape(devices, requests, 3), axis=(0, 2))
    rewards = sums / counts.astype(F32)
    d_probs = back[:, :, :part].transpose(1, 0, 2).reshape(rows, voc).astype(F32)
    d_logits = probs32 * (d_probs - jnp.sum(probs32 * d_probs, axis=-1, keepdims=True))
    guidance = (math.sqrt(VOC) * d_logits).astype(BF16)
    return (guidance, rewards)


def solution(mesh):
    placed = (
        P(("groups", "dp"), None),
        P("dp", None),
        P(),
        P(None, "dp"),
        P(None, "dp"),
        P("dp", None),
        P(),
        P("groups"),
    )
    return jax.shard_map(
        body,
        mesh=mesh,
        in_specs=placed,
        out_specs=(P(("groups", "dp"), None), P("groups")),
        check_vma=False,
    )
```

```python
import functools
import math

import jax
import jax.numpy as jnp
from jax import lax
from jax.experimental import pallas as pl
from jax.experimental.pallas import tpu as pltpu
from jax.sharding import PartitionSpec as P

VOC = 32000
F32, BF16 = jnp.float32, jnp.bfloat16
VMEM_BYTES = 12 * 1024 * 1024


def swap_cores(value, devices):
    return lax.ppermute(value, "dp", [(i, i ^ 1) for i in range(devices)])


def exchange(blocks):
    return lax.all_to_all(blocks, "dp", split_axis=0, concat_axis=0, tiled=True)


def exchange_chips(blocks, devices):
    groups = [list(range(core, devices, 2)) for core in range(2)]
    return lax.all_to_all(
        blocks, "dp", split_axis=0, concat_axis=0, axis_index_groups=groups, tiled=True
    )


def split3(value):
    hi = lax.reduce_precision(value, 8, 7)
    rest = value - hi
    mid = lax.reduce_precision(rest, 8, 7)
    low = rest - mid
    return jnp.stack([hi, mid, low], axis=-1).astype(BF16)


HBM_SPEC = pl.BlockSpec(memory_space=pltpu.HBM)
VMEM_SPEC = pl.BlockSpec(memory_space=pltpu.VMEM)
SMEM_SPEC = pl.BlockSpec(memory_space=pltpu.SMEM)


WINDOW = 128


def call(kernel, outs, *args, streamed=(), kept=(), scalars=(), flops=0, scratch=(), room=0):
    size = sum(math.prod(a.shape) * a.dtype.itemsize for a in args)
    places = {i: pltpu.HBM for i in streamed} | {i: pltpu.VMEM for i in kept}
    specs = [
        HBM_SPEC if i in streamed else SMEM_SPEC if i in scalars else VMEM_SPEC
        for i in range(len(args))
    ]
    return pl.pallas_call(
        kernel,
        out_shape=outs,
        in_specs=specs,
        out_specs=[VMEM_SPEC] * len(outs),
        scratch_shapes=list(scratch),
        compiler_params=pltpu.CompilerParams(vmem_limit_bytes=VMEM_BYTES + room),
        cost_estimate=pl.CostEstimate(flops=flops, bytes_accessed=size, transcendentals=0),
    )(*[
        pltpu.with_memory_space_constraint(a, places[i]) if i in places else a
        for i, a in enumerate(args)
    ])


class Stream:
    def __init__(self, copies):
        self.copies = copies
        self.done = 0
        for copy in copies[:WINDOW]:
            copy.start()

    def wait(self, count):
        while self.done < count:
            self.copies[self.done].wait()
            self.done += 1
            if self.done + WINDOW <= len(self.copies):
                self.copies[self.done + WINDOW - 1].start()


def struct(shape, dtype):
    return jax.ShapeDtypeStruct(shape, dtype)


def this_core():
    return lax.axis_index("dp") % 2


def span(start, size):
    return pl.ds(pl.multiple_of(start, size), size)


def softmax_kernel(logits_ref, out_ref, probs_ref):
    devices, _, part = out_ref.shape
    x = logits_ref[...].astype(F32)
    e = jnp.exp(x - jnp.max(x, axis=-1, keepdims=True))
    probs = e * (1.0 / jnp.sum(e, axis=-1, keepdims=True))
    probs_ref[...] = probs
    for d in range(devices):
        out_ref[d] = probs[:, d * part : (d + 1) * part].astype(BF16)


def final_kernel(probs_ref, back_ref, counts_ref, out_ref, rewards_ref, d_ref):
    devices, _, padded = back_ref.shape
    part = out_ref.shape[1] // devices
    requests = counts_ref.shape[1]
    sums = jnp.zeros((1, requests), F32)
    for d in range(devices):
        block = back_ref[d].astype(F32)
        d_ref[:, d * part : (d + 1) * part] = block[:, :part]
        for i in range(3):
            start = part + i * requests
            sums += block[:1, start : start + requests]
    rewards_ref[...] = sums / counts_ref[...]
    probs, d_probs = probs_ref[...], d_ref[...]
    mean = jnp.sum(probs * d_probs, axis=-1, keepdims=True)
    out_ref[...] = (math.sqrt(VOC) * (probs * (d_probs - mean))).astype(BF16)


def valid_column(counts, total):
    requests = counts.shape[1]
    length = total // requests
    position = lax.broadcasted_iota(jnp.int32, (total, requests), 0)
    start = length * lax.broadcasted_iota(jnp.int32, (total, requests), 1)
    inside = (position >= start) & (position < start + counts)
    return jnp.sum(jnp.where(inside, 1.0, 0.0), axis=-1, keepdims=True)


def bring(source_ref, out_ref, sems, columns):
    fine = 128
    return [
        pltpu.make_async_copy(
            source_ref.at[pl.ds(i, fine), columns], out_ref.at[pl.ds(i, fine)], sems.at[i // fine]
        )
        for i in range(0, out_ref.shape[0], fine)
    ]


def ready_kernel(split, source_ref, after_ref, out_ref, sems):
    del after_ref
    width = out_ref.shape[1]
    columns = span((1 - this_core()) * width, width) if split else pl.ds(0, width)
    copies = bring(source_ref, out_ref, sems, columns)
    for copy in copies:
        copy.start()
    for copy in copies:
        copy.wait()


def first_rows(rows, source, after, split):
    width = source.shape[1] // 2 if split else source.shape[1]
    return call(
        functools.partial(ready_kernel, split), [pltpu.VMEM((rows, width), source.dtype)],
        source, after, streamed=(0,), scratch=(pltpu.SemaphoreType.DMA((rows // 128,)),),
    )[0]


def half_kernel(other, slices_ref, ready_ref, embed_ref, head_ref, out_ref, score_ref, *rest):
    next_ref, table, acc, sems, next_sems = rest if other else (None, *rest, None)
    chips, total, own = out_ref.shape
    part, ready = embed_ref.shape[0], ready_ref.shape[0]
    core = this_core()
    half = (1 - core) if other else core
    columns = span(half * chips * own, chips * own)
    tile, fine = 256, 128
    stream = Stream([
        pltpu.make_async_copy(
            embed_ref.at[pl.ds(i, min(fine, part - i)), columns],
            table.at[pl.ds(i - ready, min(fine, part - i))],
            sems.at[i // fine],
        )
        for i in range(ready, part, fine)
    ])
    following = []
    if other:
        following = bring(embed_ref, next_ref, next_sems, span(core * chips * own, chips * own))
        for copy in following:
            copy.start()
    acc[...] = jnp.dot(slices_ref[:, :ready], ready_ref[...], preferred_element_type=F32)
    for start in range(ready, part, tile):
        end = min(start + tile, part)
        stream.wait(-(-(end - ready) // fine))
        acc[...] += jnp.dot(
            slices_ref[:, start:end], table[start - ready : end - ready],
            preferred_element_type=F32,
        )
    score_ref[...] = jnp.sum(
        acc[...] * head_ref[:, columns].astype(F32), axis=-1, keepdims=True
    )
    for j in range(chips):
        out_ref[j] = acc[:, j * own : (j + 1) * own].astype(out_ref.dtype)
    for copy in following:
        copy.wait()


def early_kernel(
    head_ref, down_ref, embed_ref, gate_ref, up_ref, after_ref,
    out_ref, head_row, first, both, table, head_copy, sems, first_sems, both_sems, head_sem,
):
    del after_ref
    width, lanes = down_ref.shape[1], 128
    core = this_core()

    def copy(j):
        rows = span(j * lanes, lanes)
        return pltpu.make_async_copy(down_ref.at[rows], table.at[rows], sems.at[j])

    steps = sems.shape[0]
    bring_head = pltpu.make_async_copy(head_ref, head_copy, head_sem)
    bring_head.start()
    for j in range(steps):
        copy(j).start()
    half = width // 2
    own = both.shape[0] // 2
    chips = half // own
    others = bring(embed_ref, first, first_sems, span((1 - core) * half, half))
    others += bring_blocks(gate_ref, up_ref, both, core, range(2), own, chips, both_sems)
    for other in others:
        other.start()
    bring_head.wait()
    head = head_copy[...].astype(F32).reshape(1, width)
    head_row[...] = head

    def step(j, _):
        copy(j).wait()
        rows = span(j * lanes, lanes)
        total = jnp.zeros((lanes, lanes), F32)
        for k in range(0, width, lanes):
            total += table[rows, k : k + lanes].astype(F32) * head[:, k : k + lanes]
        out_ref[:, rows] = jnp.sum(total.T, axis=0, keepdims=True)
        return 0

    lax.fori_loop(0, steps, step, 0)
    for other in others:
        other.wait()


def bring_blocks(gate_ref, up_ref, both, half, blocks, own, chips, sems):
    hidden = gate_ref.shape[1]
    return [
        pltpu.make_async_copy(
            source.at[span((half * chips + j) * own, own)],
            both.at[pl.ds((j - blocks[0]) * own, own), pl.ds(k * hidden, hidden)],
            sems.at[k, j - blocks[0]],
        )
        for j in blocks
        for k, source in enumerate((gate_ref, up_ref))
    ]


def weight_rows(ready, both, own):
    skip = ready.shape[0] // own

    def weights(j):
        if j < skip:
            return ready[j * own : (j + 1) * own]
        return both[(j - skip) * own : (j - skip + 1) * own]

    return skip, weights


def forward_half(x_ref, gain_ref, half, sums, weights, wait):
    chips, _, own = x_ref.shape
    products, squares = sums
    scaled = []
    wide = jnp.zeros(x_ref.shape[1:], F32)
    for j in range(chips):
        x = x_ref[j].astype(F32)
        wide = wide + x * x
        gain = gain_ref[:, span((half * chips + j) * own, own)].astype(F32)
        scaled.append((x * gain).astype(BF16))
    squares = squares + jnp.sum(wide, axis=-1, keepdims=True)
    for j in range(chips):
        wait(j)
        products = products + jnp.dot(scaled[j], weights(j), preferred_element_type=F32)
    return products, squares


def backward_half(d_both, weights, out_ref):
    contract = (((1,), (1,)), ((), ()))
    for j in range(out_ref.shape[0]):
        part = lax.dot_general(d_both, weights(j), contract, preferred_element_type=F32)
        out_ref[j] = part.astype(out_ref.dtype)


def first_kernel(
    x_ref, gain_ref, gate_ref, up_ref, ready_ref, counts_ref,
    products_ref, squares_ref, valid_ref, counts_row, both, ahead, sems, ahead_sems,
):
    chips, _, own = x_ref.shape
    core = this_core()
    skip, weights = weight_rows(ready_ref, both, own)
    blocks = range(skip, chips)
    stream = Stream(bring_blocks(gate_ref, up_ref, both, core, blocks, own, chips, sems))
    blocks = range(ahead.shape[0] // own)
    following = bring_blocks(gate_ref, up_ref, ahead, 1 - core, blocks, own, chips, ahead_sems)
    for copy in following:
        copy.start()
    counts = counts_ref[...]
    valid_ref[...] = valid_column(counts, valid_ref.shape[0])
    counts_row[...] = counts.astype(F32)
    sums = (jnp.zeros(products_ref.shape, F32), jnp.zeros(squares_ref.shape, F32))
    products_ref[...], squares_ref[...] = forward_half(
        x_ref, gain_ref, core, sums, weights, lambda j: stream.wait(2 * (j - skip + 1))
    )
    for copy in following:
        copy.wait()


def second_kernel(
    x_ref, gain_ref, gate_ref, up_ref, ready_ref, products_ref, squares_ref, down_ref, valid_ref,
    send_ref, score_ref, inv_ref, d_both_ref, both, sems,
):
    chips, total, own = x_ref.shape
    width, hidden = gate_ref.shape
    half = 1 - this_core()
    skip, weights = weight_rows(ready_ref, both, own)
    blocks = range(skip, chips)
    stream = Stream(bring_blocks(gate_ref, up_ref, both, half, blocks, own, chips, sems))
    sums = (products_ref[...], squares_ref[...])
    products, squares = forward_half(
        x_ref, gain_ref, half, sums, weights, lambda j: stream.wait(2 * (j - skip + 1))
    )
    inv = lax.rsqrt(squares / width + 1e-05)
    inv_ref[...] = inv
    a, b = products[:, :hidden] * inv, products[:, hidden:] * inv
    sigma = jax.nn.sigmoid(a)
    active = a * sigma
    down = down_ref[...]
    rounded = (active * b).astype(BF16).astype(F32)
    score_ref[...] = jnp.sum(rounded * down, axis=-1, keepdims=True)
    d_hidden = valid_ref[...] * down
    d_both_ref[:, :hidden] = (d_hidden * b * sigma * (1.0 + a * (1.0 - sigma))).astype(BF16)
    d_both_ref[:, hidden:] = (d_hidden * active).astype(BF16)
    backward_half(d_both_ref[...], weights, send_ref)


def third_kernel(d_both_ref, ready_ref, both_ref, keep_ref):
    _, weights = weight_rows(ready_ref, both_ref, keep_ref.shape[2])
    backward_half(d_both_ref[...], weights, keep_ref)


def input_kernel(
    mine_ref, got_ref, d_mine_ref, d_got_ref, gain_ref, head_ref, inv_ref,
    score_a_ref, score_b_ref, score_c_ref, valid_ref, counts_ref, ready_ref, embed_ref,
    out_ref, dx_ref, table, sems,
):
    chips, total, own = mine_ref.shape
    voc = embed_ref.shape[0]
    requests = counts_ref.shape[1]
    width = 2 * chips * own
    core = this_core()
    ready = ready_ref.shape[0]
    tile, fine = 256, 64
    steps = (voc - ready) // tile
    last = ready + steps * tile

    def copy(start, size):
        return pltpu.make_async_copy(
            embed_ref.at[pl.ds(start, size)],
            table.at[pl.ds(start - ready, size)],
            sems.at[start // fine],
        )

    def pieces(start, end):
        return [copy(start + i, min(fine, end - start - i)) for i in range(0, end - start, fine)]

    def step_pieces(j):
        start = pl.multiple_of(ready + j * tile, fine)
        return [copy(pl.multiple_of(start + i, fine), fine) for i in range(0, tile, fine)]

    for piece in pieces(ready, voc):
        piece.start()
    sources = ((mine_ref, d_mine_ref, core), (got_ref, d_got_ref, 1 - core))
    wide = jnp.zeros((total, own), F32)
    for x_ref, d_ref, half in sources:
        for j in range(chips):
            gain = gain_ref[:, span((half * chips + j) * own, own)].astype(F32)
            wide += d_ref[j].astype(F32) * gain * x_ref[j].astype(F32)
    inv = inv_ref[...]
    weight = inv * inv * inv * (jnp.sum(wide, axis=-1, keepdims=True) / width)
    valid = valid_ref[...]
    request = lax.broadcasted_iota(jnp.int32, (total, requests), 0) // (total // requests)
    for x_ref, d_ref, half in sources:
        for j in range(chips):
            columns = span((half * chips + j) * own, own)
            x = x_ref[j].astype(F32)
            g = d_ref[j].astype(F32) * gain_ref[:, columns].astype(F32)
            dx = inv * g - x * weight
            dx_ref[:, columns] = (dx + valid * head_ref[:, columns].astype(F32)).astype(BF16)
    score = valid * (score_a_ref[...] + score_b_ref[...] + score_c_ref[...])
    member = request == lax.broadcasted_iota(jnp.int32, (total, requests), 1)
    value = jnp.sum(jnp.where(member, score, 0.0), axis=0, keepdims=True)
    parts = []
    for _ in range(3):
        piece = value.astype(BF16).astype(F32)
        parts.append(piece)
        value = value - piece
    for i, piece in enumerate(parts):
        start = voc + i * requests
        spread = jnp.broadcast_to(piece, (total, requests)).astype(BF16)
        out_ref[:, start : start + requests] = spread
    contract = (((1,), (1,)), ((), ()))

    def product(weights):
        return lax.dot_general(
            dx_ref[...], weights, contract, preferred_element_type=F32
        ).astype(BF16)

    out_ref[:, :ready] = product(ready_ref[...])

    def step(j, _):
        for piece in step_pieces(j):
            piece.wait()

        rows = pl.ds(pl.multiple_of(j * tile, tile), tile)
        out_ref[:, pl.ds(pl.multiple_of(ready + j * tile, tile), tile)] = product(table[rows, :])
        return 0

    lax.fori_loop(0, steps, step, 0)
    if last < voc:
        for piece in pieces(last, voc):
            piece.wait()
        out_ref[:, last:voc] = product(table[last - ready :, :])


def swap_sum(send, keep, devices):
    return (keep.astype(F32) + swap_cores(send, devices).astype(F32)).astype(BF16)


def chip_sum(half, devices):
    return jnp.sum(exchange_chips(half, devices).astype(F32), axis=0).astype(BF16)


def chip_gather(total, devices):
    return exchange_chips(jnp.broadcast_to(total[None], (devices // 2,) + total.shape), devices)


def pick(blocks, index):
    return lax.dynamic_index_in_dim(blocks, index, 0, keepdims=False)


def split_halves(part, devices):
    total, width = part.shape
    core = lax.axis_index("dp") % 2
    blocks = part.reshape(total, 2, devices // 2, width // devices).transpose(1, 2, 0, 3)
    return pick(blocks, 1 - core).astype(BF16), pick(blocks, core)


def join_halves(mine, got):
    core = lax.axis_index("dp") % 2
    blocks = jnp.where(core == 1, jnp.stack([got, mine]), jnp.stack([mine, got]))
    _, chips, total, own = blocks.shape
    return blocks.transpose(2, 0, 1, 3).reshape(total, 2 * chips * own).astype(F32)


def norm_scale(x0):
    return lax.rsqrt(jnp.mean(x0 * x0, axis=-1, keepdims=True) + 1e-05)


def plain_half(slices, embed, head_row, devices):
    part = jnp.dot(slices, embed, preferred_element_type=F32)
    score = jnp.sum(part * head_row.astype(F32), axis=-1, keepdims=True)
    return *split_halves(part, devices), score


def plain_hidden(mine, got, gain_row, w_gate, w_up, down, valid, devices):
    x0 = join_halves(mine, got)
    normed = (x0 * norm_scale(x0) * gain_row.astype(F32)).astype(BF16)
    a = jnp.dot(normed, w_gate, preferred_element_type=F32)
    b = jnp.dot(normed, w_up, preferred_element_type=F32)
    sigma = jax.nn.sigmoid(a)
    active = a * sigma
    hidden = (active * b).astype(BF16).astype(F32)
    d_hidden = valid * down
    d_gate = (d_hidden * b * sigma * (1.0 + a * (1.0 - sigma))).astype(BF16)
    d_up = (d_hidden * active).astype(BF16)
    part = jnp.einsum("tf,df->td", d_gate, w_gate, preferred_element_type=F32)
    part = part + jnp.einsum("tf,df->td", d_up, w_up, preferred_element_type=F32)
    return *split_halves(part, devices), jnp.sum(hidden * down, axis=-1, keepdims=True)


def plain_input(mine, got, d_mine, d_got, gain_row, head_row, valid, embed):
    x0 = join_halves(mine, got)
    inv = norm_scale(x0)
    scaled = join_halves(d_mine, d_got) * gain_row.astype(F32)
    dx = inv * scaled - x0 * inv * inv * inv * jnp.mean(scaled * x0, axis=-1, keepdims=True)
    dx = (dx + valid * head_row.astype(F32)).astype(BF16)
    return jnp.einsum("td,vd->tv", dx, embed, preferred_element_type=F32).astype(BF16)


def body(logits, embed, norm_gain, w_gate, w_up, w_down, head, counts):
    devices = lax.axis_size("dp")
    rows, voc = logits.shape
    part = voc // devices
    width = embed.shape[1]
    hidden = w_gate.shape[1]
    own, chips = width // devices, devices // 2
    requests = counts.shape[0]
    total = rows * devices
    request_len = total // requests
    tiled = own % 128 == 0 and hidden % 128 == 0 and total % 16 == 0 and part % 16 == 0 and part > 512
    head_row, gain_row = head.reshape(1, width), norm_gain.reshape(1, width)
    if tiled:
        blocked, probs = call(
            softmax_kernel,
            [struct((devices, rows, part), BF16), pltpu.VMEM((rows, voc), F32)], logits,
        )
    else:
        probs32 = jax.nn.softmax(logits.astype(F32), axis=-1)
        blocked = probs32.astype(BF16).reshape(rows, devices, part).transpose(1, 0, 2)
    slices = exchange(blocked).reshape(total, part)
    column = struct((total, 1), F32)
    half = (chips, total, own)
    flops = total * part * width
    if tiled:
        ready = 256
        down_row, head32, first, both_first = call(
            early_kernel,
            [
                struct((1, hidden), F32), struct((1, width), F32),
                pltpu.VMEM((ready, width // 2), BF16),
                pltpu.VMEM((2 * own, 2 * hidden), BF16),
            ],
            head, w_down, embed, w_gate, w_up, blocked,
            streamed=(0, 1, 2, 3, 4), flops=2 * hidden * width, room=2 * hidden * width,
            scratch=(
                pltpu.VMEM((hidden, width), BF16), pltpu.VMEM((width,), BF16),
                pltpu.SemaphoreType.DMA((hidden // 128,)),
                pltpu.SemaphoreType.DMA((ready // 128,)), pltpu.SemaphoreType.DMA((2, 2)),
                pltpu.SemaphoreType.DMA,
            ),
        )
        table = (
            pltpu.VMEM((part - ready, width // 2), BF16), pltpu.VMEM((total, width // 2), F32),
            pltpu.SemaphoreType.DMA((-(-part // 128),)),
        )
        args = dict(streamed=(2,), kept=(1,), flops=flops, room=part * width)
        send, score_a, first = call(
            functools.partial(half_kernel, True),
            [struct(half, BF16), column, pltpu.VMEM((ready, width // 2), BF16)],
            slices, first, embed, head32,
            scratch=(*table, pltpu.SemaphoreType.DMA((ready // 128,))), **args,
        )
        keep, score_b = call(
            functools.partial(half_kernel, False), [struct(half, F32), column],
            slices, first, embed, head32, scratch=table, **args,
        )
    else:
        send, keep, score_a = plain_half(slices, embed, head_row, devices)
    summed = swap_sum(send, keep, devices)
    x_mine = chip_gather(chip_sum(summed, devices), devices)
    x_got = swap_cores(x_mine, devices)
    if tiled:
        weight = (width // 2 - 2 * own, 2 * hidden)
        sems, ahead_sems = pltpu.SemaphoreType.DMA((2, chips)), pltpu.SemaphoreType.DMA((2, 2))
        args = dict(
            streamed=(2, 3), kept=(4,), flops=2 * total * hidden * width, room=2 * width * hidden
        )
        products, squares, valid, counts_row, both, ahead = call(
            first_kernel,
            [
                struct((total, 2 * hidden), F32), column, column, struct((1, requests), F32),
                pltpu.VMEM(weight, BF16), pltpu.VMEM(both_first.shape, BF16),
            ],
            x_mine, gain_row, w_gate, w_up, both_first, counts.reshape(1, requests),
            scratch=(sems, ahead_sems), **args,
        )
        send, score_c, inv, d_both = call(
            second_kernel,
            [struct(half, BF16), column, column, struct((total, 2 * hidden), BF16)],
            x_got, gain_row, w_gate, w_up, ahead, products, squares, down_row, valid,
            scratch=(pltpu.VMEM(weight, BF16), sems), **args,
        )
        (keep,) = call(
            third_kernel, [struct(half, F32)], d_both, both_first, both,
            kept=(1, 2), flops=2 * total * hidden * width,
        )
    else:
        down_row = jnp.sum(w_down.astype(F32) * head.astype(F32)[None, :], axis=-1)[None]
        position = jnp.arange(total, dtype=jnp.int32)[:, None]
        member = position // request_len == jnp.arange(requests, dtype=jnp.int32)[None, :]
        limit = jnp.sum(jnp.where(member, counts[None, :], 0), axis=-1, keepdims=True)
        valid = (position % request_len < limit).astype(F32)
        send, keep, score_c = plain_hidden(
            x_mine, x_got, gain_row, w_gate, w_up, down_row, valid, devices
        )
    total_d = chip_sum(swap_sum(send, keep, devices), devices)
    d_mine = chip_gather(total_d, devices)
    d_got = swap_cores(d_mine, devices)
    padded = part + 3 * requests
    if tiled:
        first = first_rows(256, embed, total_d, False)
        (d_slices,) = call(
            input_kernel, [struct((total, padded), BF16)],
            x_mine, x_got, d_mine, d_got, gain_row, head32, inv,
            score_a, score_b, score_c, valid, counts_row, first, embed,
            kept=(12,), streamed=(13,), flops=2 * flops, room=2 * part * width,
            scratch=(
                pltpu.VMEM((total, width), BF16), pltpu.VMEM((part - 256, width), BF16),
                pltpu.SemaphoreType.DMA((-(-part // 64),)),
            ),
        )
    else:
        d_slices = plain_input(x_mine, x_got, d_mine, d_got, gain_row, head_row, valid, embed)
        score = jnp.where(member, valid * (score_a + score_c), 0.0)
        extra = split3(jnp.sum(score, axis=0)).reshape(1, requests * 3)
        extra = jnp.broadcast_to(extra, (total, requests * 3))
        d_slices = jnp.concatenate([d_slices, extra], axis=-1)
    back = exchange(d_slices.reshape(devices, rows, padded))
    if tiled:
        guidance, rewards = call(
            final_kernel, [struct((rows, voc), BF16), struct((1, requests), F32)],
            probs, back, counts_row, kept=(0,),
            scratch=(pltpu.VMEM((rows, voc), F32),),
        )
        return (guidance, rewards.reshape(requests))
    sums = jnp.sum(back[:, 0, part:].astype(F32).reshape(devices, requests, 3), axis=(0, 2))
    rewards = sums / counts.astype(F32)
    d_probs = back[:, :, :part].transpose(1, 0, 2).reshape(rows, voc).astype(F32)
    d_logits = probs32 * (d_probs - jnp.sum(probs32 * d_probs, axis=-1, keepdims=True))
    guidance = (math.sqrt(VOC) * d_logits).astype(BF16)
    return (guidance, rewards)


def solution(mesh):
    placed = (
        P(("groups", "dp"), None),
        P("dp", None),
        P(),
        P(None, "dp"),
        P(None, "dp"),
        P("dp", None),
        P(),
        P("groups"),
    )
    return jax.shard_map(
        body,
        mesh=mesh,
        in_specs=placed,
        out_specs=(P(("groups", "dp"), None), P("groups")),
        check_vma=False,
    )
```

```python
import functools
import math

import jax
import jax.numpy as jnp
from jax import lax
from jax.experimental import pallas as pl
from jax.experimental.pallas import tpu as pltpu
from jax.sharding import PartitionSpec as P

VOC = 32000
F32, BF16 = jnp.float32, jnp.bfloat16
VMEM_BYTES = 12 * 1024 * 1024


def swap_cores(value, devices):
    return lax.ppermute(value, "dp", [(i, i ^ 1) for i in range(devices)])


def exchange(blocks):
    return lax.all_to_all(blocks, "dp", split_axis=0, concat_axis=0, tiled=True)


def exchange_chips(blocks, devices):
    groups = [list(range(core, devices, 2)) for core in range(2)]
    return lax.all_to_all(
        blocks, "dp", split_axis=0, concat_axis=0, axis_index_groups=groups, tiled=True
    )


def split3(value):
    hi = lax.reduce_precision(value, 8, 7)
    rest = value - hi
    mid = lax.reduce_precision(rest, 8, 7)
    low = rest - mid
    return jnp.stack([hi, mid, low], axis=-1).astype(BF16)


HBM_SPEC = pl.BlockSpec(memory_space=pltpu.HBM)
VMEM_SPEC = pl.BlockSpec(memory_space=pltpu.VMEM)
SMEM_SPEC = pl.BlockSpec(memory_space=pltpu.SMEM)


WINDOW = 128


def call(kernel, outs, *args, streamed=(), kept=(), scalars=(), flops=0, scratch=(), room=0):
    size = sum(math.prod(a.shape) * a.dtype.itemsize for a in args)
    places = {i: pltpu.HBM for i in streamed} | {i: pltpu.VMEM for i in kept}
    specs = [
        HBM_SPEC if i in streamed else SMEM_SPEC if i in scalars else VMEM_SPEC
        for i in range(len(args))
    ]
    return pl.pallas_call(
        kernel,
        out_shape=outs,
        in_specs=specs,
        out_specs=[VMEM_SPEC] * len(outs),
        scratch_shapes=list(scratch),
        compiler_params=pltpu.CompilerParams(vmem_limit_bytes=VMEM_BYTES + room),
        cost_estimate=pl.CostEstimate(flops=flops, bytes_accessed=size, transcendentals=0),
    )(*[
        pltpu.with_memory_space_constraint(a, places[i]) if i in places else a
        for i, a in enumerate(args)
    ])


class Stream:
    def __init__(self, copies):
        self.copies = copies
        self.done = 0
        for copy in copies[:WINDOW]:
            copy.start()

    def wait(self, count):
        while self.done < count:
            self.copies[self.done].wait()
            self.done += 1
            if self.done + WINDOW <= len(self.copies):
                self.copies[self.done + WINDOW - 1].start()


def struct(shape, dtype):
    return jax.ShapeDtypeStruct(shape, dtype)


def this_core():
    return lax.axis_index("dp") % 2


def span(start, size):
    return pl.ds(pl.multiple_of(start, size), size)


def softmax_kernel(logits_ref, out_ref, probs_ref):
    devices, _, part = out_ref.shape
    x = logits_ref[...].astype(F32)
    e = jnp.exp(x - jnp.max(x, axis=-1, keepdims=True))
    probs = e * (1.0 / jnp.sum(e, axis=-1, keepdims=True))
    probs_ref[...] = probs
    for d in range(devices):
        out_ref[d] = probs[:, d * part : (d + 1) * part].astype(BF16)


def final_kernel(probs_ref, back_ref, counts_ref, out_ref, rewards_ref, d_ref):
    devices, _, padded = back_ref.shape
    part = out_ref.shape[1] // devices
    requests = counts_ref.shape[1]
    sums = jnp.zeros((1, requests), F32)
    for d in range(devices):
        block = back_ref[d].astype(F32)
        d_ref[:, d * part : (d + 1) * part] = block[:, :part]
        for i in range(3):
            start = part + i * requests
            sums += block[:1, start : start + requests]
    rewards_ref[...] = sums / counts_ref[...]
    probs, d_probs = probs_ref[...], d_ref[...]
    mean = jnp.sum(probs * d_probs, axis=-1, keepdims=True)
    out_ref[...] = (math.sqrt(VOC) * (probs * (d_probs - mean))).astype(BF16)


def valid_column(counts, total):
    requests = counts.shape[1]
    length = total // requests
    position = lax.broadcasted_iota(jnp.int32, (total, requests), 0)
    start = length * lax.broadcasted_iota(jnp.int32, (total, requests), 1)
    inside = (position >= start) & (position < start + counts)
    return jnp.sum(jnp.where(inside, 1.0, 0.0), axis=-1, keepdims=True)


def bring(source_ref, out_ref, sems, columns):
    fine = 128
    return [
        pltpu.make_async_copy(
            source_ref.at[pl.ds(i, fine), columns], out_ref.at[pl.ds(i, fine)], sems.at[i // fine]
        )
        for i in range(0, out_ref.shape[0], fine)
    ]


def ready_kernel(split, source_ref, after_ref, out_ref, sems):
    del after_ref
    width = out_ref.shape[1]
    columns = span((1 - this_core()) * width, width) if split else pl.ds(0, width)
    copies = bring(source_ref, out_ref, sems, columns)
    for copy in copies:
        copy.start()
    for copy in copies:
        copy.wait()


def first_rows(rows, source, after, split):
    width = source.shape[1] // 2 if split else source.shape[1]
    return call(
        functools.partial(ready_kernel, split), [pltpu.VMEM((rows, width), source.dtype)],
        source, after, streamed=(0,), scratch=(pltpu.SemaphoreType.DMA((rows // 128,)),),
    )[0]


def half_kernel(other, slices_ref, embed_ref, head_ref, *rest):
    if other:
        ready_ref = None
        out_ref, score_ref, next_ref, table, acc, sems, next_sems = rest
    else:
        ready_ref, out_ref, score_ref, table, acc, sems = rest
    chips, total, own = out_ref.shape
    part, ready = embed_ref.shape[0], 0 if other else ready_ref.shape[0]
    core = this_core()
    half = (1 - core) if other else core
    columns = span(half * chips * own, chips * own)
    tile, fine = 256, 128
    stream = Stream([
        pltpu.make_async_copy(
            embed_ref.at[pl.ds(i, min(fine, part - i)), columns],
            table.at[pl.ds(i - ready, min(fine, part - i))],
            sems.at[i // fine],
        )
        for i in range(ready, part, fine)
    ])
    following = []
    if other:
        following = bring(embed_ref, next_ref, next_sems, span(core * chips * own, chips * own))
        for copy in following:
            copy.start()
        acc[...] = jnp.zeros_like(acc)
    else:
        acc[...] = jnp.dot(slices_ref[:, :ready], ready_ref[...], preferred_element_type=F32)
    for start in range(ready, part, tile):
        end = min(start + tile, part)
        stream.wait(-(-(end - ready) // fine))
        acc[...] += jnp.dot(
            slices_ref[:, start:end], table[start - ready : end - ready],
            preferred_element_type=F32,
        )
    score_ref[...] = jnp.sum(
        acc[...] * head_ref[:, columns].astype(F32), axis=-1, keepdims=True
    )
    for j in range(chips):
        out_ref[j] = acc[:, j * own : (j + 1) * own].astype(out_ref.dtype)
    for copy in following:
        copy.wait()


def early_kernel(
    head_ref, down_ref, after_ref, out_ref, head_row, table, head_copy, sems, head_sem
):
    del after_ref
    width, lanes = down_ref.shape[1], 128

    def copy(j):
        rows = span(j * lanes, lanes)
        return pltpu.make_async_copy(down_ref.at[rows], table.at[rows], sems.at[j])

    steps = sems.shape[0]
    bring_head = pltpu.make_async_copy(head_ref, head_copy, head_sem)
    bring_head.start()
    for j in range(steps):
        copy(j).start()
    bring_head.wait()
    head = head_copy[...].astype(F32).reshape(1, width)
    head_row[...] = head

    def step(j, _):
        copy(j).wait()
        rows = span(j * lanes, lanes)
        total = jnp.zeros((lanes, lanes), F32)
        for k in range(0, width, lanes):
            total += table[rows, k : k + lanes].astype(F32) * head[:, k : k + lanes]
        out_ref[:, rows] = jnp.sum(total.T, axis=0, keepdims=True)
        return 0

    lax.fori_loop(0, steps, step, 0)


def bring_blocks(gate_ref, up_ref, both, half, blocks, own, chips, sems):
    hidden = gate_ref.shape[1]
    return [
        pltpu.make_async_copy(
            source.at[span((half * chips + j) * own, own)],
            both.at[pl.ds((j - blocks[0]) * own, own), pl.ds(k * hidden, hidden)],
            sems.at[k, j - blocks[0]],
        )
        for j in blocks
        for k, source in enumerate((gate_ref, up_ref))
    ]


def weight_rows(ready, both, own):
    skip = ready.shape[0] // own if ready is not None else 0

    def weights(j):
        if j < skip:
            return ready[j * own : (j + 1) * own]
        return both[(j - skip) * own : (j - skip + 1) * own]

    return skip, weights


def forward_half(x_ref, gain_ref, half, sums, weights, wait):
    chips, _, own = x_ref.shape
    products, squares = sums
    scaled = []
    wide = jnp.zeros(x_ref.shape[1:], F32)
    for j in range(chips):
        x = x_ref[j].astype(F32)
        wide = wide + x * x
        gain = gain_ref[:, span((half * chips + j) * own, own)].astype(F32)
        scaled.append((x * gain).astype(BF16))
    squares = squares + jnp.sum(wide, axis=-1, keepdims=True)
    for j in range(chips):
        wait(j)
        products = products + jnp.dot(scaled[j], weights(j), preferred_element_type=F32)
    return products, squares


def backward_half(d_both, weights, out_ref):
    contract = (((1,), (1,)), ((), ()))
    for j in range(out_ref.shape[0]):
        part = lax.dot_general(d_both, weights(j), contract, preferred_element_type=F32)
        out_ref[j] = part.astype(out_ref.dtype)


def first_kernel(
    x_ref, gain_ref, gate_ref, up_ref, counts_ref,
    products_ref, squares_ref, valid_ref, counts_row, both, ahead, sems, ahead_sems,
):
    chips, _, own = x_ref.shape
    core = this_core()
    skip, weights = weight_rows(None, both, own)
    blocks = range(skip, chips)
    stream = Stream(bring_blocks(gate_ref, up_ref, both, core, blocks, own, chips, sems))
    blocks = range(ahead.shape[0] // own)
    following = bring_blocks(gate_ref, up_ref, ahead, 1 - core, blocks, own, chips, ahead_sems)
    for copy in following:
        copy.start()
    counts = counts_ref[...]
    valid_ref[...] = valid_column(counts, valid_ref.shape[0])
    counts_row[...] = counts.astype(F32)
    sums = (jnp.zeros(products_ref.shape, F32), jnp.zeros(squares_ref.shape, F32))
    products_ref[...], squares_ref[...] = forward_half(
        x_ref, gain_ref, core, sums, weights, lambda j: stream.wait(2 * (j - skip + 1))
    )
    for copy in following:
        copy.wait()


def second_kernel(
    x_ref, gain_ref, gate_ref, up_ref, ready_ref, products_ref, squares_ref, down_ref, valid_ref,
    send_ref, score_ref, inv_ref, d_both_ref, both, sems,
):
    chips, total, own = x_ref.shape
    width, hidden = gate_ref.shape
    half = 1 - this_core()
    skip, weights = weight_rows(ready_ref, both, own)
    blocks = range(skip, chips)
    stream = Stream(bring_blocks(gate_ref, up_ref, both, half, blocks, own, chips, sems))
    sums = (products_ref[...], squares_ref[...])
    products, squares = forward_half(
        x_ref, gain_ref, half, sums, weights, lambda j: stream.wait(2 * (j - skip + 1))
    )
    inv = lax.rsqrt(squares / width + 1e-05)
    inv_ref[...] = inv
    a, b = products[:, :hidden] * inv, products[:, hidden:] * inv
    sigma = jax.nn.sigmoid(a)
    active = a * sigma
    down = down_ref[...]
    rounded = (active * b).astype(BF16).astype(F32)
    score_ref[...] = jnp.sum(rounded * down, axis=-1, keepdims=True)
    d_hidden = valid_ref[...] * down
    d_both_ref[:, :hidden] = (d_hidden * b * sigma * (1.0 + a * (1.0 - sigma))).astype(BF16)
    d_both_ref[:, hidden:] = (d_hidden * active).astype(BF16)
    backward_half(d_both_ref[...], weights, send_ref)


def third_kernel(d_both_ref, both_ref, keep_ref):
    _, weights = weight_rows(None, both_ref, keep_ref.shape[2])
    backward_half(d_both_ref[...], weights, keep_ref)


def input_kernel(
    mine_ref, got_ref, d_mine_ref, d_got_ref, gain_ref, head_ref, inv_ref,
    score_a_ref, score_b_ref, score_c_ref, valid_ref, counts_ref, ready_ref, embed_ref,
    out_ref, dx_ref, table, sems,
):
    chips, total, own = mine_ref.shape
    voc = embed_ref.shape[0]
    requests = counts_ref.shape[1]
    width = 2 * chips * own
    core = this_core()
    ready = ready_ref.shape[0]
    tile, fine = 256, 64
    steps = (voc - ready) // tile
    last = ready + steps * tile

    def copy(start, size):
        return pltpu.make_async_copy(
            embed_ref.at[pl.ds(start, size)],
            table.at[pl.ds(start - ready, size)],
            sems.at[start // fine],
        )

    def pieces(start, end):
        return [copy(start + i, min(fine, end - start - i)) for i in range(0, end - start, fine)]

    def step_pieces(j):
        start = pl.multiple_of(ready + j * tile, fine)
        return [copy(pl.multiple_of(start + i, fine), fine) for i in range(0, tile, fine)]

    for piece in pieces(ready, voc):
        piece.start()
    sources = ((mine_ref, d_mine_ref, core), (got_ref, d_got_ref, 1 - core))
    wide = jnp.zeros((total, own), F32)
    for x_ref, d_ref, half in sources:
        for j in range(chips):
            gain = gain_ref[:, span((half * chips + j) * own, own)].astype(F32)
            wide += d_ref[j].astype(F32) * gain * x_ref[j].astype(F32)
    inv = inv_ref[...]
    weight = inv * inv * inv * (jnp.sum(wide, axis=-1, keepdims=True) / width)
    valid = valid_ref[...]
    request = lax.broadcasted_iota(jnp.int32, (total, requests), 0) // (total // requests)
    for x_ref, d_ref, half in sources:
        for j in range(chips):
            columns = span((half * chips + j) * own, own)
            x = x_ref[j].astype(F32)
            g = d_ref[j].astype(F32) * gain_ref[:, columns].astype(F32)
            dx = inv * g - x * weight
            dx_ref[:, columns] = (dx + valid * head_ref[:, columns].astype(F32)).astype(BF16)
    score = valid * (score_a_ref[...] + score_b_ref[...] + score_c_ref[...])
    member = request == lax.broadcasted_iota(jnp.int32, (total, requests), 1)
    value = jnp.sum(jnp.where(member, score, 0.0), axis=0, keepdims=True)
    parts = []
    for _ in range(3):
        piece = value.astype(BF16).astype(F32)
        parts.append(piece)
        value = value - piece
    for i, piece in enumerate(parts):
        start = voc + i * requests
        spread = jnp.broadcast_to(piece, (total, requests)).astype(BF16)
        out_ref[:, start : start + requests] = spread
    contract = (((1,), (1,)), ((), ()))

    def product(weights):
        return lax.dot_general(
            dx_ref[...], weights, contract, preferred_element_type=F32
        ).astype(BF16)

    out_ref[:, :ready] = product(ready_ref[...])

    def step(j, _):
        for piece in step_pieces(j):
            piece.wait()

        rows = pl.ds(pl.multiple_of(j * tile, tile), tile)
        out_ref[:, pl.ds(pl.multiple_of(ready + j * tile, tile), tile)] = product(table[rows, :])
        return 0

    lax.fori_loop(0, steps, step, 0)
    if last < voc:
        for piece in pieces(last, voc):
            piece.wait()
        out_ref[:, last:voc] = product(table[last - ready :, :])


def swap_sum(send, keep, devices):
    return (keep.astype(F32) + swap_cores(send, devices).astype(F32)).astype(BF16)


def chip_sum(half, devices):
    return jnp.sum(exchange_chips(half, devices).astype(F32), axis=0).astype(BF16)


def chip_gather(total, devices):
    return exchange_chips(jnp.broadcast_to(total[None], (devices // 2,) + total.shape), devices)


def pick(blocks, index):
    return lax.dynamic_index_in_dim(blocks, index, 0, keepdims=False)


def split_halves(part, devices):
    total, width = part.shape
    core = lax.axis_index("dp") % 2
    blocks = part.reshape(total, 2, devices // 2, width // devices).transpose(1, 2, 0, 3)
    return pick(blocks, 1 - core).astype(BF16), pick(blocks, core)


def join_halves(mine, got):
    core = lax.axis_index("dp") % 2
    blocks = jnp.where(core == 1, jnp.stack([got, mine]), jnp.stack([mine, got]))
    _, chips, total, own = blocks.shape
    return blocks.transpose(2, 0, 1, 3).reshape(total, 2 * chips * own).astype(F32)


def norm_scale(x0):
    return lax.rsqrt(jnp.mean(x0 * x0, axis=-1, keepdims=True) + 1e-05)


def plain_half(slices, embed, head_row, devices):
    part = jnp.dot(slices, embed, preferred_element_type=F32)
    score = jnp.sum(part * head_row.astype(F32), axis=-1, keepdims=True)
    return *split_halves(part, devices), score


def plain_hidden(mine, got, gain_row, w_gate, w_up, down, valid, devices):
    x0 = join_halves(mine, got)
    normed = (x0 * norm_scale(x0) * gain_row.astype(F32)).astype(BF16)
    a = jnp.dot(normed, w_gate, preferred_element_type=F32)
    b = jnp.dot(normed, w_up, preferred_element_type=F32)
    sigma = jax.nn.sigmoid(a)
    active = a * sigma
    hidden = (active * b).astype(BF16).astype(F32)
    d_hidden = valid * down
    d_gate = (d_hidden * b * sigma * (1.0 + a * (1.0 - sigma))).astype(BF16)
    d_up = (d_hidden * active).astype(BF16)
    part = jnp.einsum("tf,df->td", d_gate, w_gate, preferred_element_type=F32)
    part = part + jnp.einsum("tf,df->td", d_up, w_up, preferred_element_type=F32)
    return *split_halves(part, devices), jnp.sum(hidden * down, axis=-1, keepdims=True)


def plain_input(mine, got, d_mine, d_got, gain_row, head_row, valid, embed):
    x0 = join_halves(mine, got)
    inv = norm_scale(x0)
    scaled = join_halves(d_mine, d_got) * gain_row.astype(F32)
    dx = inv * scaled - x0 * inv * inv * inv * jnp.mean(scaled * x0, axis=-1, keepdims=True)
    dx = (dx + valid * head_row.astype(F32)).astype(BF16)
    return jnp.einsum("td,vd->tv", dx, embed, preferred_element_type=F32).astype(BF16)


def body(logits, embed, norm_gain, w_gate, w_up, w_down, head, counts):
    devices = lax.axis_size("dp")
    rows, voc = logits.shape
    part = voc // devices
    width = embed.shape[1]
    hidden = w_gate.shape[1]
    own, chips = width // devices, devices // 2
    requests = counts.shape[0]
    total = rows * devices
    request_len = total // requests
    tiled = own % 128 == 0 and hidden % 128 == 0 and total % 16 == 0 and part % 16 == 0 and part > 512
    head_row, gain_row = head.reshape(1, width), norm_gain.reshape(1, width)
    if tiled:
        blocked, probs = call(
            softmax_kernel,
            [struct((devices, rows, part), BF16), pltpu.VMEM((rows, voc), F32)], logits,
        )
    else:
        probs32 = jax.nn.softmax(logits.astype(F32), axis=-1)
        blocked = probs32.astype(BF16).reshape(rows, devices, part).transpose(1, 0, 2)
    slices = exchange(blocked).reshape(total, part)
    column = struct((total, 1), F32)
    half = (chips, total, own)
    flops = total * part * width
    if tiled:
        ready = 256
        down_row, head32 = call(
            early_kernel, [struct((1, hidden), F32), struct((1, width), F32)],
            head, w_down, blocked,
            streamed=(0, 1), flops=2 * hidden * width, room=2 * hidden * width,
            scratch=(
                pltpu.VMEM((hidden, width), BF16), pltpu.VMEM((width,), BF16),
                pltpu.SemaphoreType.DMA((hidden // 128,)), pltpu.SemaphoreType.DMA,
            ),
        )
        ready = 256
        args = dict(streamed=(1,), flops=flops, room=part * width)
        acc = pltpu.VMEM((total, width // 2), F32)
        sems = pltpu.SemaphoreType.DMA((-(-part // 128),))
        send, score_a, first = call(
            functools.partial(half_kernel, True),
            [struct(half, BF16), column, pltpu.VMEM((ready, width // 2), BF16)],
            slices, embed, head32,
            scratch=(
                pltpu.VMEM((part, width // 2), BF16), acc, sems,
                pltpu.SemaphoreType.DMA((ready // 128,)),
            ),
            **args,
        )
        keep, score_b = call(
            functools.partial(half_kernel, False), [struct(half, F32), column],
            slices, embed, head32, first, kept=(3,),
            scratch=(pltpu.VMEM((part - ready, width // 2), BF16), acc, sems), **args,
        )
    else:
        send, keep, score_a = plain_half(slices, embed, head_row, devices)
    summed = swap_sum(send, keep, devices)
    x_mine = chip_gather(chip_sum(summed, devices), devices)
    x_got = swap_cores(x_mine, devices)
    if tiled:
        sems, ahead_sems = pltpu.SemaphoreType.DMA((2, chips)), pltpu.SemaphoreType.DMA((2, 2))
        args = dict(streamed=(2, 3), flops=2 * total * hidden * width, room=2 * width * hidden)
        products, squares, valid, counts_row, both, ahead = call(
            first_kernel,
            [
                struct((total, 2 * hidden), F32), column, column, struct((1, requests), F32),
                pltpu.VMEM((width // 2, 2 * hidden), BF16), pltpu.VMEM((2 * own, 2 * hidden), BF16),
            ],
            x_mine, gain_row, w_gate, w_up, counts.reshape(1, requests),
            scratch=(sems, ahead_sems), **args,
        )
        send, score_c, inv, d_both = call(
            second_kernel,
            [struct(half, BF16), column, column, struct((total, 2 * hidden), BF16)],
            x_got, gain_row, w_gate, w_up, ahead, products, squares, down_row, valid,
            scratch=(pltpu.VMEM((width // 2 - 2 * own, 2 * hidden), BF16), sems), kept=(4,), **args,
        )
        (keep,) = call(
            third_kernel, [struct(half, F32)], d_both, both,
            kept=(1,), flops=2 * total * hidden * width,
        )
    else:
        down_row = jnp.sum(w_down.astype(F32) * head.astype(F32)[None, :], axis=-1)[None]
        position = jnp.arange(total, dtype=jnp.int32)[:, None]
        member = position // request_len == jnp.arange(requests, dtype=jnp.int32)[None, :]
        limit = jnp.sum(jnp.where(member, counts[None, :], 0), axis=-1, keepdims=True)
        valid = (position % request_len < limit).astype(F32)
        send, keep, score_c = plain_hidden(
            x_mine, x_got, gain_row, w_gate, w_up, down_row, valid, devices
        )
    total_d = chip_sum(swap_sum(send, keep, devices), devices)
    d_mine = chip_gather(total_d, devices)
    d_got = swap_cores(d_mine, devices)
    padded = part + 3 * requests
    if tiled:
        first = first_rows(256, embed, total_d, False)
        (d_slices,) = call(
            input_kernel, [struct((total, padded), BF16)],
            x_mine, x_got, d_mine, d_got, gain_row, head32, inv,
            score_a, score_b, score_c, valid, counts_row, first, embed,
            kept=(12,), streamed=(13,), flops=2 * flops, room=2 * part * width,
            scratch=(
                pltpu.VMEM((total, width), BF16), pltpu.VMEM((part - 256, width), BF16),
                pltpu.SemaphoreType.DMA((-(-part // 64),)),
            ),
        )
    else:
        d_slices = plain_input(x_mine, x_got, d_mine, d_got, gain_row, head_row, valid, embed)
        score = jnp.where(member, valid * (score_a + score_c), 0.0)
        extra = split3(jnp.sum(score, axis=0)).reshape(1, requests * 3)
        extra = jnp.broadcast_to(extra, (total, requests * 3))
        d_slices = jnp.concatenate([d_slices, extra], axis=-1)
    back = exchange(d_slices.reshape(devices, rows, padded))
    if tiled:
        guidance, rewards = call(
            final_kernel, [struct((rows, voc), BF16), struct((1, requests), F32)],
            probs, back, counts_row, kept=(0,),
            scratch=(pltpu.VMEM((rows, voc), F32),),
        )
        return (guidance, rewards.reshape(requests))
    sums = jnp.sum(back[:, 0, part:].astype(F32).reshape(devices, requests, 3), axis=(0, 2))
    rewards = sums / counts.astype(F32)
    d_probs = back[:, :, :part].transpose(1, 0, 2).reshape(rows, voc).astype(F32)
    d_logits = probs32 * (d_probs - jnp.sum(probs32 * d_probs, axis=-1, keepdims=True))
    guidance = (math.sqrt(VOC) * d_logits).astype(BF16)
    return (guidance, rewards)


def solution(mesh):
    placed = (
        P(("groups", "dp"), None),
        P("dp", None),
        P(),
        P(None, "dp"),
        P(None, "dp"),
        P("dp", None),
        P(),
        P("groups"),
    )
    return jax.shard_map(
        body,
        mesh=mesh,
        in_specs=placed,
        out_specs=(P(("groups", "dp"), None), P("groups")),
        check_vma=False,
    )
```

```python
import functools
import math

import jax
import jax.numpy as jnp
from jax import lax
from jax.experimental import pallas as pl
from jax.experimental.pallas import tpu as pltpu
from jax.sharding import PartitionSpec as P

VOC = 32000
F32, BF16 = jnp.float32, jnp.bfloat16
VMEM_BYTES = 12 * 1024 * 1024


def swap_cores(value, devices):
    return lax.ppermute(value, "dp", [(i, i ^ 1) for i in range(devices)])


def exchange(blocks):
    return lax.all_to_all(blocks, "dp", split_axis=0, concat_axis=0, tiled=True)


def exchange_chips(blocks, devices):
    groups = [list(range(core, devices, 2)) for core in range(2)]
    return lax.all_to_all(
        blocks, "dp", split_axis=0, concat_axis=0, axis_index_groups=groups, tiled=True
    )


def split3(value):
    hi = lax.reduce_precision(value, 8, 7)
    rest = value - hi
    mid = lax.reduce_precision(rest, 8, 7)
    low = rest - mid
    return jnp.stack([hi, mid, low], axis=-1).astype(BF16)


HBM_SPEC = pl.BlockSpec(memory_space=pltpu.HBM)
VMEM_SPEC = pl.BlockSpec(memory_space=pltpu.VMEM)
SMEM_SPEC = pl.BlockSpec(memory_space=pltpu.SMEM)


WINDOW = 128


def call(kernel, outs, *args, streamed=(), kept=(), scalars=(), flops=0, scratch=(), room=0):
    size = sum(math.prod(a.shape) * a.dtype.itemsize for a in args)
    places = {i: pltpu.HBM for i in streamed} | {i: pltpu.VMEM for i in kept}
    specs = [
        HBM_SPEC if i in streamed else SMEM_SPEC if i in scalars else VMEM_SPEC
        for i in range(len(args))
    ]
    return pl.pallas_call(
        kernel,
        out_shape=outs,
        in_specs=specs,
        out_specs=[VMEM_SPEC] * len(outs),
        scratch_shapes=list(scratch),
        compiler_params=pltpu.CompilerParams(vmem_limit_bytes=VMEM_BYTES + room),
        cost_estimate=pl.CostEstimate(flops=flops, bytes_accessed=size, transcendentals=0),
    )(*[
        pltpu.with_memory_space_constraint(a, places[i]) if i in places else a
        for i, a in enumerate(args)
    ])


class Stream:
    def __init__(self, copies):
        self.copies = copies
        self.done = 0
        for copy in copies[:WINDOW]:
            copy.start()

    def wait(self, count):
        while self.done < count:
            self.copies[self.done].wait()
            self.done += 1
            if self.done + WINDOW <= len(self.copies):
                self.copies[self.done + WINDOW - 1].start()


def struct(shape, dtype):
    return jax.ShapeDtypeStruct(shape, dtype)


def this_core():
    return lax.axis_index("dp") % 2


def span(start, size):
    return pl.ds(pl.multiple_of(start, size), size)


def softmax_kernel(logits_ref, out_ref, probs_ref):
    devices, _, part = out_ref.shape
    x = logits_ref[...].astype(F32)
    e = jnp.exp(x - jnp.max(x, axis=-1, keepdims=True))
    probs = e * (1.0 / jnp.sum(e, axis=-1, keepdims=True))
    probs_ref[...] = probs
    for d in range(devices):
        out_ref[d] = probs[:, d * part : (d + 1) * part].astype(BF16)


def final_kernel(probs_ref, back_ref, counts_ref, out_ref, rewards_ref, d_ref):
    devices, _, padded = back_ref.shape
    part = out_ref.shape[1] // devices
    requests = counts_ref.shape[1]
    sums = jnp.zeros((1, requests), F32)
    for d in range(devices):
        block = back_ref[d].astype(F32)
        d_ref[:, d * part : (d + 1) * part] = block[:, :part]
        for i in range(3):
            start = part + i * requests
            sums += block[:1, start : start + requests]
    rewards_ref[...] = sums / counts_ref[...]
    probs, d_probs = probs_ref[...], d_ref[...]
    mean = jnp.sum(probs * d_probs, axis=-1, keepdims=True)
    out_ref[...] = (math.sqrt(VOC) * (probs * (d_probs - mean))).astype(BF16)


def valid_column(counts, total):
    requests = counts.shape[1]
    length = total // requests
    position = lax.broadcasted_iota(jnp.int32, (total, requests), 0)
    start = length * lax.broadcasted_iota(jnp.int32, (total, requests), 1)
    inside = (position >= start) & (position < start + counts)
    return jnp.sum(jnp.where(inside, 1.0, 0.0), axis=-1, keepdims=True)


def bring(source_ref, out_ref, sems, columns):
    fine = 128
    return [
        pltpu.make_async_copy(
            source_ref.at[pl.ds(i, fine), columns], out_ref.at[pl.ds(i, fine)], sems.at[i // fine]
        )
        for i in range(0, out_ref.shape[0], fine)
    ]


def ready_kernel(split, source_ref, after_ref, out_ref, sems):
    del after_ref
    width = out_ref.shape[1]
    columns = span((1 - this_core()) * width, width) if split else pl.ds(0, width)
    copies = bring(source_ref, out_ref, sems, columns)
    for copy in copies:
        copy.start()
    for copy in copies:
        copy.wait()


def first_rows(rows, source, after, split):
    width = source.shape[1] // 2 if split else source.shape[1]
    return call(
        functools.partial(ready_kernel, split), [pltpu.VMEM((rows, width), source.dtype)],
        source, after, streamed=(0,), scratch=(pltpu.SemaphoreType.DMA((rows // 128,)),),
    )[0]


def half_kernel(other, slices_ref, embed_ref, head_ref, *rest):
    if other:
        ready_ref = None
        out_ref, score_ref, next_ref, table, acc, sems, next_sems = rest
    else:
        ready_ref, out_ref, score_ref, table, acc, sems = rest
    chips, total, own = out_ref.shape
    part, ready = embed_ref.shape[0], 0 if other else ready_ref.shape[0]
    core = this_core()
    half = (1 - core) if other else core
    columns = span(half * chips * own, chips * own)
    tile, fine = 256, 128
    stream = Stream([
        pltpu.make_async_copy(
            embed_ref.at[pl.ds(i, min(fine, part - i)), columns],
            table.at[pl.ds(i - ready, min(fine, part - i))],
            sems.at[i // fine],
        )
        for i in range(ready, part, fine)
    ])
    following = []
    if other:
        following = bring(embed_ref, next_ref, next_sems, span(core * chips * own, chips * own))
        for copy in following:
            copy.start()
        acc[...] = jnp.zeros_like(acc)
    else:
        acc[...] = jnp.dot(slices_ref[:, :ready], ready_ref[...], preferred_element_type=F32)
    for start in range(ready, part, tile):
        end = min(start + tile, part)
        stream.wait(-(-(end - ready) // fine))
        acc[...] += jnp.dot(
            slices_ref[:, start:end], table[start - ready : end - ready],
            preferred_element_type=F32,
        )
    score_ref[...] = jnp.sum(
        acc[...] * head_ref[:, columns].astype(F32), axis=-1, keepdims=True
    )
    for j in range(chips):
        out_ref[j] = acc[:, j * own : (j + 1) * own].astype(out_ref.dtype)
    for copy in following:
        copy.wait()


def early_kernel(
    head_ref, down_ref, after_ref, out_ref, head_row, table, head_copy, sems, head_sem
):
    del after_ref
    width, lanes = down_ref.shape[1], 128
    steps = sems.shape[0]
    skip = lax.axis_index("groups") * (down_ref.shape[0] // lanes - steps)

    def copy(j):
        source = down_ref.at[span((skip + j) * lanes, lanes)]
        return pltpu.make_async_copy(source, table.at[span(j * lanes, lanes)], sems.at[j])

    bring_head = pltpu.make_async_copy(head_ref, head_copy, head_sem)
    bring_head.start()
    for j in range(steps):
        copy(j).start()
    bring_head.wait()
    head = head_copy[...].astype(F32).reshape(1, width)
    head_row[...] = head

    def step(j, _):
        copy(j).wait()
        rows = span(j * lanes, lanes)
        total = jnp.zeros((lanes, lanes), F32)
        for k in range(0, width, lanes):
            total += table[rows, k : k + lanes].astype(F32) * head[:, k : k + lanes]
        out_ref[:, rows] = jnp.sum(total.T, axis=0, keepdims=True)
        return 0

    lax.fori_loop(0, steps, step, 0)


def bring_blocks(gate_ref, up_ref, both, half, blocks, own, chips, sems):
    hidden = gate_ref.shape[1]
    return [
        pltpu.make_async_copy(
            source.at[span((half * chips + j) * own, own)],
            both.at[pl.ds((j - blocks[0]) * own, own), pl.ds(k * hidden, hidden)],
            sems.at[k, j - blocks[0]],
        )
        for j in blocks
        for k, source in enumerate((gate_ref, up_ref))
    ]


def weight_rows(ready, both, own):
    skip = ready.shape[0] // own if ready is not None else 0

    def weights(j):
        if j < skip:
            return ready[j * own : (j + 1) * own]
        return both[(j - skip) * own : (j - skip + 1) * own]

    return skip, weights


def forward_half(x_ref, gain_ref, half, sums, weights, wait):
    chips, _, own = x_ref.shape
    products, squares = sums
    scaled = []
    wide = jnp.zeros(x_ref.shape[1:], F32)
    for j in range(chips):
        x = x_ref[j].astype(F32)
        wide = wide + x * x
        gain = gain_ref[:, span((half * chips + j) * own, own)].astype(F32)
        scaled.append((x * gain).astype(BF16))
    squares = squares + jnp.sum(wide, axis=-1, keepdims=True)
    for j in range(chips):
        wait(j)
        products = products + jnp.dot(scaled[j], weights(j), preferred_element_type=F32)
    return products, squares


def backward_half(d_both, weights, out_ref):
    contract = (((1,), (1,)), ((), ()))
    for j in range(out_ref.shape[0]):
        part = lax.dot_general(d_both, weights(j), contract, preferred_element_type=F32)
        out_ref[j] = part.astype(out_ref.dtype)


def first_kernel(
    x_ref, gain_ref, gate_ref, up_ref, counts_ref,
    products_ref, squares_ref, valid_ref, counts_row, both, ahead, sems, ahead_sems,
):
    chips, _, own = x_ref.shape
    core = this_core()
    skip, weights = weight_rows(None, both, own)
    blocks = range(skip, chips)
    stream = Stream(bring_blocks(gate_ref, up_ref, both, core, blocks, own, chips, sems))
    blocks = range(ahead.shape[0] // own)
    following = bring_blocks(gate_ref, up_ref, ahead, 1 - core, blocks, own, chips, ahead_sems)
    for copy in following:
        copy.start()
    counts = counts_ref[...]
    valid_ref[...] = valid_column(counts, valid_ref.shape[0])
    counts_row[...] = counts.astype(F32)
    sums = (jnp.zeros(products_ref.shape, F32), jnp.zeros(squares_ref.shape, F32))
    products_ref[...], squares_ref[...] = forward_half(
        x_ref, gain_ref, core, sums, weights, lambda j: stream.wait(2 * (j - skip + 1))
    )
    for copy in following:
        copy.wait()


def second_kernel(
    x_ref, gain_ref, gate_ref, up_ref, ready_ref, products_ref, squares_ref, down_a, down_b, valid_ref,
    send_ref, score_ref, inv_ref, d_both_ref, both, sems,
):
    chips, total, own = x_ref.shape
    width, hidden = gate_ref.shape
    half = 1 - this_core()
    skip, weights = weight_rows(ready_ref, both, own)
    blocks = range(skip, chips)
    stream = Stream(bring_blocks(gate_ref, up_ref, both, half, blocks, own, chips, sems))
    sums = (products_ref[...], squares_ref[...])
    products, squares = forward_half(
        x_ref, gain_ref, half, sums, weights, lambda j: stream.wait(2 * (j - skip + 1))
    )
    inv = lax.rsqrt(squares / width + 1e-05)
    inv_ref[...] = inv
    a, b = products[:, :hidden] * inv, products[:, hidden:] * inv
    sigma = jax.nn.sigmoid(a)
    active = a * sigma
    first_group = lax.axis_index("groups") == 0
    down = jnp.where(first_group, down_a[...], down_b[...])
    rest = jnp.where(first_group, down_b[...], down_a[...])
    down = jnp.concatenate([down, rest[:, 2 * rest.shape[1] - hidden :]], axis=-1)
    rounded = (active * b).astype(BF16).astype(F32)
    score_ref[...] = jnp.sum(rounded * down, axis=-1, keepdims=True)
    d_hidden = valid_ref[...] * down
    d_both_ref[:, :hidden] = (d_hidden * b * sigma * (1.0 + a * (1.0 - sigma))).astype(BF16)
    d_both_ref[:, hidden:] = (d_hidden * active).astype(BF16)
    backward_half(d_both_ref[...], weights, send_ref)


def third_kernel(d_both_ref, both_ref, keep_ref):
    _, weights = weight_rows(None, both_ref, keep_ref.shape[2])
    backward_half(d_both_ref[...], weights, keep_ref)


def input_kernel(
    mine_ref, got_ref, d_mine_ref, d_got_ref, gain_ref, head_ref, inv_ref,
    score_a_ref, score_b_ref, score_c_ref, valid_ref, counts_ref, ready_ref, embed_ref,
    out_ref, dx_ref, table, sems,
):
    chips, total, own = mine_ref.shape
    voc = embed_ref.shape[0]
    requests = counts_ref.shape[1]
    width = 2 * chips * own
    core = this_core()
    ready = ready_ref.shape[0]
    tile, fine = 256, 64
    steps = (voc - ready) // tile
    last = ready + steps * tile

    def copy(start, size):
        return pltpu.make_async_copy(
            embed_ref.at[pl.ds(start, size)],
            table.at[pl.ds(start - ready, size)],
            sems.at[start // fine],
        )

    def pieces(start, end):
        return [copy(start + i, min(fine, end - start - i)) for i in range(0, end - start, fine)]

    def step_pieces(j):
        start = pl.multiple_of(ready + j * tile, fine)
        return [copy(pl.multiple_of(start + i, fine), fine) for i in range(0, tile, fine)]

    for piece in pieces(ready, voc):
        piece.start()
    sources = ((mine_ref, d_mine_ref, core), (got_ref, d_got_ref, 1 - core))
    wide = jnp.zeros((total, own), F32)
    for x_ref, d_ref, half in sources:
        for j in range(chips):
            gain = gain_ref[:, span((half * chips + j) * own, own)].astype(F32)
            wide += d_ref[j].astype(F32) * gain * x_ref[j].astype(F32)
    inv = inv_ref[...]
    weight = inv * inv * inv * (jnp.sum(wide, axis=-1, keepdims=True) / width)
    valid = valid_ref[...]
    request = lax.broadcasted_iota(jnp.int32, (total, requests), 0) // (total // requests)
    for x_ref, d_ref, half in sources:
        for j in range(chips):
            columns = span((half * chips + j) * own, own)
            x = x_ref[j].astype(F32)
            g = d_ref[j].astype(F32) * gain_ref[:, columns].astype(F32)
            dx = inv * g - x * weight
            dx_ref[:, columns] = (dx + valid * head_ref[:, columns].astype(F32)).astype(BF16)
    score = valid * (score_a_ref[...] + score_b_ref[...] + score_c_ref[...])
    member = request == lax.broadcasted_iota(jnp.int32, (total, requests), 1)
    value = jnp.sum(jnp.where(member, score, 0.0), axis=0, keepdims=True)
    parts = []
    for _ in range(3):
        piece = value.astype(BF16).astype(F32)
        parts.append(piece)
        value = value - piece
    for i, piece in enumerate(parts):
        start = voc + i * requests
        spread = jnp.broadcast_to(piece, (total, requests)).astype(BF16)
        out_ref[:, start : start + requests] = spread
    contract = (((1,), (1,)), ((), ()))

    def product(weights):
        return lax.dot_general(
            dx_ref[...], weights, contract, preferred_element_type=F32
        ).astype(BF16)

    out_ref[:, :ready] = product(ready_ref[...])

    def step(j, _):
        for piece in step_pieces(j):
            piece.wait()

        rows = pl.ds(pl.multiple_of(j * tile, tile), tile)
        out_ref[:, pl.ds(pl.multiple_of(ready + j * tile, tile), tile)] = product(table[rows, :])
        return 0

    lax.fori_loop(0, steps, step, 0)
    if last < voc:
        for piece in pieces(last, voc):
            piece.wait()
        out_ref[:, last:voc] = product(table[last - ready :, :])


def swap_sum(send, keep, devices):
    return (keep.astype(F32) + swap_cores(send, devices).astype(F32)).astype(BF16)


def chip_sum(half, devices):
    return jnp.sum(exchange_chips(half, devices).astype(F32), axis=0).astype(BF16)


def chip_gather(total, devices):
    return exchange_chips(jnp.broadcast_to(total[None], (devices // 2,) + total.shape), devices)


def pick(blocks, index):
    return lax.dynamic_index_in_dim(blocks, index, 0, keepdims=False)


def split_halves(part, devices):
    total, width = part.shape
    core = lax.axis_index("dp") % 2
    blocks = part.reshape(total, 2, devices // 2, width // devices).transpose(1, 2, 0, 3)
    return pick(blocks, 1 - core).astype(BF16), pick(blocks, core)


def join_halves(mine, got):
    core = lax.axis_index("dp") % 2
    blocks = jnp.where(core == 1, jnp.stack([got, mine]), jnp.stack([mine, got]))
    _, chips, total, own = blocks.shape
    return blocks.transpose(2, 0, 1, 3).reshape(total, 2 * chips * own).astype(F32)


def norm_scale(x0):
    return lax.rsqrt(jnp.mean(x0 * x0, axis=-1, keepdims=True) + 1e-05)


def plain_half(slices, embed, head_row, devices):
    part = jnp.dot(slices, embed, preferred_element_type=F32)
    score = jnp.sum(part * head_row.astype(F32), axis=-1, keepdims=True)
    return *split_halves(part, devices), score


def plain_hidden(mine, got, gain_row, w_gate, w_up, down, valid, devices):
    x0 = join_halves(mine, got)
    normed = (x0 * norm_scale(x0) * gain_row.astype(F32)).astype(BF16)
    a = jnp.dot(normed, w_gate, preferred_element_type=F32)
    b = jnp.dot(normed, w_up, preferred_element_type=F32)
    sigma = jax.nn.sigmoid(a)
    active = a * sigma
    hidden = (active * b).astype(BF16).astype(F32)
    d_hidden = valid * down
    d_gate = (d_hidden * b * sigma * (1.0 + a * (1.0 - sigma))).astype(BF16)
    d_up = (d_hidden * active).astype(BF16)
    part = jnp.einsum("tf,df->td", d_gate, w_gate, preferred_element_type=F32)
    part = part + jnp.einsum("tf,df->td", d_up, w_up, preferred_element_type=F32)
    return *split_halves(part, devices), jnp.sum(hidden * down, axis=-1, keepdims=True)


def plain_input(mine, got, d_mine, d_got, gain_row, head_row, valid, embed):
    x0 = join_halves(mine, got)
    inv = norm_scale(x0)
    scaled = join_halves(d_mine, d_got) * gain_row.astype(F32)
    dx = inv * scaled - x0 * inv * inv * inv * jnp.mean(scaled * x0, axis=-1, keepdims=True)
    dx = (dx + valid * head_row.astype(F32)).astype(BF16)
    return jnp.einsum("td,vd->tv", dx, embed, preferred_element_type=F32).astype(BF16)


def body(logits, embed, norm_gain, w_gate, w_up, w_down, head, counts):
    devices = lax.axis_size("dp")
    rows, voc = logits.shape
    part = voc // devices
    width = embed.shape[1]
    hidden = w_gate.shape[1]
    own, chips = width // devices, devices // 2
    requests = counts.shape[0]
    total = rows * devices
    request_len = total // requests
    tiled = own % 128 == 0 and hidden % 128 == 0 and total % 16 == 0 and part % 16 == 0 and part > 512
    tiled = tiled and lax.axis_size("groups") == 2
    head_row, gain_row = head.reshape(1, width), norm_gain.reshape(1, width)
    if tiled:
        blocked, probs = call(
            softmax_kernel,
            [struct((devices, rows, part), BF16), pltpu.VMEM((rows, voc), F32)], logits,
        )
    else:
        probs32 = jax.nn.softmax(logits.astype(F32), axis=-1)
        blocked = probs32.astype(BF16).reshape(rows, devices, part).transpose(1, 0, 2)
    slices = exchange(blocked).reshape(total, part)
    column = struct((total, 1), F32)
    half = (chips, total, own)
    flops = total * part * width
    if tiled:
        ready = 256
        steps = -(-hidden // 256)
        down_a, head32 = call(
            early_kernel, [struct((1, steps * 128), F32), struct((1, width), F32)],
            head, w_down, blocked,
            streamed=(0, 1), flops=2 * hidden * width, room=2 * hidden * width,
            scratch=(
                pltpu.VMEM((steps * 128, width), BF16), pltpu.VMEM((width,), BF16),
                pltpu.SemaphoreType.DMA((steps,)), pltpu.SemaphoreType.DMA,
            ),
        )
        down_b = lax.ppermute(down_a, "groups", [(0, 1), (1, 0)])
        ready = 256
        args = dict(streamed=(1,), flops=flops, room=part * width)
        acc = pltpu.VMEM((total, width // 2), F32)
        sems = pltpu.SemaphoreType.DMA((-(-part // 128),))
        send, score_a, first = call(
            functools.partial(half_kernel, True),
            [struct(half, BF16), column, pltpu.VMEM((ready, width // 2), BF16)],
            slices, embed, head32,
            scratch=(
                pltpu.VMEM((part, width // 2), BF16), acc, sems,
                pltpu.SemaphoreType.DMA((ready // 128,)),
            ),
            **args,
        )
        keep, score_b = call(
            functools.partial(half_kernel, False), [struct(half, F32), column],
            slices, embed, head32, first, kept=(3,),
            scratch=(pltpu.VMEM((part - ready, width // 2), BF16), acc, sems), **args,
        )
    else:
        send, keep, score_a = plain_half(slices, embed, head_row, devices)
    summed = swap_sum(send, keep, devices)
    x_mine = chip_gather(chip_sum(summed, devices), devices)
    x_got = swap_cores(x_mine, devices)
    if tiled:
        sems, ahead_sems = pltpu.SemaphoreType.DMA((2, chips)), pltpu.SemaphoreType.DMA((2, 2))
        args = dict(streamed=(2, 3), flops=2 * total * hidden * width, room=2 * width * hidden)
        products, squares, valid, counts_row, both, ahead = call(
            first_kernel,
            [
                struct((total, 2 * hidden), F32), column, column, struct((1, requests), F32),
                pltpu.VMEM((width // 2, 2 * hidden), BF16), pltpu.VMEM((2 * own, 2 * hidden), BF16),
            ],
            x_mine, gain_row, w_gate, w_up, counts.reshape(1, requests),
            scratch=(sems, ahead_sems), **args,
        )
        send, score_c, inv, d_both = call(
            second_kernel,
            [struct(half, BF16), column, column, struct((total, 2 * hidden), BF16)],
            x_got, gain_row, w_gate, w_up, ahead, products, squares, down_a, down_b, valid,
            scratch=(pltpu.VMEM((width // 2 - 2 * own, 2 * hidden), BF16), sems), kept=(4,), **args,
        )
        (keep,) = call(
            third_kernel, [struct(half, F32)], d_both, both,
            kept=(1,), flops=2 * total * hidden * width,
        )
    else:
        down_row = jnp.sum(w_down.astype(F32) * head.astype(F32)[None, :], axis=-1)[None]
        position = jnp.arange(total, dtype=jnp.int32)[:, None]
        member = position // request_len == jnp.arange(requests, dtype=jnp.int32)[None, :]
        limit = jnp.sum(jnp.where(member, counts[None, :], 0), axis=-1, keepdims=True)
        valid = (position % request_len < limit).astype(F32)
        send, keep, score_c = plain_hidden(
            x_mine, x_got, gain_row, w_gate, w_up, down_row, valid, devices
        )
    total_d = chip_sum(swap_sum(send, keep, devices), devices)
    d_mine = chip_gather(total_d, devices)
    d_got = swap_cores(d_mine, devices)
    padded = part + 3 * requests
    if tiled:
        first = first_rows(256, embed, total_d, False)
        (d_slices,) = call(
            input_kernel, [struct((total, padded), BF16)],
            x_mine, x_got, d_mine, d_got, gain_row, head32, inv,
            score_a, score_b, score_c, valid, counts_row, first, embed,
            kept=(12,), streamed=(13,), flops=2 * flops, room=2 * part * width,
            scratch=(
                pltpu.VMEM((total, width), BF16), pltpu.VMEM((part - 256, width), BF16),
                pltpu.SemaphoreType.DMA((-(-part // 64),)),
            ),
        )
    else:
        d_slices = plain_input(x_mine, x_got, d_mine, d_got, gain_row, head_row, valid, embed)
        score = jnp.where(member, valid * (score_a + score_c), 0.0)
        extra = split3(jnp.sum(score, axis=0)).reshape(1, requests * 3)
        extra = jnp.broadcast_to(extra, (total, requests * 3))
        d_slices = jnp.concatenate([d_slices, extra], axis=-1)
    back = exchange(d_slices.reshape(devices, rows, padded))
    if tiled:
        guidance, rewards = call(
            final_kernel, [struct((rows, voc), BF16), struct((1, requests), F32)],
            probs, back, counts_row, kept=(0,),
            scratch=(pltpu.VMEM((rows, voc), F32),),
        )
        return (guidance, rewards.reshape(requests))
    sums = jnp.sum(back[:, 0, part:].astype(F32).reshape(devices, requests, 3), axis=(0, 2))
    rewards = sums / counts.astype(F32)
    d_probs = back[:, :, :part].transpose(1, 0, 2).reshape(rows, voc).astype(F32)
    d_logits = probs32 * (d_probs - jnp.sum(probs32 * d_probs, axis=-1, keepdims=True))
    guidance = (math.sqrt(VOC) * d_logits).astype(BF16)
    return (guidance, rewards)


def solution(mesh):
    placed = (
        P(("groups", "dp"), None),
        P("dp", None),
        P(),
        P(None, "dp"),
        P(None, "dp"),
        P("dp", None),
        P(),
        P("groups"),
    )
    return jax.shard_map(
        body,
        mesh=mesh,
        in_specs=placed,
        out_specs=(P(("groups", "dp"), None), P("groups")),
        check_vma=False,
    )
```

```python
import functools
import math

import jax
import jax.numpy as jnp
from jax import lax
from jax.experimental import pallas as pl
from jax.experimental.pallas import tpu as pltpu
from jax.sharding import PartitionSpec as P

VOC = 32000
F32, BF16 = jnp.float32, jnp.bfloat16
VMEM_BYTES = 12 * 1024 * 1024


def swap_cores(value, devices):
    return lax.ppermute(value, "dp", [(i, i ^ 1) for i in range(devices)])


def exchange(blocks):
    return lax.all_to_all(blocks, "dp", split_axis=0, concat_axis=0, tiled=True)


def exchange_chips(blocks, devices):
    groups = [list(range(core, devices, 2)) for core in range(2)]
    return lax.all_to_all(
        blocks, "dp", split_axis=0, concat_axis=0, axis_index_groups=groups, tiled=True
    )


def split3(value):
    hi = lax.reduce_precision(value, 8, 7)
    rest = value - hi
    mid = lax.reduce_precision(rest, 8, 7)
    low = rest - mid
    return jnp.stack([hi, mid, low], axis=-1).astype(BF16)


HBM_SPEC = pl.BlockSpec(memory_space=pltpu.HBM)
VMEM_SPEC = pl.BlockSpec(memory_space=pltpu.VMEM)
SMEM_SPEC = pl.BlockSpec(memory_space=pltpu.SMEM)


WINDOW = 128


def call(kernel, outs, *args, streamed=(), kept=(), scalars=(), flops=0, scratch=(), room=0):
    size = sum(math.prod(a.shape) * a.dtype.itemsize for a in args)
    places = {i: pltpu.HBM for i in streamed} | {i: pltpu.VMEM for i in kept}
    specs = [
        HBM_SPEC if i in streamed else SMEM_SPEC if i in scalars else VMEM_SPEC
        for i in range(len(args))
    ]
    return pl.pallas_call(
        kernel,
        out_shape=outs,
        in_specs=specs,
        out_specs=[VMEM_SPEC] * len(outs),
        scratch_shapes=list(scratch),
        compiler_params=pltpu.CompilerParams(vmem_limit_bytes=VMEM_BYTES + room),
        cost_estimate=pl.CostEstimate(flops=flops, bytes_accessed=size, transcendentals=0),
    )(*[
        pltpu.with_memory_space_constraint(a, places[i]) if i in places else a
        for i, a in enumerate(args)
    ])


class Stream:
    def __init__(self, copies):
        self.copies = copies
        self.done = 0
        for copy in copies[:WINDOW]:
            copy.start()

    def wait(self, count):
        while self.done < count:
            self.copies[self.done].wait()
            self.done += 1
            if self.done + WINDOW <= len(self.copies):
                self.copies[self.done + WINDOW - 1].start()


def struct(shape, dtype):
    return jax.ShapeDtypeStruct(shape, dtype)


def this_core():
    return lax.axis_index("dp") % 2


def span(start, size):
    return pl.ds(pl.multiple_of(start, size), size)


def softmax_kernel(logits_ref, out_ref, probs_ref):
    devices, _, part = out_ref.shape
    x = logits_ref[...].astype(F32)
    e = jnp.exp(x - jnp.max(x, axis=-1, keepdims=True))
    probs = e * (1.0 / jnp.sum(e, axis=-1, keepdims=True))
    probs_ref[...] = probs
    for d in range(devices):
        out_ref[d] = probs[:, d * part : (d + 1) * part].astype(BF16)


def final_kernel(probs_ref, back_ref, counts_ref, out_ref, rewards_ref, d_ref):
    devices, _, padded = back_ref.shape
    part = out_ref.shape[1] // devices
    requests = counts_ref.shape[1]
    sums = jnp.zeros((1, requests), F32)
    for d in range(devices):
        block = back_ref[d].astype(F32)
        d_ref[:, d * part : (d + 1) * part] = block[:, :part]
        for i in range(3):
            start = part + i * requests
            sums += block[:1, start : start + requests]
    rewards_ref[...] = sums / counts_ref[...]
    probs, d_probs = probs_ref[...], d_ref[...]
    mean = jnp.sum(probs * d_probs, axis=-1, keepdims=True)
    out_ref[...] = (math.sqrt(VOC) * (probs * (d_probs - mean))).astype(BF16)


def valid_column(counts, total):
    requests = counts.shape[1]
    length = total // requests
    position = lax.broadcasted_iota(jnp.int32, (total, requests), 0)
    start = length * lax.broadcasted_iota(jnp.int32, (total, requests), 1)
    inside = (position >= start) & (position < start + counts)
    return jnp.sum(jnp.where(inside, 1.0, 0.0), axis=-1, keepdims=True)


def bring(source_ref, out_ref, sems, columns):
    fine = 128
    return [
        pltpu.make_async_copy(
            source_ref.at[pl.ds(i, fine), columns], out_ref.at[pl.ds(i, fine)], sems.at[i // fine]
        )
        for i in range(0, out_ref.shape[0], fine)
    ]


def ready_kernel(split, source_ref, after_ref, out_ref, sems):
    del after_ref
    width = out_ref.shape[1]
    columns = span((1 - this_core()) * width, width) if split else pl.ds(0, width)
    copies = bring(source_ref, out_ref, sems, columns)
    for copy in copies:
        copy.start()
    for copy in copies:
        copy.wait()


def first_rows(rows, source, after, split):
    width = source.shape[1] // 2 if split else source.shape[1]
    return call(
        functools.partial(ready_kernel, split), [pltpu.VMEM((rows, width), source.dtype)],
        source, after, streamed=(0,), scratch=(pltpu.SemaphoreType.DMA((rows // 128,)),),
    )[0]


def half_kernel(other, slices_ref, embed_ref, head_ref, *rest):
    if other:
        ready_ref, out_ref, score_ref, next_ref, table, acc, sems, next_sems = rest
    else:
        ready_ref, out_ref, score_ref, table, acc, sems = rest
    chips, total, own = out_ref.shape
    part, ready = embed_ref.shape[0], ready_ref.shape[0]
    core = this_core()
    half = (1 - core) if other else core
    columns = span(half * chips * own, chips * own)
    tile, fine = 256, 128
    stream = Stream([
        pltpu.make_async_copy(
            embed_ref.at[pl.ds(i, min(fine, part - i)), columns],
            table.at[pl.ds(i - ready, min(fine, part - i))],
            sems.at[i // fine],
        )
        for i in range(ready, part, fine)
    ])
    following = []
    if other:
        following = bring(embed_ref, next_ref, next_sems, span(core * chips * own, chips * own))
        for copy in following:
            copy.start()
    acc[...] = jnp.dot(slices_ref[:, :ready], ready_ref[...], preferred_element_type=F32)
    for start in range(ready, part, tile):
        end = min(start + tile, part)
        stream.wait(-(-(end - ready) // fine))
        acc[...] += jnp.dot(
            slices_ref[:, start:end], table[start - ready : end - ready],
            preferred_element_type=F32,
        )
    score_ref[...] = jnp.sum(
        acc[...] * head_ref[:, columns].astype(F32), axis=-1, keepdims=True
    )
    for j in range(chips):
        out_ref[j] = acc[:, j * own : (j + 1) * own].astype(out_ref.dtype)
    for copy in following:
        copy.wait()


def early_kernel(
    head_ref, down_ref, embed_ref, after_ref,
    out_ref, head_row, first, table, head_copy, sems, head_sem, first_sems,
):
    del after_ref
    width, lanes = down_ref.shape[1], 128
    steps = sems.shape[0]
    skip = lax.axis_index("groups") * (down_ref.shape[0] // lanes - steps)

    def copy(j):
        source = down_ref.at[span((skip + j) * lanes, lanes)]
        return pltpu.make_async_copy(source, table.at[span(j * lanes, lanes)], sems.at[j])

    bring_head = pltpu.make_async_copy(head_ref, head_copy, head_sem)
    bring_head.start()
    for j in range(steps):
        copy(j).start()
    half = first.shape[1]
    others = bring(embed_ref, first, first_sems, span((1 - this_core()) * half, half))
    for other in others:
        other.start()
    bring_head.wait()
    head = head_copy[...].astype(F32).reshape(1, width)
    head_row[...] = head

    def step(j, _):
        copy(j).wait()
        rows = span(j * lanes, lanes)
        total = jnp.zeros((lanes, lanes), F32)
        for k in range(0, width, lanes):
            total += table[rows, k : k + lanes].astype(F32) * head[:, k : k + lanes]
        out_ref[:, rows] = jnp.sum(total.T, axis=0, keepdims=True)
        return 0

    lax.fori_loop(0, steps, step, 0)
    for other in others:
        other.wait()


def bring_blocks(gate_ref, up_ref, both, half, blocks, own, chips, sems):
    hidden = gate_ref.shape[1]
    return [
        pltpu.make_async_copy(
            source.at[span((half * chips + j) * own, own)],
            both.at[pl.ds((j - blocks[0]) * own, own), pl.ds(k * hidden, hidden)],
            sems.at[k, j - blocks[0]],
        )
        for j in blocks
        for k, source in enumerate((gate_ref, up_ref))
    ]


def weight_rows(ready, both, own):
    skip = ready.shape[0] // own if ready is not None else 0

    def weights(j):
        if j < skip:
            return ready[j * own : (j + 1) * own]
        return both[(j - skip) * own : (j - skip + 1) * own]

    return skip, weights


def forward_half(x_ref, gain_ref, half, sums, weights, wait):
    chips, _, own = x_ref.shape
    products, squares = sums
    scaled = []
    wide = jnp.zeros(x_ref.shape[1:], F32)
    for j in range(chips):
        x = x_ref[j].astype(F32)
        wide = wide + x * x
        gain = gain_ref[:, span((half * chips + j) * own, own)].astype(F32)
        scaled.append((x * gain).astype(BF16))
    squares = squares + jnp.sum(wide, axis=-1, keepdims=True)
    for j in range(chips):
        wait(j)
        products = products + jnp.dot(scaled[j], weights(j), preferred_element_type=F32)
    return products, squares


def backward_half(d_both, weights, out_ref):
    contract = (((1,), (1,)), ((), ()))
    for j in range(out_ref.shape[0]):
        part = lax.dot_general(d_both, weights(j), contract, preferred_element_type=F32)
        out_ref[j] = part.astype(out_ref.dtype)


def first_kernel(
    x_ref, gain_ref, gate_ref, up_ref, counts_ref,
    products_ref, squares_ref, valid_ref, counts_row, both, ahead, sems, ahead_sems,
):
    chips, _, own = x_ref.shape
    core = this_core()
    skip, weights = weight_rows(None, both, own)
    blocks = range(skip, chips)
    stream = Stream(bring_blocks(gate_ref, up_ref, both, core, blocks, own, chips, sems))
    blocks = range(ahead.shape[0] // own)
    following = bring_blocks(gate_ref, up_ref, ahead, 1 - core, blocks, own, chips, ahead_sems)
    for copy in following:
        copy.start()
    counts = counts_ref[...]
    valid_ref[...] = valid_column(counts, valid_ref.shape[0])
    counts_row[...] = counts.astype(F32)
    sums = (jnp.zeros(products_ref.shape, F32), jnp.zeros(squares_ref.shape, F32))
    products_ref[...], squares_ref[...] = forward_half(
        x_ref, gain_ref, core, sums, weights, lambda j: stream.wait(2 * (j - skip + 1))
    )
    for copy in following:
        copy.wait()


def second_kernel(
    x_ref, gain_ref, gate_ref, up_ref, ready_ref, products_ref, squares_ref, down_a, down_b, valid_ref,
    send_ref, score_ref, inv_ref, d_both_ref, both, sems,
):
    chips, total, own = x_ref.shape
    width, hidden = gate_ref.shape
    half = 1 - this_core()
    skip, weights = weight_rows(ready_ref, both, own)
    blocks = range(skip, chips)
    stream = Stream(bring_blocks(gate_ref, up_ref, both, half, blocks, own, chips, sems))
    sums = (products_ref[...], squares_ref[...])
    products, squares = forward_half(
        x_ref, gain_ref, half, sums, weights, lambda j: stream.wait(2 * (j - skip + 1))
    )
    inv = lax.rsqrt(squares / width + 1e-05)
    inv_ref[...] = inv
    a, b = products[:, :hidden] * inv, products[:, hidden:] * inv
    sigma = jax.nn.sigmoid(a)
    active = a * sigma
    first_group = lax.axis_index("groups") == 0
    down = jnp.where(first_group, down_a[...], down_b[...])
    rest = jnp.where(first_group, down_b[...], down_a[...])
    down = jnp.concatenate([down, rest[:, 2 * rest.shape[1] - hidden :]], axis=-1)
    rounded = (active * b).astype(BF16).astype(F32)
    score_ref[...] = jnp.sum(rounded * down, axis=-1, keepdims=True)
    d_hidden = valid_ref[...] * down
    d_both_ref[:, :hidden] = (d_hidden * b * sigma * (1.0 + a * (1.0 - sigma))).astype(BF16)
    d_both_ref[:, hidden:] = (d_hidden * active).astype(BF16)
    backward_half(d_both_ref[...], weights, send_ref)


def third_kernel(d_both_ref, both_ref, keep_ref):
    _, weights = weight_rows(None, both_ref, keep_ref.shape[2])
    backward_half(d_both_ref[...], weights, keep_ref)


def input_kernel(
    mine_ref, got_ref, d_mine_ref, d_got_ref, gain_ref, head_ref, inv_ref,
    score_a_ref, score_b_ref, score_c_ref, valid_ref, counts_ref, ready_ref, embed_ref,
    out_ref, dx_ref, table, sems,
):
    chips, total, own = mine_ref.shape
    voc = embed_ref.shape[0]
    requests = counts_ref.shape[1]
    width = 2 * chips * own
    core = this_core()
    ready = ready_ref.shape[0]
    tile, fine = 256, 64
    steps = (voc - ready) // tile
    last = ready + steps * tile

    def copy(start, size):
        return pltpu.make_async_copy(
            embed_ref.at[pl.ds(start, size)],
            table.at[pl.ds(start - ready, size)],
            sems.at[start // fine],
        )

    def pieces(start, end):
        return [copy(start + i, min(fine, end - start - i)) for i in range(0, end - start, fine)]

    def step_pieces(j):
        start = pl.multiple_of(ready + j * tile, fine)
        return [copy(pl.multiple_of(start + i, fine), fine) for i in range(0, tile, fine)]

    for piece in pieces(ready, voc):
        piece.start()
    sources = ((mine_ref, d_mine_ref, core), (got_ref, d_got_ref, 1 - core))
    wide = jnp.zeros((total, own), F32)
    for x_ref, d_ref, half in sources:
        for j in range(chips):
            gain = gain_ref[:, span((half * chips + j) * own, own)].astype(F32)
            wide += d_ref[j].astype(F32) * gain * x_ref[j].astype(F32)
    inv = inv_ref[...]
    weight = inv * inv * inv * (jnp.sum(wide, axis=-1, keepdims=True) / width)
    valid = valid_ref[...]
    request = lax.broadcasted_iota(jnp.int32, (total, requests), 0) // (total // requests)
    for x_ref, d_ref, half in sources:
        for j in range(chips):
            columns = span((half * chips + j) * own, own)
            x = x_ref[j].astype(F32)
            g = d_ref[j].astype(F32) * gain_ref[:, columns].astype(F32)
            dx = inv * g - x * weight
            dx_ref[:, columns] = (dx + valid * head_ref[:, columns].astype(F32)).astype(BF16)
    score = valid * (score_a_ref[...] + score_b_ref[...] + score_c_ref[...])
    member = request == lax.broadcasted_iota(jnp.int32, (total, requests), 1)
    value = jnp.sum(jnp.where(member, score, 0.0), axis=0, keepdims=True)
    parts = []
    for _ in range(3):
        piece = value.astype(BF16).astype(F32)
        parts.append(piece)
        value = value - piece
    for i, piece in enumerate(parts):
        start = voc + i * requests
        spread = jnp.broadcast_to(piece, (total, requests)).astype(BF16)
        out_ref[:, start : start + requests] = spread
    contract = (((1,), (1,)), ((), ()))

    def product(weights):
        return lax.dot_general(
            dx_ref[...], weights, contract, preferred_element_type=F32
        ).astype(BF16)

    out_ref[:, :ready] = product(ready_ref[...])

    def step(j, _):
        for piece in step_pieces(j):
            piece.wait()

        rows = pl.ds(pl.multiple_of(j * tile, tile), tile)
        out_ref[:, pl.ds(pl.multiple_of(ready + j * tile, tile), tile)] = product(table[rows, :])
        return 0

    lax.fori_loop(0, steps, step, 0)
    if last < voc:
        for piece in pieces(last, voc):
            piece.wait()
        out_ref[:, last:voc] = product(table[last - ready :, :])


def swap_sum(send, keep, devices):
    return (keep.astype(F32) + swap_cores(send, devices).astype(F32)).astype(BF16)


def chip_sum(half, devices):
    return jnp.sum(exchange_chips(half, devices).astype(F32), axis=0).astype(BF16)


def chip_gather(total, devices):
    return exchange_chips(jnp.broadcast_to(total[None], (devices // 2,) + total.shape), devices)


def pick(blocks, index):
    return lax.dynamic_index_in_dim(blocks, index, 0, keepdims=False)


def split_halves(part, devices):
    total, width = part.shape
    core = lax.axis_index("dp") % 2
    blocks = part.reshape(total, 2, devices // 2, width // devices).transpose(1, 2, 0, 3)
    return pick(blocks, 1 - core).astype(BF16), pick(blocks, core)


def join_halves(mine, got):
    core = lax.axis_index("dp") % 2
    blocks = jnp.where(core == 1, jnp.stack([got, mine]), jnp.stack([mine, got]))
    _, chips, total, own = blocks.shape
    return blocks.transpose(2, 0, 1, 3).reshape(total, 2 * chips * own).astype(F32)


def norm_scale(x0):
    return lax.rsqrt(jnp.mean(x0 * x0, axis=-1, keepdims=True) + 1e-05)


def plain_half(slices, embed, head_row, devices):
    part = jnp.dot(slices, embed, preferred_element_type=F32)
    score = jnp.sum(part * head_row.astype(F32), axis=-1, keepdims=True)
    return *split_halves(part, devices), score


def plain_hidden(mine, got, gain_row, w_gate, w_up, down, valid, devices):
    x0 = join_halves(mine, got)
    normed = (x0 * norm_scale(x0) * gain_row.astype(F32)).astype(BF16)
    a = jnp.dot(normed, w_gate, preferred_element_type=F32)
    b = jnp.dot(normed, w_up, preferred_element_type=F32)
    sigma = jax.nn.sigmoid(a)
    active = a * sigma
    hidden = (active * b).astype(BF16).astype(F32)
    d_hidden = valid * down
    d_gate = (d_hidden * b * sigma * (1.0 + a * (1.0 - sigma))).astype(BF16)
    d_up = (d_hidden * active).astype(BF16)
    part = jnp.einsum("tf,df->td", d_gate, w_gate, preferred_element_type=F32)
    part = part + jnp.einsum("tf,df->td", d_up, w_up, preferred_element_type=F32)
    return *split_halves(part, devices), jnp.sum(hidden * down, axis=-1, keepdims=True)


def plain_input(mine, got, d_mine, d_got, gain_row, head_row, valid, embed):
    x0 = join_halves(mine, got)
    inv = norm_scale(x0)
    scaled = join_halves(d_mine, d_got) * gain_row.astype(F32)
    dx = inv * scaled - x0 * inv * inv * inv * jnp.mean(scaled * x0, axis=-1, keepdims=True)
    dx = (dx + valid * head_row.astype(F32)).astype(BF16)
    return jnp.einsum("td,vd->tv", dx, embed, preferred_element_type=F32).astype(BF16)


def body(logits, embed, norm_gain, w_gate, w_up, w_down, head, counts):
    devices = lax.axis_size("dp")
    rows, voc = logits.shape
    part = voc // devices
    width = embed.shape[1]
    hidden = w_gate.shape[1]
    own, chips = width // devices, devices // 2
    requests = counts.shape[0]
    total = rows * devices
    request_len = total // requests
    tiled = own % 128 == 0 and hidden % 128 == 0 and total % 16 == 0 and part % 16 == 0 and part > 512
    tiled = tiled and lax.axis_size("groups") == 2
    head_row, gain_row = head.reshape(1, width), norm_gain.reshape(1, width)
    if tiled:
        blocked, probs = call(
            softmax_kernel,
            [struct((devices, rows, part), BF16), pltpu.VMEM((rows, voc), F32)], logits,
        )
    else:
        probs32 = jax.nn.softmax(logits.astype(F32), axis=-1)
        blocked = probs32.astype(BF16).reshape(rows, devices, part).transpose(1, 0, 2)
    slices = exchange(blocked).reshape(total, part)
    column = struct((total, 1), F32)
    half = (chips, total, own)
    flops = total * part * width
    if tiled:
        ready = 256
        steps, ready = -(-hidden // 256), 256
        ahead = pltpu.VMEM((ready, width // 2), BF16)
        ahead_sems = pltpu.SemaphoreType.DMA((ready // 128,))
        down_a, head32, first = call(
            early_kernel, [struct((1, steps * 128), F32), struct((1, width), F32), ahead],
            head, w_down, embed, blocked,
            streamed=(0, 1, 2), flops=2 * hidden * width, room=2 * hidden * width,
            scratch=(
                pltpu.VMEM((steps * 128, width), BF16), pltpu.VMEM((width,), BF16),
                pltpu.SemaphoreType.DMA((steps,)), pltpu.SemaphoreType.DMA, ahead_sems,
            ),
        )
        down_b = lax.ppermute(down_a, "groups", [(0, 1), (1, 0)])
        args = dict(streamed=(1,), kept=(3,), flops=flops, room=part * width)
        scratch = (
            pltpu.VMEM((part - ready, width // 2), BF16), pltpu.VMEM((total, width // 2), F32),
            pltpu.SemaphoreType.DMA((-(-part // 128),)),
        )
        send, score_a, first = call(
            functools.partial(half_kernel, True), [struct(half, BF16), column, ahead],
            slices, embed, head32, first, scratch=(*scratch, ahead_sems), **args,
        )
        send, down_b = lax.optimization_barrier((send, down_b))
        keep, score_b = call(
            functools.partial(half_kernel, False), [struct(half, F32), column],
            slices, embed, head32, first, scratch=scratch, **args,
        )
    else:
        send, keep, score_a = plain_half(slices, embed, head_row, devices)
    summed = swap_sum(send, keep, devices)
    x_mine = chip_gather(chip_sum(summed, devices), devices)
    x_got = swap_cores(x_mine, devices)
    if tiled:
        sems, ahead_sems = pltpu.SemaphoreType.DMA((2, chips)), pltpu.SemaphoreType.DMA((2, 2))
        args = dict(streamed=(2, 3), flops=2 * total * hidden * width, room=2 * width * hidden)
        products, squares, valid, counts_row, both, ahead = call(
            first_kernel,
            [
                struct((total, 2 * hidden), F32), column, column, struct((1, requests), F32),
                pltpu.VMEM((width // 2, 2 * hidden), BF16), pltpu.VMEM((2 * own, 2 * hidden), BF16),
            ],
            x_mine, gain_row, w_gate, w_up, counts.reshape(1, requests),
            scratch=(sems, ahead_sems), **args,
        )
        send, score_c, inv, d_both = call(
            second_kernel,
            [struct(half, BF16), column, column, struct((total, 2 * hidden), BF16)],
            x_got, gain_row, w_gate, w_up, ahead, products, squares, down_a, down_b, valid,
            scratch=(pltpu.VMEM((width // 2 - 2 * own, 2 * hidden), BF16), sems), kept=(4,), **args,
        )
        (keep,) = call(
            third_kernel, [struct(half, F32)], d_both, both,
            kept=(1,), flops=2 * total * hidden * width,
        )
    else:
        down_row = jnp.sum(w_down.astype(F32) * head.astype(F32)[None, :], axis=-1)[None]
        position = jnp.arange(total, dtype=jnp.int32)[:, None]
        member = position // request_len == jnp.arange(requests, dtype=jnp.int32)[None, :]
        limit = jnp.sum(jnp.where(member, counts[None, :], 0), axis=-1, keepdims=True)
        valid = (position % request_len < limit).astype(F32)
        send, keep, score_c = plain_hidden(
            x_mine, x_got, gain_row, w_gate, w_up, down_row, valid, devices
        )
    total_d = chip_sum(swap_sum(send, keep, devices), devices)
    d_mine = chip_gather(total_d, devices)
    d_got = swap_cores(d_mine, devices)
    padded = part + 3 * requests
    if tiled:
        first = first_rows(256, embed, total_d, False)
        (d_slices,) = call(
            input_kernel, [struct((total, padded), BF16)],
            x_mine, x_got, d_mine, d_got, gain_row, head32, inv,
            score_a, score_b, score_c, valid, counts_row, first, embed,
            kept=(12,), streamed=(13,), flops=2 * flops, room=2 * part * width,
            scratch=(
                pltpu.VMEM((total, width), BF16), pltpu.VMEM((part - 256, width), BF16),
                pltpu.SemaphoreType.DMA((-(-part // 64),)),
            ),
        )
    else:
        d_slices = plain_input(x_mine, x_got, d_mine, d_got, gain_row, head_row, valid, embed)
        score = jnp.where(member, valid * (score_a + score_c), 0.0)
        extra = split3(jnp.sum(score, axis=0)).reshape(1, requests * 3)
        extra = jnp.broadcast_to(extra, (total, requests * 3))
        d_slices = jnp.concatenate([d_slices, extra], axis=-1)
    back = exchange(d_slices.reshape(devices, rows, padded))
    if tiled:
        guidance, rewards = call(
            final_kernel, [struct((rows, voc), BF16), struct((1, requests), F32)],
            probs, back, counts_row, kept=(0,),
            scratch=(pltpu.VMEM((rows, voc), F32),),
        )
        return (guidance, rewards.reshape(requests))
    sums = jnp.sum(back[:, 0, part:].astype(F32).reshape(devices, requests, 3), axis=(0, 2))
    rewards = sums / counts.astype(F32)
    d_probs = back[:, :, :part].transpose(1, 0, 2).reshape(rows, voc).astype(F32)
    d_logits = probs32 * (d_probs - jnp.sum(probs32 * d_probs, axis=-1, keepdims=True))
    guidance = (math.sqrt(VOC) * d_logits).astype(BF16)
    return (guidance, rewards)


def solution(mesh):
    placed = (
        P(("groups", "dp"), None),
        P("dp", None),
        P(),
        P(None, "dp"),
        P(None, "dp"),
        P("dp", None),
        P(),
        P("groups"),
    )
    return jax.shard_map(
        body,
        mesh=mesh,
        in_specs=placed,
        out_specs=(P(("groups", "dp"), None), P("groups")),
        check_vma=False,
    )
```

```python
import functools
import math

import jax
import jax.numpy as jnp
from jax import lax
from jax.experimental import pallas as pl
from jax.experimental.pallas import tpu as pltpu
from jax.sharding import PartitionSpec as P

VOC = 32000
F32, BF16 = jnp.float32, jnp.bfloat16
VMEM_BYTES = 12 * 1024 * 1024


def swap_cores(value, devices):
    return lax.ppermute(value, "dp", [(i, i ^ 1) for i in range(devices)])


def exchange(blocks):
    return lax.all_to_all(blocks, "dp", split_axis=0, concat_axis=0, tiled=True)


def exchange_chips(blocks, devices):
    groups = [list(range(core, devices, 2)) for core in range(2)]
    return lax.all_to_all(
        blocks, "dp", split_axis=0, concat_axis=0, axis_index_groups=groups, tiled=True
    )


def split3(value):
    hi = lax.reduce_precision(value, 8, 7)
    rest = value - hi
    mid = lax.reduce_precision(rest, 8, 7)
    low = rest - mid
    return jnp.stack([hi, mid, low], axis=-1).astype(BF16)


HBM_SPEC = pl.BlockSpec(memory_space=pltpu.HBM)
VMEM_SPEC = pl.BlockSpec(memory_space=pltpu.VMEM)
SMEM_SPEC = pl.BlockSpec(memory_space=pltpu.SMEM)


WINDOW = 128


def call(kernel, outs, *args, streamed=(), kept=(), scalars=(), flops=0, scratch=(), room=0):
    size = sum(math.prod(a.shape) * a.dtype.itemsize for a in args)
    places = {i: pltpu.HBM for i in streamed} | {i: pltpu.VMEM for i in kept}
    specs = [
        HBM_SPEC if i in streamed else SMEM_SPEC if i in scalars else VMEM_SPEC
        for i in range(len(args))
    ]
    return pl.pallas_call(
        kernel,
        out_shape=outs,
        in_specs=specs,
        out_specs=[VMEM_SPEC] * len(outs),
        scratch_shapes=list(scratch),
        compiler_params=pltpu.CompilerParams(vmem_limit_bytes=VMEM_BYTES + room),
        cost_estimate=pl.CostEstimate(flops=flops, bytes_accessed=size, transcendentals=0),
    )(*[
        pltpu.with_memory_space_constraint(a, places[i]) if i in places else a
        for i, a in enumerate(args)
    ])


class Stream:
    def __init__(self, copies):
        self.copies = copies
        self.done = 0
        for copy in copies[:WINDOW]:
            copy.start()

    def wait(self, count):
        while self.done < count:
            self.copies[self.done].wait()
            self.done += 1
            if self.done + WINDOW <= len(self.copies):
                self.copies[self.done + WINDOW - 1].start()


def struct(shape, dtype):
    return jax.ShapeDtypeStruct(shape, dtype)


def this_core():
    return lax.axis_index("dp") % 2


def span(start, size):
    return pl.ds(pl.multiple_of(start, size), size)


def softmax_kernel(logits_ref, out_ref, probs_ref):
    devices, _, part = out_ref.shape
    x = logits_ref[...].astype(F32)
    e = jnp.exp(x - jnp.max(x, axis=-1, keepdims=True))
    probs = e * (1.0 / jnp.sum(e, axis=-1, keepdims=True))
    probs_ref[...] = probs
    for d in range(devices):
        out_ref[d] = probs[:, d * part : (d + 1) * part].astype(BF16)


def final_kernel(probs_ref, back_ref, counts_ref, out_ref, rewards_ref, d_ref):
    devices, _, padded = back_ref.shape
    part = out_ref.shape[1] // devices
    requests = counts_ref.shape[1]
    sums = jnp.zeros((1, requests), F32)
    for d in range(devices):
        block = back_ref[d].astype(F32)
        d_ref[:, d * part : (d + 1) * part] = block[:, :part]
        for i in range(3):
            start = part + i * requests
            sums += block[:1, start : start + requests]
    rewards_ref[...] = sums / counts_ref[...]
    probs, d_probs = probs_ref[...], d_ref[...]
    mean = jnp.sum(probs * d_probs, axis=-1, keepdims=True)
    out_ref[...] = (math.sqrt(VOC) * (probs * (d_probs - mean))).astype(BF16)


def valid_column(counts, total):
    requests = counts.shape[1]
    length = total // requests
    position = lax.broadcasted_iota(jnp.int32, (total, requests), 0)
    start = length * lax.broadcasted_iota(jnp.int32, (total, requests), 1)
    inside = (position >= start) & (position < start + counts)
    return jnp.sum(jnp.where(inside, 1.0, 0.0), axis=-1, keepdims=True)


def bring(source_ref, out_ref, sems, columns):
    fine = 128
    return [
        pltpu.make_async_copy(
            source_ref.at[pl.ds(i, fine), columns], out_ref.at[pl.ds(i, fine)], sems.at[i // fine]
        )
        for i in range(0, out_ref.shape[0], fine)
    ]


def ready_kernel(split, source_ref, after_ref, out_ref, sems):
    del after_ref
    width = out_ref.shape[1]
    columns = span((1 - this_core()) * width, width) if split else pl.ds(0, width)
    copies = bring(source_ref, out_ref, sems, columns)
    for copy in copies:
        copy.start()
    for copy in copies:
        copy.wait()


def first_rows(rows, source, after, split):
    width = source.shape[1] // 2 if split else source.shape[1]
    return call(
        functools.partial(ready_kernel, split), [pltpu.VMEM((rows, width), source.dtype)],
        source, after, streamed=(0,), scratch=(pltpu.SemaphoreType.DMA((rows // 128,)),),
    )[0]


def half_kernel(other, slices_ref, ready_ref, embed_ref, head_ref, out_ref, score_ref, *rest):
    next_ref, table, acc, sems, next_sems = rest if other else (None, *rest, None)
    chips, total, own = out_ref.shape
    part, ready = embed_ref.shape[0], ready_ref.shape[0]
    core = this_core()
    half = (1 - core) if other else core
    columns = span(half * chips * own, chips * own)
    tile, fine = 512, 128
    stream = Stream([
        pltpu.make_async_copy(
            embed_ref.at[pl.ds(i, min(fine, part - i)), columns],
            table.at[pl.ds(i - ready, min(fine, part - i))],
            sems.at[i // fine],
        )
        for i in range(ready, part, fine)
    ])
    following = []
    if other:
        following = bring(embed_ref, next_ref, next_sems, span(core * chips * own, chips * own))
        for copy in following:
            copy.start()
    acc[...] = jnp.dot(slices_ref[:, :ready], ready_ref[...], preferred_element_type=F32)
    for start in range(ready, part, tile):
        end = min(start + tile, part)
        stream.wait(-(-(end - ready) // fine))
        acc[...] += jnp.dot(
            slices_ref[:, start:end], table[start - ready : end - ready],
            preferred_element_type=F32,
        )
    score_ref[...] = jnp.sum(
        acc[...] * head_ref[:, columns].astype(F32), axis=-1, keepdims=True
    )
    for j in range(chips):
        out_ref[j] = acc[:, j * own : (j + 1) * own].astype(out_ref.dtype)
    for copy in following:
        copy.wait()


def early_kernel(
    head_ref, down_ref, embed_ref, gate_ref, up_ref, after_ref,
    out_ref, head_row, first, both, table, head_copy, sems, first_sems, both_sems, head_sem,
):
    del after_ref
    width, lanes = down_ref.shape[1], 128
    core = this_core()

    def copy(j):
        rows = span(j * lanes, lanes)
        return pltpu.make_async_copy(down_ref.at[rows], table.at[rows], sems.at[j])

    steps = sems.shape[0]
    bring_head = pltpu.make_async_copy(head_ref, head_copy, head_sem)
    bring_head.start()
    for j in range(steps):
        copy(j).start()
    half = width // 2
    own = both.shape[0] // 2
    chips = half // own
    others = bring(embed_ref, first, first_sems, span((1 - core) * half, half))
    others += bring_blocks(gate_ref, up_ref, both, core, range(2), own, chips, both_sems)
    for other in others:
        other.start()
    bring_head.wait()
    head = head_copy[...].astype(F32).reshape(1, width)
    head_row[...] = head

    def step(j, _):
        copy(j).wait()
        rows = span(j * lanes, lanes)
        total = jnp.zeros((lanes, lanes), F32)
        for k in range(0, width, lanes):
            total += table[rows, k : k + lanes].astype(F32) * head[:, k : k + lanes]
        out_ref[:, rows] = jnp.sum(total.T, axis=0, keepdims=True)
        return 0

    lax.fori_loop(0, steps, step, 0)
    for other in others:
        other.wait()


def bring_blocks(gate_ref, up_ref, both, half, blocks, own, chips, sems):
    hidden = gate_ref.shape[1]
    return [
        pltpu.make_async_copy(
            source.at[span((half * chips + j) * own, own)],
            both.at[pl.ds((j - blocks[0]) * own, own), pl.ds(k * hidden, hidden)],
            sems.at[k, j - blocks[0]],
        )
        for j in blocks
        for k, source in enumerate((gate_ref, up_ref))
    ]


def weight_rows(ready, both, own):
    skip = ready.shape[0] // own

    def weights(j, count=1):
        if j < skip:
            return ready[j * own : (j + count) * own]
        return both[(j - skip) * own : (j - skip + count) * own]

    return skip, weights


def forward_half(x_ref, gain_ref, half, sums, weights, wait):
    chips, _, own = x_ref.shape
    products, squares = sums
    scaled = []
    wide = jnp.zeros(x_ref.shape[1:], F32)
    for j in range(chips):
        x = x_ref[j].astype(F32)
        wide = wide + x * x
        gain = gain_ref[:, span((half * chips + j) * own, own)].astype(F32)
        scaled.append((x * gain).astype(BF16))
    squares = squares + jnp.sum(wide, axis=-1, keepdims=True)
    for j in range(0, chips, 2):
        wait(j + 1)
        pair = jnp.concatenate(scaled[j : j + 2], axis=-1)
        products = products + jnp.dot(pair, weights(j, 2), preferred_element_type=F32)
    return products, squares


def backward_half(d_both, weights, out_ref):
    contract = (((1,), (1,)), ((), ()))
    for j in range(out_ref.shape[0]):
        part = lax.dot_general(d_both, weights(j), contract, preferred_element_type=F32)
        out_ref[j] = part.astype(out_ref.dtype)


def first_kernel(
    x_ref, gain_ref, gate_ref, up_ref, ready_ref, counts_ref,
    products_ref, squares_ref, valid_ref, counts_row, both, ahead, sems, ahead_sems,
):
    chips, _, own = x_ref.shape
    core = this_core()
    skip, weights = weight_rows(ready_ref, both, own)
    blocks = range(skip, chips)
    stream = Stream(bring_blocks(gate_ref, up_ref, both, core, blocks, own, chips, sems))
    blocks = range(ahead.shape[0] // own)
    following = bring_blocks(gate_ref, up_ref, ahead, 1 - core, blocks, own, chips, ahead_sems)
    for copy in following:
        copy.start()
    counts = counts_ref[...]
    valid_ref[...] = valid_column(counts, valid_ref.shape[0])
    counts_row[...] = counts.astype(F32)
    sums = (jnp.zeros(products_ref.shape, F32), jnp.zeros(squares_ref.shape, F32))
    products_ref[...], squares_ref[...] = forward_half(
        x_ref, gain_ref, core, sums, weights, lambda j: stream.wait(2 * (j - skip + 1))
    )
    for copy in following:
        copy.wait()


def second_kernel(
    x_ref, gain_ref, gate_ref, up_ref, ready_ref, products_ref, squares_ref, down_ref, valid_ref,
    send_ref, score_ref, inv_ref, d_both_ref, both, sems,
):
    chips, total, own = x_ref.shape
    width, hidden = gate_ref.shape
    half = 1 - this_core()
    skip, weights = weight_rows(ready_ref, both, own)
    blocks = range(skip, chips)
    stream = Stream(bring_blocks(gate_ref, up_ref, both, half, blocks, own, chips, sems))
    sums = (products_ref[...], squares_ref[...])
    products, squares = forward_half(
        x_ref, gain_ref, half, sums, weights, lambda j: stream.wait(2 * (j - skip + 1))
    )
    inv = lax.rsqrt(squares / width + 1e-05)
    inv_ref[...] = inv
    a, b = products[:, :hidden] * inv, products[:, hidden:] * inv
    sigma = jax.nn.sigmoid(a)
    active = a * sigma
    down = down_ref[...]
    rounded = (active * b).astype(BF16).astype(F32)
    score_ref[...] = jnp.sum(rounded * down, axis=-1, keepdims=True)
    d_hidden = valid_ref[...] * down
    d_both_ref[:, :hidden] = (d_hidden * b * sigma * (1.0 + a * (1.0 - sigma))).astype(BF16)
    d_both_ref[:, hidden:] = (d_hidden * active).astype(BF16)
    backward_half(d_both_ref[...], weights, send_ref)


def third_kernel(d_both_ref, ready_ref, both_ref, keep_ref):
    _, weights = weight_rows(ready_ref, both_ref, keep_ref.shape[2])
    backward_half(d_both_ref[...], weights, keep_ref)


def input_kernel(
    mine_ref, got_ref, d_mine_ref, d_got_ref, gain_ref, head_ref, inv_ref,
    score_a_ref, score_b_ref, score_c_ref, valid_ref, counts_ref, ready_ref, embed_ref,
    out_ref, dx_ref, table, sems,
):
    chips, total, own = mine_ref.shape
    voc = embed_ref.shape[0]
    requests = counts_ref.shape[1]
    width = 2 * chips * own
    core = this_core()
    ready = ready_ref.shape[0]
    tile, fine = 256, 64
    steps = (voc - ready) // tile
    last = ready + steps * tile

    def copy(start, size):
        return pltpu.make_async_copy(
            embed_ref.at[pl.ds(start, size)],
            table.at[pl.ds(start - ready, size)],
            sems.at[start // fine],
        )

    def pieces(start, end):
        return [copy(start + i, min(fine, end - start - i)) for i in range(0, end - start, fine)]

    def step_pieces(j):
        start = pl.multiple_of(ready + j * tile, fine)
        return [copy(pl.multiple_of(start + i, fine), fine) for i in range(0, tile, fine)]

    for piece in pieces(ready, voc):
        piece.start()
    sources = ((mine_ref, d_mine_ref, core), (got_ref, d_got_ref, 1 - core))
    wide = jnp.zeros((total, own), F32)
    for x_ref, d_ref, half in sources:
        for j in range(chips):
            gain = gain_ref[:, span((half * chips + j) * own, own)].astype(F32)
            wide += d_ref[j].astype(F32) * gain * x_ref[j].astype(F32)
    inv = inv_ref[...]
    weight = inv * inv * inv * (jnp.sum(wide, axis=-1, keepdims=True) / width)
    valid = valid_ref[...]
    request = lax.broadcasted_iota(jnp.int32, (total, requests), 0) // (total // requests)
    for x_ref, d_ref, half in sources:
        for j in range(chips):
            columns = span((half * chips + j) * own, own)
            x = x_ref[j].astype(F32)
            g = d_ref[j].astype(F32) * gain_ref[:, columns].astype(F32)
            dx = inv * g - x * weight
            dx_ref[:, columns] = (dx + valid * head_ref[:, columns].astype(F32)).astype(BF16)
    score = valid * (score_a_ref[...] + score_b_ref[...] + score_c_ref[...])
    member = request == lax.broadcasted_iota(jnp.int32, (total, requests), 1)
    value = jnp.sum(jnp.where(member, score, 0.0), axis=0, keepdims=True)
    parts = []
    for _ in range(3):
        piece = value.astype(BF16).astype(F32)
        parts.append(piece)
        value = value - piece
    for i, piece in enumerate(parts):
        start = voc + i * requests
        spread = jnp.broadcast_to(piece, (total, requests)).astype(BF16)
        out_ref[:, start : start + requests] = spread
    contract = (((1,), (1,)), ((), ()))

    def product(weights):
        return lax.dot_general(
            dx_ref[...], weights, contract, preferred_element_type=F32
        ).astype(BF16)

    out_ref[:, :ready] = product(ready_ref[...])

    def step(j, _):
        for piece in step_pieces(j):
            piece.wait()

        rows = pl.ds(pl.multiple_of(j * tile, tile), tile)
        out_ref[:, pl.ds(pl.multiple_of(ready + j * tile, tile), tile)] = product(table[rows, :])
        return 0

    lax.fori_loop(0, steps, step, 0)
    if last < voc:
        for piece in pieces(last, voc):
            piece.wait()
        out_ref[:, last:voc] = product(table[last - ready :, :])


def swap_sum(send, keep, devices):
    return (keep.astype(F32) + swap_cores(send, devices).astype(F32)).astype(BF16)


def chip_sum(half, devices):
    return jnp.sum(exchange_chips(half, devices).astype(F32), axis=0).astype(BF16)


def chip_gather(total, devices):
    return exchange_chips(jnp.broadcast_to(total[None], (devices // 2,) + total.shape), devices)


def pick(blocks, index):
    return lax.dynamic_index_in_dim(blocks, index, 0, keepdims=False)


def split_halves(part, devices):
    total, width = part.shape
    core = lax.axis_index("dp") % 2
    blocks = part.reshape(total, 2, devices // 2, width // devices).transpose(1, 2, 0, 3)
    return pick(blocks, 1 - core).astype(BF16), pick(blocks, core)


def join_halves(mine, got):
    core = lax.axis_index("dp") % 2
    blocks = jnp.where(core == 1, jnp.stack([got, mine]), jnp.stack([mine, got]))
    _, chips, total, own = blocks.shape
    return blocks.transpose(2, 0, 1, 3).reshape(total, 2 * chips * own).astype(F32)


def norm_scale(x0):
    return lax.rsqrt(jnp.mean(x0 * x0, axis=-1, keepdims=True) + 1e-05)


def plain_half(slices, embed, head_row, devices):
    part = jnp.dot(slices, embed, preferred_element_type=F32)
    score = jnp.sum(part * head_row.astype(F32), axis=-1, keepdims=True)
    return *split_halves(part, devices), score


def plain_hidden(mine, got, gain_row, w_gate, w_up, down, valid, devices):
    x0 = join_halves(mine, got)
    normed = (x0 * norm_scale(x0) * gain_row.astype(F32)).astype(BF16)
    a = jnp.dot(normed, w_gate, preferred_element_type=F32)
    b = jnp.dot(normed, w_up, preferred_element_type=F32)
    sigma = jax.nn.sigmoid(a)
    active = a * sigma
    hidden = (active * b).astype(BF16).astype(F32)
    d_hidden = valid * down
    d_gate = (d_hidden * b * sigma * (1.0 + a * (1.0 - sigma))).astype(BF16)
    d_up = (d_hidden * active).astype(BF16)
    part = jnp.einsum("tf,df->td", d_gate, w_gate, preferred_element_type=F32)
    part = part + jnp.einsum("tf,df->td", d_up, w_up, preferred_element_type=F32)
    return *split_halves(part, devices), jnp.sum(hidden * down, axis=-1, keepdims=True)


def plain_input(mine, got, d_mine, d_got, gain_row, head_row, valid, embed):
    x0 = join_halves(mine, got)
    inv = norm_scale(x0)
    scaled = join_halves(d_mine, d_got) * gain_row.astype(F32)
    dx = inv * scaled - x0 * inv * inv * inv * jnp.mean(scaled * x0, axis=-1, keepdims=True)
    dx = (dx + valid * head_row.astype(F32)).astype(BF16)
    return jnp.einsum("td,vd->tv", dx, embed, preferred_element_type=F32).astype(BF16)


def body(logits, embed, norm_gain, w_gate, w_up, w_down, head, counts):
    devices = lax.axis_size("dp")
    rows, voc = logits.shape
    part = voc // devices
    width = embed.shape[1]
    hidden = w_gate.shape[1]
    own, chips = width // devices, devices // 2
    requests = counts.shape[0]
    total = rows * devices
    request_len = total // requests
    tiled = chips % 2 == 0 and own % 128 == 0 and hidden % 128 == 0 and total % 16 == 0 and part % 16 == 0 and part > 512
    head_row, gain_row = head.reshape(1, width), norm_gain.reshape(1, width)
    if tiled:
        blocked, probs = call(
            softmax_kernel,
            [struct((devices, rows, part), BF16), pltpu.VMEM((rows, voc), F32)], logits,
        )
    else:
        probs32 = jax.nn.softmax(logits.astype(F32), axis=-1)
        blocked = probs32.astype(BF16).reshape(rows, devices, part).transpose(1, 0, 2)
    slices = exchange(blocked).reshape(total, part)
    column = struct((total, 1), F32)
    half = (chips, total, own)
    flops = total * part * width
    if tiled:
        ready = 256
        down_row, head32, first, both_first = call(
            early_kernel,
            [
                struct((1, hidden), F32), struct((1, width), F32),
                pltpu.VMEM((ready, width // 2), BF16),
                pltpu.VMEM((2 * own, 2 * hidden), BF16),
            ],
            head, w_down, embed, w_gate, w_up, blocked,
            streamed=(0, 1, 2, 3, 4), flops=2 * hidden * width, room=2 * hidden * width,
            scratch=(
                pltpu.VMEM((hidden, width), BF16), pltpu.VMEM((width,), BF16),
                pltpu.SemaphoreType.DMA((hidden // 128,)),
                pltpu.SemaphoreType.DMA((ready // 128,)), pltpu.SemaphoreType.DMA((2, 2)),
                pltpu.SemaphoreType.DMA,
            ),
        )
        table = (
            pltpu.VMEM((part - ready, width // 2), BF16), pltpu.VMEM((total, width // 2), F32),
            pltpu.SemaphoreType.DMA((-(-part // 128),)),
        )
        args = dict(streamed=(2,), kept=(1,), flops=flops, room=part * width)
        send, score_a, first = call(
            functools.partial(half_kernel, True),
            [struct(half, BF16), column, pltpu.VMEM((ready, width // 2), BF16)],
            slices, first, embed, head32,
            scratch=(*table, pltpu.SemaphoreType.DMA((ready // 128,))), **args,
        )
        keep, score_b = call(
            functools.partial(half_kernel, False), [struct(half, F32), column],
            slices, first, embed, head32, scratch=table, **args,
        )
    else:
        send, keep, score_a = plain_half(slices, embed, head_row, devices)
    summed = swap_sum(send, keep, devices)
    x_mine = chip_gather(chip_sum(summed, devices), devices)
    x_got = swap_cores(x_mine, devices)
    if tiled:
        weight = (width // 2 - 2 * own, 2 * hidden)
        sems, ahead_sems = pltpu.SemaphoreType.DMA((2, chips)), pltpu.SemaphoreType.DMA((2, 2))
        args = dict(
            streamed=(2, 3), kept=(4,), flops=2 * total * hidden * width, room=2 * width * hidden
        )
        products, squares, valid, counts_row, both, ahead = call(
            first_kernel,
            [
                struct((total, 2 * hidden), F32), column, column, struct((1, requests), F32),
                pltpu.VMEM(weight, BF16), pltpu.VMEM(both_first.shape, BF16),
            ],
            x_mine, gain_row, w_gate, w_up, both_first, counts.reshape(1, requests),
            scratch=(sems, ahead_sems), **args,
        )
        send, score_c, inv, d_both = call(
            second_kernel,
            [struct(half, BF16), column, column, struct((total, 2 * hidden), BF16)],
            x_got, gain_row, w_gate, w_up, ahead, products, squares, down_row, valid,
            scratch=(pltpu.VMEM(weight, BF16), sems), **args,
        )
        (keep,) = call(
            third_kernel, [struct(half, F32)], d_both, both_first, both,
            kept=(1, 2), flops=2 * total * hidden * width,
        )
    else:
        down_row = jnp.sum(w_down.astype(F32) * head.astype(F32)[None, :], axis=-1)[None]
        position = jnp.arange(total, dtype=jnp.int32)[:, None]
        member = position // request_len == jnp.arange(requests, dtype=jnp.int32)[None, :]
        limit = jnp.sum(jnp.where(member, counts[None, :], 0), axis=-1, keepdims=True)
        valid = (position % request_len < limit).astype(F32)
        send, keep, score_c = plain_hidden(
            x_mine, x_got, gain_row, w_gate, w_up, down_row, valid, devices
        )
    total_d = chip_sum(swap_sum(send, keep, devices), devices)
    d_mine = chip_gather(total_d, devices)
    d_got = swap_cores(d_mine, devices)
    padded = part + 3 * requests
    if tiled:
        first = first_rows(256, embed, total_d, False)
        (d_slices,) = call(
            input_kernel, [struct((total, padded), BF16)],
            x_mine, x_got, d_mine, d_got, gain_row, head32, inv,
            score_a, score_b, score_c, valid, counts_row, first, embed,
            kept=(12,), streamed=(13,), flops=2 * flops, room=2 * part * width,
            scratch=(
                pltpu.VMEM((total, width), BF16), pltpu.VMEM((part - 256, width), BF16),
                pltpu.SemaphoreType.DMA((-(-part // 64),)),
            ),
        )
    else:
        d_slices = plain_input(x_mine, x_got, d_mine, d_got, gain_row, head_row, valid, embed)
        score = jnp.where(member, valid * (score_a + score_c), 0.0)
        extra = split3(jnp.sum(score, axis=0)).reshape(1, requests * 3)
        extra = jnp.broadcast_to(extra, (total, requests * 3))
        d_slices = jnp.concatenate([d_slices, extra], axis=-1)
    back = exchange(d_slices.reshape(devices, rows, padded))
    if tiled:
        guidance, rewards = call(
            final_kernel, [struct((rows, voc), BF16), struct((1, requests), F32)],
            probs, back, counts_row, kept=(0,),
            scratch=(pltpu.VMEM((rows, voc), F32),),
        )
        return (guidance, rewards.reshape(requests))
    sums = jnp.sum(back[:, 0, part:].astype(F32).reshape(devices, requests, 3), axis=(0, 2))
    rewards = sums / counts.astype(F32)
    d_probs = back[:, :, :part].transpose(1, 0, 2).reshape(rows, voc).astype(F32)
    d_logits = probs32 * (d_probs - jnp.sum(probs32 * d_probs, axis=-1, keepdims=True))
    guidance = (math.sqrt(VOC) * d_logits).astype(BF16)
    return (guidance, rewards)


def solution(mesh):
    placed = (
        P(("groups", "dp"), None),
        P("dp", None),
        P(),
        P(None, "dp"),
        P(None, "dp"),
        P("dp", None),
        P(),
        P("groups"),
    )
    return jax.shard_map(
        body,
        mesh=mesh,
        in_specs=placed,
        out_specs=(P(("groups", "dp"), None), P("groups")),
        check_vma=False,
    )
```

```python
import functools
import math

import jax
import jax.numpy as jnp
from jax import lax
from jax.experimental import pallas as pl
from jax.experimental.pallas import tpu as pltpu
from jax.sharding import PartitionSpec as P

VOC = 32000
F32, BF16 = jnp.float32, jnp.bfloat16
VMEM_BYTES = 12 * 1024 * 1024


def swap_cores(value, devices):
    return lax.ppermute(value, "dp", [(i, i ^ 1) for i in range(devices)])


def exchange(blocks):
    return lax.all_to_all(blocks, "dp", split_axis=0, concat_axis=0, tiled=True)


def exchange_chips(blocks, devices):
    groups = [list(range(core, devices, 2)) for core in range(2)]
    return lax.all_to_all(
        blocks, "dp", split_axis=0, concat_axis=0, axis_index_groups=groups, tiled=True
    )


def split3(value):
    hi = lax.reduce_precision(value, 8, 7)
    rest = value - hi
    mid = lax.reduce_precision(rest, 8, 7)
    low = rest - mid
    return jnp.stack([hi, mid, low], axis=-1).astype(BF16)


HBM_SPEC = pl.BlockSpec(memory_space=pltpu.HBM)
VMEM_SPEC = pl.BlockSpec(memory_space=pltpu.VMEM)
SMEM_SPEC = pl.BlockSpec(memory_space=pltpu.SMEM)


WINDOW = 128


def call(kernel, outs, *args, streamed=(), kept=(), scalars=(), flops=0, scratch=(), room=0):
    size = sum(math.prod(a.shape) * a.dtype.itemsize for a in args)
    places = {i: pltpu.HBM for i in streamed} | {i: pltpu.VMEM for i in kept}
    specs = [
        HBM_SPEC if i in streamed else SMEM_SPEC if i in scalars else VMEM_SPEC
        for i in range(len(args))
    ]
    return pl.pallas_call(
        kernel,
        out_shape=outs,
        in_specs=specs,
        out_specs=[VMEM_SPEC] * len(outs),
        scratch_shapes=list(scratch),
        compiler_params=pltpu.CompilerParams(vmem_limit_bytes=VMEM_BYTES + room),
        cost_estimate=pl.CostEstimate(flops=flops, bytes_accessed=size, transcendentals=0),
    )(*[
        pltpu.with_memory_space_constraint(a, places[i]) if i in places else a
        for i, a in enumerate(args)
    ])


class Stream:
    def __init__(self, copies):
        self.copies = copies
        self.done = 0
        for copy in copies[:WINDOW]:
            copy.start()

    def wait(self, count):
        while self.done < count:
            self.copies[self.done].wait()
            self.done += 1
            if self.done + WINDOW <= len(self.copies):
                self.copies[self.done + WINDOW - 1].start()


def struct(shape, dtype):
    return jax.ShapeDtypeStruct(shape, dtype)


def this_core():
    return lax.axis_index("dp") % 2


def span(start, size):
    return pl.ds(pl.multiple_of(start, size), size)


def softmax_kernel(logits_ref, out_ref, probs_ref):
    devices, _, part = out_ref.shape
    x = logits_ref[...].astype(F32)
    e = jnp.exp(x - jnp.max(x, axis=-1, keepdims=True))
    probs = e * (1.0 / jnp.sum(e, axis=-1, keepdims=True))
    probs_ref[...] = probs
    for d in range(devices):
        out_ref[d] = probs[:, d * part : (d + 1) * part].astype(BF16)


def final_kernel(probs_ref, back_ref, counts_ref, out_ref, rewards_ref, d_ref):
    devices, _, padded = back_ref.shape
    part = out_ref.shape[1] // devices
    requests = counts_ref.shape[1]
    sums = jnp.zeros((1, requests), F32)
    for d in range(devices):
        block = back_ref[d].astype(F32)
        d_ref[:, d * part : (d + 1) * part] = block[:, :part]
        for i in range(3):
            start = part + i * requests
            sums += block[:1, start : start + requests]
    rewards_ref[...] = sums / counts_ref[...]
    probs, d_probs = probs_ref[...], d_ref[...]
    mean = jnp.sum(probs * d_probs, axis=-1, keepdims=True)
    out_ref[...] = (math.sqrt(VOC) * (probs * (d_probs - mean))).astype(BF16)


def valid_column(counts, total):
    requests = counts.shape[1]
    length = total // requests
    position = lax.broadcasted_iota(jnp.int32, (total, requests), 0)
    start = length * lax.broadcasted_iota(jnp.int32, (total, requests), 1)
    inside = (position >= start) & (position < start + counts)
    return jnp.sum(jnp.where(inside, 1.0, 0.0), axis=-1, keepdims=True)


def bring(source_ref, out_ref, sems, columns):
    fine = 128
    return [
        pltpu.make_async_copy(
            source_ref.at[pl.ds(i, fine), columns], out_ref.at[pl.ds(i, fine)], sems.at[i // fine]
        )
        for i in range(0, out_ref.shape[0], fine)
    ]


def ready_kernel(split, source_ref, after_ref, out_ref, sems):
    del after_ref
    width = out_ref.shape[1]
    columns = span((1 - this_core()) * width, width) if split else pl.ds(0, width)
    copies = bring(source_ref, out_ref, sems, columns)
    for copy in copies:
        copy.start()
    for copy in copies:
        copy.wait()


def first_rows(rows, source, after, split):
    width = source.shape[1] // 2 if split else source.shape[1]
    return call(
        functools.partial(ready_kernel, split), [pltpu.VMEM((rows, width), source.dtype)],
        source, after, streamed=(0,), scratch=(pltpu.SemaphoreType.DMA((rows // 128,)),),
    )[0]


def half_kernel(other, slices_ref, ready_ref, embed_ref, head_ref, out_ref, score_ref, *rest):
    next_ref, table, acc, sems, next_sems = rest if other else (None, *rest, None)
    chips, total, own = out_ref.shape
    part, ready = embed_ref.shape[0], ready_ref.shape[0]
    core = this_core()
    half = (1 - core) if other else core
    columns = span(half * chips * own, chips * own)
    tile, fine = 256, 128
    stream = Stream([
        pltpu.make_async_copy(
            embed_ref.at[pl.ds(i, min(fine, part - i)), columns],
            table.at[pl.ds(i - ready, min(fine, part - i))],
            sems.at[i // fine],
        )
        for i in range(ready, part, fine)
    ])
    following = []
    if other:
        following = bring(embed_ref, next_ref, next_sems, span(core * chips * own, chips * own))
        for copy in following:
            copy.start()
    acc[...] = jnp.dot(slices_ref[:, :ready], ready_ref[...], preferred_element_type=F32)
    for start in range(ready, part, tile):
        end = min(start + tile, part)
        stream.wait(-(-(end - ready) // fine))
        acc[...] += jnp.dot(
            slices_ref[:, start:end], table[start - ready : end - ready],
            preferred_element_type=F32,
        )
    score_ref[...] = jnp.sum(
        acc[...] * head_ref[:, columns].astype(F32), axis=-1, keepdims=True
    )
    for j in range(chips):
        out_ref[j] = acc[:, j * own : (j + 1) * own].astype(out_ref.dtype)
    for copy in following:
        copy.wait()


def early_kernel(
    head_ref, down_ref, embed_ref, gate_ref, up_ref, after_ref,
    out_ref, head_row, first, both, table, head_copy, sems, first_sems, both_sems, head_sem,
):
    del after_ref
    width, lanes = down_ref.shape[1], 128
    core = this_core()

    def copy(j):
        rows = span(j * lanes, lanes)
        return pltpu.make_async_copy(down_ref.at[rows], table.at[rows], sems.at[j])

    steps = sems.shape[0]
    bring_head = pltpu.make_async_copy(head_ref, head_copy, head_sem)
    bring_head.start()
    for j in range(steps):
        copy(j).start()
    half = width // 2
    own = both.shape[0] // 2
    chips = half // own
    others = bring(embed_ref, first, first_sems, span((1 - core) * half, half))
    others += bring_blocks(gate_ref, up_ref, both, core, range(2), own, chips, both_sems)
    for other in others:
        other.start()
    bring_head.wait()
    head = head_copy[...].astype(F32).reshape(1, width)
    head_row[...] = head

    def step(j, _):
        copy(j).wait()
        rows = span(j * lanes, lanes)
        total = jnp.zeros((lanes, lanes), F32)
        for k in range(0, width, lanes):
            total += table[rows, k : k + lanes].astype(F32) * head[:, k : k + lanes]
        out_ref[:, rows] = jnp.sum(total.T, axis=0, keepdims=True)
        return 0

    lax.fori_loop(0, steps, step, 0)
    for other in others:
        other.wait()


def bring_blocks(gate_ref, up_ref, both, half, blocks, own, chips, sems):
    hidden = gate_ref.shape[1]
    return [
        pltpu.make_async_copy(
            source.at[span((half * chips + j) * own, own)],
            both.at[pl.ds((j - blocks[0]) * own, own), pl.ds(k * hidden, hidden)],
            sems.at[k, j - blocks[0]],
        )
        for j in blocks
        for k, source in enumerate((gate_ref, up_ref))
    ]


def weight_rows(ready, both, own):
    skip = ready.shape[0] // own

    def weights(j):
        if j < skip:
            return ready[j * own : (j + 1) * own]
        return both[(j - skip) * own : (j - skip + 1) * own]

    return skip, weights


def forward_half(x_ref, gain_ref, half, sums, weights, wait):
    chips, _, own = x_ref.shape
    products, squares = sums
    scaled = []
    wide = jnp.zeros(x_ref.shape[1:], F32)
    for j in range(chips):
        x = x_ref[j].astype(F32)
        wide = wide + x * x
        gain = gain_ref[:, span((half * chips + j) * own, own)].astype(F32)
        scaled.append((x * gain).astype(BF16))
    squares = squares + jnp.sum(wide, axis=-1, keepdims=True)
    for j in range(chips):
        wait(j)
        products = products + jnp.dot(scaled[j], weights(j), preferred_element_type=F32)
    return products, squares


def backward_half(d_both, weights, out_ref):
    contract = (((1,), (1,)), ((), ()))
    for j in range(out_ref.shape[0]):
        part = lax.dot_general(d_both, weights(j), contract, preferred_element_type=F32)
        out_ref[j] = part.astype(out_ref.dtype)


def first_kernel(
    x_ref, gain_ref, gate_ref, up_ref, ready_ref, counts_ref,
    products_ref, squares_ref, valid_ref, counts_row, both, ahead, sems, ahead_sems,
):
    chips, _, own = x_ref.shape
    core = this_core()
    skip, weights = weight_rows(ready_ref, both, own)
    blocks = range(skip, chips)
    stream = Stream(bring_blocks(gate_ref, up_ref, both, core, blocks, own, chips, sems))
    blocks = range(ahead.shape[0] // own)
    following = bring_blocks(gate_ref, up_ref, ahead, 1 - core, blocks, own, chips, ahead_sems)
    for copy in following:
        copy.start()
    counts = counts_ref[...]
    valid_ref[...] = valid_column(counts, valid_ref.shape[0])
    counts_row[...] = counts.astype(F32)
    sums = (jnp.zeros(products_ref.shape, F32), jnp.zeros(squares_ref.shape, F32))
    products_ref[...], squares_ref[...] = forward_half(
        x_ref, gain_ref, core, sums, weights, lambda j: stream.wait(2 * (j - skip + 1))
    )
    for copy in following:
        copy.wait()


def second_kernel(
    x_ref, gain_ref, gate_ref, up_ref, ready_ref, products_ref, squares_ref, down_ref, valid_ref,
    send_ref, score_ref, inv_ref, d_both_ref, both, sems,
):
    chips, total, own = x_ref.shape
    width, hidden = gate_ref.shape
    half = 1 - this_core()
    skip, weights = weight_rows(ready_ref, both, own)
    blocks = range(skip, chips)
    stream = Stream(bring_blocks(gate_ref, up_ref, both, half, blocks, own, chips, sems))
    sums = (products_ref[...], squares_ref[...])
    products, squares = forward_half(
        x_ref, gain_ref, half, sums, weights, lambda j: stream.wait(2 * (j - skip + 1))
    )
    inv = lax.rsqrt(squares / width + 1e-05)
    inv_ref[...] = inv
    a, b = products[:, :hidden] * inv, products[:, hidden:] * inv
    sigma = jax.nn.sigmoid(a)
    active = a * sigma
    down = down_ref[...]
    rounded = (active * b).astype(BF16).astype(F32)
    score_ref[...] = jnp.sum(rounded * down, axis=-1, keepdims=True)
    d_hidden = valid_ref[...] * down
    d_both_ref[:, :hidden] = (d_hidden * b * sigma * (1.0 + a * (1.0 - sigma))).astype(BF16)
    d_both_ref[:, hidden:] = (d_hidden * active).astype(BF16)
    backward_half(d_both_ref[...], weights, send_ref)


def third_kernel(d_both_ref, ready_ref, both_ref, keep_ref):
    _, weights = weight_rows(ready_ref, both_ref, keep_ref.shape[2])
    backward_half(d_both_ref[...], weights, keep_ref)


def input_kernel(
    mine_ref, got_ref, d_mine_ref, d_got_ref, gain_ref, head_ref, inv_ref,
    score_a_ref, score_b_ref, score_c_ref, valid_ref, counts_ref, ready_ref, embed_ref,
    out_ref, dx_ref, table, sems,
):
    chips, total, own = mine_ref.shape
    voc = embed_ref.shape[0]
    requests = counts_ref.shape[1]
    width = 2 * chips * own
    core = this_core()
    ready = ready_ref.shape[0]
    tile, fine = 256, 128
    steps = (voc - ready) // tile
    last = ready + steps * tile

    def copy(start, size):
        return pltpu.make_async_copy(
            embed_ref.at[pl.ds(start, size)],
            table.at[pl.ds(start - ready, size)],
            sems.at[start // fine],
        )

    def pieces(start, end):
        return [copy(start + i, min(fine, end - start - i)) for i in range(0, end - start, fine)]

    def step_pieces(j):
        start = pl.multiple_of(ready + j * tile, fine)
        return [copy(pl.multiple_of(start + i, fine), fine) for i in range(0, tile, fine)]

    for piece in pieces(ready, voc):
        piece.start()
    sources = ((mine_ref, d_mine_ref, core), (got_ref, d_got_ref, 1 - core))
    wide = jnp.zeros((total, own), F32)
    for x_ref, d_ref, half in sources:
        for j in range(chips):
            gain = gain_ref[:, span((half * chips + j) * own, own)].astype(F32)
            wide += d_ref[j].astype(F32) * gain * x_ref[j].astype(F32)
    inv = inv_ref[...]
    weight = inv * inv * inv * (jnp.sum(wide, axis=-1, keepdims=True) / width)
    valid = valid_ref[...]
    request = lax.broadcasted_iota(jnp.int32, (total, requests), 0) // (total // requests)
    for x_ref, d_ref, half in sources:
        for j in range(chips):
            columns = span((half * chips + j) * own, own)
            x = x_ref[j].astype(F32)
            g = d_ref[j].astype(F32) * gain_ref[:, columns].astype(F32)
            dx = inv * g - x * weight
            dx_ref[:, columns] = (dx + valid * head_ref[:, columns].astype(F32)).astype(BF16)
    score = valid * (score_a_ref[...] + score_b_ref[...] + score_c_ref[...])
    member = request == lax.broadcasted_iota(jnp.int32, (total, requests), 1)
    value = jnp.sum(jnp.where(member, score, 0.0), axis=0, keepdims=True)
    parts = []
    for _ in range(3):
        piece = value.astype(BF16).astype(F32)
        parts.append(piece)
        value = value - piece
    for i, piece in enumerate(parts):
        start = voc + i * requests
        spread = jnp.broadcast_to(piece, (total, requests)).astype(BF16)
        out_ref[:, start : start + requests] = spread
    contract = (((1,), (1,)), ((), ()))

    def product(weights):
        return lax.dot_general(
            dx_ref[...], weights, contract, preferred_element_type=F32
        ).astype(BF16)

    out_ref[:, :ready] = product(ready_ref[...])

    def step(j, _):
        for piece in step_pieces(j):
            piece.wait()

        rows = pl.ds(pl.multiple_of(j * tile, tile), tile)
        out_ref[:, pl.ds(pl.multiple_of(ready + j * tile, tile), tile)] = product(table[rows, :])
        return 0

    lax.fori_loop(0, steps, step, 0)
    if last < voc:
        for piece in pieces(last, voc):
            piece.wait()
        out_ref[:, last:voc] = product(table[last - ready :, :])


def swap_sum(send, keep, devices):
    return (keep.astype(F32) + swap_cores(send, devices).astype(F32)).astype(BF16)


def chip_sum(half, devices):
    return jnp.sum(exchange_chips(half, devices).astype(F32), axis=0).astype(BF16)


def chip_gather(total, devices):
    return exchange_chips(jnp.broadcast_to(total[None], (devices // 2,) + total.shape), devices)


def pick(blocks, index):
    return lax.dynamic_index_in_dim(blocks, index, 0, keepdims=False)


def split_halves(part, devices):
    total, width = part.shape
    core = lax.axis_index("dp") % 2
    blocks = part.reshape(total, 2, devices // 2, width // devices).transpose(1, 2, 0, 3)
    return pick(blocks, 1 - core).astype(BF16), pick(blocks, core)


def join_halves(mine, got):
    core = lax.axis_index("dp") % 2
    blocks = jnp.where(core == 1, jnp.stack([got, mine]), jnp.stack([mine, got]))
    _, chips, total, own = blocks.shape
    return blocks.transpose(2, 0, 1, 3).reshape(total, 2 * chips * own).astype(F32)


def norm_scale(x0):
    return lax.rsqrt(jnp.mean(x0 * x0, axis=-1, keepdims=True) + 1e-05)


def plain_half(slices, embed, head_row, devices):
    part = jnp.dot(slices, embed, preferred_element_type=F32)
    score = jnp.sum(part * head_row.astype(F32), axis=-1, keepdims=True)
    return *split_halves(part, devices), score


def plain_hidden(mine, got, gain_row, w_gate, w_up, down, valid, devices):
    x0 = join_halves(mine, got)
    normed = (x0 * norm_scale(x0) * gain_row.astype(F32)).astype(BF16)
    a = jnp.dot(normed, w_gate, preferred_element_type=F32)
    b = jnp.dot(normed, w_up, preferred_element_type=F32)
    sigma = jax.nn.sigmoid(a)
    active = a * sigma
    hidden = (active * b).astype(BF16).astype(F32)
    d_hidden = valid * down
    d_gate = (d_hidden * b * sigma * (1.0 + a * (1.0 - sigma))).astype(BF16)
    d_up = (d_hidden * active).astype(BF16)
    part = jnp.einsum("tf,df->td", d_gate, w_gate, preferred_element_type=F32)
    part = part + jnp.einsum("tf,df->td", d_up, w_up, preferred_element_type=F32)
    return *split_halves(part, devices), jnp.sum(hidden * down, axis=-1, keepdims=True)


def plain_input(mine, got, d_mine, d_got, gain_row, head_row, valid, embed):
    x0 = join_halves(mine, got)
    inv = norm_scale(x0)
    scaled = join_halves(d_mine, d_got) * gain_row.astype(F32)
    dx = inv * scaled - x0 * inv * inv * inv * jnp.mean(scaled * x0, axis=-1, keepdims=True)
    dx = (dx + valid * head_row.astype(F32)).astype(BF16)
    return jnp.einsum("td,vd->tv", dx, embed, preferred_element_type=F32).astype(BF16)


def body(logits, embed, norm_gain, w_gate, w_up, w_down, head, counts):
    devices = lax.axis_size("dp")
    rows, voc = logits.shape
    part = voc // devices
    width = embed.shape[1]
    hidden = w_gate.shape[1]
    own, chips = width // devices, devices // 2
    requests = counts.shape[0]
    total = rows * devices
    request_len = total // requests
    tiled = own % 128 == 0 and hidden % 128 == 0 and total % 16 == 0 and part % 16 == 0 and part > 512
    head_row, gain_row = head.reshape(1, width), norm_gain.reshape(1, width)
    if tiled:
        blocked, probs = call(
            softmax_kernel,
            [struct((devices, rows, part), BF16), pltpu.VMEM((rows, voc), F32)], logits,
        )
    else:
        probs32 = jax.nn.softmax(logits.astype(F32), axis=-1)
        blocked = probs32.astype(BF16).reshape(rows, devices, part).transpose(1, 0, 2)
    slices = exchange(blocked).reshape(total, part)
    column = struct((total, 1), F32)
    half = (chips, total, own)
    flops = total * part * width
    if tiled:
        ready = 256
        down_row, head32, first, both_first = call(
            early_kernel,
            [
                struct((1, hidden), F32), struct((1, width), F32),
                pltpu.VMEM((ready, width // 2), BF16),
                pltpu.VMEM((2 * own, 2 * hidden), BF16),
            ],
            head, w_down, embed, w_gate, w_up, blocked,
            streamed=(0, 1, 2, 3, 4), flops=2 * hidden * width, room=2 * hidden * width,
            scratch=(
                pltpu.VMEM((hidden, width), BF16), pltpu.VMEM((width,), BF16),
                pltpu.SemaphoreType.DMA((hidden // 128,)),
                pltpu.SemaphoreType.DMA((ready // 128,)), pltpu.SemaphoreType.DMA((2, 2)),
                pltpu.SemaphoreType.DMA,
            ),
        )
        table = (
            pltpu.VMEM((part - ready, width // 2), BF16), pltpu.VMEM((total, width // 2), F32),
            pltpu.SemaphoreType.DMA((-(-part // 128),)),
        )
        args = dict(streamed=(2,), kept=(1,), flops=flops, room=part * width)
        send, score_a, first = call(
            functools.partial(half_kernel, True),
            [struct(half, BF16), column, pltpu.VMEM((ready, width // 2), BF16)],
            slices, first, embed, head32,
            scratch=(*table, pltpu.SemaphoreType.DMA((ready // 128,))), **args,
        )
        keep, score_b = call(
            functools.partial(half_kernel, False), [struct(half, F32), column],
            slices, first, embed, head32, scratch=table, **args,
        )
    else:
        send, keep, score_a = plain_half(slices, embed, head_row, devices)
    summed = swap_sum(send, keep, devices)
    x_mine = chip_gather(chip_sum(summed, devices), devices)
    x_got = swap_cores(x_mine, devices)
    if tiled:
        weight = (width // 2 - 2 * own, 2 * hidden)
        sems, ahead_sems = pltpu.SemaphoreType.DMA((2, chips)), pltpu.SemaphoreType.DMA((2, 2))
        args = dict(
            streamed=(2, 3), kept=(4,), flops=2 * total * hidden * width, room=2 * width * hidden
        )
        products, squares, valid, counts_row, both, ahead = call(
            first_kernel,
            [
                struct((total, 2 * hidden), F32), column, column, struct((1, requests), F32),
                pltpu.VMEM(weight, BF16), pltpu.VMEM(both_first.shape, BF16),
            ],
            x_mine, gain_row, w_gate, w_up, both_first, counts.reshape(1, requests),
            scratch=(sems, ahead_sems), **args,
        )
        send, score_c, inv, d_both = call(
            second_kernel,
            [struct(half, BF16), column, column, struct((total, 2 * hidden), BF16)],
            x_got, gain_row, w_gate, w_up, ahead, products, squares, down_row, valid,
            scratch=(pltpu.VMEM(weight, BF16), sems), **args,
        )
        (keep,) = call(
            third_kernel, [struct(half, F32)], d_both, both_first, both,
            kept=(1, 2), flops=2 * total * hidden * width,
        )
    else:
        down_row = jnp.sum(w_down.astype(F32) * head.astype(F32)[None, :], axis=-1)[None]
        position = jnp.arange(total, dtype=jnp.int32)[:, None]
        member = position // request_len == jnp.arange(requests, dtype=jnp.int32)[None, :]
        limit = jnp.sum(jnp.where(member, counts[None, :], 0), axis=-1, keepdims=True)
        valid = (position % request_len < limit).astype(F32)
        send, keep, score_c = plain_hidden(
            x_mine, x_got, gain_row, w_gate, w_up, down_row, valid, devices
        )
    total_d = chip_sum(swap_sum(send, keep, devices), devices)
    d_mine = chip_gather(total_d, devices)
    d_got = swap_cores(d_mine, devices)
    padded = part + 3 * requests
    if tiled:
        first = first_rows(256, embed, total_d, False)
        (d_slices,) = call(
            input_kernel, [struct((total, padded), BF16)],
            x_mine, x_got, d_mine, d_got, gain_row, head32, inv,
            score_a, score_b, score_c, valid, counts_row, first, embed,
            kept=(12,), streamed=(13,), flops=2 * flops, room=2 * part * width,
            scratch=(
                pltpu.VMEM((total, width), BF16), pltpu.VMEM((part - 256, width), BF16),
                pltpu.SemaphoreType.DMA((-(-part // 128),)),
            ),
        )
    else:
        d_slices = plain_input(x_mine, x_got, d_mine, d_got, gain_row, head_row, valid, embed)
        score = jnp.where(member, valid * (score_a + score_c), 0.0)
        extra = split3(jnp.sum(score, axis=0)).reshape(1, requests * 3)
        extra = jnp.broadcast_to(extra, (total, requests * 3))
        d_slices = jnp.concatenate([d_slices, extra], axis=-1)
    back = exchange(d_slices.reshape(devices, rows, padded))
    if tiled:
        guidance, rewards = call(
            final_kernel, [struct((rows, voc), BF16), struct((1, requests), F32)],
            probs, back, counts_row, kept=(0,),
            scratch=(pltpu.VMEM((rows, voc), F32),),
        )
        return (guidance, rewards.reshape(requests))
    sums = jnp.sum(back[:, 0, part:].astype(F32).reshape(devices, requests, 3), axis=(0, 2))
    rewards = sums / counts.astype(F32)
    d_probs = back[:, :, :part].transpose(1, 0, 2).reshape(rows, voc).astype(F32)
    d_logits = probs32 * (d_probs - jnp.sum(probs32 * d_probs, axis=-1, keepdims=True))
    guidance = (math.sqrt(VOC) * d_logits).astype(BF16)
    return (guidance, rewards)


def solution(mesh):
    placed = (
        P(("groups", "dp"), None),
        P("dp", None),
        P(),
        P(None, "dp"),
        P(None, "dp"),
        P("dp", None),
        P(),
        P("groups"),
    )
    return jax.shard_map(
        body,
        mesh=mesh,
        in_specs=placed,
        out_specs=(P(("groups", "dp"), None), P("groups")),
        check_vma=False,
    )
```

```python
import functools
import math

import jax
import jax.numpy as jnp
from jax import lax
from jax.experimental import pallas as pl
from jax.experimental.pallas import tpu as pltpu
from jax.sharding import PartitionSpec as P

VOC = 32000
F32, BF16 = jnp.float32, jnp.bfloat16
VMEM_BYTES = 12 * 1024 * 1024


def swap_cores(value, devices):
    return lax.ppermute(value, "dp", [(i, i ^ 1) for i in range(devices)])


def exchange(blocks):
    return lax.all_to_all(blocks, "dp", split_axis=0, concat_axis=0, tiled=True)


def exchange_chips(blocks, devices):
    groups = [list(range(core, devices, 2)) for core in range(2)]
    return lax.all_to_all(
        blocks, "dp", split_axis=0, concat_axis=0, axis_index_groups=groups, tiled=True
    )


def split3(value):
    hi = lax.reduce_precision(value, 8, 7)
    rest = value - hi
    mid = lax.reduce_precision(rest, 8, 7)
    low = rest - mid
    return jnp.stack([hi, mid, low], axis=-1).astype(BF16)


HBM_SPEC = pl.BlockSpec(memory_space=pltpu.HBM)
VMEM_SPEC = pl.BlockSpec(memory_space=pltpu.VMEM)
SMEM_SPEC = pl.BlockSpec(memory_space=pltpu.SMEM)


WINDOW = 128


def call(kernel, outs, *args, streamed=(), kept=(), scalars=(), flops=0, scratch=(), room=0):
    size = sum(math.prod(a.shape) * a.dtype.itemsize for a in args)
    places = {i: pltpu.HBM for i in streamed} | {i: pltpu.VMEM for i in kept}
    specs = [
        HBM_SPEC if i in streamed else SMEM_SPEC if i in scalars else VMEM_SPEC
        for i in range(len(args))
    ]
    return pl.pallas_call(
        kernel,
        out_shape=outs,
        in_specs=specs,
        out_specs=[VMEM_SPEC] * len(outs),
        scratch_shapes=list(scratch),
        compiler_params=pltpu.CompilerParams(vmem_limit_bytes=VMEM_BYTES + room),
        cost_estimate=pl.CostEstimate(flops=flops, bytes_accessed=size, transcendentals=0),
    )(*[
        pltpu.with_memory_space_constraint(a, places[i]) if i in places else a
        for i, a in enumerate(args)
    ])


class Stream:
    def __init__(self, copies):
        self.copies = copies
        self.done = 0
        for copy in copies[:WINDOW]:
            copy.start()

    def wait(self, count):
        while self.done < count:
            self.copies[self.done].wait()
            self.done += 1
            if self.done + WINDOW <= len(self.copies):
                self.copies[self.done + WINDOW - 1].start()


def struct(shape, dtype):
    return jax.ShapeDtypeStruct(shape, dtype)


def this_core():
    return lax.axis_index("dp") % 2


def span(start, size):
    return pl.ds(pl.multiple_of(start, size), size)


def softmax_kernel(logits_ref, out_ref, probs_ref):
    devices, _, part = out_ref.shape
    x = logits_ref[...].astype(F32)
    e = jnp.exp(x - jnp.max(x, axis=-1, keepdims=True))
    probs = e * (1.0 / jnp.sum(e, axis=-1, keepdims=True))
    probs_ref[...] = probs
    for d in range(devices):
        out_ref[d] = probs[:, d * part : (d + 1) * part].astype(BF16)


def final_kernel(probs_ref, back_ref, counts_ref, out_ref, rewards_ref, d_ref):
    devices, _, padded = back_ref.shape
    part = out_ref.shape[1] // devices
    requests = counts_ref.shape[1]
    sums = jnp.zeros((1, requests), F32)
    for d in range(devices):
        block = back_ref[d].astype(F32)
        d_ref[:, d * part : (d + 1) * part] = block[:, :part]
        for i in range(3):
            start = part + i * requests
            sums += block[:1, start : start + requests]
    rewards_ref[...] = sums / counts_ref[...]
    probs, d_probs = probs_ref[...], d_ref[...]
    mean = jnp.sum(probs * d_probs, axis=-1, keepdims=True)
    out_ref[...] = (math.sqrt(VOC) * (probs * (d_probs - mean))).astype(BF16)


def valid_column(counts, total):
    requests = counts.shape[1]
    length = total // requests
    position = lax.broadcasted_iota(jnp.int32, (total, requests), 0)
    start = length * lax.broadcasted_iota(jnp.int32, (total, requests), 1)
    inside = (position >= start) & (position < start + counts)
    return jnp.sum(jnp.where(inside, 1.0, 0.0), axis=-1, keepdims=True)


def bring(source_ref, out_ref, sems, columns):
    fine = 128
    return [
        pltpu.make_async_copy(
            source_ref.at[pl.ds(i, fine), columns], out_ref.at[pl.ds(i, fine)], sems.at[i // fine]
        )
        for i in range(0, out_ref.shape[0], fine)
    ]


def ready_kernel(split, source_ref, after_ref, out_ref, sems):
    del after_ref
    width = out_ref.shape[1]
    columns = span((1 - this_core()) * width, width) if split else pl.ds(0, width)
    copies = bring(source_ref, out_ref, sems, columns)
    for copy in copies:
        copy.start()
    for copy in copies:
        copy.wait()


def first_rows(rows, source, after, split):
    width = source.shape[1] // 2 if split else source.shape[1]
    return call(
        functools.partial(ready_kernel, split), [pltpu.VMEM((rows, width), source.dtype)],
        source, after, streamed=(0,), scratch=(pltpu.SemaphoreType.DMA((rows // 128,)),),
    )[0]


def half_kernel(other, slices_ref, embed_ref, head_ref, *rest):
    if other:
        ready_ref, out_ref, score_ref, next_ref, table, acc, sems, next_sems = rest
    else:
        ready_ref, out_ref, score_ref, table, acc, sems = rest
    chips, total, own = out_ref.shape
    part, ready = embed_ref.shape[0], ready_ref.shape[0]
    core = this_core()
    half = (1 - core) if other else core
    columns = span(half * chips * own, chips * own)
    tile, fine = 256, 128
    stream = Stream([
        pltpu.make_async_copy(
            embed_ref.at[pl.ds(i, min(fine, part - i)), columns],
            table.at[pl.ds(i - ready, min(fine, part - i))],
            sems.at[i // fine],
        )
        for i in range(ready, part, fine)
    ])
    following = []
    if other:
        following = bring(embed_ref, next_ref, next_sems, span(core * chips * own, chips * own))
        for copy in following:
            copy.start()
    acc[...] = jnp.dot(slices_ref[:, :ready], ready_ref[...], preferred_element_type=F32)
    for start in range(ready, part, tile):
        end = min(start + tile, part)
        stream.wait(-(-(end - ready) // fine))
        acc[...] += jnp.dot(
            slices_ref[:, start:end], table[start - ready : end - ready],
            preferred_element_type=F32,
        )
    score_ref[...] = jnp.sum(
        acc[...] * head_ref[:, columns].astype(F32), axis=-1, keepdims=True
    )
    for j in range(chips):
        out_ref[j] = acc[:, j * own : (j + 1) * own].astype(out_ref.dtype)
    for copy in following:
        copy.wait()


def early_kernel(
    head_ref, down_ref, embed_ref, after_ref,
    out_ref, head_row, first, table, head_copy, sems, head_sem, first_sems,
):
    del after_ref
    width, lanes = down_ref.shape[1], 128
    steps = sems.shape[0]
    skip = lax.axis_index("groups") * (down_ref.shape[0] // lanes - steps)

    def copy(j):
        source = down_ref.at[span((skip + j) * lanes, lanes)]
        return pltpu.make_async_copy(source, table.at[span(j * lanes, lanes)], sems.at[j])

    bring_head = pltpu.make_async_copy(head_ref, head_copy, head_sem)
    bring_head.start()
    for j in range(steps):
        copy(j).start()
    half = first.shape[1]
    others = bring(embed_ref, first, first_sems, span((1 - this_core()) * half, half))
    for other in others:
        other.start()
    bring_head.wait()
    head = head_copy[...].astype(F32).reshape(1, width)
    head_row[...] = head

    def step(j, _):
        copy(j).wait()
        rows = span(j * lanes, lanes)
        total = jnp.zeros((lanes, lanes), F32)
        for k in range(0, width, lanes):
            total += table[rows, k : k + lanes].astype(F32) * head[:, k : k + lanes]
        out_ref[:, rows] = jnp.sum(total.T, axis=0, keepdims=True)
        return 0

    lax.fori_loop(0, steps, step, 0)
    for other in others:
        other.wait()


def bring_blocks(gate_ref, up_ref, both, half, blocks, own, chips, sems):
    hidden = gate_ref.shape[1]
    return [
        pltpu.make_async_copy(
            source.at[span((half * chips + j) * own, own)],
            both.at[pl.ds((j - blocks[0]) * own, own), pl.ds(k * hidden, hidden)],
            sems.at[k, j - blocks[0]],
        )
        for j in blocks
        for k, source in enumerate((gate_ref, up_ref))
    ]


def weight_rows(ready, both, own):
    skip = ready.shape[0] // own if ready is not None else 0

    def weights(j):
        if j < skip:
            return ready[j * own : (j + 1) * own]
        return both[(j - skip) * own : (j - skip + 1) * own]

    return skip, weights


def forward_half(x_ref, gain_ref, half, sums, weights, wait):
    chips, _, own = x_ref.shape
    products, squares = sums
    scaled = []
    wide = jnp.zeros(x_ref.shape[1:], F32)
    for j in range(chips):
        x = x_ref[j].astype(F32)
        wide = wide + x * x
        gain = gain_ref[:, span((half * chips + j) * own, own)].astype(F32)
        scaled.append((x * gain).astype(BF16))
    squares = squares + jnp.sum(wide, axis=-1, keepdims=True)
    for j in range(chips):
        wait(j)
        products = products + jnp.dot(scaled[j], weights(j), preferred_element_type=F32)
    return products, squares


def backward_half(d_both, weights, out_ref):
    contract = (((1,), (1,)), ((), ()))
    for j in range(out_ref.shape[0]):
        part = lax.dot_general(d_both, weights(j), contract, preferred_element_type=F32)
        out_ref[j] = part.astype(out_ref.dtype)


def first_kernel(
    x_ref, gain_ref, gate_ref, up_ref, counts_ref,
    products_ref, squares_ref, valid_ref, counts_row, both, ahead, sems, ahead_sems,
):
    chips, _, own = x_ref.shape
    core = this_core()
    skip, weights = weight_rows(None, both, own)
    blocks = range(skip, chips)
    stream = Stream(bring_blocks(gate_ref, up_ref, both, core, blocks, own, chips, sems))
    blocks = range(ahead.shape[0] // own)
    following = bring_blocks(gate_ref, up_ref, ahead, 1 - core, blocks, own, chips, ahead_sems)
    for copy in following:
        copy.start()
    counts = counts_ref[...]
    valid_ref[...] = valid_column(counts, valid_ref.shape[0])
    counts_row[...] = counts.astype(F32)
    sums = (jnp.zeros(products_ref.shape, F32), jnp.zeros(squares_ref.shape, F32))
    products_ref[...], squares_ref[...] = forward_half(
        x_ref, gain_ref, core, sums, weights, lambda j: stream.wait(2 * (j - skip + 1))
    )
    for copy in following:
        copy.wait()


def second_kernel(
    x_ref, gain_ref, gate_ref, up_ref, ready_ref, products_ref, squares_ref, down_a, down_b, valid_ref,
    send_ref, score_ref, inv_ref, d_both_ref, both, sems,
):
    chips, total, own = x_ref.shape
    width, hidden = gate_ref.shape
    half = 1 - this_core()
    skip, weights = weight_rows(ready_ref, both, own)
    blocks = range(skip, chips)
    stream = Stream(bring_blocks(gate_ref, up_ref, both, half, blocks, own, chips, sems))
    sums = (products_ref[...], squares_ref[...])
    products, squares = forward_half(
        x_ref, gain_ref, half, sums, weights, lambda j: stream.wait(2 * (j - skip + 1))
    )
    inv = lax.rsqrt(squares / width + 1e-05)
    inv_ref[...] = inv
    a, b = products[:, :hidden] * inv, products[:, hidden:] * inv
    sigma = jax.nn.sigmoid(a)
    active = a * sigma
    first_group = lax.axis_index("groups") == 0
    down = jnp.where(first_group, down_a[...], down_b[...])
    rest = jnp.where(first_group, down_b[...], down_a[...])
    down = jnp.concatenate([down, rest[:, 2 * rest.shape[1] - hidden :]], axis=-1)
    rounded = (active * b).astype(BF16).astype(F32)
    score_ref[...] = jnp.sum(rounded * down, axis=-1, keepdims=True)
    d_hidden = valid_ref[...] * down
    d_both_ref[:, :hidden] = (d_hidden * b * sigma * (1.0 + a * (1.0 - sigma))).astype(BF16)
    d_both_ref[:, hidden:] = (d_hidden * active).astype(BF16)
    backward_half(d_both_ref[...], weights, send_ref)


def third_kernel(d_both_ref, both_ref, keep_ref):
    _, weights = weight_rows(None, both_ref, keep_ref.shape[2])
    backward_half(d_both_ref[...], weights, keep_ref)


def input_kernel(
    mine_ref, got_ref, d_mine_ref, d_got_ref, gain_ref, head_ref, inv_ref,
    score_a_ref, score_b_ref, score_c_ref, valid_ref, counts_ref, ready_ref, embed_ref,
    out_ref, dx_ref, table, sems,
):
    chips, total, own = mine_ref.shape
    voc = embed_ref.shape[0]
    requests = counts_ref.shape[1]
    width = 2 * chips * own
    core = this_core()
    ready = ready_ref.shape[0]
    tile, fine = 256, 128
    steps = (voc - ready) // tile
    last = ready + steps * tile

    def copy(start, size):
        return pltpu.make_async_copy(
            embed_ref.at[pl.ds(start, size)],
            table.at[pl.ds(start - ready, size)],
            sems.at[start // fine],
        )

    def pieces(start, end):
        return [copy(start + i, min(fine, end - start - i)) for i in range(0, end - start, fine)]

    def step_pieces(j):
        start = pl.multiple_of(ready + j * tile, fine)
        return [copy(pl.multiple_of(start + i, fine), fine) for i in range(0, tile, fine)]

    for piece in pieces(ready, voc):
        piece.start()
    sources = ((mine_ref, d_mine_ref, core), (got_ref, d_got_ref, 1 - core))
    wide = jnp.zeros((total, own), F32)
    for x_ref, d_ref, half in sources:
        for j in range(chips):
            gain = gain_ref[:, span((half * chips + j) * own, own)].astype(F32)
            wide += d_ref[j].astype(F32) * gain * x_ref[j].astype(F32)
    inv = inv_ref[...]
    weight = inv * inv * inv * (jnp.sum(wide, axis=-1, keepdims=True) / width)
    valid = valid_ref[...]
    request = lax.broadcasted_iota(jnp.int32, (total, requests), 0) // (total // requests)
    for x_ref, d_ref, half in sources:
        for j in range(chips):
            columns = span((half * chips + j) * own, own)
            x = x_ref[j].astype(F32)
            g = d_ref[j].astype(F32) * gain_ref[:, columns].astype(F32)
            dx = inv * g - x * weight
            dx_ref[:, columns] = (dx + valid * head_ref[:, columns].astype(F32)).astype(BF16)
    score = valid * (score_a_ref[...] + score_b_ref[...] + score_c_ref[...])
    member = request == lax.broadcasted_iota(jnp.int32, (total, requests), 1)
    value = jnp.sum(jnp.where(member, score, 0.0), axis=0, keepdims=True)
    parts = []
    for _ in range(3):
        piece = value.astype(BF16).astype(F32)
        parts.append(piece)
        value = value - piece
    for i, piece in enumerate(parts):
        start = voc + i * requests
        spread = jnp.broadcast_to(piece, (total, requests)).astype(BF16)
        out_ref[:, start : start + requests] = spread
    contract = (((1,), (1,)), ((), ()))

    def product(weights):
        return lax.dot_general(
            dx_ref[...], weights, contract, preferred_element_type=F32
        ).astype(BF16)

    out_ref[:, :ready] = product(ready_ref[...])

    def step(j, _):
        for piece in step_pieces(j):
            piece.wait()

        rows = pl.ds(pl.multiple_of(j * tile, tile), tile)
        out_ref[:, pl.ds(pl.multiple_of(ready + j * tile, tile), tile)] = product(table[rows, :])
        return 0

    lax.fori_loop(0, steps, step, 0)
    if last < voc:
        for piece in pieces(last, voc):
            piece.wait()
        out_ref[:, last:voc] = product(table[last - ready :, :])


def swap_sum(send, keep, devices):
    return (keep.astype(F32) + swap_cores(send, devices).astype(F32)).astype(BF16)


def chip_sum(half, devices):
    return jnp.sum(exchange_chips(half, devices).astype(F32), axis=0).astype(BF16)


def chip_gather(total, devices):
    return exchange_chips(jnp.broadcast_to(total[None], (devices // 2,) + total.shape), devices)


def pick(blocks, index):
    return lax.dynamic_index_in_dim(blocks, index, 0, keepdims=False)


def split_halves(part, devices):
    total, width = part.shape
    core = lax.axis_index("dp") % 2
    blocks = part.reshape(total, 2, devices // 2, width // devices).transpose(1, 2, 0, 3)
    return pick(blocks, 1 - core).astype(BF16), pick(blocks, core)


def join_halves(mine, got):
    core = lax.axis_index("dp") % 2
    blocks = jnp.where(core == 1, jnp.stack([got, mine]), jnp.stack([mine, got]))
    _, chips, total, own = blocks.shape
    return blocks.transpose(2, 0, 1, 3).reshape(total, 2 * chips * own).astype(F32)


def norm_scale(x0):
    return lax.rsqrt(jnp.mean(x0 * x0, axis=-1, keepdims=True) + 1e-05)


def plain_half(slices, embed, head_row, devices):
    part = jnp.dot(slices, embed, preferred_element_type=F32)
    score = jnp.sum(part * head_row.astype(F32), axis=-1, keepdims=True)
    return *split_halves(part, devices), score


def plain_hidden(mine, got, gain_row, w_gate, w_up, down, valid, devices):
    x0 = join_halves(mine, got)
    normed = (x0 * norm_scale(x0) * gain_row.astype(F32)).astype(BF16)
    a = jnp.dot(normed, w_gate, preferred_element_type=F32)
    b = jnp.dot(normed, w_up, preferred_element_type=F32)
    sigma = jax.nn.sigmoid(a)
    active = a * sigma
    hidden = (active * b).astype(BF16).astype(F32)
    d_hidden = valid * down
    d_gate = (d_hidden * b * sigma * (1.0 + a * (1.0 - sigma))).astype(BF16)
    d_up = (d_hidden * active).astype(BF16)
    part = jnp.einsum("tf,df->td", d_gate, w_gate, preferred_element_type=F32)
    part = part + jnp.einsum("tf,df->td", d_up, w_up, preferred_element_type=F32)
    return *split_halves(part, devices), jnp.sum(hidden * down, axis=-1, keepdims=True)


def plain_input(mine, got, d_mine, d_got, gain_row, head_row, valid, embed):
    x0 = join_halves(mine, got)
    inv = norm_scale(x0)
    scaled = join_halves(d_mine, d_got) * gain_row.astype(F32)
    dx = inv * scaled - x0 * inv * inv * inv * jnp.mean(scaled * x0, axis=-1, keepdims=True)
    dx = (dx + valid * head_row.astype(F32)).astype(BF16)
    return jnp.einsum("td,vd->tv", dx, embed, preferred_element_type=F32).astype(BF16)


def body(logits, embed, norm_gain, w_gate, w_up, w_down, head, counts):
    devices = lax.axis_size("dp")
    rows, voc = logits.shape
    part = voc // devices
    width = embed.shape[1]
    hidden = w_gate.shape[1]
    own, chips = width // devices, devices // 2
    requests = counts.shape[0]
    total = rows * devices
    request_len = total // requests
    tiled = own % 128 == 0 and hidden % 128 == 0 and total % 16 == 0 and part % 16 == 0 and part > 512
    tiled = tiled and lax.axis_size("groups") == 2
    head_row, gain_row = head.reshape(1, width), norm_gain.reshape(1, width)
    if tiled:
        blocked, probs = call(
            softmax_kernel,
            [struct((devices, rows, part), BF16), pltpu.VMEM((rows, voc), F32)], logits,
        )
    else:
        probs32 = jax.nn.softmax(logits.astype(F32), axis=-1)
        blocked = probs32.astype(BF16).reshape(rows, devices, part).transpose(1, 0, 2)
    slices = exchange(blocked).reshape(total, part)
    column = struct((total, 1), F32)
    half = (chips, total, own)
    flops = total * part * width
    if tiled:
        ready = 256
        steps, ready = -(-hidden // 256), 256
        ahead = pltpu.VMEM((ready, width // 2), BF16)
        ahead_sems = pltpu.SemaphoreType.DMA((ready // 128,))
        down_a, head32, first = call(
            early_kernel, [struct((1, steps * 128), F32), struct((1, width), F32), ahead],
            head, w_down, embed, blocked,
            streamed=(0, 1, 2), flops=2 * hidden * width, room=2 * hidden * width,
            scratch=(
                pltpu.VMEM((steps * 128, width), BF16), pltpu.VMEM((width,), BF16),
                pltpu.SemaphoreType.DMA((steps,)), pltpu.SemaphoreType.DMA, ahead_sems,
            ),
        )
        down_b = lax.ppermute(down_a, "groups", [(0, 1), (1, 0)])
        args = dict(streamed=(1,), kept=(3,), flops=flops, room=part * width)
        scratch = (
            pltpu.VMEM((part - ready, width // 2), BF16), pltpu.VMEM((total, width // 2), F32),
            pltpu.SemaphoreType.DMA((-(-part // 128),)),
        )
        send, score_a, first = call(
            functools.partial(half_kernel, True), [struct(half, BF16), column, ahead],
            slices, embed, head32, first, scratch=(*scratch, ahead_sems), **args,
        )
        send, down_b = lax.optimization_barrier((send, down_b))
        keep, score_b = call(
            functools.partial(half_kernel, False), [struct(half, F32), column],
            slices, embed, head32, first, scratch=scratch, **args,
        )
    else:
        send, keep, score_a = plain_half(slices, embed, head_row, devices)
    summed = swap_sum(send, keep, devices)
    x_mine = chip_gather(chip_sum(summed, devices), devices)
    x_got = swap_cores(x_mine, devices)
    if tiled:
        sems, ahead_sems = pltpu.SemaphoreType.DMA((2, chips)), pltpu.SemaphoreType.DMA((2, 2))
        args = dict(streamed=(2, 3), flops=2 * total * hidden * width, room=2 * width * hidden)
        products, squares, valid, counts_row, both, ahead = call(
            first_kernel,
            [
                struct((total, 2 * hidden), F32), column, column, struct((1, requests), F32),
                pltpu.VMEM((width // 2, 2 * hidden), BF16), pltpu.VMEM((2 * own, 2 * hidden), BF16),
            ],
            x_mine, gain_row, w_gate, w_up, counts.reshape(1, requests),
            scratch=(sems, ahead_sems), **args,
        )
        send, score_c, inv, d_both = call(
            second_kernel,
            [struct(half, BF16), column, column, struct((total, 2 * hidden), BF16)],
            x_got, gain_row, w_gate, w_up, ahead, products, squares, down_a, down_b, valid,
            scratch=(pltpu.VMEM((width // 2 - 2 * own, 2 * hidden), BF16), sems), kept=(4,), **args,
        )
        (keep,) = call(
            third_kernel, [struct(half, F32)], d_both, both,
            kept=(1,), flops=2 * total * hidden * width,
        )
    else:
        down_row = jnp.sum(w_down.astype(F32) * head.astype(F32)[None, :], axis=-1)[None]
        position = jnp.arange(total, dtype=jnp.int32)[:, None]
        member = position // request_len == jnp.arange(requests, dtype=jnp.int32)[None, :]
        limit = jnp.sum(jnp.where(member, counts[None, :], 0), axis=-1, keepdims=True)
        valid = (position % request_len < limit).astype(F32)
        send, keep, score_c = plain_hidden(
            x_mine, x_got, gain_row, w_gate, w_up, down_row, valid, devices
        )
    total_d = chip_sum(swap_sum(send, keep, devices), devices)
    d_mine = chip_gather(total_d, devices)
    d_got = swap_cores(d_mine, devices)
    padded = part + 3 * requests
    if tiled:
        first = first_rows(256, embed, total_d, False)
        (d_slices,) = call(
            input_kernel, [struct((total, padded), BF16)],
            x_mine, x_got, d_mine, d_got, gain_row, head32, inv,
            score_a, score_b, score_c, valid, counts_row, first, embed,
            kept=(12,), streamed=(13,), flops=2 * flops, room=2 * part * width,
            scratch=(
                pltpu.VMEM((total, width), BF16), pltpu.VMEM((part - 256, width), BF16),
                pltpu.SemaphoreType.DMA((-(-part // 128),)),
            ),
        )
    else:
        d_slices = plain_input(x_mine, x_got, d_mine, d_got, gain_row, head_row, valid, embed)
        score = jnp.where(member, valid * (score_a + score_c), 0.0)
        extra = split3(jnp.sum(score, axis=0)).reshape(1, requests * 3)
        extra = jnp.broadcast_to(extra, (total, requests * 3))
        d_slices = jnp.concatenate([d_slices, extra], axis=-1)
    back = exchange(d_slices.reshape(devices, rows, padded))
    if tiled:
        guidance, rewards = call(
            final_kernel, [struct((rows, voc), BF16), struct((1, requests), F32)],
            probs, back, counts_row, kept=(0,),
            scratch=(pltpu.VMEM((rows, voc), F32),),
        )
        return (guidance, rewards.reshape(requests))
    sums = jnp.sum(back[:, 0, part:].astype(F32).reshape(devices, requests, 3), axis=(0, 2))
    rewards = sums / counts.astype(F32)
    d_probs = back[:, :, :part].transpose(1, 0, 2).reshape(rows, voc).astype(F32)
    d_logits = probs32 * (d_probs - jnp.sum(probs32 * d_probs, axis=-1, keepdims=True))
    guidance = (math.sqrt(VOC) * d_logits).astype(BF16)
    return (guidance, rewards)


def solution(mesh):
    placed = (
        P(("groups", "dp"), None),
        P("dp", None),
        P(),
        P(None, "dp"),
        P(None, "dp"),
        P("dp", None),
        P(),
        P("groups"),
    )
    return jax.shard_map(
        body,
        mesh=mesh,
        in_specs=placed,
        out_specs=(P(("groups", "dp"), None), P("groups")),
        check_vma=False,
    )
```
